32 devices in a mesh: dp: 4 (over y, x), fsdp: 8 (over z, core).
Axes of the slice: x: 2, y: 2, z: 4, core: 2. Of those that a mesh axis runs over, the one named last changes fastest.
Arguments:
- inputs: bfloat16 [32, 512, 512], P(('dp', 'fsdp')), may hold values from -5 to 5
- segments: int32 [32, 512], P(('dp', 'fsdp')), may hold values from 0 to 7, never falling along the last dimension, each value on 1 to 256 neighbouring positions
- buckets: int32 [1023], replicated, may hold values from 0 to 31
- cotangent: bfloat16 [32, 512, 512], P(('dp', 'fsdp')), may hold values from -12 to 12
- ffn_norm: bfloat16 [2, 2, 512], P(None, None, ('dp', 'fsdp')), may hold values from -0.59765625 to 0.59765625
- ffn_in: bfloat16 [2, 512, 2048], P(None, ('dp', 'fsdp')), may hold values from -0.25 to 0.25
- ffn_in_bias: bfloat16 [2, 2048], P(None, ('dp', 'fsdp')), may hold values from -2.5 to 2.5
- ffn_out: bfloat16 [2, 2048, 512], P(None, ('dp', 'fsdp')), may hold values from -0.125 to 0.125
- ffn_out_bias: bfloat16 [2, 512], P(None, ('dp', 'fsdp')), may hold values from -2.5 to 2.5
- attn_norm: bfloat16 [2, 512], P(None, ('dp', 'fsdp')), may hold values from -0.59765625 to 0.59765625
- qkv_weight: bfloat16 [512, 1536], P(('dp', 'fsdp')), may hold values from -0.25 to 0.25
- attn_out: bfloat16 [512, 512], P(('dp', 'fsdp')), may hold values from -2 to 2
- attn_out_bias: bfloat16 [512], P(('dp', 'fsdp')), may hold values from -2.5 to 2.5
- rel_table: bfloat16 [256], P(('dp', 'fsdp')), may hold values from -3 to 3
- conv_norm: bfloat16 [2, 512], P(None, ('dp', 'fsdp')), may hold values from -0.59765625 to 0.59765625
- glu_weight: bfloat16 [512, 1024], P(('dp', 'fsdp')), may hold values from -0.25 to 0.25
- glu_bias: bfloat16 [1024], P(('dp', 'fsdp')), may hold values from -2.5 to 2.5
- depth_kernel: bfloat16 [32, 512], P(None, ('dp', 'fsdp')), may hold values from -1 to 1
- batch_norm: bfloat16 [2, 512], P(None, ('dp', 'fsdp')), may hold values from -0.59765625 to 0.59765625
- conv_out: bfloat16 [512, 512], P(('dp', 'fsdp')), may hold values from -0.25 to 0.25
- conv_out_bias: bfloat16 [512], P(('dp', 'fsdp')), may hold values from -2.5 to 2.5
- final_norm: bfloat16 [2, 512], P(None, ('dp', 'fsdp')), may hold values from -0.59765625 to 0.59765625
Outputs:
- output: bfloat16 [32, 512, 512], P(('dp', 'fsdp'))
- grad_inputs: float32 [32, 512, 512], P(('dp', 'fsdp'))
- grad_ffn_norm: float32 [2, 2, 512], P(None, None, ('dp', 'fsdp'))
- grad_ffn_in: float32 [2, 512, 2048], P(None, ('dp', 'fsdp'))
- grad_ffn_in_bias: float32 [2, 2048], P(None, ('dp', 'fsdp'))
- grad_ffn_out: float32 [2, 2048, 512], P(None, ('dp', 'fsdp'))
- grad_ffn_out_bias: float32 [2, 512], P(None, ('dp', 'fsdp'))
- grad_attn_norm: float32 [2, 512], P(None, ('dp', 'fsdp'))
- grad_qkv_weight: float32 [512, 1536], P(('dp', 'fsdp'))
- grad_attn_out: float32 [512, 512], P(('dp', 'fsdp'))
- grad_attn_out_bias: float32 [512], P(('dp', 'fsdp'))
- grad_rel_table: float32 [256], P(('dp', 'fsdp'))
- grad_conv_norm: float32 [2, 512], P(None, ('dp', 'fsdp'))
- grad_glu_weight: float32 [512, 1024], P(('dp', 'fsdp'))
- grad_glu_bias: float32 [1024], P(('dp', 'fsdp'))
- grad_depth_kernel: float32 [32, 512], P(None, ('dp', 'fsdp'))
- grad_batch_norm: float32 [2, 512], P(None, ('dp', 'fsdp'))
- grad_conv_out: float32 [512, 512], P(('dp', 'fsdp'))
- grad_conv_out_bias: float32 [512], P(('dp', 'fsdp'))
- grad_final_norm: float32 [2, 512], P(None, ('dp', 'fsdp'))
The draws below stay inside these ranges and needn't reach their ends.
Inputs may be any that keep to these rules, and one draw needn't show every extreme that they name: `segments`: segment numbers never fall along a row; each utterance holds 1 to 256 frames.
All inputs are finite; a program needn't handle non-finite values.
Results may differ from the reference program's by a relative error of at most 0.02.
Values may be sent and summed in bfloat16 or wider, within the bound.
A program may use at most 192 MiB of HBM per device.

```python
import math
import jax
import jax.numpy as jnp
import numpy as np
from jax import lax

D = 512
FF = 2048
HEADS = 8
HEAD_DIM = 64
KERNEL = 32
BUCKETS = 32
L = 512
ROWS = 32


def draw_cotangent(key, part):
    key = jax.random.fold_in(key, 7)
    first = jax.random.fold_in(key, 0)
    rising = 1.0 + 2.0 * jnp.arange(ROWS, dtype=jnp.float32) / max(ROWS - 1, 1)
    values = jnp.clip(jax.random.normal(first, (ROWS, L, D), jnp.float32), -4.0, 4.0)
    return (values * rising[:, None, None]).astype(jnp.bfloat16)


def set_ends(values, rng, low, largest):
    place = [jax.random.randint(jax.random.fold_in(rng, axis), (), 0, length) for axis, length in enumerate(values.shape)]
    widest = values.shape.index(max(values.shape))
    next_to = place[:widest] + [(place[widest] + 1) % values.shape[widest]] + place[widest + 1:]
    return values.at[tuple(place)].set(low).at[tuple(next_to)].set(largest)


def block_scale(key, dims, pieces, smallest, largest):
    factor_of = 1.0
    for dim, blocks in pieces:
        heights = jax.random.uniform(jax.random.fold_in(jax.random.fold_in(key, 6), dim), (blocks,), jnp.float32, smallest / len(pieces), largest / len(pieces))
        factor_of = factor_of * jnp.repeat(jnp.exp(heights), dims[dim] // blocks).reshape((-1,) + (1,) * (len(dims) - 1 - dim))
    return factor_of


def length_profile(amount, total, bound, skew):
    portions = [(1 << 20) // math.isqrt(rank ** skew) + 1 for rank in range(2, amount + 1)]
    surplus, counts = total - bound - (amount - 1), [1] * (amount - 1)
    while surplus > 0:
        movable = [i for i in range(amount - 1) if counts[i] < bound]
        mass, remaining = sum([portions[i] for i in movable]), surplus
        for i in movable:
            addition = min(bound - counts[i], max(1, remaining * portions[i] // mass), surplus)
            counts[i] = counts[i] + addition
            surplus = surplus - addition
    return np.array([bound] + counts)


def ragged(stream_key, count, total, limit, slope):
    if count == 2:
        one = jax.random.randint(stream_key, (), max(1, total - limit), min(limit, total - 1) + 1)
        return jnp.stack([one, total - one])
    tallies = jnp.asarray(length_profile(count, total, limit, slope), jnp.int32)
    pairs = (count - 1) // 2
    giver, sink = tallies[1:1 + 2 * pairs:2], tallies[2:2 + 2 * pairs:2]
    slack = jnp.minimum(giver - 1, limit - sink)
    moved = jax.random.randint(jax.random.fold_in(stream_key, 1), (pairs,), 0, 1 << 20) % (slack + 1)
    tallies = tallies.at[1:1 + 2 * pairs:2].set(giver - moved).at[2:2 + 2 * pairs:2].set(sink + moved)
    return tallies[jax.random.permutation(jax.random.fold_in(stream_key, 2), count)]


def normal_values(own_key, extent, width, limit, cuts=(), kind=jnp.bfloat16):
    gain = block_scale(own_key, extent, cuts, -0.22, 0.18) if cuts else 1.0
    array = jax.random.normal(own_key, extent, jnp.float32) * width * gain
    return jnp.minimum(jnp.maximum(array, -limit), limit).astype(kind)


def setup_inputs(seed: int = 0) -> dict:
    streams_of = jax.random.split(jax.random.key(seed), 23)
    return {
        "inputs": normal_values(streams_of[0], (ROWS, L, D), 1.0, 5.0, ((0, 32),)),
        "segments": jax.vmap(lambda own: jnp.searchsorted(jnp.cumsum(ragged(own, max(4, L // 64), L, L // 2, 2)), jnp.arange(L), side="right"))(jax.random.split(streams_of[1], ROWS)).reshape((ROWS, L)).astype(jnp.int32),
        "buckets": set_ends(jax.random.randint(streams_of[2], (2 * L - 1,), 0, BUCKETS), jax.random.fold_in(streams_of[2], 1), 0, BUCKETS - 1).astype(jnp.int32),
        "cotangent": draw_cotangent(jax.random.fold_in(streams_of[22], 71), 0),
        "ffn_norm": normal_values(streams_of[4], (2, 2, D), 0.2, 0.59765625, ((2, 32),)),
        "ffn_in": normal_values(streams_of[5], (2, D, FF), D ** -0.5, 0.25, ((1, 32),)),
        "ffn_in_bias": normal_values(streams_of[6], (2, FF), 0.5, 2.5, ((1, 32),)),
        "ffn_out": normal_values(streams_of[7], (2, FF, D), FF ** -0.5, 0.125, ((1, 32),)),
        "ffn_out_bias": normal_values(streams_of[8], (2, D), 0.5, 2.5, ((1, 32),)),
        "attn_norm": normal_values(streams_of[9], (2, D), 0.2, 0.59765625, ((1, 32),)),
        "qkv_weight": normal_values(streams_of[10], (D, 3 * D), D ** -0.5, 0.25, ((0, 32),)),
        "attn_out": normal_values(streams_of[11], (D, D), (D // 64) ** -0.5, 2.0, ((0, 32),)),
        "attn_out_bias": normal_values(streams_of[12], (D,), 0.5, 2.5, ((0, 32),)),
        "rel_table": normal_values(streams_of[13], (HEADS * BUCKETS,), 1.0, 3.0, ((0, 32),)),
        "conv_norm": normal_values(streams_of[14], (2, D), 0.2, 0.59765625, ((1, 32),)),
        "glu_weight": normal_values(streams_of[15], (D, 2 * D), D ** -0.5, 0.25, ((0, 32),)),
        "glu_bias": normal_values(streams_of[16], (2 * D,), 0.5, 2.5, ((0, 32),)),
        "depth_kernel": normal_values(streams_of[17], (KERNEL, D), KERNEL ** -0.5, 1.0, ((1, 32),)),
        "batch_norm": normal_values(streams_of[18], (2, D), 0.2, 0.59765625, ((1, 32),)),
        "conv_out": normal_values(streams_of[19], (D, D), D ** -0.5, 0.25, ((0, 32),)),
        "conv_out_bias": normal_values(streams_of[20], (D,), 0.5, 2.5, ((0, 32),)),
        "final_norm": normal_values(streams_of[21], (2, D), 0.2, 0.59765625, ((1, 32),)),
    }


epsilon = 1e-05
highest = lax.Precision.HIGHEST

@jax.custom_vjp
def low(v):
    return lax.optimization_barrier(v.astype(jnp.bfloat16)).astype(jnp.float32)

@jax.custom_vjp
def low_back(v):
    return v

def low_keep(v):
    return (low(v), None)

def low_pass(kept, grad):
    return (grad,)

def back_keep(v):
    return (v, None)

def back_low(kept, grad):
    return (low(grad),)
low.defvjp(low_keep, low_pass)
low_back.defvjp(back_keep, back_low)

def layer_norm(values, params):
    center = values - lax.optimization_barrier(jnp.mean(values, axis=-1, keepdims=True))
    spread = lax.optimization_barrier(jnp.mean(center * center, axis=-1, keepdims=True))
    return center * lax.rsqrt(spread + epsilon) * (1.0 + params[0]) + params[1]

def matmul(left, right):
    return jnp.dot(left, right, precision=highest)

def by_groups(function, arrays):
    size = min(ROWS, max(1, 4096 // L))
    shaped = tuple((item.reshape((ROWS // size, size) + item.shape[1:]) for item in arrays))
    result = lax.map(jax.checkpoint(lambda items: function(*items)), shaped)
    return result.reshape((ROWS,) + result.shape[2:])

def feed_forward(values, norm, weight_in, bias_in, weight_out, bias_out):
    normed = low(layer_norm(values, norm))
    inner = low_back(matmul(normed, weight_in)) + bias_in
    active = low(jax.nn.silu(inner))
    return values + 0.5 * (low_back(matmul(active, weight_out)) + bias_out)

def attention(values, marks, square_bias, norm, mixer, weight_out, bias_out):
    groups = values.shape[0]
    normed = low(layer_norm(values, norm))
    mixed = low(low_back(matmul(normed, mixer))).reshape(groups, L, 3, HEADS, HEAD_DIM)
    queries, keys_all, contents = (mixed[:, :, 0], mixed[:, :, 1], mixed[:, :, 2])
    raw = low_back(jnp.einsum('gihd,gjhd->ghij', queries, keys_all, precision=highest))
    scores = raw * HEAD_DIM ** (-0.5) + square_bias[None]
    same = (marks[:, :, None] == marks[:, None, :])[:, None]
    scores = jnp.where(same, scores, -1e+30)
    weights = low(jax.nn.softmax(scores, axis=-1))
    attended = low(low_back(jnp.einsum('ghij,gjhd->gihd', weights, contents, precision=highest)))
    return values + low_back(matmul(attended.reshape(groups, L, D), weight_out)) + bias_out

def depthwise(gated, kernel, marks):
    half = KERNEL // 2
    padded = jnp.pad(gated, ((0, 0), (half, half), (0, 0)))
    bounds = jnp.pad(marks, ((0, 0), (half, half)), constant_values=-1)
    total = jnp.zeros(gated.shape, gated.dtype)
    for step in range(KERNEL):
        same = (bounds[:, step:step + L] == marks)[:, :, None]
        total = total + jnp.where(same, padded[:, step:step + L], 0.0) * kernel[step]
    return total

def conv_front(values, marks, norm, weight_glu, bias_glu, kernel):
    normed = low(layer_norm(values, norm))
    joined = low_back(matmul(normed, weight_glu)) + bias_glu
    gated = joined[..., :D] * jax.nn.sigmoid(joined[..., D:])
    return depthwise(gated, kernel, marks)

def conv_rest(values, middle, center, inverse, batch, weight_out, bias_out):
    normal = (middle - center) * inverse * (1.0 + batch[0]) + batch[1]
    active = low(jax.nn.silu(normal))
    return values + low_back(matmul(active, weight_out)) + bias_out

def forward(inputs, params, segments, buckets):
    ffn_norm, ffn_in, ffn_in_bias, ffn_out, ffn_out_bias, attn_norm, qkv_weight, attn_out, attn_out_bias, rel_table, conv_norm, glu_weight, glu_bias, depth_kernel, batch_norm, conv_out, conv_out_bias, final_norm = params
    first = by_groups(lambda values: feed_forward(values, ffn_norm[0], ffn_in[0], ffn_in_bias[0], ffn_out[0], ffn_out_bias[0]), (inputs,))
    lines = rel_table.reshape(HEADS, BUCKETS)[:, buckets]
    offsets = jnp.arange(L)[None, :] - jnp.arange(L)[:, None] + L - 1
    square_bias = lines[:, offsets]
    second = by_groups(lambda values, marks: attention(values, marks, square_bias, attn_norm, qkv_weight, attn_out, attn_out_bias), (first, segments))
    middle = by_groups(lambda values, marks: conv_front(values, marks, conv_norm, glu_weight, glu_bias, depth_kernel), (second, segments))
    center = lax.optimization_barrier(jnp.mean(middle, axis=(0, 1)))
    inverse = lax.rsqrt(lax.optimization_barrier(jnp.mean(middle * middle, axis=(0, 1))) - center * center + epsilon)
    third = by_groups(lambda values, mids: conv_rest(values, mids, center, inverse, batch_norm, conv_out, conv_out_bias), (second, middle))
    return by_groups(lambda values: layer_norm(feed_forward(values, ffn_norm[1], ffn_in[1], ffn_in_bias[1], ffn_out[1], ffn_out_bias[1]), final_norm), (third,))

def reference(inputs, segments, buckets, cotangent, ffn_norm, ffn_in, ffn_in_bias, ffn_out, ffn_out_bias, attn_norm, qkv_weight, attn_out, attn_out_bias, rel_table, conv_norm, glu_weight, glu_bias, depth_kernel, batch_norm, conv_out, conv_out_bias, final_norm):
    params = tuple((item.astype(jnp.float32) for item in (ffn_norm, ffn_in, ffn_in_bias, ffn_out, ffn_out_bias, attn_norm, qkv_weight, attn_out, attn_out_bias, rel_table, conv_norm, glu_weight, glu_bias, depth_kernel, batch_norm, conv_out, conv_out_bias, final_norm)))
    result, pullback = jax.vjp(lambda values, weights: forward(values, weights, segments, buckets), inputs.astype(jnp.float32), params)
    grad_values, grads = pullback(cotangent.astype(jnp.float32))
    return (result.astype(jnp.bfloat16), grad_values, grads[0], grads[1], grads[2], grads[3], grads[4], grads[5], grads[6], grads[7], grads[8], grads[9], grads[10], grads[11], grads[12], grads[13], grads[14], grads[15], grads[16], grads[17])
```

```python
import jax
import jax.numpy as jnp
from jax import lax
from jax.experimental import pallas as pl
from jax.experimental.pallas import tpu as pltpu
from jax.sharding import PartitionSpec as P

D = 512
FF = 2048
HEADS = 8
HEAD_DIM = 64
BUCKETS = 32
L = 512
TAPS = 32
PAD = 16
epsilon = 1e-05
F32, BF16 = jnp.float32, jnp.bfloat16

SMALL, IN0, OUT0, QKV, ATT, GLU, CONV, IN1, OUT1, ROWS = 0, 16, 80, 144, 192, 208, 240, 256, 320, 384
(S_FFN, S_FOB, S_ATTN, S_AOB, S_CONV, S_BATCH, S_COB, S_FINAL, S_TAPS, S_ROWS) = (0, 4, 6, 8, 9, 11, 13, 14, 16, 48)
CHUNK = 64


def dot(a, b):
    return jnp.dot(a, b, preferred_element_type=F32)


def dot_nt(a, b):
    return lax.dot_general(a, b, (((1,), (1,)), ((), ())), preferred_element_type=F32)


def dot_tn(a, b):
    return lax.dot_general(a, b, (((0,), (0,)), ((), ())), preferred_element_type=F32)


def chunks(body, carry=None, size=CHUNK):
    def step(i, carry):
        return body(pl.ds(pl.multiple_of(i * size, size), size), carry)

    return lax.fori_loop(0, L // size, step, carry)


def fold(values):
    return jnp.sum(values.reshape(values.shape[0] // 8, 8, values.shape[1]), axis=0)


def zeros8(width=D):
    return jnp.zeros((8, width), F32)


def standard(values):
    values = values.astype(F32)
    center = values - jnp.mean(values, axis=-1, keepdims=True)
    inverse = lax.rsqrt(jnp.mean(center * center, axis=-1, keepdims=True) + epsilon)
    return center * inverse, inverse


def norm_rows(source, target, small, row):
    gain, shift = 1.0 + small[row : row + 1, :], small[row + 1 : row + 2, :]

    def body(rows, carry):
        target[rows, :] = (standard(source[rows, :])[0] * gain + shift).astype(target.dtype)
        return carry

    chunks(body, 0)


def norm_back(source, grad, upstream, result, small, row, grads):
    gain = 1.0 + small[row : row + 1, :]

    def body(rows, carry):
        unit, inverse = standard(source[rows, :])
        given = grad[rows, :]
        inner = given * gain
        back = inverse * (
            inner
            - jnp.mean(inner, axis=-1, keepdims=True)
            - unit * jnp.mean(inner * unit, axis=-1, keepdims=True)
        )
        result[rows, :] = (upstream[rows, :] + back).astype(result.dtype)
        return carry[0] + fold(given * unit), carry[1] + fold(given)

    first, second = chunks(body, (zeros8(), zeros8()))
    grads[row : row + 1, :] = jnp.sum(first, axis=0, keepdims=True)
    grads[row + 1 : row + 2, :] = jnp.sum(second, axis=0, keepdims=True)


def columns(weights, start, block):
    begin = pl.multiple_of(start + 16 * block, 16)
    return weights[:, pl.ds(begin, 16), :].reshape(D, D)


def lines_of(weights, start, block):
    return weights[pl.ds(pl.multiple_of(8 * block, 8), 8), start : start + 64, :].reshape(D, D)


def feed_forward(source, normed, active, slope, result, hold, weights, small, inner_bias, layer):
    begin_in, begin_out = ((IN0, OUT0), (IN1, OUT1))[layer]
    norm_rows(source, normed, small, S_FFN + 2 * layer)

    def block(c, carry):
        cols = pl.ds(pl.multiple_of(c * D, D), D)
        hold[...] = dot(normed[...], columns(weights, begin_in, c))
        bias = inner_bias[layer : layer + 1, cols]

        def body(rows, carry):
            inner = hold[rows, :] + bias
            sigma = jax.nn.sigmoid(inner)
            value = inner * sigma
            active[rows, cols] = value.astype(BF16)
            slope[rows, cols] = (sigma + value * (1.0 - sigma)).astype(BF16)
            return carry

        chunks(body, 0)
        part = dot(active[:, cols], lines_of(weights, begin_out, c))

        @pl.when(c == 0)
        def _():
            result[...] = part

        @pl.when(c > 0)
        def _():
            result[...] += part

        return carry

    lax.fori_loop(0, FF // D, block, 0)
    bias = small[S_FOB + layer : S_FOB + layer + 1, :]

    def body(rows, carry):
        result[rows, :] = source[rows, :].astype(F32) + 0.5 * (result[rows, :] + bias)
        return carry

    chunks(body, 0)


def feed_backward(
    upstream, source, normed, active, slope, result, low, low_in, hold, total, weights, small, out, base, grads, inner_grads, layer
):
    begin_in, begin_out = ((IN0, OUT0), (IN1, OUT1))[layer]

    def start(rows, carry):
        half = 0.5 * upstream[rows, :]
        low[rows, :] = half.astype(BF16)
        return carry + fold(half)

    grads[S_FOB + layer : S_FOB + layer + 1, :] = jnp.sum(chunks(start, zeros8()), axis=0, keepdims=True)

    def block(c, carry):
        cols = pl.ds(pl.multiple_of(c * D, D), D)
        hold[...] = dot_nt(low[...], lines_of(weights, begin_out, c))

        def body(rows, carry):
            grad = hold[rows, :] * slope[rows, cols].astype(F32)
            low_in[rows, :] = grad.astype(BF16)
            return carry + fold(grad)

        inner_grads[layer : layer + 1, cols] = jnp.sum(chunks(body, zeros8()), axis=0, keepdims=True)
        outer = dot_tn(active[:, cols], low[...]).astype(BF16).reshape(8, 64, D)
        out[pl.ds(pl.multiple_of(8 * c, 8), 8), begin_out - base : begin_out - base + 64, :] = outer
        inner = dot_tn(normed[...], low_in[...]).astype(BF16).reshape(32, 16, D)
        out[:, pl.ds(pl.multiple_of(begin_in - base + 16 * c, 16), 16), :] = inner
        part = dot_nt(low_in[...], columns(weights, begin_in, c))

        @pl.when(c == 0)
        def _():
            total[...] = part

        @pl.when(c > 0)
        def _():
            total[...] += part

        return carry

    lax.fori_loop(0, FF // D, block, 0)
    norm_back(source, total, upstream, result, small, S_FFN + 2 * layer, grads)


def bucket_choice(buckets):
    return (lax.broadcasted_iota(jnp.int32, (BUCKETS, 2 * L), 0) == buckets[...]).astype(F32)


def attention_forward(source, normed, mixed, probs, joined, result, lines, hold, weights, small, table, buckets, bounds, marks):
    norm_rows(source, normed, small, S_ATTN)

    def mix(c, carry):
        cols = pl.ds(pl.multiple_of(c * D, D), D)
        mixed[:, cols] = dot(normed[...], columns(weights, QKV, c)).astype(BF16)
        return carry

    lax.fori_loop(0, 3, mix, 0)
    lines[...] = dot(table[...].astype(BF16), bucket_choice(buckets).astype(BF16))
    lane = lax.broadcasted_iota(jnp.int32, (1, 128), 1)
    size = 128

    def pair(index, carry):
        begin = pl.multiple_of(128 * index, 128)
        keys = mixed[:, pl.ds(D + begin, 128)]
        contents = mixed[:, pl.ds(2 * D + begin, 128)]
        for block in range(L // size):
            rows = pl.ds(block * size, size)
            query = mixed[rows, pl.ds(begin, 128)]
            same = bounds[PAD + block * size : PAD + (block + 1) * size, 0:1] == marks[...]
            parts = []
            for half in range(2):
                head = 2 * index + half
                here = (lane // HEAD_DIM) == half
                raw = dot_nt(jnp.where(here, query, jnp.zeros_like(query)), keys)
                window = lines[pl.ds(head, 1), 384 - block * size : 1024 - block * size]
                square = pltpu.roll(jnp.broadcast_to(window, (size, 640)), 513, 1, stride=1, stride_axis=0)
                scores = jnp.where(same, raw * HEAD_DIM ** (-0.5) + square[:, :L], -1e30)
                raised = jnp.exp(scores - jnp.max(scores, axis=1, keepdims=True))
                share = (raised * (1.0 / jnp.sum(raised, axis=1, keepdims=True))).astype(BF16)
                probs[head, rows, :] = share
                parts.append(dot(share, contents))
            joined[rows, pl.ds(begin, 128)] = jnp.where(lane < HEAD_DIM, parts[0], parts[1]).astype(BF16)
        return carry

    lax.fori_loop(0, HEADS // 2, pair, 0)
    hold[...] = dot(joined[...], columns(weights, ATT, 0))
    bias = small[S_AOB : S_AOB + 1, :]

    def body(rows, carry):
        result[rows, :] = source[rows, :] + hold[rows, :] + bias
        return carry

    chunks(body, 0)


def attention_backward(
    upstream, source, normed, mixed, probs, joined, result, low, spread, grad_mixed, scaled, hold, total, lines,
    weights, small, buckets, out, base, grads, table_grad,
):
    def start(rows, carry):
        given = upstream[rows, :]
        low[rows, :] = given.astype(BF16)
        return carry + fold(given)

    grads[S_AOB : S_AOB + 1, :] = jnp.sum(chunks(start, zeros8()), axis=0, keepdims=True)
    out[:, ATT - base : ATT - base + 16, :] = dot_tn(joined[...], low[...]).astype(BF16).reshape(32, 16, D)
    spread[...] = dot_nt(low[...], columns(weights, ATT, 0)).astype(BF16)
    lane = lax.broadcasted_iota(jnp.int32, (1, 128), 1)
    row8 = lax.broadcasted_iota(jnp.int32, (8, 2 * L), 0)
    size = 128

    def pair(index, carry):
        begin = pl.multiple_of(128 * index, 128)
        query = mixed[:, pl.ds(begin, 128)]
        keys = mixed[:, pl.ds(D + begin, 128)]
        contents = mixed[:, pl.ds(2 * D + begin, 128)]
        incoming = spread[:, pl.ds(begin, 128)]
        parts = []
        for half in range(2):
            head = 2 * index + half
            here = (lane // HEAD_DIM) == half
            hold[...] = dot_nt(jnp.where(here, incoming, jnp.zeros_like(incoming)), contents)
            sums = zeros8(2 * L)
            for block in range(L // size):
                rows = pl.ds(block * size, size)
                share = probs[head, rows, :].astype(F32)
                given = hold[rows, :]
                slant = share * (given - jnp.sum(given * share, axis=1, keepdims=True))
                scaled[rows, :] = (slant * HEAD_DIM ** (-0.5)).astype(BF16)
                part = zeros8(640)
                for t in range(size // 8):
                    tile = jnp.concatenate([slant[8 * t : 8 * t + 8], zeros8(128)], axis=1)
                    part += pltpu.roll(tile, 120 - 8 * t, 1)
                first = 384 - block * size
                pieces = [part]
                if first:
                    pieces = [zeros8(first)] + pieces
                if block:
                    pieces = pieces + [zeros8(block * size)]
                sums += jnp.concatenate(pieces, axis=1)
            line = zeros8(2 * L)
            for r in range(8):
                line += jnp.where(row8 == r, pltpu.roll(sums, 7 - r, 1), 0.0)
            lines[pl.ds(head, 1), :] = jnp.sum(line, axis=0, keepdims=True)
            parts.append((dot(scaled[...], keys), dot_tn(scaled[...], query), dot_tn(probs[head], incoming)))
        for third in range(3):
            merged = jnp.where(lane < HEAD_DIM, parts[0][third], parts[1][third])
            grad_mixed[:, pl.ds(third * D + begin, 128)] = merged.astype(BF16)
        return carry

    lax.fori_loop(0, HEADS // 2, pair, 0)
    table_grad[...] = lax.dot_general(
        lines[...], bucket_choice(buckets), (((1,), (1,)), ((), ())),
        precision=lax.Precision.HIGHEST, preferred_element_type=F32,
    )

    def mix(c, carry):
        cols = pl.ds(pl.multiple_of(c * D, D), D)
        inner = dot_tn(normed[...], grad_mixed[:, cols]).astype(BF16).reshape(32, 16, D)
        out[:, pl.ds(pl.multiple_of(QKV - base + 16 * c, 16), 16), :] = inner
        part = dot_nt(grad_mixed[:, cols], columns(weights, QKV, c))

        @pl.when(c == 0)
        def _():
            total[...] = part

        @pl.when(c > 0)
        def _():
            total[...] += part

        return carry

    lax.fori_loop(0, 3, mix, 0)
    norm_back(source, total, upstream, result, small, S_ATTN, grads)


def clear_pads(padded):
    edge = jnp.zeros((4, PAD, 128), F32)
    padded[:, 0:PAD, :] = edge
    padded[:, PAD + L : 2 * PAD + L, :] = edge


def conv_front(source, normed, sigma, gated, middle, sums, hold, weights, small, gate_bias, bounds):
    norm_rows(source, normed, small, S_CONV)
    clear_pads(gated)
    hold[...] = dot(normed[...], columns(weights, GLU, 1))
    bias = gate_bias[0:1, D:]

    def gate(rows, carry):
        sigma[rows, :] = jax.nn.sigmoid(hold[rows, :] + bias)
        return carry

    chunks(gate, 0)
    hold[...] = dot(normed[...], columns(weights, GLU, 0))
    bias = gate_bias[0:1, :D]

    def unit(rows, carry):
        values = (hold[rows, :] + bias) * sigma[rows, :]
        for j in range(4):
            gated[j, pl.ds(rows.start + PAD, CHUNK), :] = values[:, 128 * j : 128 * j + 128]
        return carry

    chunks(unit, 0)
    size = 16

    def slide(i, carry):
        begin = pl.multiple_of(i * size, size)
        marks = bounds[pl.ds(begin + PAD, size), :]
        accs = [jnp.zeros((size, 128), F32) for _ in range(4)]
        for k in range(TAPS):
            same = bounds[pl.ds(begin + k, size), :] == marks
            for j in range(4):
                tap = small[S_TAPS + k : S_TAPS + k + 1, 128 * j : 128 * j + 128]
                accs[j] += jnp.where(same, gated[j, pl.ds(begin + k, size), :], 0.0) * tap
        result = []
        for j in range(4):
            middle[pl.ds(begin, size), 128 * j : 128 * j + 128] = accs[j]
            result.append(carry[j] + fold(accs[j]))
            result.append(carry[4 + j] + fold(accs[j] * accs[j]))
        return result[0::2] + result[1::2]

    ends = lax.fori_loop(0, L // size, slide, [zeros8(128)] * 8)
    sums[...] = zeros8()
    for j in range(4):
        sums[0:1, 128 * j : 128 * j + 128] = jnp.sum(ends[j], axis=0, keepdims=True)
        sums[1:2, 128 * j : 128 * j + 128] = jnp.sum(ends[4 + j], axis=0, keepdims=True)


def conv_rest(source, middle, sums, unit, active, slope, result, hold, weights, small, frames):
    center = sums[0:1, :] * (1.0 / frames)
    inverse = lax.rsqrt(sums[1:2, :] * (1.0 / frames) - center * center + epsilon)
    gain, shift = 1.0 + small[S_BATCH : S_BATCH + 1, :], small[S_BATCH + 1 : S_BATCH + 2, :]

    def body(rows, carry):
        values = (middle[rows, :] - center) * inverse
        unit[rows, :] = values
        normal = values * gain + shift
        sigma = jax.nn.sigmoid(normal)
        value = normal * sigma
        active[rows, :] = value.astype(BF16)
        slope[rows, :] = sigma + value * (1.0 - sigma)
        return carry

    chunks(body, 0)
    hold[...] = dot(active[...], columns(weights, CONV, 0))
    bias = small[S_COB : S_COB + 1, :]

    def add(rows, carry):
        result[rows, :] = source[rows, :] + hold[rows, :] + bias
        return carry

    chunks(add, 0)


def conv_back_rest(upstream, unit, active, slope, grad_normal, low, hold, weights, out, base, grads, sums):
    def start(rows, carry):
        given = upstream[rows, :]
        low[rows, :] = given.astype(BF16)
        return carry + fold(given)

    grads[S_COB : S_COB + 1, :] = jnp.sum(chunks(start, zeros8()), axis=0, keepdims=True)
    out[:, CONV - base : CONV - base + 16, :] = dot_tn(active[...], low[...]).astype(BF16).reshape(32, 16, D)
    hold[...] = dot_nt(low[...], columns(weights, CONV, 0))

    def body(rows, carry):
        grad = hold[rows, :] * slope[rows, :]
        grad_normal[rows, :] = grad
        return carry[0] + fold(grad), carry[1] + fold(grad * unit[rows, :])

    first, second = chunks(body, (zeros8(), zeros8()))
    sums[...] = zeros8()
    sums[0:1, :] = jnp.sum(first, axis=0, keepdims=True)
    sums[1:2, :] = jnp.sum(second, axis=0, keepdims=True)


def conv_back_front(
    upstream, source, normed, sigma, gated, unit, grad_normal, front_sums, sums, result, padded, grad_joined, hold, total, tap_sums,
    weights, small, bounds, out, base, grads, gate_grads, frames,
):
    center = front_sums[0:1, :] * (1.0 / frames)
    inverse = lax.rsqrt(front_sums[1:2, :] * (1.0 / frames) - center * center + epsilon)
    gain = 1.0 + small[S_BATCH : S_BATCH + 1, :]
    mean0, mean1 = gain * sums[0:1, :] * (1.0 / frames), gain * sums[1:2, :] * (1.0 / frames)
    clear_pads(padded)

    def start(rows, carry):
        grad = inverse * (gain * grad_normal[rows, :] - mean0 - unit[rows, :] * mean1)
        for j in range(4):
            padded[j, pl.ds(rows.start + PAD, CHUNK), :] = grad[:, 128 * j : 128 * j + 128]
        return carry

    chunks(start, 0)
    tap_sums[...] = jnp.zeros_like(tap_sums)
    size = 16

    def slide(i, carry):
        begin = pl.multiple_of(i * size, size)
        marks = bounds[pl.ds(begin + PAD, size), :]
        accs = [jnp.zeros((size, 128), F32) for _ in range(4)]
        for k in range(TAPS):
            same = bounds[pl.ds(begin + 2 * PAD - k, size), :] == marks
            for j in range(4):
                tap = small[S_TAPS + k : S_TAPS + k + 1, 128 * j : 128 * j + 128]
                accs[j] += jnp.where(same, padded[j, pl.ds(begin + 2 * PAD - k, size), :], 0.0) * tap
        for j in range(4):
            hold[pl.ds(begin, size), 128 * j : 128 * j + 128] = accs[j]
        grads_here = [padded[j, pl.ds(begin + PAD, size), :] for j in range(4)]
        for k in range(TAPS):
            same = bounds[pl.ds(begin + k, size), :] == marks
            for j in range(4):
                term = jnp.where(same, gated[j, pl.ds(begin + k, size), :], 0.0) * grads_here[j]
                tap_sums[k, :, 128 * j : 128 * j + 128] += fold(term)
        return carry

    lax.fori_loop(0, L // size, slide, 0)
    grads[S_TAPS : S_TAPS + TAPS, :] = jnp.sum(tap_sums[...], axis=1)

    def split(rows, carry):
        grad = hold[rows, :]
        gate = sigma[rows, :]
        values = jnp.concatenate([gated[j, pl.ds(rows.start + PAD, CHUNK), :] for j in range(4)], axis=1)
        first = grad * gate
        second = grad * values * (1.0 - gate)
        grad_joined[rows, :D] = first.astype(BF16)
        grad_joined[rows, D : 2 * D] = second.astype(BF16)
        return carry[0] + fold(first), carry[1] + fold(second)

    first, second = chunks(split, (zeros8(), zeros8()))
    gate_grads[0:1, :D] = jnp.sum(first, axis=0, keepdims=True)
    gate_grads[0:1, D:] = jnp.sum(second, axis=0, keepdims=True)

    def mix(c, carry):
        cols = pl.ds(pl.multiple_of(c * D, D), D)
        inner = dot_tn(normed[...], grad_joined[:, cols]).astype(BF16).reshape(32, 16, D)
        out[:, pl.ds(pl.multiple_of(GLU - base + 16 * c, 16), 16), :] = inner
        part = dot_nt(grad_joined[:, cols], columns(weights, GLU, c))

        @pl.when(c == 0)
        def _():
            total[...] = part

        @pl.when(c > 0)
        def _():
            total[...] += part

        return carry

    lax.fori_loop(0, 2, mix, 0)
    norm_back(source, total, upstream, result, small, S_CONV, grads)


def kernel_one(
    x0, bounds, marks, buckets, weights, small, inner_bias, gate_bias, table,
    x1, x2, normed0, active0, slope0, normed_a, mixed, probs, joined, normed_c, sigma, gated, middle, sums,
    hold, lines,
):
    feed_forward(x0, normed0, active0, slope0, x1, hold, weights, small, inner_bias, 0)
    attention_forward(x1, normed_a, mixed, probs, joined, x2, lines, hold, weights, small, table, buckets, bounds, marks)
    conv_front(x2, normed_c, sigma, gated, middle, sums, hold, weights, small, gate_bias, bounds)


def kernel_two(
    frames, cotangent, x2, middle, sums, weights, small, inner_bias,
    output, unit, grad_normal, g3, out, grads, inner_grads, back_sums,
    x3, x4, active_c, slope_c, normed, active, slope, low, low_in, hold, total,
):
    grads[...] = jnp.zeros_like(grads)
    inner_grads[...] = jnp.zeros_like(inner_grads)
    conv_rest(x2, middle, sums, unit, active_c, slope_c, x3, hold, weights, small, frames)
    feed_forward(x3, normed, active, slope, x4, hold, weights, small, inner_bias, 1)
    norm_rows(x4, output, small, S_FINAL)

    def zero(rows, carry):
        hold[rows, :] = jnp.zeros((CHUNK, D), F32)
        total[rows, :] = cotangent[rows, :].astype(F32)
        return carry

    chunks(zero, 0)
    norm_back(x4, total, hold, x4, small, S_FINAL, grads)
    feed_backward(
        x4, x3, normed, active, slope, g3, low, low_in, hold, total, weights, small, out, CONV, grads, inner_grads, 1
    )
    conv_back_rest(g3, unit, active_c, slope_c, grad_normal, low, hold, weights, out, CONV, grads, back_sums)


def kernel_three(
    frames, x0, bounds, buckets, weights, small,
    x1, x2, normed0, active0, slope0, normed_a, mixed, probs, joined, normed_c, sigma, gated,
    unit, grad_normal, g3, front_sums, back_sums, grads_in, inner_in,
    grad_x, out, grads, inner_grads, gate_grads, table_grad,
    g2, g1, padded, grad_mixed, scaled, low, low_in, hold, total, tap_sums, lines,
):
    grads[...] = grads_in[...]
    inner_grads[...] = inner_in[...]
    grads[S_BATCH : S_BATCH + 1, :] = back_sums[1:2, :]
    grads[S_BATCH + 1 : S_BATCH + 2, :] = back_sums[0:1, :]
    conv_back_front(
        g3, x2, normed_c, sigma, gated, unit, grad_normal, front_sums, back_sums, g2, padded, grad_mixed, hold, total, tap_sums,
        weights, small, bounds, out, IN0, grads, gate_grads, frames,
    )
    attention_backward(
        g2, x1, normed_a, mixed, probs, joined, g1, low, low_in, grad_mixed, scaled, hold, total, lines,
        weights, small, buckets, out, IN0, grads, table_grad,
    )
    feed_backward(
        g1, x0, normed0, active0, slope0, grad_x, low, low_in, hold, total, weights, small, out, IN0, grads, inner_grads, 0
    )


def shape(dims, kind=F32):
    return jax.ShapeDtypeStruct(dims, kind)


def call(kernel, name, args, outs, scratch):
    return pl.pallas_call(
        kernel,
        out_shape=outs,
        in_specs=[pl.BlockSpec(memory_space=pltpu.VMEM)] * len(args),
        out_specs=[pl.BlockSpec(memory_space=pltpu.VMEM)] * len(outs),
        scratch_shapes=scratch,
        compiler_params=pltpu.CompilerParams(vmem_limit_bytes=60 * 1024 * 1024),
        name=name,
    )(*args)


def compute(x0, segments, buckets, cotangent, weights, small, inner_bias, gate_bias, table, total_of, frames):
    wide, low = shape((L, D)), shape((L, D), BF16)
    big, pads = shape((L, FF), BF16), shape((4, L + 2 * PAD, 128))
    vwide, vlow, vbig = pltpu.VMEM((L, D), F32), pltpu.VMEM((L, D), BF16), pltpu.VMEM((L, FF), BF16)
    bounds = jnp.broadcast_to(jnp.pad(segments, (PAD, PAD), constant_values=-1)[:, None], (L + 2 * PAD, 128))
    marks = segments[None, :]
    choice = jnp.pad(buckets, (0, 1), constant_values=-1)[None, :]
    x1, x2, normed0, active0, slope0, normed_a, mixed, probs, joined, normed_c, sigma, gated, middle, sums = call(
        kernel_one, "front", (x0, bounds, marks, choice, weights, small, inner_bias, gate_bias, table),
        [wide, wide, low, big, big, low, shape((L, 3 * D), BF16), shape((HEADS, L, L), BF16), low, low, wide, pads, wide, shape((8, D))],
        [vwide, pltpu.VMEM((8, 2 * L), F32)],
    )
    sums = total_of(sums)
    output, unit, grad_normal, g3, late, grads, inner_grads, back = call(
        lambda *refs: kernel_two(frames, *refs), "turn", (cotangent, x2, middle, sums, weights, small, inner_bias),
        [low, wide, wide, wide, shape((32, ROWS - CONV, D), BF16), shape((S_ROWS, D)), shape((2, FF)), shape((8, D))],
        [vwide, vwide, vlow, vwide, vlow, vbig, vbig, vlow, vlow, vwide, vwide],
    )
    back = total_of(back)
    grad_x, early, grads, inner_grads, gate_grads, table_grad = call(
        lambda *refs: kernel_three(frames, *refs), "back",
        (x0, bounds, choice, weights, small, x1, x2, normed0, active0, slope0, normed_a, mixed, probs, joined, normed_c, sigma, gated,
         unit, grad_normal, g3, sums, back, grads, inner_grads),
        [wide, shape((32, CONV - IN0, D), BF16), shape((S_ROWS, D)), shape((2, FF)), shape((1, 2 * D)), shape((HEADS, BUCKETS))],
        [vwide, vwide, pltpu.VMEM((4, L + 2 * PAD, 128), F32), pltpu.VMEM((L, 3 * D), BF16), vlow, vlow, vlow, vwide, vwide,
         pltpu.VMEM((TAPS, 8, D), F32), pltpu.VMEM((8, 2 * L), F32)],
    )
    return output, grad_x, early, late, grads, inner_grads, gate_grads, table_grad


MESH = pl.DeviceIdType.MESH


class Place:
    def __init__(self):
        self.width = lax.axis_size("fsdp")
        self.chips = self.width // 2
        plane, inner = lax.axis_index("dp"), lax.axis_index("fsdp")
        self.y, self.x = plane // 2, plane % 2
        self.z, self.core = inner // 2, inner % 2
        self.me = self.slot(self.y, self.x, self.z, self.core)

    def slot(self, y, x, z, core):
        return (y * 2 + x) * self.width + z * 2 + core

    def device(self, y, x, z, core):
        return (y * 2 + x, z * 2 + core)

    def twin(self):
        return self.device(self.y, self.x, self.z, 1 - self.core)

    def over_x(self):
        return self.device(self.y, 1 - self.x, self.z, self.core)

    def over_y(self):
        return self.device(1 - self.y, self.x, self.z, self.core)

    def along_z(self, step):
        return self.device(self.y, self.x, self.z + step, self.core)

    def greet(self):
        barrier = pltpu.get_barrier_semaphore()
        for near in (self.twin(), self.over_x(), self.over_y()):
            pl.semaphore_signal(barrier, inc=1, device_id=near, device_id_type=MESH)

        @pl.when(self.z > 0)
        def _():
            pl.semaphore_signal(barrier, inc=1, device_id=self.along_z(-1), device_id_type=MESH)

        @pl.when(self.z < self.chips - 1)
        def _():
            pl.semaphore_signal(barrier, inc=1, device_id=self.along_z(1), device_id_type=MESH)

        ends = jnp.where(self.z > 0, 1, 0) + jnp.where(self.z < self.chips - 1, 1, 0)
        pl.semaphore_wait(barrier, 3 + ends)


def when(condition, action):
    if condition is True:
        action()
    else:
        pl.when(condition)(action)


def gather_kernel(split, own, out, sends, receives, local_sem):
    place = Place()
    rows = own.shape[0]
    y, x, z, core, chips = place.y, place.x, place.z, place.core, place.chips
    halves = ((0, split), (split, rows - split))
    place.greet()
    keep = pltpu.make_async_copy(own, out.at[place.me], local_sem)
    keep.start()
    sent = []

    def piece(slot, half, mine=False):
        start, size = halves[half]
        if mine:
            return own.at[pl.ds(start, size)]
        return out.at[slot, pl.ds(start, size)]

    def send(slot, half, device, condition=True, mine=False):
        start, size = halves[half]
        copy = pltpu.make_async_remote_copy(
            src_ref=piece(slot, half, mine),
            dst_ref=out.at[slot, pl.ds(start, size)],
            send_sem=sends.at[len(sent)],
            recv_sem=receives.at[slot, half],
            device_id=device,
            device_id_type=MESH,
        )
        when(condition, copy.start)
        sent.append((condition, copy))

    def arrive(slot, half, condition=True):
        start, size = halves[half]
        block = out.at[slot, pl.ds(start, size)]
        copy = pltpu.make_async_remote_copy(
            src_ref=block, dst_ref=block, send_sem=local_sem, recv_sem=receives.at[slot, half],
            device_id=place.twin(), device_id_type=MESH,
        )
        when(condition, copy.wait_recv)

    def across(zz, condition, mine):
        slot = place.slot(y, x, zz, core)
        send(slot, 0, place.over_x(), condition, mine)
        send(slot, 1, place.over_y(), condition, mine)
        send(slot, 0, place.over_y(), condition, mine)
        send(slot, 1, place.over_x(), condition, mine)

    def turn(zz, condition):
        first = place.slot(y, 1 - x, zz, core)
        arrive(first, 0, condition)
        send(first, 0, place.over_y(), condition)
        second = place.slot(1 - y, x, zz, core)
        arrive(second, 1, condition)
        send(second, 1, place.over_x(), condition)
        for half in range(2):
            send((first, second)[half], half, place.twin(), condition)

    def both(slot, condition=True, mine=False):
        for half in range(2):
            send(slot, half, place.twin(), condition, mine)

    steps = [(0, True)]
    for k in range(1, chips):
        steps += [(-k, z - k >= 0), (k, z + k < chips)]
    for offset, there in steps:
        zz = z + offset
        slot = place.slot(y, x, zz, core)
        if offset:
            for half in range(2):
                arrive(slot, half, there)
        for half in range(2):
            if offset <= 0 and -offset < chips - 1:
                ok = z < chips - 1 if offset == 0 else jnp.logical_and(there, z < chips - 1)
                send(slot, half, place.along_z(1), ok, offset == 0)
            if offset >= 0 and offset < chips - 1:
                ok = z > 0 if offset == 0 else jnp.logical_and(there, z > 0)
                send(slot, half, place.along_z(-1), ok, offset == 0)
        across(zz, there, offset == 0)
        both(slot, there, offset == 0)
        turn(zz, there)
    for offset, there in steps:
        zz = z + offset
        for first, second in (
            (place.slot(1 - y, x, zz, core), place.slot(y, 1 - x, zz, core)),
            (place.slot(1 - y, 1 - x, zz, core), place.slot(1 - y, 1 - x, zz, core)),
        ):
            arrive(first, 0, there)
            send(first, 0, place.twin(), there)
            arrive(second, 1, there)
            send(second, 1, place.twin(), there)
    for yy in range(2):
        for xx in range(2):
            for zz in range(chips):
                for half in range(2):
                    arrive(place.slot(yy, xx, zz, 1 - core), half)
    for condition, copy in sent:
        when(condition, copy.wait_send)
    keep.wait()


def gather_all(own, split):
    devices = lax.axis_size(("dp", "fsdp"))
    rows, lanes = own.shape
    return pl.pallas_call(
        lambda *refs: gather_kernel(split, *refs),
        out_shape=jax.ShapeDtypeStruct((devices, rows, lanes), own.dtype),
        in_specs=[pl.BlockSpec(memory_space=pl.ANY)],
        out_specs=pl.BlockSpec(memory_space=pl.ANY),
        scratch_shapes=[
            pltpu.SemaphoreType.DMA((16 * devices,)),
            pltpu.SemaphoreType.DMA((devices, 2)),
            pltpu.SemaphoreType.DMA,
        ],
        compiler_params=pltpu.CompilerParams(collective_id=0, has_side_effects=True),
        name="gather_all",
    )(own)


def total_kernel(own, out, near, far, part, near_send, near_recv, far_send, far_recv):
    place = Place()
    planes = lax.axis_size("dp")
    plane = lax.axis_index("dp")
    z, core, chips = place.z, place.core, place.chips
    barrier = pltpu.get_barrier_semaphore()
    group = [(step, flip) for step in range(planes) for flip in range(2) if step or flip]

    def member(step, flip):
        return (lax.rem(plane + step, planes), 2 * z + lax.rem(core + flip, 2))

    def rank(step, flip):
        return lax.rem(plane + step, planes) * 2 + lax.rem(core + flip, 2)

    def along(step):
        return (plane, 2 * lax.rem(z + step, chips) + core)

    for step, flip in group:
        pl.semaphore_signal(barrier, inc=1, device_id=member(step, flip), device_id_type=MESH)
    for step in range(1, chips):
        pl.semaphore_signal(barrier, inc=1, device_id=along(step), device_id_type=MESH)
    pl.semaphore_wait(barrier, len(group) + chips - 1)
    me = rank(0, 0)
    copies = []
    for i, (step, flip) in enumerate(group):
        copy = pltpu.make_async_remote_copy(
            src_ref=own, dst_ref=near.at[me], send_sem=near_send.at[i], recv_sem=near_recv.at[me],
            device_id=member(step, flip), device_id_type=MESH,
        )
        copy.start()
        copies.append(copy)
    near[me] = own[...]
    for step, flip in group:
        pltpu.make_async_remote_copy(
            src_ref=own, dst_ref=near.at[rank(step, flip)], send_sem=near_send.at[0], recv_sem=near_recv.at[rank(step, flip)],
            device_id=member(step, flip), device_id_type=MESH,
        ).wait_recv()
    value = near[0]
    for i in range(1, 2 * planes):
        value = value + near[i]
    part[...] = value
    for step in range(1, chips):
        copy = pltpu.make_async_remote_copy(
            src_ref=part, dst_ref=far.at[z], send_sem=far_send.at[step], recv_sem=far_recv.at[z],
            device_id=along(step), device_id_type=MESH,
        )
        copy.start()
        copies.append(copy)
    far[z] = part[...]
    for step in range(1, chips):
        other = lax.rem(z + step, chips)
        pltpu.make_async_remote_copy(
            src_ref=part, dst_ref=far.at[other], send_sem=far_send.at[0], recv_sem=far_recv.at[other],
            device_id=along(step), device_id_type=MESH,
        ).wait_recv()
    value = far[0]
    for i in range(1, chips):
        value = value + far[i]
    out[...] = value
    for copy in copies:
        copy.wait_send()


def total_of(own, identity):
    planes, chips = lax.axis_size("dp"), lax.axis_size("fsdp") // 2
    block = own.shape
    return pl.pallas_call(
        total_kernel,
        out_shape=jax.ShapeDtypeStruct(block, own.dtype),
        in_specs=[pl.BlockSpec(memory_space=pltpu.VMEM)],
        out_specs=pl.BlockSpec(memory_space=pltpu.VMEM),
        scratch_shapes=[
            pltpu.VMEM((2 * planes,) + block, own.dtype),
            pltpu.VMEM((chips,) + block, own.dtype),
            pltpu.VMEM(block, own.dtype),
            pltpu.SemaphoreType.DMA((2 * planes,)),
            pltpu.SemaphoreType.DMA((2 * planes,)),
            pltpu.SemaphoreType.DMA((chips,)),
            pltpu.SemaphoreType.DMA((chips,)),
        ],
        compiler_params=pltpu.CompilerParams(collective_id=identity, has_side_effects=True),
        name="total_of",
    )(own)


def reduce_kernel(split, early, late, small, out, small_out, data, twins, firsts, seconds, rights, lefts, edges, sends, receives, local_sem):
    place = Place()
    y, x, z, core, chips = place.y, place.x, place.z, place.core, place.chips
    rows = data.shape[1]
    cut = early.shape[1]
    loads = [
        pltpu.make_async_copy(early, data.at[:, pl.ds(0, cut)], local_sem.at[0]),
        pltpu.make_async_copy(late, data.at[:, pl.ds(cut, rows - cut)], local_sem.at[1]),
        pltpu.make_async_copy(small, edges, local_sem.at[2]),
    ]
    for load in loads:
        load.start()
    place.greet()
    for load in loads:
        load.wait()
    parts = (0, 1, 2)
    kinds = ((data, 0, split), (data, split, rows - split), (edges, 0, small.shape[1]))
    sent = []

    def mine(part, slot):
        ref, begin, size = kinds[part]
        return ref.at[slot, pl.ds(begin, size)]

    def copy_of(part, slot, landing, stage, index, device, number):
        return pltpu.make_async_remote_copy(
            src_ref=mine(part, slot), dst_ref=landing, send_sem=sends.at[number],
            recv_sem=receives.at[part, stage, index], device_id=device, device_id_type=MESH,
        )

    def send(part, slot, landing, stage, index, device, condition=True):
        copy = copy_of(part, slot, landing, stage, index, device, len(sent))
        when(condition, copy.start)
        sent.append((condition, copy))

    def add(part, slot, landing, stage, index, condition=True):
        ref, begin, size = kinds[part]

        def act():
            copy_of(part, slot, landing, stage, index, place.twin(), 0).wait_recv()
            if part == 2:
                ref[slot] = ref[slot] + landing[...]
                return
            piece = 16

            def step(i, carry):
                at = pl.multiple_of(i * piece, piece)
                here = pl.ds(begin + at, piece)
                ref[slot, here, :] = ref[slot, here, :] + landing[pl.ds(at, piece), :]
                return carry

            lax.fori_loop(0, size // piece, step, 0)

        when(condition, act)

    def first_side(part, flip):
        return 1 - flip if flip is not None else None

    def at(part, first, second, zz, core_of):
        if part == 1:
            yy, xx = (y if second == 0 else 1 - y), (x if first == 0 else 1 - x)
        else:
            yy, xx = (y if first == 0 else 1 - y), (x if second == 0 else 1 - x)
        return place.slot(yy, xx, zz, core_of)

    def index(part, first, second, zz):
        if part == 1:
            yy, xx = (y if second == 0 else 1 - y), (x if first == 0 else 1 - x)
        else:
            yy, xx = (y if first == 0 else 1 - y), (x if second == 0 else 1 - x)
        return (yy * 2 + xx) * chips + zz

    def second_index(part, second, zz):
        along = (y if second == 0 else 1 - y) if part == 1 else (x if second == 0 else 1 - x)
        return along * chips + zz

    def over(part, axis):
        return place.over_x() if (part == 1) == (axis == 0) else place.over_y()

    order = [(1, 1), (1, 0), (0, 1), (0, 0)]
    for first, second in order:
        for zz in range(chips):
            for part in parts:
                where = index(part, first, second, zz)
                send(part, at(part, first, second, zz, 1 - core), twins[part].at[where], 0, where, place.twin())
    for second in (1, 0):
        for zz in range(chips):
            for part in parts:
                slot, where = at(part, 1, second, zz, core), index(part, 1, second, zz)
                add(part, slot, twins[part].at[where], 0, where)
                where = second_index(part, second, zz)
                send(part, slot, firsts[part].at[where], 1, where, over(part, 0))
    for zz in range(chips):
        for part in parts:
            slot, where = at(part, 0, 1, zz, core), index(part, 0, 1, zz)
            add(part, slot, twins[part].at[where], 0, where)
            where = second_index(part, 1, zz)
            add(part, slot, firsts[part].at[where], 1, where)
            send(part, slot, seconds[part].at[zz], 2, zz, over(part, 1))
    for zz in range(chips):
        for part in parts:
            slot, where = at(part, 0, 0, zz, core), index(part, 0, 0, zz)
            add(part, slot, twins[part].at[where], 0, where)
            where = second_index(part, 0, zz)
            add(part, slot, firsts[part].at[where], 1, where)
    for zz in range(chips):
        for part in parts:
            add(part, at(part, 0, 0, zz, core), seconds[part].at[zz], 2, zz)
    for k in range(chips - 1, 0, -1):
        for part in parts:
            slot = at(part, 0, 0, k, core)
            below = z < k
            add(part, slot, rights[part].at[k], 3, k, jnp.logical_and(below, z > 0))
            send(part, slot, rights[part].at[k], 3, k, place.along_z(1), below)
            goal = chips - 1 - k
            slot = at(part, 0, 0, goal, core)
            above = z > goal
            add(part, slot, lefts[part].at[goal], 4, goal, jnp.logical_and(above, z < chips - 1))
            send(part, slot, lefts[part].at[goal], 4, goal, place.along_z(-1), above)
    for part in parts:
        add(part, place.me, rights[part].at[z], 3, z, z > 0)
        add(part, place.me, lefts[part].at[z], 4, z, z < chips - 1)

    def finish(i, carry):
        here = pl.ds(pl.multiple_of(i * 16, 16), 16)
        out[here, :] = data[place.me, here, :].astype(jnp.float32)
        return carry

    lax.fori_loop(0, rows // 16, finish, 0)
    small_out[...] = edges[place.me]
    for condition, copy in sent:
        when(condition, copy.wait_send)


def reduce_all(early, late, small, split):
    devices = lax.axis_size(("dp", "fsdp"))
    chips = lax.axis_size("fsdp") // 2
    rows = early.shape[1] + late.shape[1]
    lanes = early.shape[2]

    def buffers(count):
        return [
            pltpu.VMEM((count, split, lanes), early.dtype),
            pltpu.VMEM((count, rows - split, lanes), early.dtype),
            pltpu.VMEM((count,) + small.shape[1:], small.dtype),
        ]

    return pl.pallas_call(
        lambda *refs: reduce_kernel(split, *refs),
        out_shape=[jax.ShapeDtypeStruct((rows, lanes), jnp.float32), jax.ShapeDtypeStruct(small.shape[1:], small.dtype)],
        in_specs=[pl.BlockSpec(memory_space=pl.ANY)] * 3,
        out_specs=[pl.BlockSpec(memory_space=pltpu.VMEM)] * 2,
        scratch_shapes=[
            pltpu.VMEM((devices, rows, lanes), early.dtype),
            buffers(4 * chips), buffers(2 * chips), buffers(chips), buffers(chips), buffers(chips),
            pltpu.VMEM(small.shape, small.dtype),
            pltpu.SemaphoreType.DMA((160,)),
            pltpu.SemaphoreType.DMA((3, 5, 4 * chips)),
            pltpu.SemaphoreType.DMA((3,)),
        ],
        compiler_params=pltpu.CompilerParams(collective_id=3, has_side_effects=True, vmem_limit_bytes=60 * 1024 * 1024),
        name="reduce_all",
    )(early, late, small)


SMALL_SIZE = 1024


def pack_rows(weight):
    rows = weight.shape[0]
    return weight.reshape(rows, -1, D).transpose(1, 0, 2).reshape(-1, D)


def unpack_rows(rows, count):
    return rows.reshape(count, -1, D).transpose(1, 0, 2).reshape(-1, count * D)


def local(
    inputs, segments, buckets, cotangent, ffn_norm, ffn_in, ffn_in_bias, ffn_out, ffn_out_bias, attn_norm, qkv_weight,
    attn_out, attn_out_bias, rel_table, conv_norm, glu_weight, glu_bias, depth_kernel, batch_norm, conv_out, conv_out_bias,
    final_norm,
):
    devices = lax.axis_size(("dp", "fsdp"))
    width = D // devices
    thin = [
        ffn_norm.reshape(4, width), ffn_out_bias, attn_norm, attn_out_bias[None], conv_norm, batch_norm,
        conv_out_bias[None], final_norm, depth_kernel,
    ]
    tiny = jnp.concatenate([item.reshape(-1) for item in thin + [ffn_in_bias, glu_bias, rel_table]])
    tiny = jnp.pad(tiny, (0, 16 * D - tiny.shape[0])).reshape(16, D)
    own = jnp.concatenate(
        [
            tiny, pack_rows(ffn_in[0]), ffn_out[0], pack_rows(qkv_weight), attn_out, pack_rows(glu_weight), conv_out,
            pack_rows(ffn_in[1]), ffn_out[1],
        ]
    )
    weights = gather_all(own, ROWS // 2)
    flat = weights[:, 0:2, :].reshape(devices, 2 * D)
    small = flat[:, : S_ROWS * width].reshape(devices, S_ROWS, width).transpose(1, 0, 2).reshape(S_ROWS, D).astype(F32)
    at = S_ROWS * width
    inner_bias = flat[:, at : at + 8 * width].reshape(devices, 2, -1).transpose(1, 0, 2).reshape(2, FF).astype(F32)
    at += 8 * width
    gate_bias = flat[:, at : at + 2 * width].reshape(1, 2 * D).astype(F32)
    at += 2 * width
    table = flat[:, at : at + width // 2].reshape(HEADS, BUCKETS).astype(F32)
    numbers = [1, 2]
    output, grad_x, early, late, grads, inner_grads, gate_grads, table_grad = compute(
        inputs[0], segments[0], buckets, cotangent[0], weights, small, inner_bias, gate_bias, table,
        lambda item: total_of(item, numbers.pop(0)), L * devices,
    )
    tiny_grads = jnp.concatenate(
        [
            grads.reshape(S_ROWS, devices, width).transpose(1, 0, 2).reshape(devices, -1),
            inner_grads.reshape(2, devices, -1).transpose(1, 0, 2).reshape(devices, -1),
            gate_grads.reshape(devices, -1),
            table_grad.reshape(devices, -1),
        ],
        axis=1,
    )
    tiny_grads = jnp.pad(tiny_grads, ((0, 0), (0, SMALL_SIZE - tiny_grads.shape[1]))).reshape(devices, 8, 128)
    shard, tiny = reduce_all(early, late, tiny_grads, 176)
    tiny = tiny.reshape(-1)
    own_rows = tiny[: S_ROWS * width].reshape(S_ROWS, width)
    at = S_ROWS * width
    cut = lambda begin, size: shard[begin - IN0 : begin - IN0 + size]
    me = lax.axis_index(("dp", "fsdp"))
    batch = lax.dynamic_slice_in_dim(grads[S_BATCH : S_BATCH + 2], me * width, width, 1)
    return (
        output[None],
        grad_x[None],
        own_rows[0:4].reshape(2, 2, width),
        jnp.stack([unpack_rows(cut(IN0, 64), 4), unpack_rows(cut(IN1, 64), 4)]),
        tiny[at : at + 8 * width].reshape(2, -1),
        jnp.stack([cut(OUT0, 64), cut(OUT1, 64)]),
        own_rows[S_FOB : S_FOB + 2],
        own_rows[S_ATTN : S_ATTN + 2],
        unpack_rows(cut(QKV, 48), 3),
        cut(ATT, 16),
        own_rows[S_AOB],
        tiny[at + 10 * width : at + 10 * width + width // 2],
        own_rows[S_CONV : S_CONV + 2],
        unpack_rows(cut(GLU, 32), 2),
        tiny[at + 8 * width : at + 10 * width],
        own_rows[S_TAPS : S_TAPS + TAPS],
        batch,
        cut(CONV, 16),
        own_rows[S_COB],
        own_rows[S_FINAL : S_FINAL + 2],
    )


highest = lax.Precision.HIGHEST


def layer_norm(values, params):
    center = values - jnp.mean(values, axis=-1, keepdims=True)
    spread = jnp.mean(center * center, axis=-1, keepdims=True)
    return center * lax.rsqrt(spread + epsilon) * (1.0 + params[0]) + params[1]


def silu_slope(values):
    sigma = jax.nn.sigmoid(values)
    return sigma * (1.0 + values * (1.0 - sigma))


def product(left, right):
    return jnp.dot(left, right, preferred_element_type=jnp.float32)


def product_left(left, right):
    return lax.dot_general(
        left, right, (((0,), (0,)), ((), ())), preferred_element_type=jnp.float32
    )


def product_right(left, right):
    return lax.dot_general(
        left, right, (((1,), (1,)), ((), ())), preferred_element_type=jnp.float32
    )


def plain_fetch_feed(norms, inner_weight, inner_bias, outer_weight, outer_bias, layer):
    return (
        lax.all_gather(norms[layer], ("dp", "fsdp"), axis=1, tiled=True),
        lax.all_gather(inner_weight[layer], ("dp", "fsdp"), axis=0, tiled=True),
        lax.all_gather(inner_bias[layer], ("dp", "fsdp"), axis=0, tiled=True),
        lax.all_gather(outer_weight[layer], ("dp", "fsdp"), axis=0, tiled=True),
        lax.all_gather(outer_bias[layer], ("dp", "fsdp"), axis=0, tiled=True),
    )


def plain_reduce_feed(grads):
    return (
        lax.psum_scatter(grads[0], ("dp", "fsdp"), scatter_dimension=1, tiled=True),
        lax.psum_scatter(grads[1], ("dp", "fsdp"), scatter_dimension=0, tiled=True),
        lax.psum_scatter(grads[2], ("dp", "fsdp"), scatter_dimension=0, tiled=True),
        lax.psum_scatter(grads[3], ("dp", "fsdp"), scatter_dimension=0, tiled=True),
        lax.psum_scatter(grads[4], ("dp", "fsdp"), scatter_dimension=0, tiled=True),
    )


def fetch_attention(attn_norm, qkv_weight, attn_out, attn_out_bias, rel_table):
    return (
        lax.all_gather(attn_norm, ("dp", "fsdp"), axis=1, tiled=True),
        lax.all_gather(qkv_weight, ("dp", "fsdp"), axis=0, tiled=True),
        lax.all_gather(attn_out, ("dp", "fsdp"), axis=0, tiled=True),
        lax.all_gather(attn_out_bias, ("dp", "fsdp"), axis=0, tiled=True),
        lax.all_gather(rel_table, ("dp", "fsdp"), axis=0, tiled=True),
    )


def fetch_conv(
    conv_norm, glu_weight, glu_bias, depth_kernel, batch_norm, conv_out, conv_out_bias, final_norm
):
    return (
        lax.all_gather(conv_norm, ("dp", "fsdp"), axis=1, tiled=True),
        lax.all_gather(glu_weight, ("dp", "fsdp"), axis=0, tiled=True),
        lax.all_gather(glu_bias, ("dp", "fsdp"), axis=0, tiled=True),
        lax.all_gather(depth_kernel, ("dp", "fsdp"), axis=1, tiled=True),
        lax.all_gather(batch_norm, ("dp", "fsdp"), axis=1, tiled=True),
        lax.all_gather(conv_out, ("dp", "fsdp"), axis=0, tiled=True),
        lax.all_gather(conv_out_bias, ("dp", "fsdp"), axis=0, tiled=True),
        lax.all_gather(final_norm, ("dp", "fsdp"), axis=1, tiled=True),
    )


def plain_feed_forward(values, weights):
    norm, weight_in, bias_in, weight_out, bias_out = weights
    normed, norm_back = jax.vjp(layer_norm, values, norm.astype(jnp.float32))
    normed_low = normed.astype(jnp.bfloat16)
    inner = product(normed_low, weight_in) + bias_in.astype(jnp.float32)
    active = jax.nn.silu(inner).astype(jnp.bfloat16)
    result = values + 0.5 * (product(active, weight_out) + bias_out.astype(jnp.float32))
    return (result, (normed_low, inner, active, norm_back))


def plain_feed_backward(upstream, weights, saved):
    norm, weight_in, bias_in, weight_out, bias_out = weights
    normed_low, inner, active, norm_back = saved
    branch = 0.5 * upstream
    branch_low = branch.astype(jnp.bfloat16)
    grad_weight_out = product_left(active, branch_low)
    grad_inner = product_right(branch_low, weight_out) * silu_slope(inner)
    inner_low = grad_inner.astype(jnp.bfloat16)
    grad_weight_in = product_left(normed_low, inner_low)
    grad_values, grad_norm = norm_back(product_right(inner_low, weight_in))
    return (
        upstream + grad_values,
        (
            grad_norm,
            grad_weight_in,
            jnp.sum(grad_inner, axis=0),
            grad_weight_out,
            jnp.sum(branch, axis=0),
        ),
    )


def relative_lines(table, buckets):
    choose = (buckets[None, :] == jnp.arange(BUCKETS, dtype=jnp.int32)[:, None]).astype(jnp.float32)
    lines = jnp.dot(table.astype(jnp.float32).reshape(HEADS, BUCKETS), choose, precision=highest)
    return (lines, choose)


def bias_square(line, length):
    tiled = jnp.broadcast_to(line, (length, 2 * length - 1)).reshape(-1)
    tiled = jnp.concatenate([tiled, jnp.zeros((length,), line.dtype)])
    return tiled.reshape(length, 2 * length)[:, :length][::-1]


def diagonal_sums(square):
    length = square.shape[0]
    padded = jnp.concatenate([square[::-1], jnp.zeros_like(square)], axis=1).reshape(-1)
    return jnp.sum(padded[: length * (2 * length - 1)].reshape(length, 2 * length - 1), axis=0)


def head_scores(query, keys_head, line, same):
    raw = product_right(query, keys_head)
    return jnp.where(same, raw * HEAD_DIM ** (-0.5) + bias_square(line, query.shape[0]), -1e30)


def plain_attention_forward(values, weights, marks, buckets):
    norm, mixer, weight_out, bias_out, table = weights
    length = values.shape[0]
    normed, norm_back = jax.vjp(layer_norm, values, norm.astype(jnp.float32))
    normed_low = normed.astype(jnp.bfloat16)
    mixed = (
        product(normed_low, mixer)
        .astype(jnp.bfloat16)
        .reshape(length, 3, HEADS, HEAD_DIM)
        .transpose(1, 2, 0, 3)
    )
    lines, choose = relative_lines(table, buckets)
    same = marks[:, None] == marks[None, :]

    def head_forward(items):
        query, keys_head, contents, line = items
        scores = head_scores(query, keys_head, line, same)
        peak = jnp.max(scores, axis=1, keepdims=True)
        raised = jnp.exp(scores - peak)
        total = jnp.sum(raised, axis=1, keepdims=True)
        probs = (raised / total).astype(jnp.bfloat16)
        return (product(probs, contents).astype(jnp.bfloat16), (peak + jnp.log(total))[:, 0])

    attended, logsum = lax.map(head_forward, (mixed[0], mixed[1], mixed[2], lines))
    joined = attended.transpose(1, 0, 2).reshape(length, D)
    result = values + product(joined, weight_out) + bias_out.astype(jnp.float32)
    return (result, (normed_low, mixed, lines, choose, same, joined, logsum, norm_back))


def plain_attention_backward(upstream, weights, saved):
    norm, mixer, weight_out, bias_out, table = weights
    normed_low, mixed, lines, choose, same, joined, logsum, norm_back = saved
    length = upstream.shape[0]
    upstream_low = upstream.astype(jnp.bfloat16)
    grad_weight_out = product_left(joined, upstream_low)
    grad_joined = (
        product_right(upstream_low, weight_out)
        .astype(jnp.bfloat16)
        .reshape(length, HEADS, HEAD_DIM)
        .transpose(1, 0, 2)
    )

    def head_backward(items):
        query, keys_head, contents, line, incoming, logs = items
        scores = head_scores(query, keys_head, line, same)
        probs = jnp.exp(scores - logs[:, None])
        grad_contents = product_left(probs.astype(jnp.bfloat16), incoming)
        grad_probs = product_right(incoming, contents)
        grad_scores = probs * (grad_probs - jnp.sum(grad_probs * probs, axis=1, keepdims=True))
        scaled = (grad_scores * HEAD_DIM ** (-0.5)).astype(jnp.bfloat16)
        grad_query = product(scaled, keys_head)
        grad_keys = product_left(scaled, query)
        return (
            jnp.stack([grad_query, grad_keys, grad_contents]).astype(jnp.bfloat16),
            diagonal_sums(grad_scores),
        )

    grad_mixed, grad_lines = lax.map(
        head_backward, (mixed[0], mixed[1], mixed[2], lines, grad_joined, logsum)
    )
    grad_flat = grad_mixed.transpose(2, 1, 0, 3).reshape(length, 3 * D)
    grad_mixer = product_left(normed_low, grad_flat)
    grad_values, grad_norm = norm_back(product_right(grad_flat, mixer))
    grad_table = jnp.dot(grad_lines, choose.T, precision=highest).reshape(-1)
    return (
        upstream + grad_values,
        (grad_norm, grad_mixer, grad_weight_out, jnp.sum(upstream, axis=0), grad_table),
    )


def gate_unit(joined):
    width = joined.shape[1] // 2
    return joined[:, :width] * jax.nn.sigmoid(joined[:, width:])


def plain_depthwise(gated, kernel, marks):
    length = gated.shape[0]
    half = kernel.shape[0] // 2
    padded = jnp.pad(gated, ((half, half), (0, 0)))
    bounds = jnp.pad(marks, (half, half), constant_values=-1)
    total = jnp.zeros(gated.shape, gated.dtype)
    for step in range(kernel.shape[0]):
        same = (bounds[step : step + length] == marks)[:, None]
        total = total + jnp.where(same, padded[step : step + length], 0.0) * kernel[step]
    return total


def plain_conv_forward(values, weights, marks, frames):
    norm, weight_glu, bias_glu, kernel, batch, weight_out, bias_out, final = weights
    normed, norm_back = jax.vjp(layer_norm, values, norm.astype(jnp.float32))
    normed_low = normed.astype(jnp.bfloat16)
    joined = product(normed_low, weight_glu) + bias_glu.astype(jnp.float32)
    gated, gate_back = jax.vjp(gate_unit, joined)
    middle, depth_back = jax.vjp(
        lambda inner, taps: plain_depthwise(inner, taps, marks), gated, kernel.astype(jnp.float32)
    )
    sums = lax.psum((jnp.sum(middle, axis=0), jnp.sum(middle * middle, axis=0)), ("dp", "fsdp"))
    center = sums[0] / frames
    inverse = lax.rsqrt(sums[1] / frames - center * center + epsilon)
    gain = 1.0 + batch[0].astype(jnp.float32)
    unit = (middle - center) * inverse
    normal = unit * gain + batch[1].astype(jnp.float32)
    active = jax.nn.silu(normal).astype(jnp.bfloat16)
    result = values + product(active, weight_out) + bias_out.astype(jnp.float32)
    return (
        result,
        (normed_low, gate_back, depth_back, inverse, gain, unit, normal, active, norm_back),
    )


def plain_conv_backward(upstream, weights, saved, frames):
    norm, weight_glu, bias_glu, kernel, batch, weight_out, bias_out, final = weights
    normed_low, gate_back, depth_back, inverse, gain, unit, normal, active, norm_back = saved
    upstream_low = upstream.astype(jnp.bfloat16)
    grad_weight_out = product_left(active, upstream_low)
    grad_normal = product_right(upstream_low, weight_out) * silu_slope(normal)
    sums = lax.psum(
        (jnp.sum(grad_normal, axis=0), jnp.sum(grad_normal * unit, axis=0)), ("dp", "fsdp")
    )
    grad_middle = inverse * (
        grad_normal * gain - gain * sums[0] / frames - unit * (gain * sums[1] / frames)
    )
    grad_gated, grad_kernel = depth_back(grad_middle)
    grad_joined = gate_back(grad_gated)[0]
    joined_low = grad_joined.astype(jnp.bfloat16)
    grad_weight_glu = product_left(normed_low, joined_low)
    grad_values, grad_norm = norm_back(product_right(joined_low, weight_glu))
    grad_batch = jnp.stack([sums[1], sums[0]])
    return (
        upstream + grad_values,
        (
            grad_norm,
            grad_weight_glu,
            jnp.sum(grad_joined, axis=0),
            grad_kernel,
            grad_weight_out,
            jnp.sum(upstream, axis=0),
        ),
        grad_batch,
    )


def plain(
    inputs,
    segments,
    buckets,
    cotangent,
    ffn_norm,
    ffn_in,
    ffn_in_bias,
    ffn_out,
    ffn_out_bias,
    attn_norm,
    qkv_weight,
    attn_out,
    attn_out_bias,
    rel_table,
    conv_norm,
    glu_weight,
    glu_bias,
    depth_kernel,
    batch_norm,
    conv_out,
    conv_out_bias,
    final_norm,
):
    values = inputs[0].astype(jnp.float32)
    marks = segments[0]
    devices = lax.axis_size(("dp", "fsdp"))
    frames = values.shape[0] * devices
    feed_first = plain_fetch_feed(ffn_norm, ffn_in, ffn_in_bias, ffn_out, ffn_out_bias, 0)
    first, first_saved = plain_feed_forward(values, feed_first)
    attn_weights = fetch_attention(attn_norm, qkv_weight, attn_out, attn_out_bias, rel_table)
    second, attn_saved = plain_attention_forward(first, attn_weights, marks, buckets)
    conv_weights = fetch_conv(
        conv_norm,
        glu_weight,
        glu_bias,
        depth_kernel,
        batch_norm,
        conv_out,
        conv_out_bias,
        final_norm,
    )
    third, conv_saved = plain_conv_forward(second, conv_weights, marks, frames)
    feed_second = plain_fetch_feed(ffn_norm, ffn_in, ffn_in_bias, ffn_out, ffn_out_bias, 1)
    fourth, second_saved = plain_feed_forward(third, feed_second)
    result, final_back = jax.vjp(layer_norm, fourth, conv_weights[7].astype(jnp.float32))
    grad_fourth, grad_final = final_back(cotangent[0].astype(jnp.float32))
    second_back = plain_fetch_feed(ffn_norm, ffn_in, ffn_in_bias, ffn_out, ffn_out_bias, 1)
    grad_third, second_grads = plain_feed_backward(grad_fourth, second_back, second_saved)
    conv_back = fetch_conv(
        conv_norm,
        glu_weight,
        glu_bias,
        depth_kernel,
        batch_norm,
        conv_out,
        conv_out_bias,
        final_norm,
    )
    grad_second, conv_grads, grad_batch = plain_conv_backward(grad_third, conv_back, conv_saved, frames)
    attn_back = fetch_attention(attn_norm, qkv_weight, attn_out, attn_out_bias, rel_table)
    grad_first, attn_grads = plain_attention_backward(grad_second, attn_back, attn_saved)
    first_back = plain_fetch_feed(ffn_norm, ffn_in, ffn_in_bias, ffn_out, ffn_out_bias, 0)
    grad_start, first_grads = plain_feed_backward(grad_first, first_back, first_saved)
    first_shards = plain_reduce_feed(first_grads)
    second_shards = plain_reduce_feed(second_grads)
    attn_shards = (
        lax.psum_scatter(attn_grads[0], ("dp", "fsdp"), scatter_dimension=1, tiled=True),
        lax.psum_scatter(attn_grads[1], ("dp", "fsdp"), scatter_dimension=0, tiled=True),
        lax.psum_scatter(attn_grads[2], ("dp", "fsdp"), scatter_dimension=0, tiled=True),
        lax.psum_scatter(attn_grads[3], ("dp", "fsdp"), scatter_dimension=0, tiled=True),
        lax.psum_scatter(attn_grads[4], ("dp", "fsdp"), scatter_dimension=0, tiled=True),
    )
    conv_shards = (
        lax.psum_scatter(conv_grads[0], ("dp", "fsdp"), scatter_dimension=1, tiled=True),
        lax.psum_scatter(conv_grads[1], ("dp", "fsdp"), scatter_dimension=0, tiled=True),
        lax.psum_scatter(conv_grads[2], ("dp", "fsdp"), scatter_dimension=0, tiled=True),
        lax.psum_scatter(conv_grads[3], ("dp", "fsdp"), scatter_dimension=1, tiled=True),
        lax.psum_scatter(conv_grads[4], ("dp", "fsdp"), scatter_dimension=0, tiled=True),
        lax.psum_scatter(conv_grads[5], ("dp", "fsdp"), scatter_dimension=0, tiled=True),
        lax.psum_scatter(grad_final, ("dp", "fsdp"), scatter_dimension=1, tiled=True),
    )
    width = D // devices
    batch_shard = lax.dynamic_slice_in_dim(
        grad_batch, lax.axis_index(("dp", "fsdp")) * width, width, 1
    )
    return (
        result[None].astype(jnp.bfloat16),
        grad_start[None],
        jnp.stack([first_shards[0], second_shards[0]]),
        jnp.stack([first_shards[1], second_shards[1]]),
        jnp.stack([first_shards[2], second_shards[2]]),
        jnp.stack([first_shards[3], second_shards[3]]),
        jnp.stack([first_shards[4], second_shards[4]]),
        attn_shards[0],
        attn_shards[1],
        attn_shards[2],
        attn_shards[3],
        attn_shards[4],
        conv_shards[0],
        conv_shards[1],
        conv_shards[2],
        conv_shards[3],
        batch_shard,
        conv_shards[4],
        conv_shards[5],
        conv_shards[6],
    )


def solution(mesh):
    in_specs = (
        P(("dp", "fsdp"), None, None),
        P(("dp", "fsdp"), None),
        P(),
        P(("dp", "fsdp"), None, None),
        P(None, None, ("dp", "fsdp")),
        P(None, ("dp", "fsdp"), None),
        P(None, ("dp", "fsdp")),
        P(None, ("dp", "fsdp"), None),
        P(None, ("dp", "fsdp")),
        P(None, ("dp", "fsdp")),
        P(("dp", "fsdp"), None),
        P(("dp", "fsdp"), None),
        P(("dp", "fsdp")),
        P(("dp", "fsdp")),
        P(None, ("dp", "fsdp")),
        P(("dp", "fsdp"), None),
        P(("dp", "fsdp")),
        P(None, ("dp", "fsdp")),
        P(None, ("dp", "fsdp")),
        P(("dp", "fsdp"), None),
        P(("dp", "fsdp")),
        P(None, ("dp", "fsdp")),
    )
    out_specs = (
        P(("dp", "fsdp"), None, None),
        P(("dp", "fsdp"), None, None),
        P(None, None, ("dp", "fsdp")),
        P(None, ("dp", "fsdp"), None),
        P(None, ("dp", "fsdp")),
        P(None, ("dp", "fsdp"), None),
        P(None, ("dp", "fsdp")),
        P(None, ("dp", "fsdp")),
        P(("dp", "fsdp"), None),
        P(("dp", "fsdp"), None),
        P(("dp", "fsdp")),
        P(("dp", "fsdp")),
        P(None, ("dp", "fsdp")),
        P(("dp", "fsdp"), None),
        P(("dp", "fsdp")),
        P(None, ("dp", "fsdp")),
        P(None, ("dp", "fsdp")),
        P(("dp", "fsdp"), None),
        P(("dp", "fsdp")),
        P(None, ("dp", "fsdp")),
    )
    fast = mesh.shape["dp"] == 4 and mesh.shape["fsdp"] == 8
    return jax.shard_map(local if fast else plain, mesh=mesh, in_specs=in_specs, out_specs=out_specs, check_vma=False)
```

```python
import jax
import jax.numpy as jnp
from jax import lax
from jax.experimental import pallas as pl
from jax.experimental.pallas import tpu as pltpu
from jax.sharding import PartitionSpec as P

D = 512
FF = 2048
HEADS = 8
HEAD_DIM = 64
BUCKETS = 32
L = 512
TAPS = 32
PAD = 16
epsilon = 1e-05
F32, BF16 = jnp.float32, jnp.bfloat16
MESH = pl.DeviceIdType.MESH

SMALL, IN0, OUT0, QKV, ATT, GLU, CONV, IN1, OUT1, ROWS = 0, 16, 80, 144, 192, 208, 240, 256, 320, 384
GRADS = ROWS - IN0
(S_FFN, S_FOB, S_ATTN, S_AOB, S_CONV, S_BATCH, S_COB, S_FINAL, S_TAPS, S_ROWS) = (0, 4, 6, 8, 9, 11, 13, 14, 16, 48)
CHUNK = 64


def dot(a, b):
    return jnp.dot(a, b, preferred_element_type=F32)


def dot_nt(a, b):
    return lax.dot_general(a, b, (((1,), (1,)), ((), ())), preferred_element_type=F32)


def dot_tn(a, b):
    return lax.dot_general(a, b, (((0,), (0,)), ((), ())), preferred_element_type=F32)


def chunks(body, carry=None, size=CHUNK):
    def step(i, carry):
        return body(pl.ds(pl.multiple_of(i * size, size), size), carry)

    return lax.fori_loop(0, L // size, step, carry)


def fold(values):
    return jnp.sum(values.reshape(values.shape[0] // 8, 8, values.shape[1]), axis=0)


def zeros8(width=D):
    return jnp.zeros((8, width), F32)


def total_row(values):
    return jnp.sum(values, axis=0, keepdims=True)


class Bag:
    pass


class Place:
    def __init__(self):
        self.planes = lax.axis_size("dp")
        self.chips = lax.axis_size("fsdp") // 2
        self.plane, inner = lax.axis_index("dp"), lax.axis_index("fsdp")
        self.z, self.core = inner // 2, inner % 2
        y, x = self.plane // 2, self.plane % 2
        self.plane_x, self.plane_y, self.plane_d = y * 2 + 1 - x, (1 - y) * 2 + x, (1 - y) * 2 + 1 - x
        self.twin = (self.plane, 2 * self.z + 1 - self.core)
        self.over_x = (self.plane_x, inner)
        self.over_y = (self.plane_y, inner)
        self.chip = [lax.rem(self.z + step, self.chips) for step in range(self.chips)]
        self.along = [(self.plane, 2 * chip + self.core) for chip in self.chip]
        self.rank = self.plane * 2 + self.core
        self.members = []
        for step in range(self.planes):
            for flip in range(2):
                if step or flip:
                    plane, core = lax.rem(self.plane + step, self.planes), lax.rem(self.core + flip, 2)
                    self.members.append(((plane, 2 * self.z + core), plane * 2 + core))


class Copies:
    def __init__(self, sends, receives, place):
        self.sends, self.receives, self.place = sends, receives, place
        self.begun = []

    def start(self, number, make, receive=None):
        def copy():
            source, target, device = make()
            return pltpu.make_async_remote_copy(
                source, target, self.sends.at[number], self.receives.at[number if receive is None else receive],
                device_id=device, device_id_type=MESH,
            )

        copy().start()
        self.begun.append(copy)

    def arrived(self, number, target):
        pltpu.make_async_remote_copy(
            target, target, self.sends.at[number], self.receives.at[number],
            device_id=self.place.twin, device_id_type=MESH,
        ).wait_recv()

    def sent(self):
        for copy in self.begun:
            copy().wait_send()
        self.begun = []


def gather_steps(place, weights, copies, first, begin, size, split):
    p, core, chips = place, place.core, place.chips
    rows = pl.ds(begin, size)
    parts = (pl.ds(begin, split), pl.ds(begin + split, size - split))

    def column(plane, side, which):
        return weights.at[plane, :, side, which]

    def move(number, ref, device):
        copies.start(first + number, lambda: (ref(), ref(), device))

    def along_z():
        for d in range(1, chips):
            move(d - 1, lambda: weights.at[p.plane, p.z, core, rows], p.along[d])

    def own_column():
        for d in range(1, chips):
            copies.arrived(first + d - 1, weights.at[p.plane, p.chip[chips - d], core, rows])
        own = lambda: column(p.plane, core, rows)
        move(chips - 1, own, p.over_x)
        move(chips, own, p.over_y)
        move(chips + 3, own, p.twin)

    def beside():
        copies.arrived(first + chips - 1, column(p.plane_x, core, rows))
        move(chips + 1, lambda: column(p.plane_x, core, parts[0]), p.over_y)
        copies.arrived(first + chips, column(p.plane_y, core, rows))
        move(chips + 2, lambda: column(p.plane_y, core, parts[1]), p.over_x)
        move(chips + 4, lambda: column(p.plane_x, core, rows), p.twin)
        move(chips + 5, lambda: column(p.plane_y, core, rows), p.twin)

    def across():
        copies.arrived(first + chips + 1, column(p.plane_d, core, parts[0]))
        copies.arrived(first + chips + 2, column(p.plane_d, core, parts[1]))
        move(chips + 6, lambda: column(p.plane_d, core, rows), p.twin)

    def twins():
        for number, plane in enumerate((p.plane, p.plane_x, p.plane_y, p.plane_d)):
            copies.arrived(first + chips + 3 + number, column(plane, 1 - core, rows))

    return [along_z, own_column, beside, across, twins]


def reduce_steps(place, data, twin, diagonal, from_x, from_y, from_z, copies, first, begin, size, split, landing, finish):
    p, core, chips = place, place.core, place.chips
    rows, lands = pl.ds(begin, size), pl.ds(landing, size)
    parts = (pl.ds(begin, split), pl.ds(begin + split, size - split))
    parts_land = (pl.ds(landing, split), pl.ds(landing + split, size - split))

    def column(plane, side, which):
        return data.at[plane, :, side, which]

    def add(plane, which, *sources):
        def step(zz, carry):
            value = data[plane, zz, core, which, :]
            for ref in sources:
                value = value + ref(zz)
            data[plane, zz, core, which, :] = value
            return carry

        lax.fori_loop(0, chips, step, 0)

    def read(ref, which, *lead):
        return lambda zz: ref[lead + (zz, which, slice(None))]

    def to_twin():
        for number, plane in enumerate((p.plane_d, p.plane_y, p.plane_x, p.plane)):
            copies.start(
                first + number, lambda plane=plane: (column(plane, 1 - core, rows), twin.at[plane, :, lands], p.twin)
            )

    def across():
        copies.arrived(first, twin.at[p.plane_d, :, lands])
        add(p.plane_d, rows, read(twin, lands, p.plane_d))
        copies.start(first + 4, lambda: (column(p.plane_d, core, parts[0]), diagonal.at[:, parts_land[0]], p.over_y))
        if split < size:
            copies.start(first + 5, lambda: (column(p.plane_d, core, parts[1]), diagonal.at[:, parts_land[1]], p.over_x))

    def beside():
        copies.arrived(first + 2, twin.at[p.plane_x, :, lands])
        copies.arrived(first + 4, diagonal.at[:, parts_land[0]])
        add(p.plane_x, rows, read(twin, lands, p.plane_x))
        add(p.plane_x, parts[0], read(diagonal, parts_land[0]))
        copies.start(first + 7, lambda: (column(p.plane_x, core, rows), from_x.at[:, lands], p.over_x))
        copies.arrived(first + 1, twin.at[p.plane_y, :, lands])
        add(p.plane_y, rows, read(twin, lands, p.plane_y))
        if split < size:
            copies.arrived(first + 5, diagonal.at[:, parts_land[1]])
            add(p.plane_y, parts[1], read(diagonal, parts_land[1]))
        copies.start(first + 6, lambda: (column(p.plane_y, core, rows), from_y.at[:, lands], p.over_y))

    def own_column():
        copies.arrived(first + 3, twin.at[p.plane, :, lands])
        copies.arrived(first + 6, from_y.at[:, lands])
        copies.arrived(first + 7, from_x.at[:, lands])
        add(p.plane, rows, read(twin, lands, p.plane), read(from_x, lands), read(from_y, lands))
        for d in range(1, chips):
            copies.start(
                first + 7 + d,
                lambda d=d: (data.at[p.plane, p.chip[d], core, rows], from_z.at[d - 1, lands], p.along[d]),
            )

    def along_z():
        for d in range(1, chips):
            copies.arrived(first + 7 + d, from_z.at[d - 1, lands])
        value = data[p.plane, p.z, core, rows, :].astype(F32)
        for d in range(1, chips):
            value = value + from_z[d - 1, lands, :].astype(F32)
        finish(value)

    return [to_twin, across, beside, own_column, along_z]


class Total:
    def __init__(self, place, own, near, part, far, result, copies, first):
        self.place, self.own, self.near, self.part, self.far, self.result = place, own, near, part, far, result
        self.copies, self.first = copies, first

    def start(self):
        p = self.place
        me = p.rank
        for i, (device, rank) in enumerate(p.members):
            self.copies.start(self.first + i, lambda device=device: (self.own, self.near.at[me], device), self.first + me)
        self.near[me] = self.own[...]

    def turn(self):
        p = self.place
        for device, rank in p.members:
            self.copies.arrived(self.first + rank, self.near.at[rank])
        value = self.near[0]
        for i in range(1, 2 * p.planes):
            value = value + self.near[i]
        self.part[...] = value
        base = self.first + 2 * p.planes
        for d in range(1, p.chips):
            self.copies.start(base + d, lambda d=d: (self.part, self.far.at[d], p.along[d]))

    def finish(self):
        p = self.place
        base = self.first + 2 * p.planes
        value = self.part[...]
        for d in range(1, p.chips):
            self.copies.arrived(base + d, self.far.at[d])
            value = value + self.far[d]
        self.result[...] = value


class Queue:
    def __init__(self):
        self.steps, self.taken = [], 0

    def add(self, *steps):
        self.steps += steps

    def take(self, count=1):
        for step in self.steps[self.taken : self.taken + count]:
            step()
        self.taken = min(len(self.steps), self.taken + count)

    def until(self, step):
        self.take(self.steps.index(step) + 1 - self.taken)

    def drain(self):
        self.take(len(self.steps) - self.taken)

    def inside(self, index, *at):
        for i in at:
            if self.taken < len(self.steps):
                pl.when(index == i)(self.steps[self.taken])
                self.taken += 1


def standard(values):
    values = values.astype(F32)
    center = values - jnp.mean(values, axis=-1, keepdims=True)
    inverse = lax.rsqrt(jnp.mean(center * center, axis=-1, keepdims=True) + epsilon)
    return center * inverse, inverse


def norm_rows(source, target, small, row):
    gain, shift = 1.0 + small[row : row + 1, :], small[row + 1 : row + 2, :]

    def body(rows, carry):
        target[rows, :] = (standard(source[rows, :])[0] * gain + shift).astype(target.dtype)
        return carry

    chunks(body, 0)


def norm_back(source, grad, upstream, result, small, row, grads):
    gain = 1.0 + small[row : row + 1, :]

    def body(rows, carry):
        unit, inverse = standard(source[rows, :])
        given = grad[rows, :].astype(F32)
        inner = given * gain
        back = inverse * (
            inner
            - jnp.mean(inner, axis=-1, keepdims=True)
            - unit * jnp.mean(inner * unit, axis=-1, keepdims=True)
        )
        result[rows, :] = back if upstream is None else upstream[rows, :] + back
        return carry[0] + fold(given * unit), carry[1] + fold(given)

    first, second = chunks(body, (zeros8(), zeros8()))
    grads[row : row + 1, :] = total_row(first)
    grads[row + 1 : row + 2, :] = total_row(second)


def block_cols(c):
    return pl.ds(pl.multiple_of(c * D, D), D)


def columns(weights, start, block):
    return weights[:, :, :, pl.ds(pl.multiple_of(start + 16 * block, 16), 16), :].reshape(D, D)


def put_columns(weights, start, block, value):
    rows = pl.ds(pl.multiple_of(start + 16 * block, 16), 16)
    weights[:, :, :, rows, :] = value.astype(BF16).reshape(weights.shape[:3] + (16, D))


def lines_of(weights, start, block):
    return weights[block, :, :, start : start + 64, :].reshape(D, D)


def put_lines(weights, start, block, value):
    weights[block, :, :, start : start + 64, :] = value.astype(BF16).reshape(weights.shape[1:3] + (64, D))


def feed_inner(source, normed, active, slope, hold, weights, small, inner_bias, layer, pump):
    norm_rows(source, normed, small, S_FFN + 2 * layer)

    def block(c, carry):
        cols = block_cols(c)
        hold[...] = dot(normed[...], columns(weights, (IN0, IN1)[layer], c))
        bias = inner_bias[layer : layer + 1, cols]

        def body(rows, carry):
            inner = hold[rows, :] + bias
            sigma = jax.nn.sigmoid(inner)
            value = inner * sigma
            active[rows, cols] = value.astype(BF16)
            slope[rows, cols] = (sigma + value * (1.0 - sigma)).astype(BF16)
            return carry

        chunks(body, 0)
        pump(c)
        return carry

    lax.fori_loop(0, FF // D, block, 0)


def feed_outer(source, active, result, hold, weights, small, layer):
    begin = (OUT0, OUT1)[layer]

    def block(c, carry):
        part = dot(active[:, block_cols(c)], lines_of(weights, begin, c))

        @pl.when(c == 0)
        def _():
            hold[...] = part

        @pl.when(c > 0)
        def _():
            hold[...] += part

        return carry

    lax.fori_loop(0, FF // D, block, 0)
    bias = small[S_FOB + layer : S_FOB + layer + 1, :]

    def body(rows, carry):
        result[rows, :] = source[rows, :].astype(F32) + 0.5 * (hold[rows, :] + bias)
        return carry

    chunks(body, 0)


def feed_back_outer(upstream, active, slope, low, hold, weights, grads, inner_grads, layer, pump):
    begin = (OUT0, OUT1)[layer]

    def start(rows, carry):
        half = 0.5 * upstream[rows, :]
        low[rows, :] = half.astype(BF16)
        return carry + fold(half)

    grads[S_FOB + layer : S_FOB + layer + 1, :] = total_row(chunks(start, zeros8()))

    def block(c, carry):
        cols = block_cols(c)
        hold[...] = dot_nt(low[...], lines_of(weights, begin, c))

        def body(rows, carry):
            grad = hold[rows, :] * slope[rows, cols].astype(F32)
            slope[rows, cols] = grad.astype(BF16)
            return carry + fold(grad)

        inner_grads[layer : layer + 1, cols] = total_row(chunks(body, zeros8()))
        put_lines(weights, begin, c, dot_tn(active[:, cols], low[...]))
        pump(c)
        return carry

    lax.fori_loop(0, FF // D, block, 0)


def product_back(grad, normed, total, weights, begin, blocks, pump):
    def block(c, carry):
        cols = block_cols(c)
        part = dot_nt(grad[:, cols], columns(weights, begin, c))

        @pl.when(c == 0)
        def _():
            total[...] = part

        @pl.when(c > 0)
        def _():
            total[...] += part

        put_columns(weights, begin, c, dot_tn(normed[...], grad[:, cols]))
        pump(c)
        return carry

    lax.fori_loop(0, blocks, block, 0)


def bucket_choice(buckets):
    return (lax.broadcasted_iota(jnp.int32, (BUCKETS, 2 * L), 0) == buckets[...]).astype(F32)


def attention_mix(source, normed, mixed, weights, small):
    norm_rows(source, normed, small, S_ATTN)

    def mix(c, carry):
        mixed[:, block_cols(c)] = dot(normed[...], columns(weights, QKV, c)).astype(BF16)
        return carry

    lax.fori_loop(0, 3, mix, 0)


def attention_forward(source, mixed, probs, joined, result, lines, hold, weights, small, table, buckets, bounds, marks, pump):
    lines[...] = dot(table[...].astype(BF16), bucket_choice(buckets).astype(BF16))
    lane = lax.broadcasted_iota(jnp.int32, (1, 128), 1)
    size = 128

    def pair(index, carry):
        begin = pl.multiple_of(128 * index, 128)
        keys = mixed[:, pl.ds(D + begin, 128)]
        contents = mixed[:, pl.ds(2 * D + begin, 128)]
        for block in range(L // size):
            rows = pl.ds(block * size, size)
            query = mixed[rows, pl.ds(begin, 128)]
            same = bounds[PAD + block * size : PAD + (block + 1) * size, 0:1] == marks[...]
            parts = []
            for half in range(2):
                head = 2 * index + half
                here = (lane // HEAD_DIM) == half
                raw = dot_nt(jnp.where(here, query, jnp.zeros_like(query)), keys)
                window = lines[pl.ds(head, 1), 384 - block * size : 1024 - block * size]
                square = pltpu.roll(jnp.broadcast_to(window, (size, 640)), 513, 1, stride=1, stride_axis=0)
                scores = jnp.where(same, raw * HEAD_DIM ** (-0.5) + square[:, :L], -1e30)
                raised = jnp.exp(scores - jnp.max(scores, axis=1, keepdims=True))
                share = (raised * (1.0 / jnp.sum(raised, axis=1, keepdims=True))).astype(BF16)
                probs[head, rows, :] = share
                parts.append(dot(share, contents))
            joined[rows, pl.ds(begin, 128)] = jnp.where(lane < HEAD_DIM, parts[0], parts[1]).astype(BF16)
        pump(index)
        return carry

    lax.fori_loop(0, HEADS // 2, pair, 0)
    hold[...] = dot(joined[...], columns(weights, ATT, 0))
    bias = small[S_AOB : S_AOB + 1, :]

    def body(rows, carry):
        result[rows, :] = source[rows, :] + hold[rows, :] + bias
        return carry

    chunks(body, 0)


def attention_backward(
    upstream, mixed, probs, joined, low, spread, grad_mixed, scaled, hold, lines, weights, buckets, grads, table_grad, pump
):
    def start(rows, carry):
        given = upstream[rows, :]
        low[rows, :] = given.astype(BF16)
        return carry + fold(given)

    grads[S_AOB : S_AOB + 1, :] = total_row(chunks(start, zeros8()))
    spread[...] = dot_nt(low[...], columns(weights, ATT, 0)).astype(BF16)
    put_columns(weights, ATT, 0, dot_tn(joined[...], low[...]))
    lane = lax.broadcasted_iota(jnp.int32, (1, 128), 1)
    row8 = lax.broadcasted_iota(jnp.int32, (8, 2 * L), 0)
    size = 128

    def pair(index, carry):
        begin = pl.multiple_of(128 * index, 128)
        query = mixed[:, pl.ds(begin, 128)]
        keys = mixed[:, pl.ds(D + begin, 128)]
        contents = mixed[:, pl.ds(2 * D + begin, 128)]
        incoming = spread[:, pl.ds(begin, 128)]
        parts = []
        for half in range(2):
            head = 2 * index + half
            here = (lane // HEAD_DIM) == half
            hold[...] = dot_nt(jnp.where(here, incoming, jnp.zeros_like(incoming)), contents)
            sums = zeros8(2 * L)
            for block in range(L // size):
                rows = pl.ds(block * size, size)
                share = probs[head, rows, :].astype(F32)
                given = hold[rows, :]
                slant = share * (given - jnp.sum(given * share, axis=1, keepdims=True))
                scaled[rows, :] = (slant * HEAD_DIM ** (-0.5)).astype(BF16)
                part = zeros8(640)
                for t in range(size // 8):
                    tile = jnp.concatenate([slant[8 * t : 8 * t + 8], zeros8(128)], axis=1)
                    part += pltpu.roll(tile, 120 - 8 * t, 1)
                first = 384 - block * size
                pieces = [part]
                if first:
                    pieces = [zeros8(first)] + pieces
                if block:
                    pieces = pieces + [zeros8(block * size)]
                sums += jnp.concatenate(pieces, axis=1)
            line = zeros8(2 * L)
            for r in range(8):
                line += jnp.where(row8 == r, pltpu.roll(sums, 7 - r, 1), 0.0)
            lines[pl.ds(head, 1), :] = total_row(line)
            parts.append((dot(scaled[...], keys), dot_tn(scaled[...], query), dot_tn(probs[head], incoming)))
        for third in range(3):
            merged = jnp.where(lane < HEAD_DIM, parts[0][third], parts[1][third])
            grad_mixed[:, pl.ds(third * D + begin, 128)] = merged.astype(BF16)
        pump(index)
        return carry

    lax.fori_loop(0, HEADS // 2, pair, 0)
    table_grad[...] = lax.dot_general(
        lines[...], bucket_choice(buckets), (((1,), (1,)), ((), ())),
        precision=lax.Precision.HIGHEST, preferred_element_type=F32,
    )


def clear_pads(padded):
    edge = jnp.zeros((4, PAD, 128), F32)
    padded[:, 0:PAD, :] = edge
    padded[:, PAD + L : 2 * PAD + L, :] = edge


def conv_front(source, normed, sigma, gated, middle, sums, hold, weights, small, gate_bias, bounds, pump):
    norm_rows(source, normed, small, S_CONV)
    clear_pads(gated)
    hold[...] = dot(normed[...], columns(weights, GLU, 1))
    bias = gate_bias[0:1, D:]

    def gate(rows, carry):
        sigma[rows, :] = jax.nn.sigmoid(hold[rows, :] + bias)
        return carry

    chunks(gate, 0)
    hold[...] = dot(normed[...], columns(weights, GLU, 0))
    bias = gate_bias[0:1, :D]

    def unit(rows, carry):
        values = (hold[rows, :] + bias) * sigma[rows, :]
        for j in range(4):
            gated[j, pl.ds(rows.start + PAD, CHUNK), :] = values[:, 128 * j : 128 * j + 128]
        return carry

    chunks(unit, 0)
    size = 16

    def slide(i, carry):
        begin = pl.multiple_of(i * size, size)
        marks = bounds[pl.ds(begin + PAD, size), :]
        accs = [jnp.zeros((size, 128), F32) for _ in range(4)]
        for k in range(TAPS):
            same = bounds[pl.ds(begin + k, size), :] == marks
            for j in range(4):
                tap = small[S_TAPS + k : S_TAPS + k + 1, 128 * j : 128 * j + 128]
                accs[j] += jnp.where(same, gated[j, pl.ds(begin + k, size), :], 0.0) * tap
        result = []
        for j in range(4):
            middle[pl.ds(begin, size), 128 * j : 128 * j + 128] = accs[j]
            result.append(carry[j] + fold(accs[j]))
            result.append(carry[4 + j] + fold(accs[j] * accs[j]))
        pump(i)
        return result[0::2] + result[1::2]

    ends = lax.fori_loop(0, L // size, slide, [zeros8(128)] * 8)
    sums[...] = zeros8()
    for j in range(4):
        sums[0:1, 128 * j : 128 * j + 128] = total_row(ends[j])
        sums[1:2, 128 * j : 128 * j + 128] = total_row(ends[4 + j])


def conv_rest(source, middle, sums, unit, active, slope, result, hold, weights, small, frames):
    center = sums[0:1, :] * (1.0 / frames)
    inverse = lax.rsqrt(sums[1:2, :] * (1.0 / frames) - center * center + epsilon)
    gain, shift = 1.0 + small[S_BATCH : S_BATCH + 1, :], small[S_BATCH + 1 : S_BATCH + 2, :]

    def body(rows, carry):
        values = (middle[rows, :] - center) * inverse
        unit[rows, :] = values
        normal = values * gain + shift
        sigma = jax.nn.sigmoid(normal)
        value = normal * sigma
        active[rows, :] = value.astype(BF16)
        slope[rows, :] = (sigma + value * (1.0 - sigma)).astype(slope.dtype)
        return carry

    chunks(body, 0)
    hold[...] = dot(active[...], columns(weights, CONV, 0))
    bias = small[S_COB : S_COB + 1, :]

    def add(rows, carry):
        result[rows, :] = source[rows, :] + hold[rows, :] + bias
        return carry

    chunks(add, 0)


def conv_back_rest(upstream, unit, slope, grad_normal, low, hold, weights, grads, sums):
    def start(rows, carry):
        given = upstream[rows, :]
        low[rows, :] = given.astype(BF16)
        return carry + fold(given)

    grads[S_COB : S_COB + 1, :] = total_row(chunks(start, zeros8()))
    hold[...] = dot_nt(low[...], columns(weights, CONV, 0))

    def body(rows, carry):
        grad = hold[rows, :] * slope[rows, :].astype(F32)
        grad_normal[rows, :] = grad
        return carry[0] + fold(grad), carry[1] + fold(grad * unit[rows, :])

    first, second = chunks(body, (zeros8(), zeros8()))
    sums[...] = zeros8()
    sums[0:1, :] = total_row(first)
    sums[1:2, :] = total_row(second)
    grads[S_BATCH : S_BATCH + 1, :] = total_row(second)
    grads[S_BATCH + 1 : S_BATCH + 2, :] = total_row(first)


def conv_back_front(
    sigma, gated, unit, grad_normal, front_sums, sums, padded, grad_joined, hold, tap_sums, small, bounds, grads, gate_grads,
    frames, pump,
):
    center = front_sums[0:1, :] * (1.0 / frames)
    inverse = lax.rsqrt(front_sums[1:2, :] * (1.0 / frames) - center * center + epsilon)
    gain = 1.0 + small[S_BATCH : S_BATCH + 1, :]
    mean0, mean1 = gain * sums[0:1, :] * (1.0 / frames), gain * sums[1:2, :] * (1.0 / frames)
    clear_pads(padded)

    def start(rows, carry):
        grad = inverse * (gain * grad_normal[rows, :] - mean0 - unit[rows, :] * mean1)
        for j in range(4):
            padded[j, pl.ds(rows.start + PAD, CHUNK), :] = grad[:, 128 * j : 128 * j + 128]
        return carry

    chunks(start, 0)
    tap_sums[...] = jnp.zeros_like(tap_sums)
    size = 16

    def slide(i, carry):
        begin = pl.multiple_of(i * size, size)
        marks = bounds[pl.ds(begin + PAD, size), :]
        accs = [jnp.zeros((size, 128), F32) for _ in range(4)]
        for k in range(TAPS):
            same = bounds[pl.ds(begin + 2 * PAD - k, size), :] == marks
            for j in range(4):
                tap = small[S_TAPS + k : S_TAPS + k + 1, 128 * j : 128 * j + 128]
                accs[j] += jnp.where(same, padded[j, pl.ds(begin + 2 * PAD - k, size), :], 0.0) * tap
        for j in range(4):
            hold[pl.ds(begin, size), 128 * j : 128 * j + 128] = accs[j]
        grads_here = [padded[j, pl.ds(begin + PAD, size), :] for j in range(4)]
        for k in range(TAPS):
            same = bounds[pl.ds(begin + k, size), :] == marks
            for j in range(4):
                term = jnp.where(same, gated[j, pl.ds(begin + k, size), :], 0.0) * grads_here[j]
                tap_sums[k, :, 128 * j : 128 * j + 128] += fold(term)
        pump(i)
        return carry

    lax.fori_loop(0, L // size, slide, 0)
    grads[S_TAPS : S_TAPS + TAPS, :] = jnp.sum(tap_sums[...], axis=1)

    def split(rows, carry):
        grad = hold[rows, :]
        gate = sigma[rows, :]
        values = jnp.concatenate([gated[j, pl.ds(rows.start + PAD, CHUNK), :] for j in range(4)], axis=1)
        first = grad * gate
        second = grad * values * (1.0 - gate)
        grad_joined[rows, :D] = first.astype(BF16)
        grad_joined[rows, D : 2 * D] = second.astype(BF16)
        return carry[0] + fold(first), carry[1] + fold(second)

    first, second = chunks(split, (zeros8(), zeros8()))
    gate_grads[0:1, :D] = total_row(first)
    gate_grads[0:1, D:] = total_row(second)


THIN = (
    ("ffn_norm", S_FFN), ("ffn_out_bias", S_FOB), ("attn_norm", S_ATTN), ("attn_out_bias", S_AOB), ("conv_norm", S_CONV),
    ("batch_norm", S_BATCH), ("conv_out_bias", S_COB), ("final_norm", S_FINAL), ("depth_kernel", S_TAPS),
)


def pack_small(b, tile):
    tile[...] = jnp.zeros_like(tile)
    for name, row in THIN:
        value = getattr(b, name)[...].astype(F32)
        value = value.reshape(-1, value.shape[-1])
        for r in range(0, value.shape[0], 16):
            part = value[r : r + 16]
            begin = (row + r) % 16
            at = 128 * ((row + r) // 16)
            tile[begin : begin + part.shape[0], at : at + part.shape[1]] = part
    tile[0:2, 384 : 384 + b.ffn_in_bias.shape[1]] = b.ffn_in_bias[...].astype(F32)
    wide, few = b.glu_bias.shape[0], b.rel_table.shape[0]
    tile[2:3, 384 : 384 + wide] = b.glu_bias[...].astype(F32).reshape(1, wide)
    tile[3:4, 384 : 384 + few] = b.rel_table[...].astype(F32).reshape(1, few)


def pack_weights(b, put):
    for layer in range(2):
        for c in range(FF // D):
            put((IN0, IN1)[layer] + 16 * c, b.ffn_in[layer, :, D * c : D * c + D])
        put((OUT0, OUT1)[layer], b.ffn_out[layer])
    for c in range(3):
        put(QKV + 16 * c, b.qkv_weight[:, D * c : D * c + D])
    put(ATT, b.attn_out[...])
    for c in range(2):
        put(GLU + 16 * c, b.glu_weight[:, D * c : D * c + D])
    put(CONV, b.conv_out[...])


def unpack_small(b, place):
    per = 2 * place.chips
    count = place.planes * per
    width = D // count
    for device in range(count):
        tile = b.weights[device // per, (device % per) // 2, device % 2, 0:16, :].astype(F32)
        for q in range(3):
            b.small[16 * q : 16 * q + 16, width * device : width * device + width] = tile[:, 128 * q : 128 * q + width]
        b.inner_bias[:, 4 * width * device : 4 * width * (device + 1)] = tile[0:2, 384 : 384 + 4 * width]
        b.gate_bias[:, 2 * width * device : 2 * width * (device + 1)] = tile[2:3, 384 : 384 + 2 * width]
        few = HEADS * BUCKETS // count
        head, at = few * device // BUCKETS, few * device % BUCKETS
        b.table[head : head + 1, at : at + few] = tile[3:4, 384 : 384 + few]


def pack_small_grads(b, place):
    per = 2 * place.chips
    count = place.planes * per
    width = D // count
    few = HEADS * BUCKETS // count
    for device in range(count):
        tile = b.edges.at[device // per, (device % per) // 2, device % 2]
        for g in range(8):
            tile[0:6, 16 * g : 16 * g + width] = b.grads[6 * g : 6 * g + 6, width * device : width * device + width]
        for m in range(2):
            tile[6:7, 64 * m : 64 * m + 4 * width] = b.inner_grads[m : m + 1, 4 * width * device : 4 * width * (device + 1)]
        tile[7:8, 0 : 2 * width] = b.gate_grads[:, 2 * width * device : 2 * width * (device + 1)]
        head, at = few * device // BUCKETS, few * device % BUCKETS
        tile[7:8, 64 : 64 + few] = b.table_grad[head : head + 1, at : at + few]


INPUTS = (
    "inputs", "segments", "buckets", "cotangent", "ffn_norm", "ffn_in", "ffn_in_bias", "ffn_out", "ffn_out_bias", "attn_norm",
    "qkv_weight", "attn_out", "attn_out_bias", "rel_table", "conv_norm", "glu_weight", "glu_bias", "depth_kernel", "batch_norm",
    "conv_out", "conv_out_bias", "final_norm",
)
OUTPUTS = ("output", "grad_x", "shard", "thin")
GATHERS = ((0, 80, 48), (80, 64, 32), (144, 112, 64), (256, 128, 64))
REDUCES = ((OUT1, 64, 32), (IN1, 64, 32), (GLU, 48, 32), (QKV, 64, 32), (OUT0, 64, 32), (IN0, 64, 32))


def scratch_of(planes, chips):
    wide, low, big = pltpu.VMEM((L, D), F32), pltpu.VMEM((L, D), BF16), pltpu.VMEM((L, FF), BF16)
    pads = pltpu.VMEM((4, L + 2 * PAD, 128), F32)
    stats = pltpu.VMEM((8, D), F32)
    return dict(
        weights=pltpu.VMEM((planes, chips, 2, ROWS, D), BF16),
        twin=pltpu.VMEM((planes, chips, GRADS, D), BF16),
        diagonal=pltpu.VMEM((chips, GRADS, D), BF16),
        from_x=pltpu.VMEM((chips, GRADS, D), BF16),
        from_y=pltpu.VMEM((chips, GRADS, D), BF16),
        from_z=pltpu.VMEM((chips - 1, GRADS, D), BF16),
        edges=pltpu.VMEM((planes, chips, 2, 8, 128), F32),
        edge_twin=pltpu.VMEM((planes, chips, 8, 128), F32),
        edge_diagonal=pltpu.VMEM((chips, 8, 128), F32),
        edge_x=pltpu.VMEM((chips, 8, 128), F32),
        edge_y=pltpu.VMEM((chips, 8, 128), F32),
        edge_z=pltpu.VMEM((chips - 1, 8, 128), F32),
        small=pltpu.VMEM((S_ROWS, D), F32),
        inner_bias=pltpu.VMEM((2, FF), F32),
        gate_bias=pltpu.VMEM((1, 2 * D), F32),
        table=pltpu.VMEM((HEADS, BUCKETS), F32),
        tile=pltpu.VMEM((16, D), F32),
        grads=pltpu.VMEM((S_ROWS, D), F32),
        inner_grads=pltpu.VMEM((2, FF), F32),
        gate_grads=pltpu.VMEM((1, 2 * D), F32),
        table_grad=pltpu.VMEM((HEADS, BUCKETS), F32),
        lines=pltpu.VMEM((HEADS, 2 * L), F32),
        choice=pltpu.VMEM((1, 2 * L), jnp.int32),
        bounds=pltpu.VMEM((L + 2 * PAD, 128), F32),
        marks=pltpu.VMEM((1, L), F32),
        front_own=stats, back_own=stats, front_sums=stats, back_sums=stats, front_part=stats, back_part=stats,
        front_near=pltpu.VMEM((2 * planes, 8, D), F32), back_near=pltpu.VMEM((2 * planes, 8, D), F32),
        front_far=pltpu.VMEM((chips, 8, D), F32), back_far=pltpu.VMEM((chips, 8, D), F32),
        x1=wide, x2=wide, x3=wide, x4=wide, normed0=low, normed_a=low, normed_c=low, normed1=low,
        active0=big, slope0=big, active1=big, slope1=big, mixed=pltpu.VMEM((L, 3 * D), BF16),
        probs=pltpu.VMEM((HEADS, L, L), BF16), joined=low, sigma=wide, gated=pads, middle=wide, active_c=low, slope_c=low,
        padded=pads, low=low, spread=low, hold=wide, total=wide, taps=pltpu.VMEM((TAPS, 8, D), F32),
        gather_sends=pltpu.SemaphoreType.DMA((len(GATHERS) * (chips + 7),)),
        gather_receives=pltpu.SemaphoreType.DMA((len(GATHERS) * (chips + 7),)),
        reduce_sends=pltpu.SemaphoreType.DMA(((len(REDUCES) + 1) * (chips + 7),)),
        reduce_receives=pltpu.SemaphoreType.DMA(((len(REDUCES) + 1) * (chips + 7),)),
        total_sends=pltpu.SemaphoreType.DMA((2 * (2 * planes + chips),)),
        total_receives=pltpu.SemaphoreType.DMA((2 * (2 * planes + chips),)),
    )


def whole_kernel(names, *refs):
    b = Bag()
    for name, ref in zip(names, refs):
        setattr(b, name, ref)
    place = Place()
    planes, chips = place.planes, place.chips
    frames = L * planes * chips * 2
    barrier = pltpu.get_barrier_semaphore()
    near = [device for device, rank in place.members] + [place.along[d] for d in range(1, chips)]
    for device in near:
        pl.semaphore_signal(barrier, inc=1, device_id=device, device_id_type=MESH)
    pack_small(b, b.tile)

    def put(row, value):
        b.weights[place.plane, place.z, place.core, row : row + value.shape[0], :] = value

    put(0, b.tile[...].astype(BF16))
    pack_weights(b, put)
    pl.semaphore_wait(barrier, len(near))

    gathers = Copies(b.gather_sends, b.gather_receives, place)
    rounds = [
        gather_steps(place, b.weights, gathers, i * (chips + 7), begin, size, split)
        for i, (begin, size, split) in enumerate(GATHERS)
    ]
    queue = Queue()
    queue.add(
        rounds[0][0], rounds[1][0], rounds[0][1], rounds[0][2], rounds[1][1], rounds[2][0], rounds[0][3], rounds[1][2],
        rounds[0][4],
    )
    queue.add(
        rounds[2][1], rounds[1][3], rounds[3][0], rounds[1][4], rounds[2][2], rounds[3][1], rounds[2][3], rounds[2][4],
        rounds[3][2], rounds[3][3], rounds[3][4],
    )
    still = lambda index: None
    queue.take(2)
    b.marks[...] = b.segments[...].astype(F32)
    b.bounds[...] = jnp.full(b.bounds.shape, -1.0, F32)
    b.bounds[PAD : PAD + L, :] = jnp.broadcast_to(b.marks[...], (128, L)).T
    b.choice[...] = jnp.full(b.choice.shape, -1, jnp.int32)
    b.choice[:, 0 : 2 * L - 1] = b.buckets[...].reshape(1, 2 * L - 1)
    queue.until(rounds[0][4])
    unpack_small(b, place)

    x0 = b.inputs.at[0]
    feed_inner(
        x0, b.normed0, b.active0, b.slope0, b.hold, b.weights, b.small, b.inner_bias, 0, lambda c: queue.inside(c, 0, 1, 2)
    )
    queue.until(rounds[1][4])
    feed_outer(x0, b.active0, b.x1, b.hold, b.weights, b.small, 0)
    queue.until(rounds[2][4])
    attention_mix(b.x1, b.normed_a, b.mixed, b.weights, b.small)
    attention_forward(
        b.x1, b.mixed, b.probs, b.joined, b.x2, b.lines, b.hold, b.weights, b.small, b.table, b.choice, b.bounds, b.marks,
        lambda index: queue.inside(index, 0, 1, 2),
    )
    conv_front(
        b.x2, b.normed_c, b.sigma, b.gated, b.middle, b.front_own, b.hold, b.weights, b.small, b.gate_bias, b.bounds, still
    )
    totals = Copies(b.total_sends, b.total_receives, place)
    front = Total(place, b.front_own, b.front_near, b.front_part, b.front_far, b.front_sums, totals, 0)
    front.start()
    queue.drain()
    front.turn()
    front.finish()
    conv_rest(b.x2, b.middle, b.front_sums, b.middle, b.active_c, b.slope_c, b.x3, b.hold, b.weights, b.small, frames)
    feed_inner(b.x3, b.normed1, b.active1, b.slope1, b.hold, b.weights, b.small, b.inner_bias, 1, still)
    feed_outer(b.x3, b.active1, b.x4, b.hold, b.weights, b.small, 1)
    norm_rows(b.x4, b.output.at[0], b.small, S_FINAL)
    flow = b.x4
    norm_back(b.x4, b.cotangent.at[0], None, flow, b.small, S_FINAL, b.grads)
    gathers.sent()

    reduces = Copies(b.reduce_sends, b.reduce_receives, place)
    landings = (b.twin, b.diagonal, b.from_x, b.from_y, b.from_z)

    def finish(begin, size):
        def act(value):
            b.shard[begin - IN0 : begin - IN0 + size, :] = value

        return act

    backs = [
        reduce_steps(
            place, b.weights, *landings, reduces, i * (chips + 7), begin, size, split, begin - IN0, finish(begin, size)
        )
        for i, (begin, size, split) in enumerate(REDUCES)
    ]

    def finish_thin(value):
        b.thin[...] = value

    thin = reduce_steps(
        place, b.edges, b.edge_twin, b.edge_diagonal, b.edge_x, b.edge_y, b.edge_z, reduces, len(REDUCES) * (chips + 7),
        0, 8, 8, 0, finish_thin,
    )
    queue = Queue()
    feed_back_outer(flow, b.active1, b.slope1, b.low, b.hold, b.weights, b.grads, b.inner_grads, 1, still)
    queue.add(backs[0][0])
    queue.take()
    queue.add(backs[0][1])
    product_back(b.slope1, b.normed1, b.total, b.weights, IN1, 4, lambda c: queue.inside(c, 2))
    queue.add(backs[1][0], backs[0][2])
    queue.take()
    norm_back(b.x3, b.total, flow, flow, b.small, S_FFN + 2, b.grads)
    queue.take()
    grad_normal = b.x3
    conv_back_rest(flow, b.middle, b.slope_c, grad_normal, b.low, b.hold, b.weights, b.grads, b.back_own)
    back = Total(place, b.back_own, b.back_near, b.back_part, b.back_far, b.back_sums, totals, 2 * planes + chips)
    back.start()
    put_columns(b.weights, CONV, 0, dot_tn(b.active_c[...], b.low[...]))
    back.turn()
    queue.add(backs[1][1], backs[0][3], backs[1][2], backs[0][4], backs[1][3], backs[1][4])
    queue.take()
    back.finish()
    queue.take()
    conv_back_front(
        b.sigma, b.gated, b.middle, grad_normal, b.front_sums, b.back_sums, b.padded, b.active1, b.hold, b.taps, b.small,
        b.bounds, b.grads, b.gate_grads, frames, lambda i: queue.inside(i, 4, 12, 20, 28),
    )
    product_back(b.active1, b.normed_c, b.total, b.weights, GLU, 2, still)
    queue.add(backs[2][0])
    queue.take()
    norm_back(b.x2, b.total, flow, flow, b.small, S_CONV, b.grads)
    queue.add(backs[2][1], backs[2][2], backs[2][3], backs[2][4])
    attention_backward(
        flow, b.mixed, b.probs, b.joined, b.low, b.spread, b.active1, b.slope1.at[:, pl.ds(0, D)], b.hold, b.lines, b.weights,
        b.choice, b.grads, b.table_grad, lambda index: queue.inside(index, 0, 1, 2, 3),
    )
    product_back(b.active1, b.normed_a, b.total, b.weights, QKV, 3, still)
    queue.add(backs[3][0])
    queue.take()
    norm_back(b.x1, b.total, flow, flow, b.small, S_ATTN, b.grads)
    queue.add(backs[3][1], backs[3][2], backs[3][3], backs[3][4])
    feed_back_outer(
        flow, b.active0, b.slope0, b.low, b.hold, b.weights, b.grads, b.inner_grads, 0, lambda c: queue.inside(c, 0, 2)
    )
    queue.add(backs[4][0])
    product_back(b.slope0, b.normed0, b.total, b.weights, IN0, 4, lambda c: queue.inside(c, 0, 1, 3))
    queue.add(backs[5][0], backs[4][1], backs[5][1], backs[4][2])
    queue.take(2)
    norm_back(x0, b.total, flow, b.grad_x.at[0], b.small, S_FFN, b.grads)
    queue.take(2)
    pack_small_grads(b, place)
    queue.add(
        thin[0], backs[5][2], thin[1], backs[4][3], thin[2], backs[5][3], backs[4][4], thin[3], backs[5][4], thin[4]
    )
    queue.drain()
    reduces.sent()
    totals.sent()


def finish_kernel(*refs):
    (
        shard, thin, grad_ffn_norm, grad_ffn_in, grad_ffn_in_bias, grad_ffn_out, grad_ffn_out_bias, grad_attn_norm,
        grad_qkv, grad_attn_out, grad_attn_out_bias, grad_rel, grad_conv_norm, grad_glu, grad_glu_bias, grad_depth, grad_batch,
        grad_conv_out, grad_conv_out_bias, grad_final,
    ) = refs
    cut = lambda begin, size: shard[begin - IN0 : begin - IN0 + size, :]
    width = grad_final.shape[-1]

    def thin_rows(begin, count):
        rows = []
        for p in range(begin, begin + count):
            rows.append(thin[p % 6 : p % 6 + 1, 16 * (p // 6) : 16 * (p // 6) + width])
        return rows

    for layer in range(2):
        for c in range(FF // D):
            grad_ffn_in[layer, :, D * c : D * c + D] = cut((IN0, IN1)[layer] + 16 * c, 16)
        grad_ffn_out[layer] = cut((OUT0, OUT1)[layer], 64)
        grad_ffn_in_bias[layer : layer + 1, :] = thin[6:7, 64 * layer : 64 * layer + 4 * width]
        for r, row in enumerate(thin_rows(S_FFN + 2 * layer, 2)):
            grad_ffn_norm[layer, r : r + 1, :] = row
    for c in range(3):
        grad_qkv[:, D * c : D * c + D] = cut(QKV + 16 * c, 16)
    grad_attn_out[...] = cut(ATT, 16)
    for c in range(2):
        grad_glu[:, D * c : D * c + D] = cut(GLU + 16 * c, 16)
    grad_conv_out[...] = cut(CONV, 16)
    for ref, begin in (
        (grad_ffn_out_bias, S_FOB), (grad_attn_norm, S_ATTN), (grad_conv_norm, S_CONV), (grad_batch, S_BATCH),
        (grad_final, S_FINAL), (grad_depth, S_TAPS),
    ):
        for r, row in enumerate(thin_rows(begin, ref.shape[0])):
            ref[r : r + 1, :] = row
    grad_attn_out_bias[...] = thin_rows(S_AOB, 1)[0][0]
    grad_conv_out_bias[...] = thin_rows(S_COB, 1)[0][0]
    grad_glu_bias[...] = thin[7:8, 0 : 2 * width][0]
    grad_rel[...] = thin[7:8, 64 : 64 + grad_rel.shape[0]][0]


def shape(dims, kind=F32):
    return jax.ShapeDtypeStruct(dims, kind)


def local(*args):
    planes, chips = lax.axis_size("dp"), lax.axis_size("fsdp") // 2
    scratch = scratch_of(planes, chips)
    names = INPUTS + OUTPUTS + tuple(scratch)
    vmem = pl.BlockSpec(memory_space=pltpu.VMEM)
    output, grad_x, shard, thin = pl.pallas_call(
        lambda *refs: whole_kernel(names, *refs),
        out_shape=[shape((1, L, D), BF16), shape((1, L, D)), shape((GRADS, D)), shape((8, 128))],
        in_specs=[vmem] * len(args),
        out_specs=[vmem] * 4,
        scratch_shapes=list(scratch.values()),
        compiler_params=pltpu.CompilerParams(collective_id=0, has_side_effects=True, vmem_limit_bytes=VMEM_BYTES),
        name="layer",
    )(*args)
    given = dict(zip(INPUTS, args))
    outs = [
        shape(given[name].shape)
        for name in (
            "ffn_norm", "ffn_in", "ffn_in_bias", "ffn_out", "ffn_out_bias", "attn_norm", "qkv_weight", "attn_out",
            "attn_out_bias", "rel_table", "conv_norm", "glu_weight", "glu_bias", "depth_kernel", "batch_norm", "conv_out",
            "conv_out_bias", "final_norm",
        )
    ]
    grads = pl.pallas_call(
        finish_kernel, out_shape=outs, in_specs=[vmem] * 2, out_specs=[vmem] * len(outs), name="unpack",
    )(shard, thin)
    return (output, grad_x) + tuple(grads)


VMEM_BYTES = 62 * 1024 * 1024


highest = lax.Precision.HIGHEST


def layer_norm(values, params):
    center = values - jnp.mean(values, axis=-1, keepdims=True)
    spread = jnp.mean(center * center, axis=-1, keepdims=True)
    return center * lax.rsqrt(spread + epsilon) * (1.0 + params[0]) + params[1]


def silu_slope(values):
    sigma = jax.nn.sigmoid(values)
    return sigma * (1.0 + values * (1.0 - sigma))


def product(left, right):
    return jnp.dot(left, right, preferred_element_type=jnp.float32)


def product_left(left, right):
    return lax.dot_general(
        left, right, (((0,), (0,)), ((), ())), preferred_element_type=jnp.float32
    )


def product_right(left, right):
    return lax.dot_general(
        left, right, (((1,), (1,)), ((), ())), preferred_element_type=jnp.float32
    )


def plain_fetch_feed(norms, inner_weight, inner_bias, outer_weight, outer_bias, layer):
    return (
        lax.all_gather(norms[layer], ("dp", "fsdp"), axis=1, tiled=True),
        lax.all_gather(inner_weight[layer], ("dp", "fsdp"), axis=0, tiled=True),
        lax.all_gather(inner_bias[layer], ("dp", "fsdp"), axis=0, tiled=True),
        lax.all_gather(outer_weight[layer], ("dp", "fsdp"), axis=0, tiled=True),
        lax.all_gather(outer_bias[layer], ("dp", "fsdp"), axis=0, tiled=True),
    )


def plain_reduce_feed(grads):
    return (
        lax.psum_scatter(grads[0], ("dp", "fsdp"), scatter_dimension=1, tiled=True),
        lax.psum_scatter(grads[1], ("dp", "fsdp"), scatter_dimension=0, tiled=True),
        lax.psum_scatter(grads[2], ("dp", "fsdp"), scatter_dimension=0, tiled=True),
        lax.psum_scatter(grads[3], ("dp", "fsdp"), scatter_dimension=0, tiled=True),
        lax.psum_scatter(grads[4], ("dp", "fsdp"), scatter_dimension=0, tiled=True),
    )


def fetch_attention(attn_norm, qkv_weight, attn_out, attn_out_bias, rel_table):
    return (
        lax.all_gather(attn_norm, ("dp", "fsdp"), axis=1, tiled=True),
        lax.all_gather(qkv_weight, ("dp", "fsdp"), axis=0, tiled=True),
        lax.all_gather(attn_out, ("dp", "fsdp"), axis=0, tiled=True),
        lax.all_gather(attn_out_bias, ("dp", "fsdp"), axis=0, tiled=True),
        lax.all_gather(rel_table, ("dp", "fsdp"), axis=0, tiled=True),
    )


def fetch_conv(
    conv_norm, glu_weight, glu_bias, depth_kernel, batch_norm, conv_out, conv_out_bias, final_norm
):
    return (
        lax.all_gather(conv_norm, ("dp", "fsdp"), axis=1, tiled=True),
        lax.all_gather(glu_weight, ("dp", "fsdp"), axis=0, tiled=True),
        lax.all_gather(glu_bias, ("dp", "fsdp"), axis=0, tiled=True),
        lax.all_gather(depth_kernel, ("dp", "fsdp"), axis=1, tiled=True),
        lax.all_gather(batch_norm, ("dp", "fsdp"), axis=1, tiled=True),
        lax.all_gather(conv_out, ("dp", "fsdp"), axis=0, tiled=True),
        lax.all_gather(conv_out_bias, ("dp", "fsdp"), axis=0, tiled=True),
        lax.all_gather(final_norm, ("dp", "fsdp"), axis=1, tiled=True),
    )


def plain_feed_forward(values, weights):
    norm, weight_in, bias_in, weight_out, bias_out = weights
    normed, norm_back = jax.vjp(layer_norm, values, norm.astype(jnp.float32))
    normed_low = normed.astype(jnp.bfloat16)
    inner = product(normed_low, weight_in) + bias_in.astype(jnp.float32)
    active = jax.nn.silu(inner).astype(jnp.bfloat16)
    result = values + 0.5 * (product(active, weight_out) + bias_out.astype(jnp.float32))
    return (result, (normed_low, inner, active, norm_back))


def plain_feed_backward(upstream, weights, saved):
    norm, weight_in, bias_in, weight_out, bias_out = weights
    normed_low, inner, active, norm_back = saved
    branch = 0.5 * upstream
    branch_low = branch.astype(jnp.bfloat16)
    grad_weight_out = product_left(active, branch_low)
    grad_inner = product_right(branch_low, weight_out) * silu_slope(inner)
    inner_low = grad_inner.astype(jnp.bfloat16)
    grad_weight_in = product_left(normed_low, inner_low)
    grad_values, grad_norm = norm_back(product_right(inner_low, weight_in))
    return (
        upstream + grad_values,
        (
            grad_norm,
            grad_weight_in,
            jnp.sum(grad_inner, axis=0),
            grad_weight_out,
            jnp.sum(branch, axis=0),
        ),
    )


def relative_lines(table, buckets):
    choose = (buckets[None, :] == jnp.arange(BUCKETS, dtype=jnp.int32)[:, None]).astype(jnp.float32)
    lines = jnp.dot(table.astype(jnp.float32).reshape(HEADS, BUCKETS), choose, precision=highest)
    return (lines, choose)


def bias_square(line, length):
    tiled = jnp.broadcast_to(line, (length, 2 * length - 1)).reshape(-1)
    tiled = jnp.concatenate([tiled, jnp.zeros((length,), line.dtype)])
    return tiled.reshape(length, 2 * length)[:, :length][::-1]


def diagonal_sums(square):
    length = square.shape[0]
    padded = jnp.concatenate([square[::-1], jnp.zeros_like(square)], axis=1).reshape(-1)
    return jnp.sum(padded[: length * (2 * length - 1)].reshape(length, 2 * length - 1), axis=0)


def head_scores(query, keys_head, line, same):
    raw = product_right(query, keys_head)
    return jnp.where(same, raw * HEAD_DIM ** (-0.5) + bias_square(line, query.shape[0]), -1e30)


def plain_attention_forward(values, weights, marks, buckets):
    norm, mixer, weight_out, bias_out, table = weights
    length = values.shape[0]
    normed, norm_back = jax.vjp(layer_norm, values, norm.astype(jnp.float32))
    normed_low = normed.astype(jnp.bfloat16)
    mixed = (
        product(normed_low, mixer)
        .astype(jnp.bfloat16)
        .reshape(length, 3, HEADS, HEAD_DIM)
        .transpose(1, 2, 0, 3)
    )
    lines, choose = relative_lines(table, buckets)
    same = marks[:, None] == marks[None, :]

    def head_forward(items):
        query, keys_head, contents, line = items
        scores = head_scores(query, keys_head, line, same)
        peak = jnp.max(scores, axis=1, keepdims=True)
        raised = jnp.exp(scores - peak)
        total = jnp.sum(raised, axis=1, keepdims=True)
        probs = (raised / total).astype(jnp.bfloat16)
        return (product(probs, contents).astype(jnp.bfloat16), (peak + jnp.log(total))[:, 0])

    attended, logsum = lax.map(head_forward, (mixed[0], mixed[1], mixed[2], lines))
    joined = attended.transpose(1, 0, 2).reshape(length, D)
    result = values + product(joined, weight_out) + bias_out.astype(jnp.float32)
    return (result, (normed_low, mixed, lines, choose, same, joined, logsum, norm_back))


def plain_attention_backward(upstream, weights, saved):
    norm, mixer, weight_out, bias_out, table = weights
    normed_low, mixed, lines, choose, same, joined, logsum, norm_back = saved
    length = upstream.shape[0]
    upstream_low = upstream.astype(jnp.bfloat16)
    grad_weight_out = product_left(joined, upstream_low)
    grad_joined = (
        product_right(upstream_low, weight_out)
        .astype(jnp.bfloat16)
        .reshape(length, HEADS, HEAD_DIM)
        .transpose(1, 0, 2)
    )

    def head_backward(items):
        query, keys_head, contents, line, incoming, logs = items
        scores = head_scores(query, keys_head, line, same)
        probs = jnp.exp(scores - logs[:, None])
        grad_contents = product_left(probs.astype(jnp.bfloat16), incoming)
        grad_probs = product_right(incoming, contents)
        grad_scores = probs * (grad_probs - jnp.sum(grad_probs * probs, axis=1, keepdims=True))
        scaled = (grad_scores * HEAD_DIM ** (-0.5)).astype(jnp.bfloat16)
        grad_query = product(scaled, keys_head)
        grad_keys = product_left(scaled, query)
        return (
            jnp.stack([grad_query, grad_keys, grad_contents]).astype(jnp.bfloat16),
            diagonal_sums(grad_scores),
        )

    grad_mixed, grad_lines = lax.map(
        head_backward, (mixed[0], mixed[1], mixed[2], lines, grad_joined, logsum)
    )
    grad_flat = grad_mixed.transpose(2, 1, 0, 3).reshape(length, 3 * D)
    grad_mixer = product_left(normed_low, grad_flat)
    grad_values, grad_norm = norm_back(product_right(grad_flat, mixer))
    grad_table = jnp.dot(grad_lines, choose.T, precision=highest).reshape(-1)
    return (
        upstream + grad_values,
        (grad_norm, grad_mixer, grad_weight_out, jnp.sum(upstream, axis=0), grad_table),
    )


def gate_unit(joined):
    width = joined.shape[1] // 2
    return joined[:, :width] * jax.nn.sigmoid(joined[:, width:])


def plain_depthwise(gated, kernel, marks):
    length = gated.shape[0]
    half = kernel.shape[0] // 2
    padded = jnp.pad(gated, ((half, half), (0, 0)))
    bounds = jnp.pad(marks, (half, half), constant_values=-1)
    total = jnp.zeros(gated.shape, gated.dtype)
    for step in range(kernel.shape[0]):
        same = (bounds[step : step + length] == marks)[:, None]
        total = total + jnp.where(same, padded[step : step + length], 0.0) * kernel[step]
    return total


def plain_conv_forward(values, weights, marks, frames):
    norm, weight_glu, bias_glu, kernel, batch, weight_out, bias_out, final = weights
    normed, norm_back = jax.vjp(layer_norm, values, norm.astype(jnp.float32))
    normed_low = normed.astype(jnp.bfloat16)
    joined = product(normed_low, weight_glu) + bias_glu.astype(jnp.float32)
    gated, gate_back = jax.vjp(gate_unit, joined)
    middle, depth_back = jax.vjp(
        lambda inner, taps: plain_depthwise(inner, taps, marks), gated, kernel.astype(jnp.float32)
    )
    sums = lax.psum((jnp.sum(middle, axis=0), jnp.sum(middle * middle, axis=0)), ("dp", "fsdp"))
    center = sums[0] / frames
    inverse = lax.rsqrt(sums[1] / frames - center * center + epsilon)
    gain = 1.0 + batch[0].astype(jnp.float32)
    unit = (middle - center) * inverse
    normal = unit * gain + batch[1].astype(jnp.float32)
    active = jax.nn.silu(normal).astype(jnp.bfloat16)
    result = values + product(active, weight_out) + bias_out.astype(jnp.float32)
    return (
        result,
        (normed_low, gate_back, depth_back, inverse, gain, unit, normal, active, norm_back),
    )


def plain_conv_backward(upstream, weights, saved, frames):
    norm, weight_glu, bias_glu, kernel, batch, weight_out, bias_out, final = weights
    normed_low, gate_back, depth_back, inverse, gain, unit, normal, active, norm_back = saved
    upstream_low = upstream.astype(jnp.bfloat16)
    grad_weight_out = product_left(active, upstream_low)
    grad_normal = product_right(upstream_low, weight_out) * silu_slope(normal)
    sums = lax.psum(
        (jnp.sum(grad_normal, axis=0), jnp.sum(grad_normal * unit, axis=0)), ("dp", "fsdp")
    )
    grad_middle = inverse * (
        grad_normal * gain - gain * sums[0] / frames - unit * (gain * sums[1] / frames)
    )
    grad_gated, grad_kernel = depth_back(grad_middle)
    grad_joined = gate_back(grad_gated)[0]
    joined_low = grad_joined.astype(jnp.bfloat16)
    grad_weight_glu = product_left(normed_low, joined_low)
    grad_values, grad_norm = norm_back(product_right(joined_low, weight_glu))
    grad_batch = jnp.stack([sums[1], sums[0]])
    return (
        upstream + grad_values,
        (
            grad_norm,
            grad_weight_glu,
            jnp.sum(grad_joined, axis=0),
            grad_kernel,
            grad_weight_out,
            jnp.sum(upstream, axis=0),
        ),
        grad_batch,
    )


def plain(
    inputs,
    segments,
    buckets,
    cotangent,
    ffn_norm,
    ffn_in,
    ffn_in_bias,
    ffn_out,
    ffn_out_bias,
    attn_norm,
    qkv_weight,
    attn_out,
    attn_out_bias,
    rel_table,
    conv_norm,
    glu_weight,
    glu_bias,
    depth_kernel,
    batch_norm,
    conv_out,
    conv_out_bias,
    final_norm,
):
    values = inputs[0].astype(jnp.float32)
    marks = segments[0]
    devices = lax.axis_size(("dp", "fsdp"))
    frames = values.shape[0] * devices
    feed_first = plain_fetch_feed(ffn_norm, ffn_in, ffn_in_bias, ffn_out, ffn_out_bias, 0)
    first, first_saved = plain_feed_forward(values, feed_first)
    attn_weights = fetch_attention(attn_norm, qkv_weight, attn_out, attn_out_bias, rel_table)
    second, attn_saved = plain_attention_forward(first, attn_weights, marks, buckets)
    conv_weights = fetch_conv(
        conv_norm,
        glu_weight,
        glu_bias,
        depth_kernel,
        batch_norm,
        conv_out,
        conv_out_bias,
        final_norm,
    )
    third, conv_saved = plain_conv_forward(second, conv_weights, marks, frames)
    feed_second = plain_fetch_feed(ffn_norm, ffn_in, ffn_in_bias, ffn_out, ffn_out_bias, 1)
    fourth, second_saved = plain_feed_forward(third, feed_second)
    result, final_back = jax.vjp(layer_norm, fourth, conv_weights[7].astype(jnp.float32))
    grad_fourth, grad_final = final_back(cotangent[0].astype(jnp.float32))
    second_back = plain_fetch_feed(ffn_norm, ffn_in, ffn_in_bias, ffn_out, ffn_out_bias, 1)
    grad_third, second_grads = plain_feed_backward(grad_fourth, second_back, second_saved)
    conv_back = fetch_conv(
        conv_norm,
        glu_weight,
        glu_bias,
        depth_kernel,
        batch_norm,
        conv_out,
        conv_out_bias,
        final_norm,
    )
    grad_second, conv_grads, grad_batch = plain_conv_backward(grad_third, conv_back, conv_saved, frames)
    attn_back = fetch_attention(attn_norm, qkv_weight, attn_out, attn_out_bias, rel_table)
    grad_first, attn_grads = plain_attention_backward(grad_second, attn_back, attn_saved)
    first_back = plain_fetch_feed(ffn_norm, ffn_in, ffn_in_bias, ffn_out, ffn_out_bias, 0)
    grad_start, first_grads = plain_feed_backward(grad_first, first_back, first_saved)
    first_shards = plain_reduce_feed(first_grads)
    second_shards = plain_reduce_feed(second_grads)
    attn_shards = (
        lax.psum_scatter(attn_grads[0], ("dp", "fsdp"), scatter_dimension=1, tiled=True),
        lax.psum_scatter(attn_grads[1], ("dp", "fsdp"), scatter_dimension=0, tiled=True),
        lax.psum_scatter(attn_grads[2], ("dp", "fsdp"), scatter_dimension=0, tiled=True),
        lax.psum_scatter(attn_grads[3], ("dp", "fsdp"), scatter_dimension=0, tiled=True),
        lax.psum_scatter(attn_grads[4], ("dp", "fsdp"), scatter_dimension=0, tiled=True),
    )
    conv_shards = (
        lax.psum_scatter(conv_grads[0], ("dp", "fsdp"), scatter_dimension=1, tiled=True),
        lax.psum_scatter(conv_grads[1], ("dp", "fsdp"), scatter_dimension=0, tiled=True),
        lax.psum_scatter(conv_grads[2], ("dp", "fsdp"), scatter_dimension=0, tiled=True),
        lax.psum_scatter(conv_grads[3], ("dp", "fsdp"), scatter_dimension=1, tiled=True),
        lax.psum_scatter(conv_grads[4], ("dp", "fsdp"), scatter_dimension=0, tiled=True),
        lax.psum_scatter(conv_grads[5], ("dp", "fsdp"), scatter_dimension=0, tiled=True),
        lax.psum_scatter(grad_final, ("dp", "fsdp"), scatter_dimension=1, tiled=True),
    )
    width = D // devices
    batch_shard = lax.dynamic_slice_in_dim(
        grad_batch, lax.axis_index(("dp", "fsdp")) * width, width, 1
    )
    return (
        result[None].astype(jnp.bfloat16),
        grad_start[None],
        jnp.stack([first_shards[0], second_shards[0]]),
        jnp.stack([first_shards[1], second_shards[1]]),
        jnp.stack([first_shards[2], second_shards[2]]),
        jnp.stack([first_shards[3], second_shards[3]]),
        jnp.stack([first_shards[4], second_shards[4]]),
        attn_shards[0],
        attn_shards[1],
        attn_shards[2],
        attn_shards[3],
        attn_shards[4],
        conv_shards[0],
        conv_shards[1],
        conv_shards[2],
        conv_shards[3],
        batch_shard,
        conv_shards[4],
        conv_shards[5],
        conv_shards[6],
    )


def solution(mesh):
    in_specs = (
        P(("dp", "fsdp"), None, None),
        P(("dp", "fsdp"), None),
        P(),
        P(("dp", "fsdp"), None, None),
        P(None, None, ("dp", "fsdp")),
        P(None, ("dp", "fsdp"), None),
        P(None, ("dp", "fsdp")),
        P(None, ("dp", "fsdp"), None),
        P(None, ("dp", "fsdp")),
        P(None, ("dp", "fsdp")),
        P(("dp", "fsdp"), None),
        P(("dp", "fsdp"), None),
        P(("dp", "fsdp")),
        P(("dp", "fsdp")),
        P(None, ("dp", "fsdp")),
        P(("dp", "fsdp"), None),
        P(("dp", "fsdp")),
        P(None, ("dp", "fsdp")),
        P(None, ("dp", "fsdp")),
        P(("dp", "fsdp"), None),
        P(("dp", "fsdp")),
        P(None, ("dp", "fsdp")),
    )
    out_specs = (
        P(("dp", "fsdp"), None, None),
        P(("dp", "fsdp"), None, None),
        P(None, None, ("dp", "fsdp")),
        P(None, ("dp", "fsdp"), None),
        P(None, ("dp", "fsdp")),
        P(None, ("dp", "fsdp"), None),
        P(None, ("dp", "fsdp")),
        P(None, ("dp", "fsdp")),
        P(("dp", "fsdp"), None),
        P(("dp", "fsdp"), None),
        P(("dp", "fsdp")),
        P(("dp", "fsdp")),
        P(None, ("dp", "fsdp")),
        P(("dp", "fsdp"), None),
        P(("dp", "fsdp")),
        P(None, ("dp", "fsdp")),
        P(None, ("dp", "fsdp")),
        P(("dp", "fsdp"), None),
        P(("dp", "fsdp")),
        P(None, ("dp", "fsdp")),
    )
    fast = mesh.shape["dp"] == 4 and mesh.shape["fsdp"] == 8
    return jax.shard_map(local if fast else plain, mesh=mesh, in_specs=in_specs, out_specs=out_specs, check_vma=False)
```

```python
import jax
import jax.numpy as jnp
from jax import lax
from jax.experimental import pallas as pl
from jax.experimental.pallas import tpu as pltpu
from jax.sharding import PartitionSpec as P

D = 512
FF = 2048
HEADS = 8
HEAD_DIM = 64
BUCKETS = 32
L = 512
TAPS = 32
PAD = 16
epsilon = 1e-05
F32, BF16 = jnp.float32, jnp.bfloat16
MESH = pl.DeviceIdType.MESH

SMALL, IN0, OUT0, QKV, ATT, GLU, CONV, IN1, OUT1, ROWS = 0, 16, 80, 144, 192, 208, 240, 256, 320, 384
GRADS = ROWS - IN0
(S_FFN, S_FOB, S_ATTN, S_AOB, S_CONV, S_BATCH, S_COB, S_FINAL, S_TAPS, S_ROWS) = (0, 4, 6, 8, 9, 11, 13, 14, 16, 48)
CHUNK = 64


def dot(a, b):
    return jnp.dot(a, b, preferred_element_type=F32)


def dot_nt(a, b):
    return lax.dot_general(a, b, (((1,), (1,)), ((), ())), preferred_element_type=F32)


def dot_tn(a, b):
    return lax.dot_general(a, b, (((0,), (0,)), ((), ())), preferred_element_type=F32)


def chunks(body, carry=None, size=CHUNK):
    def step(i, carry):
        return body(pl.ds(pl.multiple_of(i * size, size), size), carry)

    return lax.fori_loop(0, L // size, step, carry)


def fold(values):
    return jnp.sum(values.reshape(values.shape[0] // 8, 8, values.shape[1]), axis=0)


def zeros8(width=D):
    return jnp.zeros((8, width), F32)


def total_row(values):
    return jnp.sum(values, axis=0, keepdims=True)


class Bag:
    pass


class Place:
    def __init__(self):
        self.planes = lax.axis_size("dp")
        self.chips = lax.axis_size("fsdp") // 2
        self.plane, inner = lax.axis_index("dp"), lax.axis_index("fsdp")
        self.z, self.core = inner // 2, inner % 2
        y, x = self.plane // 2, self.plane % 2
        self.plane_x, self.plane_y, self.plane_d = y * 2 + 1 - x, (1 - y) * 2 + x, (1 - y) * 2 + 1 - x
        self.twin = (self.plane, 2 * self.z + 1 - self.core)
        self.over_x = (self.plane_x, inner)
        self.over_y = (self.plane_y, inner)
        self.chip = [lax.rem(self.z + step, self.chips) for step in range(self.chips)]
        self.along = [(self.plane, 2 * chip + self.core) for chip in self.chip]
        self.rank = self.plane * 2 + self.core
        self.members = []
        for step in range(self.planes):
            for flip in range(2):
                if step or flip:
                    plane, core = lax.rem(self.plane + step, self.planes), lax.rem(self.core + flip, 2)
                    self.members.append(((plane, 2 * self.z + core), plane * 2 + core))


class Copies:
    def __init__(self, sends, receives, place):
        self.sends, self.receives, self.place = sends, receives, place
        self.begun = []

    def start(self, number, make, receive=None):
        def copy():
            source, target, device = make()
            return pltpu.make_async_remote_copy(
                source, target, self.sends.at[number], self.receives.at[number if receive is None else receive],
                device_id=device, device_id_type=MESH,
            )

        copy().start()
        self.begun.append(copy)

    def arrived(self, number, target):
        pltpu.make_async_remote_copy(
            target, target, self.sends.at[number], self.receives.at[number],
            device_id=self.place.twin, device_id_type=MESH,
        ).wait_recv()

    def sent(self):
        for copy in self.begun:
            copy().wait_send()
        self.begun = []


class Gather:
    def __init__(self, place, weights, copies, first, begin, size, split):
        self.place, self.weights, self.copies, self.first = place, weights, copies, first
        self.rows = pl.ds(begin, size)
        self.parts = (pl.ds(begin, split), pl.ds(begin + split, size - split))
        chips = place.chips
        self.x, self.y, self.d, self.t = chips, 2 * chips, 3 * chips, 3 * chips + 2

    @staticmethod
    def semaphores(chips):
        return 3 * chips + 6

    def column(self, plane, side, which):
        return self.weights.at[plane, :, side, which]

    def slot(self, plane, step):
        p = self.place
        return self.weights.at[plane, p.chip[(p.chips - step) % p.chips], p.core, self.rows]

    def move(self, number, ref, device):
        self.copies.start(self.first + number, lambda: (ref(), ref(), device))

    def arrived(self, number, ref):
        self.copies.arrived(self.first + number, ref)

    def along_z(self):
        p = self.place
        for d in range(1, p.chips):
            self.move(d, lambda: self.slot(p.plane, 0), p.along[d])

    def beside(self, step):
        p = self.place
        self.move(self.x + step, lambda: self.slot(p.plane, step), p.over_x)
        self.move(self.y + step, lambda: self.slot(p.plane, step), p.over_y)

    def own(self):
        self.beside(0)

    def forward(self):
        p = self.place
        for d in range(1, p.chips):
            self.arrived(d, self.slot(p.plane, d))
            self.beside(d)
        self.move(self.t, lambda: self.column(p.plane, p.core, self.rows), p.twin)

    def turn(self):
        p = self.place
        for d in range(p.chips):
            self.arrived(self.x + d, self.slot(p.plane_x, d))
        self.move(self.d, lambda: self.column(p.plane_x, p.core, self.parts[0]), p.over_y)
        for d in range(p.chips):
            self.arrived(self.y + d, self.slot(p.plane_y, d))
        self.move(self.d + 1, lambda: self.column(p.plane_y, p.core, self.parts[1]), p.over_x)
        self.move(self.t + 1, lambda: self.column(p.plane_x, p.core, self.rows), p.twin)
        self.move(self.t + 2, lambda: self.column(p.plane_y, p.core, self.rows), p.twin)

    def across(self):
        p = self.place
        self.arrived(self.d, self.column(p.plane_d, p.core, self.parts[0]))
        self.arrived(self.d + 1, self.column(p.plane_d, p.core, self.parts[1]))
        self.move(self.t + 3, lambda: self.column(p.plane_d, p.core, self.rows), p.twin)

    def done(self):
        p = self.place
        for number, plane in enumerate((p.plane, p.plane_x, p.plane_y, p.plane_d)):
            self.arrived(self.t + number, self.column(plane, 1 - p.core, self.rows))


def reduce_steps(place, data, twin, diagonal, from_x, from_y, from_z, copies, first, begin, size, split, landing, finish):
    p, core, chips = place, place.core, place.chips
    rows, lands = pl.ds(begin, size), pl.ds(landing, size)
    parts = (pl.ds(begin, split), pl.ds(begin + split, size - split))
    parts_land = (pl.ds(landing, split), pl.ds(landing + split, size - split))

    def column(plane, side, which):
        return data.at[plane, :, side, which]

    def add(plane, which, *sources):
        def step(zz, carry):
            value = data[plane, zz, core, which, :]
            for ref in sources:
                value = value + ref(zz)
            data[plane, zz, core, which, :] = value
            return carry

        lax.fori_loop(0, chips, step, 0)

    def read(ref, which, *lead):
        return lambda zz: ref[lead + (zz, which, slice(None))]

    def to_twin():
        for number, plane in enumerate((p.plane_d, p.plane_y, p.plane_x, p.plane)):
            copies.start(
                first + number, lambda plane=plane: (column(plane, 1 - core, rows), twin.at[plane, :, lands], p.twin)
            )

    def across():
        copies.arrived(first, twin.at[p.plane_d, :, lands])
        add(p.plane_d, rows, read(twin, lands, p.plane_d))
        copies.start(first + 4, lambda: (column(p.plane_d, core, parts[0]), diagonal.at[:, parts_land[0]], p.over_y))
        if split < size:
            copies.start(first + 5, lambda: (column(p.plane_d, core, parts[1]), diagonal.at[:, parts_land[1]], p.over_x))

    def beside():
        copies.arrived(first + 2, twin.at[p.plane_x, :, lands])
        copies.arrived(first + 4, diagonal.at[:, parts_land[0]])
        add(p.plane_x, rows, read(twin, lands, p.plane_x))
        add(p.plane_x, parts[0], read(diagonal, parts_land[0]))
        copies.start(first + 7, lambda: (column(p.plane_x, core, rows), from_x.at[:, lands], p.over_x))
        copies.arrived(first + 1, twin.at[p.plane_y, :, lands])
        add(p.plane_y, rows, read(twin, lands, p.plane_y))
        if split < size:
            copies.arrived(first + 5, diagonal.at[:, parts_land[1]])
            add(p.plane_y, parts[1], read(diagonal, parts_land[1]))
        copies.start(first + 6, lambda: (column(p.plane_y, core, rows), from_y.at[:, lands], p.over_y))

    def own_column():
        copies.arrived(first + 3, twin.at[p.plane, :, lands])
        copies.arrived(first + 6, from_y.at[:, lands])
        copies.arrived(first + 7, from_x.at[:, lands])
        add(p.plane, rows, read(twin, lands, p.plane), read(from_x, lands), read(from_y, lands))
        for d in range(1, chips):
            copies.start(
                first + 7 + d,
                lambda d=d: (data.at[p.plane, p.chip[d], core, rows], from_z.at[d - 1, lands], p.along[d]),
            )

    def along_z():
        for d in range(1, chips):
            copies.arrived(first + 7 + d, from_z.at[d - 1, lands])
        value = data[p.plane, p.z, core, rows, :].astype(F32)
        for d in range(1, chips):
            value = value + from_z[d - 1, lands, :].astype(F32)
        finish(value)

    return [to_twin, across, beside, own_column, along_z]


class Thin:
    def __init__(self, place, tiles, near, part, far, result, copies, first):
        self.place, self.tiles, self.near, self.part, self.far, self.result = place, tiles, near, part, far, result
        self.copies, self.first = copies, first

    def start(self):
        p = self.place
        for i, (device, rank) in enumerate(p.members):
            self.copies.start(
                self.first + i,
                lambda device=device: (self.tiles.at[device[0], :, lax.rem(device[1], 2)], self.near.at[p.rank], device),
                self.first + p.rank,
            )
        self.near[p.rank] = self.tiles[p.plane, :, p.core]

    def turn(self):
        p = self.place
        for device, rank in p.members:
            self.copies.arrived(self.first + rank, self.near.at[rank])
        value = self.near[0]
        for i in range(1, 2 * p.planes):
            value = value + self.near[i]
        self.part[...] = value
        base = self.first + 2 * p.planes
        for d in range(1, p.chips):
            self.copies.start(base + d, lambda d=d: (self.part.at[p.chip[d]], self.far.at[d], p.along[d]))

    def finish(self):
        p = self.place
        base = self.first + 2 * p.planes
        value = self.part[p.z]
        for d in range(1, p.chips):
            self.copies.arrived(base + d, self.far.at[d])
            value = value + self.far[d]
        self.result[...] = value


class Total:
    def __init__(self, place, own, near, part, far, result, copies, first):
        self.place, self.own, self.near, self.part, self.far, self.result = place, own, near, part, far, result
        self.copies, self.first = copies, first

    def start(self):
        p = self.place
        me = p.rank
        for i, (device, rank) in enumerate(p.members):
            self.copies.start(self.first + i, lambda device=device: (self.own, self.near.at[me], device), self.first + me)
        self.near[me] = self.own[...]

    def turn(self):
        p = self.place
        for device, rank in p.members:
            self.copies.arrived(self.first + rank, self.near.at[rank])
        value = self.near[0]
        for i in range(1, 2 * p.planes):
            value = value + self.near[i]
        self.part[...] = value
        base = self.first + 2 * p.planes
        for d in range(1, p.chips):
            self.copies.start(base + d, lambda d=d: (self.part, self.far.at[d], p.along[d]))

    def finish(self):
        p = self.place
        base = self.first + 2 * p.planes
        value = self.part[...]
        for d in range(1, p.chips):
            self.copies.arrived(base + d, self.far.at[d])
            value = value + self.far[d]
        self.result[...] = value


def at_points(table):
    def pump(index, place=0):
        for (iteration, where), steps in table.items():
            if where == place:

                @pl.when(index == iteration)
                def _(steps=steps):
                    for step in steps:
                        step()

    return pump


def still(index, place=0):
    pass


def standard(values):
    values = values.astype(F32)
    center = values - jnp.mean(values, axis=-1, keepdims=True)
    inverse = lax.rsqrt(jnp.mean(center * center, axis=-1, keepdims=True) + epsilon)
    return center * inverse, inverse


def norm_rows(source, target, small, row):
    gain, shift = 1.0 + small[row : row + 1, :], small[row + 1 : row + 2, :]

    def body(rows, carry):
        target[rows, :] = (standard(source[rows, :])[0] * gain + shift).astype(target.dtype)
        return carry

    chunks(body, 0)


def norm_back(source, grad, upstream, result, small, row, grads):
    gain = 1.0 + small[row : row + 1, :]

    def body(rows, carry):
        unit, inverse = standard(source[rows, :])
        given = grad[rows, :].astype(F32)
        inner = given * gain
        back = inverse * (
            inner
            - jnp.mean(inner, axis=-1, keepdims=True)
            - unit * jnp.mean(inner * unit, axis=-1, keepdims=True)
        )
        result[rows, :] = back if upstream is None else upstream[rows, :] + back
        return carry[0] + fold(given * unit), carry[1] + fold(given)

    first, second = chunks(body, (zeros8(), zeros8()))
    grads[row : row + 1, :] = total_row(first)
    grads[row + 1 : row + 2, :] = total_row(second)


def block_cols(c):
    return pl.ds(pl.multiple_of(c * D, D), D)


def columns(weights, start, block):
    return weights[:, :, :, pl.ds(pl.multiple_of(start + 16 * block, 16), 16), :].reshape(D, D)


def put_columns(weights, start, block, value):
    rows = pl.ds(pl.multiple_of(start + 16 * block, 16), 16)
    weights[:, :, :, rows, :] = value.astype(BF16).reshape(weights.shape[:3] + (16, D))


def lines_of(weights, start, block):
    return weights[block, :, :, start : start + 64, :].reshape(D, D)


def put_lines(weights, start, block, value):
    weights[block, :, :, start : start + 64, :] = value.astype(BF16).reshape(weights.shape[1:3] + (64, D))


def feed_inner(source, normed, active, slope, hold, weights, small, inner_bias, layer, pump):
    norm_rows(source, normed, small, S_FFN + 2 * layer)

    def block(c, carry):
        pump(c)
        cols = block_cols(c)
        hold[...] = dot(normed[...], columns(weights, (IN0, IN1)[layer], c))
        bias = inner_bias[layer : layer + 1, cols]

        def body(rows, carry):
            inner = hold[rows, :] + bias
            sigma = jax.nn.sigmoid(inner)
            value = inner * sigma
            active[rows, cols] = value.astype(BF16)
            slope[rows, cols] = (sigma + value * (1.0 - sigma)).astype(BF16)
            return carry

        chunks(body, 0)
        return carry

    lax.fori_loop(0, FF // D, block, 0)


def feed_outer(source, active, result, hold, weights, small, layer):
    begin = (OUT0, OUT1)[layer]

    def block(c, carry):
        part = dot(active[:, block_cols(c)], lines_of(weights, begin, c))

        @pl.when(c == 0)
        def _():
            hold[...] = part

        @pl.when(c > 0)
        def _():
            hold[...] += part

        return carry

    lax.fori_loop(0, FF // D, block, 0)
    bias = small[S_FOB + layer : S_FOB + layer + 1, :]

    def body(rows, carry):
        result[rows, :] = source[rows, :].astype(F32) + 0.5 * (hold[rows, :] + bias)
        return carry

    chunks(body, 0)


def feed_back_start(upstream, low, grads, layer):
    def start(rows, carry):
        half = 0.5 * upstream[rows, :]
        low[rows, :] = half.astype(BF16)
        return carry + fold(half)

    grads[S_FOB + layer : S_FOB + layer + 1, :] = total_row(chunks(start, zeros8()))


def feed_back_outer(active, low, weights, begin, pump):
    def block(c, carry):
        put_lines(weights, begin, c, dot_tn(active[:, block_cols(c)], low[...]))
        pump(c)
        return carry

    lax.fori_loop(0, FF // D, block, 0)


def feed_back_inner(normed, slope, low, hold, weights, target, inner_grads, layer, pump):
    begin = (OUT0, OUT1)[layer]

    def block(c, carry):
        cols = block_cols(c)
        hold[...] = dot_nt(low[...], lines_of(weights, begin, c))

        def body(rows, carry):
            grad = hold[rows, :] * slope[rows, cols].astype(F32)
            slope[rows, cols] = grad.astype(BF16)
            return carry + fold(grad)

        inner_grads[layer : layer + 1, cols] = total_row(chunks(body, zeros8()))
        if target is not None:
            put_columns(weights, target, c, dot_tn(normed[...], slope[:, cols]))
        pump(c)
        return carry

    lax.fori_loop(0, FF // D, block, 0)


def product_back(grad, normed, total, weights, begin, blocks, pump):
    def block(c, carry):
        cols = block_cols(c)
        part = dot_nt(grad[:, cols], columns(weights, begin, c))

        @pl.when(c == 0)
        def _():
            total[...] = part

        @pl.when(c > 0)
        def _():
            total[...] += part

        if normed is not None:
            put_columns(weights, begin, c, dot_tn(normed[...], grad[:, cols]))
        pump(c)
        return carry

    lax.fori_loop(0, blocks, block, 0)


def bucket_choice(buckets):
    return (lax.broadcasted_iota(jnp.int32, (BUCKETS, 2 * L), 0) == buckets[...]).astype(F32)


def attention_mix(source, normed, mixed, weights, small):
    norm_rows(source, normed, small, S_ATTN)

    def mix(c, carry):
        mixed[:, block_cols(c)] = dot(normed[...], columns(weights, QKV, c)).astype(BF16)
        return carry

    lax.fori_loop(0, 3, mix, 0)


def attention_forward(source, mixed, probs, joined, result, lines, hold, weights, small, table, buckets, bounds, marks, pump):
    lines[...] = dot(table[...].astype(BF16), bucket_choice(buckets).astype(BF16))
    lane = lax.broadcasted_iota(jnp.int32, (1, 128), 1)
    size = 128

    def pair(index, carry):
        begin = pl.multiple_of(128 * index, 128)
        keys = mixed[:, pl.ds(D + begin, 128)]
        contents = mixed[:, pl.ds(2 * D + begin, 128)]
        for block in range(L // size):
            rows = pl.ds(block * size, size)
            query = mixed[rows, pl.ds(begin, 128)]
            same = bounds[PAD + block * size : PAD + (block + 1) * size, 0:1] == marks[...]
            parts = []
            for half in range(2):
                head = 2 * index + half
                here = (lane // HEAD_DIM) == half
                raw = dot_nt(jnp.where(here, query, jnp.zeros_like(query)), keys)
                window = lines[pl.ds(head, 1), 384 - block * size : 1024 - block * size]
                square = pltpu.roll(jnp.broadcast_to(window, (size, 640)), 513, 1, stride=1, stride_axis=0)
                scores = jnp.where(same, raw * HEAD_DIM ** (-0.5) + square[:, :L], -1e30)
                raised = jnp.exp(scores - jnp.max(scores, axis=1, keepdims=True))
                share = (raised * (1.0 / jnp.sum(raised, axis=1, keepdims=True))).astype(BF16)
                probs[head, rows, :] = share
                parts.append(dot(share, contents))
            joined[rows, pl.ds(begin, 128)] = jnp.where(lane < HEAD_DIM, parts[0], parts[1]).astype(BF16)
            pump(index, block)
        return carry

    lax.fori_loop(0, HEADS // 2, pair, 0)
    hold[...] = dot(joined[...], columns(weights, ATT, 0))
    bias = small[S_AOB : S_AOB + 1, :]

    def body(rows, carry):
        result[rows, :] = source[rows, :] + hold[rows, :] + bias
        return carry

    chunks(body, 0)


def attention_back_start(upstream, joined, low, spread, weights, grads):
    def start(rows, carry):
        given = upstream[rows, :]
        low[rows, :] = given.astype(BF16)
        return carry + fold(given)

    grads[S_AOB : S_AOB + 1, :] = total_row(chunks(start, zeros8()))
    spread[...] = dot_nt(low[...], columns(weights, ATT, 0)).astype(BF16)
    put_columns(weights, ATT, 0, dot_tn(joined[...], low[...]))


def attention_backward(mixed, probs, spread, grad_mixed, scaled, hold, lines, buckets, table_grad, pump):
    lane = lax.broadcasted_iota(jnp.int32, (1, 128), 1)
    row8 = lax.broadcasted_iota(jnp.int32, (8, 2 * L), 0)
    size = 128

    def pair(index, carry):
        begin = pl.multiple_of(128 * index, 128)
        query = mixed[:, pl.ds(begin, 128)]
        keys = mixed[:, pl.ds(D + begin, 128)]
        contents = mixed[:, pl.ds(2 * D + begin, 128)]
        incoming = spread[:, pl.ds(begin, 128)]
        parts = []
        for half in range(2):
            head = 2 * index + half
            here = (lane // HEAD_DIM) == half
            hold[...] = dot_nt(jnp.where(here, incoming, jnp.zeros_like(incoming)), contents)
            sums = zeros8(2 * L)
            for block in range(L // size):
                rows = pl.ds(block * size, size)
                share = probs[head, rows, :].astype(F32)
                given = hold[rows, :]
                slant = share * (given - jnp.sum(given * share, axis=1, keepdims=True))
                scaled[rows, :] = (slant * HEAD_DIM ** (-0.5)).astype(BF16)
                part = zeros8(640)
                for t in range(size // 8):
                    tile = jnp.concatenate([slant[8 * t : 8 * t + 8], zeros8(128)], axis=1)
                    part += pltpu.roll(tile, 120 - 8 * t, 1)
                first = 384 - block * size
                pieces = [part]
                if first:
                    pieces = [zeros8(first)] + pieces
                if block:
                    pieces = pieces + [zeros8(block * size)]
                sums += jnp.concatenate(pieces, axis=1)
            line = zeros8(2 * L)
            for r in range(8):
                line += jnp.where(row8 == r, pltpu.roll(sums, 7 - r, 1), 0.0)
            lines[pl.ds(head, 1), :] = total_row(line)
            parts.append((dot(scaled[...], keys), dot_tn(scaled[...], query), dot_tn(probs[head], incoming)))
            pump(index, half)
        for third in range(3):
            merged = jnp.where(lane < HEAD_DIM, parts[0][third], parts[1][third])
            grad_mixed[:, pl.ds(third * D + begin, 128)] = merged.astype(BF16)
        return carry

    lax.fori_loop(0, HEADS // 2, pair, 0)
    table_grad[...] = lax.dot_general(
        lines[...], bucket_choice(buckets), (((1,), (1,)), ((), ())),
        precision=lax.Precision.HIGHEST, preferred_element_type=F32,
    )


def clear_pads(padded):
    edge = jnp.zeros((4, PAD, 128), F32)
    padded[:, 0:PAD, :] = edge
    padded[:, PAD + L : 2 * PAD + L, :] = edge


def conv_front(source, normed, sigma, gated, middle, sums, hold, weights, small, gate_bias, bounds, pump):
    norm_rows(source, normed, small, S_CONV)
    clear_pads(gated)
    hold[...] = dot(normed[...], columns(weights, GLU, 1))
    bias = gate_bias[0:1, D:]

    def gate(rows, carry):
        sigma[rows, :] = jax.nn.sigmoid(hold[rows, :] + bias)
        return carry

    chunks(gate, 0)
    hold[...] = dot(normed[...], columns(weights, GLU, 0))
    bias = gate_bias[0:1, :D]

    def unit(rows, carry):
        values = (hold[rows, :] + bias) * sigma[rows, :]
        for j in range(4):
            gated[j, pl.ds(rows.start + PAD, CHUNK), :] = values[:, 128 * j : 128 * j + 128]
        return carry

    chunks(unit, 0)
    size = 16

    def slide(i, carry):
        begin = pl.multiple_of(i * size, size)
        marks = bounds[pl.ds(begin + PAD, size), :]
        accs = [jnp.zeros((size, 128), F32) for _ in range(4)]
        for k in range(TAPS):
            same = bounds[pl.ds(begin + k, size), :] == marks
            for j in range(4):
                tap = small[S_TAPS + k : S_TAPS + k + 1, 128 * j : 128 * j + 128]
                accs[j] += jnp.where(same, gated[j, pl.ds(begin + k, size), :], 0.0) * tap
        result = []
        for j in range(4):
            middle[pl.ds(begin, size), 128 * j : 128 * j + 128] = accs[j]
            result.append(carry[j] + fold(accs[j]))
            result.append(carry[4 + j] + fold(accs[j] * accs[j]))
        pump(i)
        return result[0::2] + result[1::2]

    ends = lax.fori_loop(0, L // size, slide, [zeros8(128)] * 8)
    sums[...] = zeros8()
    for j in range(4):
        sums[0:1, 128 * j : 128 * j + 128] = total_row(ends[j])
        sums[1:2, 128 * j : 128 * j + 128] = total_row(ends[4 + j])


def conv_rest(source, middle, sums, unit, active, slope, result, hold, weights, small, frames):
    center = sums[0:1, :] * (1.0 / frames)
    inverse = lax.rsqrt(sums[1:2, :] * (1.0 / frames) - center * center + epsilon)
    gain, shift = 1.0 + small[S_BATCH : S_BATCH + 1, :], small[S_BATCH + 1 : S_BATCH + 2, :]

    def body(rows, carry):
        values = (middle[rows, :] - center) * inverse
        unit[rows, :] = values
        normal = values * gain + shift
        sigma = jax.nn.sigmoid(normal)
        value = normal * sigma
        active[rows, :] = value.astype(BF16)
        slope[rows, :] = (sigma + value * (1.0 - sigma)).astype(slope.dtype)
        return carry

    chunks(body, 0)
    hold[...] = dot(active[...], columns(weights, CONV, 0))
    bias = small[S_COB : S_COB + 1, :]

    def add(rows, carry):
        result[rows, :] = source[rows, :] + hold[rows, :] + bias
        return carry

    chunks(add, 0)


def conv_back_rest(upstream, unit, slope, grad_normal, low, hold, weights, grads, sums):
    def start(rows, carry):
        given = upstream[rows, :]
        low[rows, :] = given.astype(BF16)
        return carry + fold(given)

    grads[S_COB : S_COB + 1, :] = total_row(chunks(start, zeros8()))
    hold[...] = dot_nt(low[...], columns(weights, CONV, 0))

    def body(rows, carry):
        grad = hold[rows, :] * slope[rows, :].astype(F32)
        grad_normal[rows, :] = grad
        return carry[0] + fold(grad), carry[1] + fold(grad * unit[rows, :])

    first, second = chunks(body, (zeros8(), zeros8()))
    sums[...] = zeros8()
    sums[0:1, :] = total_row(first)
    sums[1:2, :] = total_row(second)
    grads[S_BATCH : S_BATCH + 1, :] = total_row(second)
    grads[S_BATCH + 1 : S_BATCH + 2, :] = total_row(first)


def conv_back_front(
    sigma, gated, unit, grad_normal, front_sums, sums, padded, grad_joined, hold, tap_sums, small, bounds, grads, gate_grads,
    frames, pump,
):
    center = front_sums[0:1, :] * (1.0 / frames)
    inverse = lax.rsqrt(front_sums[1:2, :] * (1.0 / frames) - center * center + epsilon)
    gain = 1.0 + small[S_BATCH : S_BATCH + 1, :]
    mean0, mean1 = gain * sums[0:1, :] * (1.0 / frames), gain * sums[1:2, :] * (1.0 / frames)
    clear_pads(padded)

    def start(rows, carry):
        grad = inverse * (gain * grad_normal[rows, :] - mean0 - unit[rows, :] * mean1)
        for j in range(4):
            padded[j, pl.ds(rows.start + PAD, CHUNK), :] = grad[:, 128 * j : 128 * j + 128]
        return carry

    chunks(start, 0)
    tap_sums[...] = jnp.zeros_like(tap_sums)
    size = 16

    def slide(i, carry):
        begin = pl.multiple_of(i * size, size)
        marks = bounds[pl.ds(begin + PAD, size), :]
        accs = [jnp.zeros((size, 128), F32) for _ in range(4)]
        for k in range(TAPS):
            same = bounds[pl.ds(begin + 2 * PAD - k, size), :] == marks
            for j in range(4):
                tap = small[S_TAPS + k : S_TAPS + k + 1, 128 * j : 128 * j + 128]
                accs[j] += jnp.where(same, padded[j, pl.ds(begin + 2 * PAD - k, size), :], 0.0) * tap
        for j in range(4):
            hold[pl.ds(begin, size), 128 * j : 128 * j + 128] = accs[j]
        grads_here = [padded[j, pl.ds(begin + PAD, size), :] for j in range(4)]
        for k in range(TAPS):
            same = bounds[pl.ds(begin + k, size), :] == marks
            for j in range(4):
                term = jnp.where(same, gated[j, pl.ds(begin + k, size), :], 0.0) * grads_here[j]
                tap_sums[k, :, 128 * j : 128 * j + 128] += fold(term)
        pump(i)
        return carry

    lax.fori_loop(0, L // size, slide, 0)
    grads[S_TAPS : S_TAPS + TAPS, :] = jnp.sum(tap_sums[...], axis=1)

    def split(rows, carry):
        grad = hold[rows, :]
        gate = sigma[rows, :]
        values = jnp.concatenate([gated[j, pl.ds(rows.start + PAD, CHUNK), :] for j in range(4)], axis=1)
        first = grad * gate
        second = grad * values * (1.0 - gate)
        grad_joined[rows, :D] = first.astype(BF16)
        grad_joined[rows, D : 2 * D] = second.astype(BF16)
        return carry[0] + fold(first), carry[1] + fold(second)

    first, second = chunks(split, (zeros8(), zeros8()))
    gate_grads[0:1, :D] = total_row(first)
    gate_grads[0:1, D:] = total_row(second)


THIN = (
    ("ffn_norm", S_FFN), ("ffn_out_bias", S_FOB), ("attn_norm", S_ATTN), ("attn_out_bias", S_AOB), ("conv_norm", S_CONV),
    ("batch_norm", S_BATCH), ("conv_out_bias", S_COB), ("final_norm", S_FINAL), ("depth_kernel", S_TAPS),
)


def turned(value):
    rows, lanes = value.shape
    value = jnp.concatenate([value, jnp.zeros((rows, 128 - lanes), F32)], axis=1)
    return jnp.concatenate([value, jnp.zeros((128 - rows, 128), F32)], axis=0).T[:lanes, :rows]


def pack_small(b, tile):
    tile[...] = jnp.zeros_like(tile)
    for name, row in THIN:
        value = getattr(b, name)[...].astype(F32)
        if name == "depth_kernel":
            value = turned(value)
        value = value.reshape(-1, value.shape[-1])
        for r in range(0, value.shape[0], 16):
            part = value[r : r + 16]
            begin = (row + r) % 16
            at = 128 * ((row + r) // 16)
            tile[begin : begin + part.shape[0], at : at + part.shape[1]] = part
    tile[0:2, 384 : 384 + b.ffn_in_bias.shape[1]] = b.ffn_in_bias[...].astype(F32)
    wide, few = b.glu_bias.shape[0], b.rel_table.shape[0]
    tile[2:3, 384 : 384 + wide] = b.glu_bias[...].astype(F32).reshape(1, wide)
    tile[3:4, 384 : 384 + few] = b.rel_table[...].astype(F32).reshape(1, few)


def pack_weights(b, put):
    for layer in range(2):
        for c in range(FF // D):
            put((IN0, IN1)[layer] + 16 * c, b.ffn_in[layer, :, D * c : D * c + D])
        put((OUT0, OUT1)[layer], b.ffn_out[layer])
    for c in range(3):
        put(QKV + 16 * c, b.qkv_weight[:, D * c : D * c + D])
    put(ATT, b.attn_out[...])
    for c in range(2):
        put(GLU + 16 * c, b.glu_weight[:, D * c : D * c + D])
    put(CONV, b.conv_out[...])


def unpack_small(b, place):
    per = 2 * place.chips
    count = place.planes * per
    width = D // count
    for device in range(count):
        tile = b.weights[device // per, (device % per) // 2, device % 2, 0:16, :].astype(F32)
        for q in range(3):
            b.small[16 * q : 16 * q + 16, width * device : width * device + width] = tile[:, 128 * q : 128 * q + width]
        b.inner_bias[:, 4 * width * device : 4 * width * (device + 1)] = tile[0:2, 384 : 384 + 4 * width]
        b.gate_bias[:, 2 * width * device : 2 * width * (device + 1)] = tile[2:3, 384 : 384 + 2 * width]
        few = HEADS * BUCKETS // count
        head, at = few * device // BUCKETS, few * device % BUCKETS
        b.table[head : head + 1, at : at + few] = tile[3:4, 384 : 384 + few]


def pack_small_grads(b, place):
    per = 2 * place.chips
    count = place.planes * per
    width = D // count
    few = HEADS * BUCKETS // count
    for device in range(count):
        tile = b.edges.at[device // per, (device % per) // 2, device % 2]
        for g in range(8):
            tile[0:6, 16 * g : 16 * g + width] = b.grads[6 * g : 6 * g + 6, width * device : width * device + width]
        for m in range(2):
            tile[6:7, 64 * m : 64 * m + 4 * width] = b.inner_grads[m : m + 1, 4 * width * device : 4 * width * (device + 1)]
        tile[7:8, 0 : 2 * width] = b.gate_grads[:, 2 * width * device : 2 * width * (device + 1)]
        head, at = few * device // BUCKETS, few * device % BUCKETS
        tile[7:8, 64 : 64 + few] = b.table_grad[head : head + 1, at : at + few]


INPUTS = (
    "inputs", "segments", "buckets", "cotangent", "ffn_norm", "ffn_in", "ffn_in_bias", "ffn_out", "ffn_out_bias", "attn_norm",
    "qkv_weight", "attn_out", "attn_out_bias", "rel_table", "conv_norm", "glu_weight", "glu_bias", "depth_kernel", "batch_norm",
    "conv_out", "conv_out_bias", "final_norm",
)
OUTPUTS = ("output", "grad_x", "shard", "thin")
GATHERS = ((SMALL, 48, 32), (IN0 + 32, 32, 16), (OUT0, 64, 32), (QKV, 64, 32), (GLU, 48, 32), (IN1, 64, 32), (OUT1, 64, 32))
REDUCES = (
    (OUT1, OUT1, 64, 32), (IN1, IN1, 64, 32), (ATT, ATT, 64, 32), (QKV, QKV, 48, 32), (OUT1, OUT0, 64, 32),
    (IN1, IN0, 32, 16), (IN1 + 32, IN0 + 32, 32, 16),
)


def scratch_of(planes, chips):
    wide, low, big = pltpu.VMEM((L, D), F32), pltpu.VMEM((L, D), BF16), pltpu.VMEM((L, FF), BF16)
    pads = pltpu.VMEM((4, L + 2 * PAD, 128), F32)
    stats = pltpu.VMEM((8, D), F32)
    return dict(
        weights=pltpu.VMEM((planes, chips, 2, ROWS, D), BF16),
        twin=pltpu.VMEM((planes, chips, GRADS, D), BF16),
        diagonal=pltpu.VMEM((chips, GRADS, D), BF16),
        from_x=pltpu.VMEM((chips, GRADS, D), BF16),
        from_y=pltpu.VMEM((chips, GRADS, D), BF16),
        from_z=pltpu.VMEM((chips - 1, GRADS, D), BF16),
        edges=pltpu.VMEM((planes, chips, 2, 8, 128), F32),
        edge_near=pltpu.VMEM((2 * planes, chips, 8, 128), F32),
        edge_part=pltpu.VMEM((chips, 8, 128), F32),
        edge_far=pltpu.VMEM((chips, 8, 128), F32),
        small=pltpu.VMEM((S_ROWS, D), F32),
        inner_bias=pltpu.VMEM((2, FF), F32),
        gate_bias=pltpu.VMEM((1, 2 * D), F32),
        table=pltpu.VMEM((HEADS, BUCKETS), F32),
        tile=pltpu.VMEM((16, D), F32),
        grads=pltpu.VMEM((S_ROWS, D), F32),
        inner_grads=pltpu.VMEM((2, FF), F32),
        gate_grads=pltpu.VMEM((1, 2 * D), F32),
        table_grad=pltpu.VMEM((HEADS, BUCKETS), F32),
        lines=pltpu.VMEM((HEADS, 2 * L), F32),
        choice=pltpu.VMEM((1, 2 * L), jnp.int32),
        bounds=pltpu.VMEM((L + 2 * PAD, 128), F32),
        marks=pltpu.VMEM((1, L), F32),
        front_own=stats, back_own=stats, front_sums=stats, back_sums=stats, front_part=stats, back_part=stats,
        front_near=pltpu.VMEM((2 * planes, 8, D), F32), back_near=pltpu.VMEM((2 * planes, 8, D), F32),
        front_far=pltpu.VMEM((chips, 8, D), F32), back_far=pltpu.VMEM((chips, 8, D), F32),
        x1=wide, x2=wide, x3=wide, x4=wide, normed0=low, normed_a=low, normed_c=low, normed1=low,
        active0=big, slope0=big, active1=big, slope1=big, mixed=pltpu.VMEM((L, 3 * D), BF16),
        probs=pltpu.VMEM((HEADS, L, L), BF16), joined=low, sigma=wide, gated=pads, middle=wide, active_c=low, slope_c=low,
        padded=pads, low=low, spread=low, hold=wide, total=wide, taps=pltpu.VMEM((TAPS, 8, D), F32),
        gather_sends=pltpu.SemaphoreType.DMA((len(GATHERS) * Gather.semaphores(chips),)),
        gather_receives=pltpu.SemaphoreType.DMA((len(GATHERS) * Gather.semaphores(chips),)),
        reduce_sends=pltpu.SemaphoreType.DMA((len(REDUCES) * (chips + 7),)),
        reduce_receives=pltpu.SemaphoreType.DMA((len(REDUCES) * (chips + 7),)),
        total_sends=pltpu.SemaphoreType.DMA((3 * (2 * planes + chips),)),
        total_receives=pltpu.SemaphoreType.DMA((3 * (2 * planes + chips),)),
    )


def whole_kernel(names, *refs):
    b = Bag()
    for name, ref in zip(names, refs):
        setattr(b, name, ref)
    place = Place()
    planes, chips = place.planes, place.chips
    frames = L * planes * chips * 2
    barrier = pltpu.get_barrier_semaphore()
    near = [device for device, rank in place.members] + [place.along[d] for d in range(1, chips)]
    for device in near:
        pl.semaphore_signal(barrier, inc=1, device_id=device, device_id_type=MESH)
    pack_small(b, b.tile)

    def put(row, value):
        b.weights[place.plane, place.z, place.core, row : row + value.shape[0], :] = value

    put(0, b.tile[...].astype(BF16))
    pack_weights(b, put)
    pl.semaphore_wait(barrier, len(near))

    gathers = Copies(b.gather_sends, b.gather_receives, place)
    rounds = [
        Gather(place, b.weights, gathers, i * Gather.semaphores(chips), begin, size, split)
        for i, (begin, size, split) in enumerate(GATHERS)
    ]
    r0, r1, r2, r3, r4, r5, r6 = rounds
    r0.along_z()
    r0.own()
    r1.along_z()
    r1.own()
    for r in rounds[2:]:
        r.along_z()
    b.marks[...] = b.segments[...].astype(F32)
    b.bounds[...] = jnp.full(b.bounds.shape, -1.0, F32)
    b.bounds[PAD : PAD + L, :] = jnp.broadcast_to(b.marks[...], (128, L)).T
    b.choice[...] = jnp.full(b.choice.shape, -1, jnp.int32)
    b.choice[:, 0 : 2 * L - 1] = b.buckets[...].reshape(1, 2 * L - 1)
    for step in (r0.forward, r1.forward, r2.own, r0.turn, r1.turn, r2.forward, r3.own, r0.across, r0.done):
        step()
    unpack_small(b, place)

    x0 = b.inputs.at[0]
    feed_inner(
        x0, b.normed0, b.active0, b.slope0, b.hold, b.weights, b.small, b.inner_bias, 0,
        at_points({(1, 0): (r1.across, r2.turn), (2, 0): (r1.done, r3.forward), (3, 0): (r4.own,)}),
    )
    r2.across()
    r2.done()
    feed_outer(x0, b.active0, b.x1, b.hold, b.weights, b.small, 0)
    for step in (r4.forward, r3.turn, r5.own, r5.forward, r3.across, r3.done):
        step()
    attention_mix(b.x1, b.normed_a, b.mixed, b.weights, b.small)
    for step in (r4.turn, r6.own, r6.forward):
        step()
    attention_forward(
        b.x1, b.mixed, b.probs, b.joined, b.x2, b.lines, b.hold, b.weights, b.small, b.table, b.choice, b.bounds, b.marks,
        at_points({(2, 1): (r5.turn,), (2, 3): (r4.across,), (3, 3): (r4.done,)}),
    )
    conv_front(
        b.x2, b.normed_c, b.sigma, b.gated, b.middle, b.front_own, b.hold, b.weights, b.small, b.gate_bias, b.bounds,
        at_points({(4, 0): (r6.turn,), (16, 0): (r5.across,), (28, 0): (r6.across,)}),
    )
    totals = Copies(b.total_sends, b.total_receives, place)
    front = Total(place, b.front_own, b.front_near, b.front_part, b.front_far, b.front_sums, totals, 0)
    front.start()
    r5.done()
    front.turn()
    r6.done()
    front.finish()
    conv_rest(b.x2, b.middle, b.front_sums, b.middle, b.active_c, b.slope_c, b.x3, b.hold, b.weights, b.small, frames)
    feed_inner(b.x3, b.normed1, b.active1, b.slope1, b.hold, b.weights, b.small, b.inner_bias, 1, still)
    feed_outer(b.x3, b.active1, b.x4, b.hold, b.weights, b.small, 1)
    norm_rows(b.x4, b.output.at[0], b.small, S_FINAL)
    flow = b.x4
    norm_back(b.x4, b.cotangent.at[0], None, flow, b.small, S_FINAL, b.grads)
    gathers.sent()

    reduces = Copies(b.reduce_sends, b.reduce_receives, place)
    landings = (b.twin, b.diagonal, b.from_x, b.from_y, b.from_z)

    def finish(begin, size):
        def act(value):
            b.shard[begin - IN0 : begin - IN0 + size, :] = value

        return act

    backs = [
        reduce_steps(
            place, b.weights, *landings, reduces, i * (chips + 7), begin, size, split, owner - IN0, finish(owner, size)
        )
        for i, (begin, owner, size, split) in enumerate(REDUCES)
    ]
    out1, in1, conv, mix, out0, in0, in0_end = backs
    feed_back_start(flow, b.low, b.grads, 1)
    feed_back_inner(b.normed1, b.slope1, b.low, b.hold, b.weights, None, b.inner_grads, 1, still)
    feed_back_outer(b.active1, b.low, b.weights, OUT1, still)
    out1[0]()
    product_back(b.slope1, b.normed1, b.total, b.weights, IN1, 4, at_points({(1, 0): (out1[1],)}))
    in1[0]()
    norm_back(b.x3, b.total, flow, flow, b.small, S_FFN + 2, b.grads)
    in1[1]()
    grad_normal = b.x3
    conv_back_rest(flow, b.middle, b.slope_c, grad_normal, b.low, b.hold, b.weights, b.grads, b.back_own)
    back = Total(place, b.back_own, b.back_near, b.back_part, b.back_far, b.back_sums, totals, 2 * planes + chips)
    back.start()
    put_columns(b.weights, CONV, 0, dot_tn(b.active_c[...], b.low[...]))
    out1[2]()
    back.turn()
    in1[2]()
    back.finish()
    conv_back_front(
        b.sigma, b.gated, b.middle, grad_normal, b.front_sums, b.back_sums, b.padded, b.active1, b.hold, b.taps, b.small,
        b.bounds, b.grads, b.gate_grads, frames, at_points({(10, 0): (out1[3],), (26, 0): (in1[3],)}),
    )
    out1[4]()
    product_back(b.active1, b.normed_c, b.total, b.weights, GLU, 2, still)
    norm_back(b.x2, b.total, flow, flow, b.small, S_CONV, b.grads)
    attention_back_start(flow, b.joined, b.low, b.spread, b.weights, b.grads)
    conv[0]()
    attention_backward(
        b.mixed, b.probs, b.spread, b.active1, b.slope1.at[:, pl.ds(0, D)], b.hold, b.lines, b.choice, b.table_grad,
        at_points({(0, 1): (conv[1], in1[4]), (2, 0): (conv[2],), (3, 1): (conv[3],)}),
    )
    product_back(b.active1, b.normed_a, b.total, b.weights, QKV, 3, still)
    mix[0]()
    norm_back(b.x1, b.total, flow, flow, b.small, S_ATTN, b.grads)
    mix[1]()
    conv[4]()
    reduces.sent()
    feed_back_start(flow, b.low, b.grads, 0)
    feed_back_outer(b.active0, b.low, b.weights, OUT1, still)
    out0[0]()
    feed_back_inner(
        b.normed0, b.slope0, b.low, b.hold, b.weights, IN1, b.inner_grads, 0,
        at_points({(0, 0): (mix[2],), (1, 0): (in0[0], out0[1]), (2, 0): (in0[1],)}),
    )
    in0_end[0]()
    out0[2]()
    product_back(b.slope0, None, b.total, b.weights, IN0, 4, at_points({(1, 0): (in0_end[1], mix[3])}))
    in0[2]()
    norm_back(x0, b.total, flow, b.grad_x.at[0], b.small, S_FFN, b.grads)
    pack_small_grads(b, place)
    thin = Thin(place, b.edges, b.edge_near, b.edge_part, b.edge_far, b.thin, totals, 2 * (2 * planes + chips))
    thin.start()
    for step in (in0_end[2], out0[3], mix[4], thin.turn, in0[3], in0_end[3], out0[4], thin.finish, in0[4], in0_end[4]):
        step()
    reduces.sent()
    totals.sent()


def finish_kernel(*refs):
    (
        output_in, grad_x_in, shard, thin, output, grad_x, grad_ffn_norm, grad_ffn_in, grad_ffn_in_bias, grad_ffn_out,
        grad_ffn_out_bias, grad_attn_norm, grad_qkv, grad_attn_out, grad_attn_out_bias, grad_rel, grad_conv_norm, grad_glu,
        grad_glu_bias, grad_depth, grad_batch, grad_conv_out, grad_conv_out_bias, grad_final, taps, semaphores,
    ) = refs
    copies = [
        pltpu.make_async_copy(output_in, output, semaphores.at[0]), pltpu.make_async_copy(grad_x_in, grad_x, semaphores.at[1])
    ]
    for copy in copies:
        copy.start()
    cut = lambda begin, size: shard[begin - IN0 : begin - IN0 + size, :]
    width = grad_final.shape[-1]

    def thin_rows(begin, count):
        rows = []
        for p in range(begin, begin + count):
            rows.append(thin[p % 6 : p % 6 + 1, 16 * (p // 6) : 16 * (p // 6) + width])
        return rows

    for layer in range(2):
        for c in range(FF // D):
            grad_ffn_in[layer, :, D * c : D * c + D] = cut((IN0, IN1)[layer] + 16 * c, 16)
        grad_ffn_out[layer] = cut((OUT0, OUT1)[layer], 64)
        grad_ffn_in_bias[layer : layer + 1, :] = thin[6:7, 64 * layer : 64 * layer + 4 * width]
        for r, row in enumerate(thin_rows(S_FFN + 2 * layer, 2)):
            grad_ffn_norm[layer, r : r + 1, :] = row
    for c in range(3):
        grad_qkv[:, D * c : D * c + D] = cut(QKV + 16 * c, 16)
    grad_attn_out[...] = cut(ATT, 16)
    for c in range(2):
        grad_glu[:, D * c : D * c + D] = cut(GLU + 16 * c, 16)
    grad_conv_out[...] = cut(CONV, 16)
    for ref, begin in (
        (grad_ffn_out_bias, S_FOB), (grad_attn_norm, S_ATTN), (grad_conv_norm, S_CONV), (grad_batch, S_BATCH),
        (grad_final, S_FINAL),
    ):
        for r, row in enumerate(thin_rows(begin, ref.shape[0])):
            ref[r : r + 1, :] = row
    for r, row in enumerate(thin_rows(S_TAPS, TAPS)):
        taps[r : r + 1, 0:width] = row
    grad_depth[...] = taps[...].T[0:width, 0:TAPS]
    grad_attn_out_bias[...] = thin_rows(S_AOB, 1)[0][0]
    grad_conv_out_bias[...] = thin_rows(S_COB, 1)[0][0]
    grad_glu_bias[...] = thin[7:8, 0 : 2 * width][0]
    grad_rel[...] = thin[7:8, 64 : 64 + grad_rel.shape[0]][0]
    for copy in copies:
        copy.wait()


def shape(dims, kind=F32):
    return jax.ShapeDtypeStruct(dims, kind)


def local(*args):
    planes, chips = lax.axis_size("dp"), lax.axis_size("fsdp") // 2
    scratch = scratch_of(planes, chips)
    names = INPUTS + OUTPUTS + tuple(scratch)
    vmem, anywhere = pl.BlockSpec(memory_space=pltpu.VMEM), pl.BlockSpec(memory_space=pl.ANY)
    given = dict(zip(INPUTS, args))
    given["depth_kernel"] = given["depth_kernel"].T
    firsts = [shape((1, L, D), BF16), shape((1, L, D))]
    passed = pl.pallas_call(
        lambda *refs: whole_kernel(names, *refs),
        out_shape=firsts + [shape((GRADS, D)), shape((8, 128))],
        in_specs=[vmem] * len(args),
        out_specs=[vmem] * 4,
        scratch_shapes=list(scratch.values()),
        compiler_params=pltpu.CompilerParams(collective_id=0, has_side_effects=True, vmem_limit_bytes=VMEM_BYTES),
        name="layer",
    )(*given.values())
    outs = [
        shape(given[name].shape)
        for name in (
            "ffn_norm", "ffn_in", "ffn_in_bias", "ffn_out", "ffn_out_bias", "attn_norm", "qkv_weight", "attn_out",
            "attn_out_bias", "rel_table", "conv_norm", "glu_weight", "glu_bias", "depth_kernel", "batch_norm", "conv_out",
            "conv_out_bias", "final_norm",
        )
    ]
    grads = pl.pallas_call(
        finish_kernel,
        out_shape=firsts + outs,
        in_specs=[anywhere, anywhere, vmem, vmem],
        out_specs=[vmem] * (2 + len(outs)),
        scratch_shapes=[pltpu.VMEM((128, 128), F32), pltpu.SemaphoreType.DMA((2,))],
        name="unpack",
    )(*passed)
    grads = list(grads)
    grads[15] = grads[15].T
    return tuple(grads)


VMEM_BYTES = 62 * 1024 * 1024


highest = lax.Precision.HIGHEST


def layer_norm(values, params):
    center = values - jnp.mean(values, axis=-1, keepdims=True)
    spread = jnp.mean(center * center, axis=-1, keepdims=True)
    return center * lax.rsqrt(spread + epsilon) * (1.0 + params[0]) + params[1]


def silu_slope(values):
    sigma = jax.nn.sigmoid(values)
    return sigma * (1.0 + values * (1.0 - sigma))


def product(left, right):
    return jnp.dot(left, right, preferred_element_type=jnp.float32)


def product_left(left, right):
    return lax.dot_general(
        left, right, (((0,), (0,)), ((), ())), preferred_element_type=jnp.float32
    )


def product_right(left, right):
    return lax.dot_general(
        left, right, (((1,), (1,)), ((), ())), preferred_element_type=jnp.float32
    )


def plain_fetch_feed(norms, inner_weight, inner_bias, outer_weight, outer_bias, layer):
    return (
        lax.all_gather(norms[layer], ("dp", "fsdp"), axis=1, tiled=True),
        lax.all_gather(inner_weight[layer], ("dp", "fsdp"), axis=0, tiled=True),
        lax.all_gather(inner_bias[layer], ("dp", "fsdp"), axis=0, tiled=True),
        lax.all_gather(outer_weight[layer], ("dp", "fsdp"), axis=0, tiled=True),
        lax.all_gather(outer_bias[layer], ("dp", "fsdp"), axis=0, tiled=True),
    )


def plain_reduce_feed(grads):
    return (
        lax.psum_scatter(grads[0], ("dp", "fsdp"), scatter_dimension=1, tiled=True),
        lax.psum_scatter(grads[1], ("dp", "fsdp"), scatter_dimension=0, tiled=True),
        lax.psum_scatter(grads[2], ("dp", "fsdp"), scatter_dimension=0, tiled=True),
        lax.psum_scatter(grads[3], ("dp", "fsdp"), scatter_dimension=0, tiled=True),
        lax.psum_scatter(grads[4], ("dp", "fsdp"), scatter_dimension=0, tiled=True),
    )


def fetch_attention(attn_norm, qkv_weight, attn_out, attn_out_bias, rel_table):
    return (
        lax.all_gather(attn_norm, ("dp", "fsdp"), axis=1, tiled=True),
        lax.all_gather(qkv_weight, ("dp", "fsdp"), axis=0, tiled=True),
        lax.all_gather(attn_out, ("dp", "fsdp"), axis=0, tiled=True),
        lax.all_gather(attn_out_bias, ("dp", "fsdp"), axis=0, tiled=True),
        lax.all_gather(rel_table, ("dp", "fsdp"), axis=0, tiled=True),
    )


def fetch_conv(
    conv_norm, glu_weight, glu_bias, depth_kernel, batch_norm, conv_out, conv_out_bias, final_norm
):
    return (
        lax.all_gather(conv_norm, ("dp", "fsdp"), axis=1, tiled=True),
        lax.all_gather(glu_weight, ("dp", "fsdp"), axis=0, tiled=True),
        lax.all_gather(glu_bias, ("dp", "fsdp"), axis=0, tiled=True),
        lax.all_gather(depth_kernel, ("dp", "fsdp"), axis=1, tiled=True),
        lax.all_gather(batch_norm, ("dp", "fsdp"), axis=1, tiled=True),
        lax.all_gather(conv_out, ("dp", "fsdp"), axis=0, tiled=True),
        lax.all_gather(conv_out_bias, ("dp", "fsdp"), axis=0, tiled=True),
        lax.all_gather(final_norm, ("dp", "fsdp"), axis=1, tiled=True),
    )


def plain_feed_forward(values, weights):
    norm, weight_in, bias_in, weight_out, bias_out = weights
    normed, norm_back = jax.vjp(layer_norm, values, norm.astype(jnp.float32))
    normed_low = normed.astype(jnp.bfloat16)
    inner = product(normed_low, weight_in) + bias_in.astype(jnp.float32)
    active = jax.nn.silu(inner).astype(jnp.bfloat16)
    result = values + 0.5 * (product(active, weight_out) + bias_out.astype(jnp.float32))
    return (result, (normed_low, inner, active, norm_back))


def plain_feed_backward(upstream, weights, saved):
    norm, weight_in, bias_in, weight_out, bias_out = weights
    normed_low, inner, active, norm_back = saved
    branch = 0.5 * upstream
    branch_low = branch.astype(jnp.bfloat16)
    grad_weight_out = product_left(active, branch_low)
    grad_inner = product_right(branch_low, weight_out) * silu_slope(inner)
    inner_low = grad_inner.astype(jnp.bfloat16)
    grad_weight_in = product_left(normed_low, inner_low)
    grad_values, grad_norm = norm_back(product_right(inner_low, weight_in))
    return (
        upstream + grad_values,
        (
            grad_norm,
            grad_weight_in,
            jnp.sum(grad_inner, axis=0),
            grad_weight_out,
            jnp.sum(branch, axis=0),
        ),
    )


def relative_lines(table, buckets):
    choose = (buckets[None, :] == jnp.arange(BUCKETS, dtype=jnp.int32)[:, None]).astype(jnp.float32)
    lines = jnp.dot(table.astype(jnp.float32).reshape(HEADS, BUCKETS), choose, precision=highest)
    return (lines, choose)


def bias_square(line, length):
    tiled = jnp.broadcast_to(line, (length, 2 * length - 1)).reshape(-1)
    tiled = jnp.concatenate([tiled, jnp.zeros((length,), line.dtype)])
    return tiled.reshape(length, 2 * length)[:, :length][::-1]


def diagonal_sums(square):
    length = square.shape[0]
    padded = jnp.concatenate([square[::-1], jnp.zeros_like(square)], axis=1).reshape(-1)
    return jnp.sum(padded[: length * (2 * length - 1)].reshape(length, 2 * length - 1), axis=0)


def head_scores(query, keys_head, line, same):
    raw = product_right(query, keys_head)
    return jnp.where(same, raw * HEAD_DIM ** (-0.5) + bias_square(line, query.shape[0]), -1e30)


def plain_attention_forward(values, weights, marks, buckets):
    norm, mixer, weight_out, bias_out, table = weights
    length = values.shape[0]
    normed, norm_back = jax.vjp(layer_norm, values, norm.astype(jnp.float32))
    normed_low = normed.astype(jnp.bfloat16)
    mixed = (
        product(normed_low, mixer)
        .astype(jnp.bfloat16)
        .reshape(length, 3, HEADS, HEAD_DIM)
        .transpose(1, 2, 0, 3)
    )
    lines, choose = relative_lines(table, buckets)
    same = marks[:, None] == marks[None, :]

    def head_forward(items):
        query, keys_head, contents, line = items
        scores = head_scores(query, keys_head, line, same)
        peak = jnp.max(scores, axis=1, keepdims=True)
        raised = jnp.exp(scores - peak)
        total = jnp.sum(raised, axis=1, keepdims=True)
        probs = (raised / total).astype(jnp.bfloat16)
        return (product(probs, contents).astype(jnp.bfloat16), (peak + jnp.log(total))[:, 0])

    attended, logsum = lax.map(head_forward, (mixed[0], mixed[1], mixed[2], lines))
    joined = attended.transpose(1, 0, 2).reshape(length, D)
    result = values + product(joined, weight_out) + bias_out.astype(jnp.float32)
    return (result, (normed_low, mixed, lines, choose, same, joined, logsum, norm_back))


def plain_attention_backward(upstream, weights, saved):
    norm, mixer, weight_out, bias_out, table = weights
    normed_low, mixed, lines, choose, same, joined, logsum, norm_back = saved
    length = upstream.shape[0]
    upstream_low = upstream.astype(jnp.bfloat16)
    grad_weight_out = product_left(joined, upstream_low)
    grad_joined = (
        product_right(upstream_low, weight_out)
        .astype(jnp.bfloat16)
        .reshape(length, HEADS, HEAD_DIM)
        .transpose(1, 0, 2)
    )

    def head_backward(items):
        query, keys_head, contents, line, incoming, logs = items
        scores = head_scores(query, keys_head, line, same)
        probs = jnp.exp(scores - logs[:, None])
        grad_contents = product_left(probs.astype(jnp.bfloat16), incoming)
        grad_probs = product_right(incoming, contents)
        grad_scores = probs * (grad_probs - jnp.sum(grad_probs * probs, axis=1, keepdims=True))
        scaled = (grad_scores * HEAD_DIM ** (-0.5)).astype(jnp.bfloat16)
        grad_query = product(scaled, keys_head)
        grad_keys = product_left(scaled, query)
        return (
            jnp.stack([grad_query, grad_keys, grad_contents]).astype(jnp.bfloat16),
            diagonal_sums(grad_scores),
        )

    grad_mixed, grad_lines = lax.map(
        head_backward, (mixed[0], mixed[1], mixed[2], lines, grad_joined, logsum)
    )
    grad_flat = grad_mixed.transpose(2, 1, 0, 3).reshape(length, 3 * D)
    grad_mixer = product_left(normed_low, grad_flat)
    grad_values, grad_norm = norm_back(product_right(grad_flat, mixer))
    grad_table = jnp.dot(grad_lines, choose.T, precision=highest).reshape(-1)
    return (
        upstream + grad_values,
        (grad_norm, grad_mixer, grad_weight_out, jnp.sum(upstream, axis=0), grad_table),
    )


def gate_unit(joined):
    width = joined.shape[1] // 2
    return joined[:, :width] * jax.nn.sigmoid(joined[:, width:])


def plain_depthwise(gated, kernel, marks):
    length = gated.shape[0]
    half = kernel.shape[0] // 2
    padded = jnp.pad(gated, ((half, half), (0, 0)))
    bounds = jnp.pad(marks, (half, half), constant_values=-1)
    total = jnp.zeros(gated.shape, gated.dtype)
    for step in range(kernel.shape[0]):
        same = (bounds[step : step + length] == marks)[:, None]
        total = total + jnp.where(same, padded[step : step + length], 0.0) * kernel[step]
    return total


def plain_conv_forward(values, weights, marks, frames):
    norm, weight_glu, bias_glu, kernel, batch, weight_out, bias_out, final = weights
    normed, norm_back = jax.vjp(layer_norm, values, norm.astype(jnp.float32))
    normed_low = normed.astype(jnp.bfloat16)
    joined = product(normed_low, weight_glu) + bias_glu.astype(jnp.float32)
    gated, gate_back = jax.vjp(gate_unit, joined)
    middle, depth_back = jax.vjp(
        lambda inner, taps: plain_depthwise(inner, taps, marks), gated, kernel.astype(jnp.float32)
    )
    sums = lax.psum((jnp.sum(middle, axis=0), jnp.sum(middle * middle, axis=0)), ("dp", "fsdp"))
    center = sums[0] / frames
    inverse = lax.rsqrt(sums[1] / frames - center * center + epsilon)
    gain = 1.0 + batch[0].astype(jnp.float32)
    unit = (middle - center) * inverse
    normal = unit * gain + batch[1].astype(jnp.float32)
    active = jax.nn.silu(normal).astype(jnp.bfloat16)
    result = values + product(active, weight_out) + bias_out.astype(jnp.float32)
    return (
        result,
        (normed_low, gate_back, depth_back, inverse, gain, unit, normal, active, norm_back),
    )


def plain_conv_backward(upstream, weights, saved, frames):
    norm, weight_glu, bias_glu, kernel, batch, weight_out, bias_out, final = weights
    normed_low, gate_back, depth_back, inverse, gain, unit, normal, active, norm_back = saved
    upstream_low = upstream.astype(jnp.bfloat16)
    grad_weight_out = product_left(active, upstream_low)
    grad_normal = product_right(upstream_low, weight_out) * silu_slope(normal)
    sums = lax.psum(
        (jnp.sum(grad_normal, axis=0), jnp.sum(grad_normal * unit, axis=0)), ("dp", "fsdp")
    )
    grad_middle = inverse * (
        grad_normal * gain - gain * sums[0] / frames - unit * (gain * sums[1] / frames)
    )
    grad_gated, grad_kernel = depth_back(grad_middle)
    grad_joined = gate_back(grad_gated)[0]
    joined_low = grad_joined.astype(jnp.bfloat16)
    grad_weight_glu = product_left(normed_low, joined_low)
    grad_values, grad_norm = norm_back(product_right(joined_low, weight_glu))
    grad_batch = jnp.stack([sums[1], sums[0]])
    return (
        upstream + grad_values,
        (
            grad_norm,
            grad_weight_glu,
            jnp.sum(grad_joined, axis=0),
            grad_kernel,
            grad_weight_out,
            jnp.sum(upstream, axis=0),
        ),
        grad_batch,
    )


def plain(
    inputs,
    segments,
    buckets,
    cotangent,
    ffn_norm,
    ffn_in,
    ffn_in_bias,
    ffn_out,
    ffn_out_bias,
    attn_norm,
    qkv_weight,
    attn_out,
    attn_out_bias,
    rel_table,
    conv_norm,
    glu_weight,
    glu_bias,
    depth_kernel,
    batch_norm,
    conv_out,
    conv_out_bias,
    final_norm,
):
    values = inputs[0].astype(jnp.float32)
    marks = segments[0]
    devices = lax.axis_size(("dp", "fsdp"))
    frames = values.shape[0] * devices
    feed_first = plain_fetch_feed(ffn_norm, ffn_in, ffn_in_bias, ffn_out, ffn_out_bias, 0)
    first, first_saved = plain_feed_forward(values, feed_first)
    attn_weights = fetch_attention(attn_norm, qkv_weight, attn_out, attn_out_bias, rel_table)
    second, attn_saved = plain_attention_forward(first, attn_weights, marks, buckets)
    conv_weights = fetch_conv(
        conv_norm,
        glu_weight,
        glu_bias,
        depth_kernel,
        batch_norm,
        conv_out,
        conv_out_bias,
        final_norm,
    )
    third, conv_saved = plain_conv_forward(second, conv_weights, marks, frames)
    feed_second = plain_fetch_feed(ffn_norm, ffn_in, ffn_in_bias, ffn_out, ffn_out_bias, 1)
    fourth, second_saved = plain_feed_forward(third, feed_second)
    result, final_back = jax.vjp(layer_norm, fourth, conv_weights[7].astype(jnp.float32))
    grad_fourth, grad_final = final_back(cotangent[0].astype(jnp.float32))
    second_back = plain_fetch_feed(ffn_norm, ffn_in, ffn_in_bias, ffn_out, ffn_out_bias, 1)
    grad_third, second_grads = plain_feed_backward(grad_fourth, second_back, second_saved)
    conv_back = fetch_conv(
        conv_norm,
        glu_weight,
        glu_bias,
        depth_kernel,
        batch_norm,
        conv_out,
        conv_out_bias,
        final_norm,
    )
    grad_second, conv_grads, grad_batch = plain_conv_backward(grad_third, conv_back, conv_saved, frames)
    attn_back = fetch_attention(attn_norm, qkv_weight, attn_out, attn_out_bias, rel_table)
    grad_first, attn_grads = plain_attention_backward(grad_second, attn_back, attn_saved)
    first_back = plain_fetch_feed(ffn_norm, ffn_in, ffn_in_bias, ffn_out, ffn_out_bias, 0)
    grad_start, first_grads = plain_feed_backward(grad_first, first_back, first_saved)
    first_shards = plain_reduce_feed(first_grads)
    second_shards = plain_reduce_feed(second_grads)
    attn_shards = (
        lax.psum_scatter(attn_grads[0], ("dp", "fsdp"), scatter_dimension=1, tiled=True),
        lax.psum_scatter(attn_grads[1], ("dp", "fsdp"), scatter_dimension=0, tiled=True),
        lax.psum_scatter(attn_grads[2], ("dp", "fsdp"), scatter_dimension=0, tiled=True),
        lax.psum_scatter(attn_grads[3], ("dp", "fsdp"), scatter_dimension=0, tiled=True),
        lax.psum_scatter(attn_grads[4], ("dp", "fsdp"), scatter_dimension=0, tiled=True),
    )
    conv_shards = (
        lax.psum_scatter(conv_grads[0], ("dp", "fsdp"), scatter_dimension=1, tiled=True),
        lax.psum_scatter(conv_grads[1], ("dp", "fsdp"), scatter_dimension=0, tiled=True),
        lax.psum_scatter(conv_grads[2], ("dp", "fsdp"), scatter_dimension=0, tiled=True),
        lax.psum_scatter(conv_grads[3], ("dp", "fsdp"), scatter_dimension=1, tiled=True),
        lax.psum_scatter(conv_grads[4], ("dp", "fsdp"), scatter_dimension=0, tiled=True),
        lax.psum_scatter(conv_grads[5], ("dp", "fsdp"), scatter_dimension=0, tiled=True),
        lax.psum_scatter(grad_final, ("dp", "fsdp"), scatter_dimension=1, tiled=True),
    )
    width = D // devices
    batch_shard = lax.dynamic_slice_in_dim(
        grad_batch, lax.axis_index(("dp", "fsdp")) * width, width, 1
    )
    return (
        result[None].astype(jnp.bfloat16),
        grad_start[None],
        jnp.stack([first_shards[0], second_shards[0]]),
        jnp.stack([first_shards[1], second_shards[1]]),
        jnp.stack([first_shards[2], second_shards[2]]),
        jnp.stack([first_shards[3], second_shards[3]]),
        jnp.stack([first_shards[4], second_shards[4]]),
        attn_shards[0],
        attn_shards[1],
        attn_shards[2],
        attn_shards[3],
        attn_shards[4],
        conv_shards[0],
        conv_shards[1],
        conv_shards[2],
        conv_shards[3],
        batch_shard,
        conv_shards[4],
        conv_shards[5],
        conv_shards[6],
    )


def solution(mesh):
    in_specs = (
        P(("dp", "fsdp"), None, None),
        P(("dp", "fsdp"), None),
        P(),
        P(("dp", "fsdp"), None, None),
        P(None, None, ("dp", "fsdp")),
        P(None, ("dp", "fsdp"), None),
        P(None, ("dp", "fsdp")),
        P(None, ("dp", "fsdp"), None),
        P(None, ("dp", "fsdp")),
        P(None, ("dp", "fsdp")),
        P(("dp", "fsdp"), None),
        P(("dp", "fsdp"), None),
        P(("dp", "fsdp")),
        P(("dp", "fsdp")),
        P(None, ("dp", "fsdp")),
        P(("dp", "fsdp"), None),
        P(("dp", "fsdp")),
        P(None, ("dp", "fsdp")),
        P(None, ("dp", "fsdp")),
        P(("dp", "fsdp"), None),
        P(("dp", "fsdp")),
        P(None, ("dp", "fsdp")),
    )
    out_specs = (
        P(("dp", "fsdp"), None, None),
        P(("dp", "fsdp"), None, None),
        P(None, None, ("dp", "fsdp")),
        P(None, ("dp", "fsdp"), None),
        P(None, ("dp", "fsdp")),
        P(None, ("dp", "fsdp"), None),
        P(None, ("dp", "fsdp")),
        P(None, ("dp", "fsdp")),
        P(("dp", "fsdp"), None),
        P(("dp", "fsdp"), None),
        P(("dp", "fsdp")),
        P(("dp", "fsdp")),
        P(None, ("dp", "fsdp")),
        P(("dp", "fsdp"), None),
        P(("dp", "fsdp")),
        P(None, ("dp", "fsdp")),
        P(None, ("dp", "fsdp")),
        P(("dp", "fsdp"), None),
        P(("dp", "fsdp")),
        P(None, ("dp", "fsdp")),
    )
    fast = mesh.shape["dp"] == 4 and mesh.shape["fsdp"] == 8
    return jax.shard_map(local if fast else plain, mesh=mesh, in_specs=in_specs, out_specs=out_specs, check_vma=False)
```

```python
import jax
import jax.numpy as jnp
from jax import lax
from jax.experimental import pallas as pl
from jax.experimental.pallas import tpu as pltpu
from jax.sharding import PartitionSpec as P

D = 512
FF = 2048
HEADS = 8
HEAD_DIM = 64
BUCKETS = 32
L = 512
TAPS = 32
PAD = 16
epsilon = 1e-05
F32, BF16 = jnp.float32, jnp.bfloat16
MESH = pl.DeviceIdType.MESH

SMALL, IN0, OUT0, QKV, ATT, GLU, CONV, IN1, OUT1, ROWS = 0, 16, 80, 144, 192, 208, 240, 256, 320, 384
GRADS = ROWS - IN0
(S_FFN, S_FOB, S_ATTN, S_AOB, S_CONV, S_BATCH, S_COB, S_FINAL, S_TAPS, S_ROWS) = (0, 4, 6, 8, 9, 11, 13, 14, 16, 48)
CHUNK = 64
BLOCK = 128
SOFT = 32
UNROLL = True


def dot(a, b):
    return jnp.dot(a, b, preferred_element_type=F32)


def dot_nt(a, b):
    return lax.dot_general(a, b, (((1,), (1,)), ((), ())), preferred_element_type=F32)


def dot_tn(a, b):
    return lax.dot_general(a, b, (((0,), (0,)), ((), ())), preferred_element_type=F32)


def chunks(body, carry=None, size=CHUNK):
    def step(i, carry):
        return body(pl.ds(pl.multiple_of(i * size, size), size), carry)

    return lax.fori_loop(0, L // size, step, carry, unroll=True)


def fold(values):
    return jnp.sum(values.reshape(values.shape[0] // 8, 8, values.shape[1]), axis=0)


def zeros8(width=D):
    return jnp.zeros((8, width), F32)


def total_row(values):
    return jnp.sum(values, axis=0, keepdims=True)


class Bag:
    pass


class Place:
    def __init__(self):
        self.planes = lax.axis_size("dp")
        self.chips = lax.axis_size("fsdp") // 2
        self.plane, inner = lax.axis_index("dp"), lax.axis_index("fsdp")
        self.z, self.core = inner // 2, inner % 2
        y, x = self.plane // 2, self.plane % 2
        self.plane_x, self.plane_y, self.plane_d = y * 2 + 1 - x, (1 - y) * 2 + x, (1 - y) * 2 + 1 - x
        self.twin = (self.plane, 2 * self.z + 1 - self.core)
        self.over_x = (self.plane_x, inner)
        self.over_y = (self.plane_y, inner)
        self.chip = [lax.rem(self.z + step, self.chips) for step in range(self.chips)]
        self.along = [(self.plane, 2 * chip + self.core) for chip in self.chip]
        self.rank = self.plane * 2 + self.core
        self.members = []
        for step in range(self.planes):
            for flip in range(2):
                if step or flip:
                    plane, core = lax.rem(self.plane + step, self.planes), lax.rem(self.core + flip, 2)
                    self.members.append(((plane, 2 * self.z + core), plane * 2 + core))


class Copies:
    def __init__(self, sends, receives, place):
        self.sends, self.receives, self.place = sends, receives, place
        self.begun = []

    def start(self, number, make, receive=None):
        def copy():
            source, target, device = make()
            return pltpu.make_async_remote_copy(
                source, target, self.sends.at[number], self.receives.at[number if receive is None else receive],
                device_id=device, device_id_type=MESH,
            )

        copy().start()
        self.begun.append(copy)

    def arrived(self, number, target):
        pltpu.make_async_remote_copy(
            target, target, self.sends.at[number], self.receives.at[number],
            device_id=self.place.twin, device_id_type=MESH,
        ).wait_recv()

    def sent(self):
        for copy in self.begun:
            copy().wait_send()
        self.begun = []


class Gather:
    def __init__(self, place, weights, copies, first, begin, size, split):
        self.place, self.weights, self.copies, self.first = place, weights, copies, first
        self.rows = pl.ds(begin, size)
        self.parts = (pl.ds(begin, split), pl.ds(begin + split, size - split))
        chips = place.chips
        self.x, self.y, self.d, self.t = chips, 2 * chips, 3 * chips, 3 * chips + 2

    @staticmethod
    def semaphores(chips):
        return 3 * chips + 6

    def column(self, plane, side, which):
        return self.weights.at[plane, :, side, which]

    def slot(self, plane, step):
        p = self.place
        return self.weights.at[plane, p.chip[(p.chips - step) % p.chips], p.core, self.rows]

    def move(self, number, ref, device):
        self.copies.start(self.first + number, lambda: (ref(), ref(), device))

    def arrived(self, number, ref):
        self.copies.arrived(self.first + number, ref)

    def along_z(self):
        p = self.place
        for d in range(1, p.chips):
            self.move(d, lambda: self.slot(p.plane, 0), p.along[d])

    def beside(self, step):
        p = self.place
        self.move(self.x + step, lambda: self.slot(p.plane, step), p.over_x)
        self.move(self.y + step, lambda: self.slot(p.plane, step), p.over_y)

    def own(self):
        self.beside(0)

    def forward(self):
        p = self.place
        for d in range(1, p.chips):
            self.arrived(d, self.slot(p.plane, d))
            self.beside(d)
        self.move(self.t, lambda: self.column(p.plane, p.core, self.rows), p.twin)

    def turn(self):
        p = self.place
        for d in range(p.chips):
            self.arrived(self.x + d, self.slot(p.plane_x, d))
        self.move(self.d, lambda: self.column(p.plane_x, p.core, self.parts[0]), p.over_y)
        for d in range(p.chips):
            self.arrived(self.y + d, self.slot(p.plane_y, d))
        self.move(self.d + 1, lambda: self.column(p.plane_y, p.core, self.parts[1]), p.over_x)
        self.move(self.t + 1, lambda: self.column(p.plane_x, p.core, self.rows), p.twin)
        self.move(self.t + 2, lambda: self.column(p.plane_y, p.core, self.rows), p.twin)

    def across(self):
        p = self.place
        self.arrived(self.d, self.column(p.plane_d, p.core, self.parts[0]))
        self.arrived(self.d + 1, self.column(p.plane_d, p.core, self.parts[1]))
        self.move(self.t + 3, lambda: self.column(p.plane_d, p.core, self.rows), p.twin)

    def done(self):
        p = self.place
        for number, plane in enumerate((p.plane, p.plane_x, p.plane_y, p.plane_d)):
            self.arrived(self.t + number, self.column(plane, 1 - p.core, self.rows))


def reduce_steps(place, data, twin, diagonal, from_x, from_y, from_z, copies, first, begin, size, split, landing, finish):
    p, core, chips = place, place.core, place.chips
    rows, lands = pl.ds(begin, size), pl.ds(landing, size)
    parts = (pl.ds(begin, split), pl.ds(begin + split, size - split))
    parts_land = (pl.ds(landing, split), pl.ds(landing + split, size - split))

    def column(plane, side, which):
        return data.at[plane, :, side, which]

    def add(plane, which, *sources):
        def step(zz, carry):
            value = data[plane, zz, core, which, :]
            for ref in sources:
                value = value + ref(zz)
            data[plane, zz, core, which, :] = value
            return carry

        lax.fori_loop(0, chips, step, 0)

    def read(ref, which, *lead):
        return lambda zz: ref[lead + (zz, which, slice(None))]

    def to_twin():
        for number, plane in enumerate((p.plane_d, p.plane_y, p.plane_x, p.plane)):
            copies.start(
                first + number, lambda plane=plane: (column(plane, 1 - core, rows), twin.at[plane, :, lands], p.twin)
            )

    def across():
        copies.arrived(first, twin.at[p.plane_d, :, lands])
        add(p.plane_d, rows, read(twin, lands, p.plane_d))
        copies.start(first + 4, lambda: (column(p.plane_d, core, parts[0]), diagonal.at[:, parts_land[0]], p.over_y))
        if split < size:
            copies.start(first + 5, lambda: (column(p.plane_d, core, parts[1]), diagonal.at[:, parts_land[1]], p.over_x))

    def beside():
        copies.arrived(first + 2, twin.at[p.plane_x, :, lands])
        copies.arrived(first + 4, diagonal.at[:, parts_land[0]])
        add(p.plane_x, rows, read(twin, lands, p.plane_x))
        add(p.plane_x, parts[0], read(diagonal, parts_land[0]))
        copies.start(first + 7, lambda: (column(p.plane_x, core, rows), from_x.at[:, lands], p.over_x))
        copies.arrived(first + 1, twin.at[p.plane_y, :, lands])
        add(p.plane_y, rows, read(twin, lands, p.plane_y))
        if split < size:
            copies.arrived(first + 5, diagonal.at[:, parts_land[1]])
            add(p.plane_y, parts[1], read(diagonal, parts_land[1]))
        copies.start(first + 6, lambda: (column(p.plane_y, core, rows), from_y.at[:, lands], p.over_y))

    def own_column():
        copies.arrived(first + 3, twin.at[p.plane, :, lands])
        copies.arrived(first + 6, from_y.at[:, lands])
        copies.arrived(first + 7, from_x.at[:, lands])
        add(p.plane, rows, read(twin, lands, p.plane), read(from_x, lands), read(from_y, lands))
        for d in range(1, chips):
            copies.start(
                first + 7 + d,
                lambda d=d: (data.at[p.plane, p.chip[d], core, rows], from_z.at[d - 1, lands], p.along[d]),
            )

    def along_z():
        for d in range(1, chips):
            copies.arrived(first + 7 + d, from_z.at[d - 1, lands])
        value = data[p.plane, p.z, core, rows, :].astype(F32)
        for d in range(1, chips):
            value = value + from_z[d - 1, lands, :].astype(F32)
        finish(value)

    return [to_twin, across, beside, own_column, along_z]


class Thin:
    def __init__(self, place, tiles, near, part, far, result, copies, first):
        self.place, self.tiles, self.near, self.part, self.far, self.result = place, tiles, near, part, far, result
        self.copies, self.first = copies, first

    def start(self):
        p = self.place
        for i, (device, rank) in enumerate(p.members):
            self.copies.start(
                self.first + i,
                lambda device=device: (self.tiles.at[device[0], :, lax.rem(device[1], 2)], self.near.at[p.rank], device),
                self.first + p.rank,
            )
        self.near[p.rank] = self.tiles[p.plane, :, p.core]

    def turn(self):
        p = self.place
        for device, rank in p.members:
            self.copies.arrived(self.first + rank, self.near.at[rank])
        value = self.near[0]
        for i in range(1, 2 * p.planes):
            value = value + self.near[i]
        self.part[...] = value
        base = self.first + 2 * p.planes
        for d in range(1, p.chips):
            self.copies.start(base + d, lambda d=d: (self.part.at[p.chip[d]], self.far.at[d], p.along[d]))

    def finish(self):
        p = self.place
        base = self.first + 2 * p.planes
        value = self.part[p.z]
        for d in range(1, p.chips):
            self.copies.arrived(base + d, self.far.at[d])
            value = value + self.far[d]
        self.result[...] = value


class Total:
    def __init__(self, place, own, near, part, far, result, copies, first):
        self.place, self.own, self.near, self.part, self.far, self.result = place, own, near, part, far, result
        self.copies, self.first = copies, first

    def start(self):
        p = self.place
        me = p.rank
        for i, (device, rank) in enumerate(p.members):
            self.copies.start(self.first + i, lambda device=device: (self.own, self.near.at[me], device), self.first + me)
        self.near[me] = self.own[...]

    def turn(self):
        p = self.place
        for device, rank in p.members:
            self.copies.arrived(self.first + rank, self.near.at[rank])
        value = self.near[0]
        for i in range(1, 2 * p.planes):
            value = value + self.near[i]
        self.part[...] = value
        base = self.first + 2 * p.planes
        for d in range(1, p.chips):
            self.copies.start(base + d, lambda d=d: (self.part, self.far.at[d], p.along[d]))

    def finish(self):
        p = self.place
        base = self.first + 2 * p.planes
        value = self.part[...]
        for d in range(1, p.chips):
            self.copies.arrived(base + d, self.far.at[d])
            value = value + self.far[d]
        self.result[...] = value


def at_points(table):
    def pump(index, place=0):
        for (iteration, where), steps in table.items():
            if where != place or (isinstance(index, int) and index != iteration):
                continue

            def act(steps=steps):
                for step in steps:
                    step()

            if isinstance(index, int):
                act()
            else:
                pl.when(index == iteration)(act)

    return pump


def still(index, place=0):
    pass


def standard(values):
    values = values.astype(F32)
    center = values - jnp.mean(values, axis=-1, keepdims=True)
    inverse = lax.rsqrt(jnp.mean(center * center, axis=-1, keepdims=True) + epsilon)
    return center * inverse, inverse


def norm_rows(source, target, small, row):
    gain, shift = 1.0 + small[row : row + 1, :], small[row + 1 : row + 2, :]

    def body(rows, carry):
        target[rows, :] = (standard(source[rows, :])[0] * gain + shift).astype(target.dtype)
        return carry

    chunks(body, 0)


def norm_back(source, grad, upstream, result, small, row, grads):
    gain = 1.0 + small[row : row + 1, :]

    def body(rows, carry):
        unit, inverse = standard(source[rows, :])
        given = grad[rows, :].astype(F32)
        inner = given * gain
        back = inverse * (
            inner
            - jnp.mean(inner, axis=-1, keepdims=True)
            - unit * jnp.mean(inner * unit, axis=-1, keepdims=True)
        )
        result[rows, :] = back if upstream is None else upstream[rows, :] + back
        return carry[0] + fold(given * unit), carry[1] + fold(given)

    first, second = chunks(body, (zeros8(), zeros8()))
    grads[row : row + 1, :] = total_row(first)
    grads[row + 1 : row + 2, :] = total_row(second)


def block_cols(c):
    return pl.ds(c * D if isinstance(c, int) else pl.multiple_of(c * D, D), D)


def columns(weights, start, block):
    return weights[:, :, :, start + 16 * block : start + 16 * block + 16, :].reshape(D, D)


def put_columns(weights, start, block, value):
    rows = pl.ds(start + 16 * block, 16)
    weights[:, :, :, rows, :] = value.astype(BF16).reshape(weights.shape[:3] + (16, D))


def lines_of(weights, start, block):
    return weights[block, :, :, start : start + 64, :].reshape(D, D)


def put_lines(weights, start, block, value):
    weights[block, :, :, start : start + 64, :] = value.astype(BF16).reshape(weights.shape[1:3] + (64, D))


def feed_inner(source, normed, active, slope, raws, weights, small, inner_bias, layer, pump):
    norm_rows(source, normed, small, S_FFN + 2 * layer)
    for c in range(FF // D):
        pump(c)
        cols, raw = block_cols(c), raws[c % 2]
        raw[...] = dot(normed[...], columns(weights, (IN0, IN1)[layer], c))
        bias = inner_bias[layer : layer + 1, cols]

        def body(rows, carry, cols=cols, raw=raw, bias=bias):
            inner = raw[rows, :] + bias
            sigma = jax.nn.sigmoid(inner)
            value = inner * sigma
            active[rows, cols] = value.astype(BF16)
            slope[rows, cols] = (sigma + value * (1.0 - sigma)).astype(BF16)
            return carry

        chunks(body, 0)


def feed_outer(source, active, result, hold, weights, small, layer):
    begin = (OUT0, OUT1)[layer]
    hold[...] = dot(active[...], weights[:, :, :, begin : begin + 64, :].reshape(FF, D))
    bias = small[S_FOB + layer : S_FOB + layer + 1, :]

    def body(rows, carry):
        result[rows, :] = source[rows, :].astype(F32) + 0.5 * (hold[rows, :] + bias)
        return carry

    chunks(body, 0)


def feed_back_start(upstream, low, grads, layer):
    def start(rows, carry):
        half = 0.5 * upstream[rows, :]
        low[rows, :] = half.astype(BF16)
        return carry + fold(half)

    grads[S_FOB + layer : S_FOB + layer + 1, :] = total_row(chunks(start, zeros8()))


def feed_back_outer(active, low, weights, begin, pump):
    for c in range(FF // D):
        put_lines(weights, begin, c, dot_tn(active[:, block_cols(c)], low[...]))
        pump(c)


def feed_back_inner(normed, slope, low, raws, weights, target, inner_grads, layer, pump):
    begin = (OUT0, OUT1)[layer]
    for c in range(FF // D):
        cols, raw = block_cols(c), raws[c % 2]
        raw[...] = dot_nt(low[...], lines_of(weights, begin, c))

        def body(rows, carry, cols=cols, raw=raw):
            grad = raw[rows, :] * slope[rows, cols].astype(F32)
            slope[rows, cols] = grad.astype(BF16)
            return carry + fold(grad)

        inner_grads[layer : layer + 1, cols] = total_row(chunks(body, zeros8()))
        if target is not None:
            put_columns(weights, target, c, dot_tn(normed[...], slope[:, cols]))
        pump(c)


def product_back(grad, normed, total, weights, begin, blocks, pump):
    value = None
    for c in range(blocks):
        part = dot_nt(grad[:, block_cols(c)], columns(weights, begin, c))
        value = part if value is None else value + part
    total[...] = value
    for c in range(blocks):
        if normed is not None:
            put_columns(weights, begin, c, dot_tn(normed[...], grad[:, block_cols(c)]))
        pump(c)


def bucket_choice(buckets):
    return (lax.broadcasted_iota(jnp.int32, (BUCKETS, 2 * L), 0) == buckets[...]).astype(F32)


def attention_mix(source, normed, mixed, weights, small):
    norm_rows(source, normed, small, S_ATTN)

    for c in range(3):
        mixed[:, block_cols(c)] = dot(normed[...], columns(weights, QKV, c)).astype(BF16)


def attention_squares(lines, squares, mask, table, buckets, bounds, marks):
    lines[...] = dot(table[...].astype(BF16), bucket_choice(buckets).astype(BF16))

    def head(h, carry):
        line = jnp.broadcast_to(lines[pl.ds(h, 1), :], (BLOCK, 2 * L))
        square = pltpu.roll(line, 2 * L - BLOCK + 1, 1, stride=1, stride_axis=0).astype(BF16)
        for part in range(2):
            squares[lax.rem(h, 4), lax.div(h, 4), part * BLOCK : (part + 1) * BLOCK, :] = square[:, part * L : (part + 1) * L]
        return carry

    lax.fori_loop(0, HEADS, head, 0)

    def body(rows, carry):
        same = bounds[pl.ds(rows.start + PAD, CHUNK), 0:1] == marks[...]
        mask[rows, :] = jnp.where(same, 3e38, -1e30)
        return carry

    chunks(body, 0)


def attention_forward(source, mixed, probs, joined, recips, result, squares, mask, hold, hold2, weights, small, pump):
    lane = lax.broadcasted_iota(jnp.int32, (1, 128), 1)

    def pair(index, carry):
        begin = pl.multiple_of(128 * index, 128)
        query = mixed[:, pl.ds(begin, 128)] * HEAD_DIM ** (-0.5)
        keys = mixed[:, pl.ds(D + begin, 128)]
        contents = mixed[:, pl.ds(2 * D + begin, 128)]
        parts = []
        for half, raw in enumerate((hold, hold2)):
            here = (lane // HEAD_DIM) == half
            raw[...] = dot_nt(jnp.where(here, query, jnp.zeros_like(query)), keys)
        for half, raw in enumerate((hold, hold2)):
            head = 2 * index + half
            here = (lane // HEAD_DIM) == half
            for block in range(L // BLOCK):

                def body(i, carry, block=block, raw=raw, head=head):
                    at = pl.multiple_of(i * SOFT, SOFT)
                    rows = pl.ds(block * BLOCK + at, SOFT)
                    square = squares[lax.rem(head, 4), lax.div(head, 4), pl.ds(at, SOFT), 384 - block * BLOCK : L]
                    if block < L // BLOCK - 1:
                        more = squares[lax.rem(head, 4), lax.div(head, 4), pl.ds(BLOCK + at, SOFT), 0 : 384 - block * BLOCK]
                        square = jnp.concatenate([square, more], axis=1)
                    scores = jnp.minimum(raw[rows, :] + square.astype(F32), mask[rows, :])
                    probs[head, rows, :] = jnp.exp(scores - jnp.max(scores, axis=1, keepdims=True)).astype(BF16)
                    return carry

                lax.fori_loop(0, BLOCK // SOFT, body, 0, unroll=UNROLL)
                if half:
                    pump(index, block)
            parts.append(dot(probs[head], jnp.where(here, contents, jnp.ones_like(contents))))
        value = jnp.where(lane < HEAD_DIM, parts[0], parts[1])
        sums = jnp.where(lane < HEAD_DIM, pltpu.roll(parts[0], HEAD_DIM, 1), pltpu.roll(parts[1], HEAD_DIM, 1))
        recip = 1.0 / sums
        recips[:, pl.ds(begin, 128)] = recip
        joined[:, pl.ds(begin, 128)] = value * recip
        return carry

    lax.fori_loop(0, HEADS // 2, pair, 0)
    hold[...] = dot(joined[...].astype(BF16), columns(weights, ATT, 0))
    bias = small[S_AOB : S_AOB + 1, :]

    def body(rows, carry):
        result[rows, :] = source[rows, :] + hold[rows, :] + bias
        return carry

    chunks(body, 0)


def attention_back_start(upstream, joined, recips, low, spread, hold, weights, grads):
    def start(rows, carry):
        given = upstream[rows, :]
        low[rows, :] = given.astype(BF16)
        return carry + fold(given)

    grads[S_AOB : S_AOB + 1, :] = total_row(chunks(start, zeros8()))
    hold[...] = dot_nt(low[...], columns(weights, ATT, 0))

    def body(rows, carry):
        spread[rows, :] = (hold[rows, :] * recips[rows, :]).astype(BF16)
        return carry

    chunks(body, 0)
    put_columns(weights, ATT, 0, dot_tn(joined[...].astype(BF16), low[...]))


def attention_backward(mixed, probs, spread, joined, grad_mixed, scaled, hold, hold2, means, diagonals, lines, buckets, table_grad, pump):
    lane = lax.broadcasted_iota(jnp.int32, (1, 128), 1)
    sides = lax.broadcasted_iota(jnp.int32, (256, 256), 0) // HEAD_DIM % 2 == lax.broadcasted_iota(jnp.int32, (256, 256), 1) // 128
    sides = jnp.where(sides, 1.0, 0.0).astype(BF16)

    def pair(index, carry):
        begin = pl.multiple_of(128 * index, 128)
        query = mixed[:, pl.ds(begin, 128)]
        keys = mixed[:, pl.ds(D + begin, 128)]
        contents = mixed[:, pl.ds(2 * D + begin, 128)]
        incoming = spread[:, pl.ds(begin, 128)]
        for half, raw in enumerate((hold, hold2)):
            here = (lane // HEAD_DIM) == half
            raw[...] = dot_nt(jnp.where(here, incoming, jnp.zeros_like(incoming)), contents)
        both = incoming.astype(F32) * joined[:, pl.ds(begin, 128)]
        upper = both.astype(BF16)
        lower = (both - upper.astype(F32)).astype(BF16)
        means[:, 0:256] = dot(jnp.concatenate([upper, lower], axis=1), sides)
        turned_query, turned_incoming = query.T, incoming.T
        grads_query, grads_keys, grads_contents = [], [], []
        for half, raw in enumerate((hold, hold2)):
            head = 2 * index + half
            side = slice(half * HEAD_DIM, (half + 1) * HEAD_DIM)
            cols = pl.ds(half * L, L)
            part = zeros8(2 * L)
            for u in range(BLOCK // 16):
                tiles = [None] * 7 + [jnp.zeros((16, 128), F32)]
                for block in range(L // BLOCK):
                    rows = pl.ds(block * BLOCK + 16 * u, 16)
                    mean = means[rows, 128 * half : 128 * half + 128]
                    slant = probs[head, rows, :].astype(F32) * (raw[rows, :] - jnp.concatenate([mean] * 4, axis=1))
                    scaled[rows, cols] = slant.astype(BF16)
                    for j in range(4):
                        piece = slant[:, 128 * j : 128 * j + 128]
                        at = 3 - block + j
                        tiles[at] = piece if tiles[at] is None else tiles[at] + piece
                full = jnp.concatenate(tiles, axis=1)
                part = part + pltpu.roll(full[0:8], BLOCK - 8 - 16 * u, 1) + pltpu.roll(full[8:16], BLOCK - 16 - 16 * u, 1)
            diagonals[:, pl.ds(head, 1), :] = part.reshape(8, 1, 2 * L)
            grads_query.append(dot(scaled[:, cols], keys))
            grads_keys.append(dot(turned_query[side], scaled[:, cols]))
            grads_contents.append(dot(turned_incoming[side], probs[head]))
            pump(index, half)
        scale = HEAD_DIM ** (-0.5)
        grad_mixed[:, pl.ds(begin, 128)] = (jnp.where(lane < HEAD_DIM, *grads_query) * scale).astype(BF16)
        grad_mixed[:, pl.ds(D + begin, 128)] = (jnp.concatenate(grads_keys, axis=0).T * scale).astype(BF16)
        grad_mixed[:, pl.ds(2 * D + begin, 128)] = jnp.concatenate(grads_contents, axis=0).T.astype(BF16)
        return carry

    lax.fori_loop(0, HEADS // 2, pair, 0)
    line = diagonals[7]
    for r in range(7):
        line = line + pltpu.roll(diagonals[r], 7 - r, 1)
    table_grad[...] = lax.dot_general(
        line, bucket_choice(buckets), (((1,), (1,)), ((), ())),
        precision=lax.Precision.HIGHEST, preferred_element_type=F32,
    )


def clear_pads(padded):
    edge = jnp.zeros((4, PAD, 128), F32)
    padded[:, 0:PAD, :] = edge
    padded[:, PAD + L : 2 * PAD + L, :] = edge


def conv_front(source, normed, sigma, tilt, gated, middle, sums, hold, spare, weights, small, gate_bias, bounds, pump):
    norm_rows(source, normed, small, S_CONV)
    clear_pads(gated)
    hold[...] = dot(normed[...], columns(weights, GLU, 1))
    bias = gate_bias[0:1, D:]

    def gate(rows, carry):
        gate = jax.nn.sigmoid(hold[rows, :] + bias)
        spare[rows, :] = gate
        sigma[rows, :] = gate.astype(BF16)
        return carry

    chunks(gate, 0)
    hold[...] = dot(normed[...], columns(weights, GLU, 0))
    bias = gate_bias[0:1, :D]

    def unit(rows, carry):
        gate = spare[rows, :]
        values = (hold[rows, :] + bias) * gate
        tilt[rows, :] = (values * (1.0 - gate)).astype(BF16)
        for j in range(4):
            gated[j, pl.ds(rows.start + PAD, CHUNK), :] = values[:, 128 * j : 128 * j + 128]
        return carry

    chunks(unit, 0)
    size = 32

    def slide(i, carry):
        begin = pl.multiple_of(i * size, size)
        marks = bounds[pl.ds(begin + PAD, size), :]
        accs = [jnp.zeros((size, 128), F32) for _ in range(4)]
        for k in range(TAPS):
            same = bounds[pl.ds(begin + k, size), :] == marks
            for j in range(4):
                tap = small[S_TAPS + k : S_TAPS + k + 1, 128 * j : 128 * j + 128]
                accs[j] += jnp.where(same, gated[j, pl.ds(begin + k, size), :], 0.0) * tap
        result = []
        for j in range(4):
            middle[pl.ds(begin, size), 128 * j : 128 * j + 128] = accs[j]
            result.append(carry[j] + fold(accs[j]))
            result.append(carry[4 + j] + fold(accs[j] * accs[j]))
        pump(i)
        return result[0::2] + result[1::2]

    ends = lax.fori_loop(0, L // size, slide, [zeros8(128)] * 8, unroll=2)
    sums[...] = zeros8()
    for j in range(4):
        sums[0:1, 128 * j : 128 * j + 128] = total_row(ends[j])
        sums[1:2, 128 * j : 128 * j + 128] = total_row(ends[4 + j])


def conv_rest(source, middle, sums, unit, active, slope, result, hold, weights, small, frames):
    center = sums[0:1, :] * (1.0 / frames)
    inverse = lax.rsqrt(sums[1:2, :] * (1.0 / frames) - center * center + epsilon)
    gain, shift = 1.0 + small[S_BATCH : S_BATCH + 1, :], small[S_BATCH + 1 : S_BATCH + 2, :]

    def body(rows, carry):
        values = (middle[rows, :] - center) * inverse
        unit[rows, :] = values
        normal = values * gain + shift
        sigma = jax.nn.sigmoid(normal)
        value = normal * sigma
        active[rows, :] = value.astype(BF16)
        slope[rows, :] = (sigma + value * (1.0 - sigma)).astype(slope.dtype)
        return carry

    chunks(body, 0)
    hold[...] = dot(active[...], columns(weights, CONV, 0))
    bias = small[S_COB : S_COB + 1, :]

    def add(rows, carry):
        result[rows, :] = source[rows, :] + hold[rows, :] + bias
        return carry

    chunks(add, 0)


def conv_back_rest(upstream, unit, slope, grad_normal, low, hold, weights, grads, sums):
    def start(rows, carry):
        given = upstream[rows, :]
        low[rows, :] = given.astype(BF16)
        return carry + fold(given)

    grads[S_COB : S_COB + 1, :] = total_row(chunks(start, zeros8()))
    hold[...] = dot_nt(low[...], columns(weights, CONV, 0))

    def body(rows, carry):
        grad = hold[rows, :] * slope[rows, :].astype(F32)
        grad_normal[rows, :] = grad
        return carry[0] + fold(grad), carry[1] + fold(grad * unit[rows, :])

    first, second = chunks(body, (zeros8(), zeros8()))
    sums[...] = zeros8()
    sums[0:1, :] = total_row(first)
    sums[1:2, :] = total_row(second)
    grads[S_BATCH : S_BATCH + 1, :] = total_row(second)
    grads[S_BATCH + 1 : S_BATCH + 2, :] = total_row(first)


def conv_back_front(
    sigma, tilt, gated, unit, grad_normal, front_sums, sums, padded, grad_joined, hold, tap_sums, small, bounds, grads, gate_grads,
    frames, pump,
):
    center = front_sums[0:1, :] * (1.0 / frames)
    inverse = lax.rsqrt(front_sums[1:2, :] * (1.0 / frames) - center * center + epsilon)
    gain = 1.0 + small[S_BATCH : S_BATCH + 1, :]
    mean0, mean1 = gain * sums[0:1, :] * (1.0 / frames), gain * sums[1:2, :] * (1.0 / frames)
    clear_pads(padded)

    def start(rows, carry):
        grad = inverse * (gain * grad_normal[rows, :] - mean0 - unit[rows, :] * mean1)
        for j in range(4):
            padded[j, pl.ds(rows.start + PAD, CHUNK), :] = grad[:, 128 * j : 128 * j + 128]
        return carry

    chunks(start, 0)
    tap_sums[...] = jnp.zeros_like(tap_sums)
    size = 32

    def slide(i, carry):
        begin = pl.multiple_of(i * size, size)
        marks = bounds[pl.ds(begin + PAD, size), :]
        accs = [jnp.zeros((size, 128), F32) for _ in range(4)]
        for k in range(TAPS):
            same = bounds[pl.ds(begin + 2 * PAD - k, size), :] == marks
            for j in range(4):
                tap = small[S_TAPS + k : S_TAPS + k + 1, 128 * j : 128 * j + 128]
                accs[j] += jnp.where(same, padded[j, pl.ds(begin + 2 * PAD - k, size), :], 0.0) * tap
        for j in range(4):
            hold[pl.ds(begin, size), 128 * j : 128 * j + 128] = accs[j]
        grads_here = [padded[j, pl.ds(begin + PAD, size), :] for j in range(4)]
        for k in range(TAPS):
            same = bounds[pl.ds(begin + k, size), :] == marks
            for j in range(4):
                term = jnp.where(same, gated[j, pl.ds(begin + k, size), :], 0.0) * grads_here[j]
                tap_sums[k, :, 128 * j : 128 * j + 128] += fold(term)
        pump(i)
        return carry

    lax.fori_loop(0, L // size, slide, 0, unroll=2)
    grads[S_TAPS : S_TAPS + TAPS, :] = jnp.sum(tap_sums[...], axis=1)

    def split(rows, carry):
        grad = hold[rows, :]
        first = grad * sigma[rows, :].astype(F32)
        second = grad * tilt[rows, :].astype(F32)
        grad_joined[rows, :D] = first.astype(BF16)
        grad_joined[rows, D : 2 * D] = second.astype(BF16)
        return carry[0] + fold(first), carry[1] + fold(second)

    first, second = chunks(split, (zeros8(), zeros8()))
    gate_grads[0:1, :D] = total_row(first)
    gate_grads[0:1, D:] = total_row(second)


THIN = (
    ("ffn_norm", S_FFN), ("ffn_out_bias", S_FOB), ("attn_norm", S_ATTN), ("attn_out_bias", S_AOB), ("conv_norm", S_CONV),
    ("batch_norm", S_BATCH), ("conv_out_bias", S_COB), ("final_norm", S_FINAL), ("depth_kernel", S_TAPS),
)


def turned(value):
    rows, lanes = value.shape
    value = jnp.concatenate([value, jnp.zeros((rows, 128 - lanes), F32)], axis=1)
    return jnp.concatenate([value, jnp.zeros((128 - rows, 128), F32)], axis=0).T[:lanes, :rows]


def pack_small(b, tile):
    tile[...] = jnp.zeros_like(tile)
    for name, row in THIN:
        value = getattr(b, name)[...].astype(F32)
        if name == "depth_kernel":
            value = turned(value)
        value = value.reshape(-1, value.shape[-1])
        for r in range(0, value.shape[0], 16):
            part = value[r : r + 16]
            begin = (row + r) % 16
            at = 128 * ((row + r) // 16)
            tile[begin : begin + part.shape[0], at : at + part.shape[1]] = part
    tile[0:2, 384 : 384 + b.ffn_in_bias.shape[1]] = b.ffn_in_bias[...].astype(F32)
    wide, few = b.glu_bias.shape[0], b.rel_table.shape[0]
    tile[2:3, 384 : 384 + wide] = b.glu_bias[...].astype(F32).reshape(1, wide)
    tile[3:4, 384 : 384 + few] = b.rel_table[...].astype(F32).reshape(1, few)


def pack_weights(b, put):
    for layer in range(2):
        for c in range(FF // D):
            put((IN0, IN1)[layer] + 16 * c, b.ffn_in[layer, :, D * c : D * c + D])
        put((OUT0, OUT1)[layer], b.ffn_out[layer])
    for c in range(3):
        put(QKV + 16 * c, b.qkv_weight[:, D * c : D * c + D])
    put(ATT, b.attn_out[...])
    for c in range(2):
        put(GLU + 16 * c, b.glu_weight[:, D * c : D * c + D])
    put(CONV, b.conv_out[...])


def unpack_small(b, place):
    per = 2 * place.chips
    count = place.planes * per
    width = D // count
    for device in range(count):
        tile = b.weights[device // per, (device % per) // 2, device % 2, 0:16, :].astype(F32)
        for q in range(3):
            b.small[16 * q : 16 * q + 16, width * device : width * device + width] = tile[:, 128 * q : 128 * q + width]
        b.inner_bias[:, 4 * width * device : 4 * width * (device + 1)] = tile[0:2, 384 : 384 + 4 * width]
        b.gate_bias[:, 2 * width * device : 2 * width * (device + 1)] = tile[2:3, 384 : 384 + 2 * width]
        few = HEADS * BUCKETS // count
        head, at = few * device // BUCKETS, few * device % BUCKETS
        b.table[head : head + 1, at : at + few] = tile[3:4, 384 : 384 + few]


def pack_small_grads(b, place):
    per = 2 * place.chips
    count = place.planes * per
    width = D // count
    few = HEADS * BUCKETS // count
    for device in range(count):
        tile = b.edges.at[device // per, (device % per) // 2, device % 2]
        for g in range(8):
            tile[0:6, 16 * g : 16 * g + width] = b.grads[6 * g : 6 * g + 6, width * device : width * device + width]
        for m in range(2):
            tile[6:7, 64 * m : 64 * m + 4 * width] = b.inner_grads[m : m + 1, 4 * width * device : 4 * width * (device + 1)]
        tile[7:8, 0 : 2 * width] = b.gate_grads[:, 2 * width * device : 2 * width * (device + 1)]
        head, at = few * device // BUCKETS, few * device % BUCKETS
        tile[7:8, 64 : 64 + few] = b.table_grad[head : head + 1, at : at + few]


INPUTS = (
    "inputs", "segments", "buckets", "cotangent", "ffn_norm", "ffn_in", "ffn_in_bias", "ffn_out", "ffn_out_bias", "attn_norm",
    "qkv_weight", "attn_out", "attn_out_bias", "rel_table", "conv_norm", "glu_weight", "glu_bias", "depth_kernel", "batch_norm",
    "conv_out", "conv_out_bias", "final_norm",
)
OUTPUTS = ("output", "grad_x", "shard", "thin")
GATHERS = ((SMALL, 48, 32), (IN0 + 32, 32, 16), (OUT0, 64, 32), (QKV, 64, 32), (GLU, 48, 32), (IN1, 64, 32), (OUT1, 64, 32))
REDUCES = (
    (OUT1, OUT1, 64, 32), (IN1, IN1, 64, 32), (ATT, ATT, 64, 32), (QKV, QKV, 48, 32), (OUT1, OUT0, 64, 32),
    (IN1, IN0, 32, 16), (IN1 + 32, IN0 + 32, 32, 16),
)


def scratch_of(planes, chips):
    wide, low, big = pltpu.VMEM((L, D), F32), pltpu.VMEM((L, D), BF16), pltpu.VMEM((L, FF), BF16)
    pads = pltpu.VMEM((4, L + 2 * PAD, 128), F32)
    stats = pltpu.VMEM((8, D), F32)
    return dict(
        weights=pltpu.VMEM((planes, chips, 2, ROWS, D), BF16),
        twin=pltpu.VMEM((planes, chips, GRADS, D), BF16),
        diagonal=pltpu.VMEM((chips, GRADS, D), BF16),
        from_x=pltpu.VMEM((chips, GRADS, D), BF16),
        from_y=pltpu.VMEM((chips, GRADS, D), BF16),
        from_z=pltpu.VMEM((chips - 1, GRADS, D), BF16),
        edges=pltpu.VMEM((planes, chips, 2, 8, 128), F32),
        edge_near=pltpu.VMEM((2 * planes, chips, 8, 128), F32),
        edge_part=pltpu.VMEM((chips, 8, 128), F32),
        edge_far=pltpu.VMEM((chips, 8, 128), F32),
        small=pltpu.VMEM((S_ROWS, D), F32),
        inner_bias=pltpu.VMEM((2, FF), F32),
        gate_bias=pltpu.VMEM((1, 2 * D), F32),
        table=pltpu.VMEM((HEADS, BUCKETS), F32),
        tile=pltpu.VMEM((16, D), F32),
        grads=pltpu.VMEM((S_ROWS, D), F32),
        inner_grads=pltpu.VMEM((2, FF), F32),
        gate_grads=pltpu.VMEM((1, 2 * D), F32),
        table_grad=pltpu.VMEM((HEADS, BUCKETS), F32),
        lines=pltpu.VMEM((HEADS, 2 * L), F32),
        choice=pltpu.VMEM((1, 2 * L), jnp.int32),
        bounds=pltpu.VMEM((L + 2 * PAD, 128), F32),
        marks=pltpu.VMEM((1, L), F32),
        front_own=stats, back_own=stats, front_sums=stats, back_sums=stats, front_part=stats, back_part=stats,
        front_near=pltpu.VMEM((2 * planes, 8, D), F32), back_near=pltpu.VMEM((2 * planes, 8, D), F32),
        front_far=pltpu.VMEM((chips, 8, D), F32), back_far=pltpu.VMEM((chips, 8, D), F32),
        x1=wide, x2=wide, x3=wide, x4=wide, normed_a=low, normed_c=low, normed1=low,
        active0=big, slope0=big, active1=big, slope1=big, mixed=pltpu.VMEM((L, 3 * D), BF16),
        probs=pltpu.VMEM((HEADS, L, L), BF16), joined=wide, recips=wide, diagonals=pltpu.VMEM((8, HEADS, 2 * L), F32), sigma=low, tilt=low, gated=pads, middle=wide, active_c=low, slope_c=low,
        padded=pads, low=low, hold=wide, total=wide, taps=pltpu.VMEM((TAPS, 8, D), F32),
        gather_sends=pltpu.SemaphoreType.DMA((len(GATHERS) * Gather.semaphores(chips),)),
        gather_receives=pltpu.SemaphoreType.DMA((len(GATHERS) * Gather.semaphores(chips),)),
        reduce_sends=pltpu.SemaphoreType.DMA((len(REDUCES) * (chips + 7),)),
        reduce_receives=pltpu.SemaphoreType.DMA((len(REDUCES) * (chips + 7),)),
        total_sends=pltpu.SemaphoreType.DMA((3 * (2 * planes + chips),)),
        total_receives=pltpu.SemaphoreType.DMA((3 * (2 * planes + chips),)),
    )


def whole_kernel(names, *refs):
    b = Bag()
    for name, ref in zip(names, refs):
        setattr(b, name, ref)
    place = Place()
    planes, chips = place.planes, place.chips
    frames = L * planes * chips * 2
    barrier = pltpu.get_barrier_semaphore()
    near = [device for device, rank in place.members] + [place.along[d] for d in range(1, chips)]
    for device in near:
        pl.semaphore_signal(barrier, inc=1, device_id=device, device_id_type=MESH)
    pack_small(b, b.tile)

    def put(row, value):
        b.weights[place.plane, place.z, place.core, row : row + value.shape[0], :] = value

    put(0, b.tile[...].astype(BF16))
    pack_weights(b, put)
    pl.semaphore_wait(barrier, len(near))

    gathers = Copies(b.gather_sends, b.gather_receives, place)
    rounds = [
        Gather(place, b.weights, gathers, i * Gather.semaphores(chips), begin, size, split)
        for i, (begin, size, split) in enumerate(GATHERS)
    ]
    r0, r1, r2, r3, r4, r5, r6 = rounds
    r0.along_z()
    r0.own()
    r1.along_z()
    r1.own()
    for r in rounds[2:]:
        r.along_z()
    b.marks[...] = b.segments[...].astype(F32)
    b.bounds[...] = jnp.full(b.bounds.shape, -1.0, F32)
    b.bounds[PAD : PAD + L, :] = jnp.broadcast_to(b.marks[...], (128, L)).T
    b.choice[...] = jnp.full(b.choice.shape, -1, jnp.int32)
    b.choice[:, 0 : 2 * L - 1] = b.buckets[...].reshape(1, 2 * L - 1)
    for step in (r0.forward, r1.forward, r2.own, r0.turn, r1.turn, r2.forward, r3.own, r0.across, r0.done):
        step()
    unpack_small(b, place)

    x0 = b.inputs.at[0]
    raws = (b.hold, b.total)
    feed_inner(
        x0, b.normed_c, b.active0, b.slope0, raws, b.weights, b.small, b.inner_bias, 0,
        at_points({(2, 0): (r1.across, r1.done, r3.forward)}),
    )
    r4.own()
    attention_squares(b.lines, b.twin, b.x4, b.table, b.choice, b.bounds, b.marks)
    r2.turn()
    r4.forward()
    r2.across()
    r2.done()
    feed_outer(x0, b.active0, b.x1, b.hold, b.weights, b.small, 0)
    for step in (r3.turn, r5.own, r5.forward, r3.across, r3.done):
        step()
    attention_mix(b.x1, b.normed_a, b.mixed, b.weights, b.small)
    for step in (r4.turn, r6.own, r6.forward):
        step()
    attention_forward(
        b.x1, b.mixed, b.probs, b.joined, b.recips, b.x2, b.twin, b.x4, b.hold, b.x3, b.weights, b.small, still
    )
    r4.across()
    r5.turn()
    r4.done()
    conv_front(
        b.x2, b.normed_c, b.sigma, b.tilt, b.gated, b.middle, b.front_own, b.hold, b.total, b.weights, b.small, b.gate_bias, b.bounds,
        at_points({(4, 0): (r5.across,), (10, 0): (r6.turn,)}),
    )
    totals = Copies(b.total_sends, b.total_receives, place)
    front = Total(place, b.front_own, b.front_near, b.front_part, b.front_far, b.front_sums, totals, 0)
    front.start()
    r5.done()
    front.turn()
    r6.across()
    front.finish()
    conv_rest(b.x2, b.middle, b.front_sums, b.middle, b.active_c, b.slope_c, b.x3, b.hold, b.weights, b.small, frames)
    feed_inner(b.x3, b.normed1, b.active1, b.slope1, raws, b.weights, b.small, b.inner_bias, 1, still)
    r6.done()
    feed_outer(b.x3, b.active1, b.x4, b.hold, b.weights, b.small, 1)
    norm_rows(b.x4, b.output.at[0], b.small, S_FINAL)
    flow = b.x4
    norm_back(b.x4, b.cotangent.at[0], None, flow, b.small, S_FINAL, b.grads)
    gathers.sent()

    reduces = Copies(b.reduce_sends, b.reduce_receives, place)
    landings = (b.twin, b.diagonal, b.from_x, b.from_y, b.from_z)

    def finish(begin, size):
        def act(value):
            b.shard[begin - IN0 : begin - IN0 + size, :] = value

        return act

    backs = [
        reduce_steps(
            place, b.weights, *landings, reduces, i * (chips + 7), begin, size, split, owner - IN0, finish(owner, size)
        )
        for i, (begin, owner, size, split) in enumerate(REDUCES)
    ]
    out1, in1, conv, mix, out0, in0, in0_end = backs
    feed_back_start(flow, b.low, b.grads, 1)
    feed_back_inner(b.normed1, b.slope1, b.low, raws, b.weights, None, b.inner_grads, 1, still)
    feed_back_outer(b.active1, b.low, b.weights, OUT1, still)
    out1[0]()
    product_back(b.slope1, b.normed1, b.total, b.weights, IN1, 4, still)
    in1[0]()
    out1[1]()
    norm_back(b.x3, b.total, flow, flow, b.small, S_FFN + 2, b.grads)
    in1[1]()
    grad_normal = b.x3
    conv_back_rest(flow, b.middle, b.slope_c, grad_normal, b.low, b.hold, b.weights, b.grads, b.back_own)
    back = Total(place, b.back_own, b.back_near, b.back_part, b.back_far, b.back_sums, totals, 2 * planes + chips)
    back.start()
    put_columns(b.weights, CONV, 0, dot_tn(b.active_c[...], b.low[...]))
    back.turn()
    out1[2]()
    back.finish()
    conv_back_front(
        b.sigma, b.tilt, b.gated, b.middle, grad_normal, b.front_sums, b.back_sums, b.padded, b.active1, b.hold, b.taps, b.small,
        b.bounds, b.grads, b.gate_grads, frames, at_points({(4, 0): (in1[2],), (14, 0): (out1[3],)}),
    )
    product_back(b.active1, b.normed_c, b.total, b.weights, GLU, 2, still)
    norm_back(b.x2, b.total, flow, flow, b.small, S_CONV, b.grads)
    attention_back_start(flow, b.joined, b.recips, b.low, b.normed1, b.hold, b.weights, b.grads)
    conv[0]()
    attention_backward(
        b.mixed, b.probs, b.normed1, b.joined, b.active1, b.slope1, b.hold, b.x3, b.total, b.diagonals, b.lines, b.choice,
        b.table_grad, at_points({(0, 1): (in1[3],), (1, 0): (conv[1],), (3, 0): (out1[4],)}),
    )
    product_back(b.active1, b.normed_a, b.total, b.weights, QKV, 3, still)
    mix[0]()
    conv[2]()
    norm_back(b.x1, b.total, flow, flow, b.small, S_ATTN, b.grads)
    mix[1]()
    in1[4]()
    reduces.sent()
    norm_rows(x0, b.normed_c, b.small, S_FFN)
    feed_back_start(flow, b.low, b.grads, 0)
    feed_back_outer(b.active0, b.low, b.weights, OUT1, still)
    out0[0]()
    feed_back_inner(
        b.normed_c, b.slope0, b.low, raws, b.weights, IN1, b.inner_grads, 0,
        at_points({(1, 0): (in0[0], out0[1])}),
    )
    in0_end[0]()
    in0[1]()
    product_back(b.slope0, None, b.total, b.weights, IN0, 4, still)
    norm_back(x0, b.total, flow, b.grad_x.at[0], b.small, S_FFN, b.grads)
    pack_small_grads(b, place)
    thin = Thin(place, b.edges, b.edge_near, b.edge_part, b.edge_far, b.thin, totals, 2 * (2 * planes + chips))
    thin.start()
    for step in (
        conv[3], mix[2], in0_end[1], thin.turn, out0[2], conv[4], mix[3], in0[2], in0_end[2], thin.finish, out0[3], mix[4], in0[3],
        in0_end[3], out0[4], in0[4], in0_end[4],
    ):
        step()
    reduces.sent()
    totals.sent()


def finish_kernel(*refs):
    (
        output_in, grad_x_in, shard, thin, output, grad_x, grad_ffn_norm, grad_ffn_in, grad_ffn_in_bias, grad_ffn_out,
        grad_ffn_out_bias, grad_attn_norm, grad_qkv, grad_attn_out, grad_attn_out_bias, grad_rel, grad_conv_norm, grad_glu,
        grad_glu_bias, grad_depth, grad_batch, grad_conv_out, grad_conv_out_bias, grad_final, taps, semaphores,
    ) = refs
    copies = [
        pltpu.make_async_copy(output_in, output, semaphores.at[0]), pltpu.make_async_copy(grad_x_in, grad_x, semaphores.at[1])
    ]
    for copy in copies:
        copy.start()
    cut = lambda begin, size: shard[begin - IN0 : begin - IN0 + size, :]
    width = grad_final.shape[-1]

    def thin_rows(begin, count):
        rows = []
        for p in range(begin, begin + count):
            rows.append(thin[p % 6 : p % 6 + 1, 16 * (p // 6) : 16 * (p // 6) + width])
        return rows

    for layer in range(2):
        for c in range(FF // D):
            grad_ffn_in[layer, :, D * c : D * c + D] = cut((IN0, IN1)[layer] + 16 * c, 16)
        grad_ffn_out[layer] = cut((OUT0, OUT1)[layer], 64)
        grad_ffn_in_bias[layer : layer + 1, :] = thin[6:7, 64 * layer : 64 * layer + 4 * width]
        for r, row in enumerate(thin_rows(S_FFN + 2 * layer, 2)):
            grad_ffn_norm[layer, r : r + 1, :] = row
    for c in range(3):
        grad_qkv[:, D * c : D * c + D] = cut(QKV + 16 * c, 16)
    grad_attn_out[...] = cut(ATT, 16)
    for c in range(2):
        grad_glu[:, D * c : D * c + D] = cut(GLU + 16 * c, 16)
    grad_conv_out[...] = cut(CONV, 16)
    for ref, begin in (
        (grad_ffn_out_bias, S_FOB), (grad_attn_norm, S_ATTN), (grad_conv_norm, S_CONV), (grad_batch, S_BATCH),
        (grad_final, S_FINAL),
    ):
        for r, row in enumerate(thin_rows(begin, ref.shape[0])):
            ref[r : r + 1, :] = row
    for r, row in enumerate(thin_rows(S_TAPS, TAPS)):
        taps[r : r + 1, 0:width] = row
    grad_depth[...] = taps[...].T[0:width, 0:TAPS]
    grad_attn_out_bias[...] = thin_rows(S_AOB, 1)[0][0]
    grad_conv_out_bias[...] = thin_rows(S_COB, 1)[0][0]
    grad_glu_bias[...] = thin[7:8, 0 : 2 * width][0]
    grad_rel[...] = thin[7:8, 64 : 64 + grad_rel.shape[0]][0]
    for copy in copies:
        copy.wait()


def shape(dims, kind=F32):
    return jax.ShapeDtypeStruct(dims, kind)


def local(*args):
    planes, chips = lax.axis_size("dp"), lax.axis_size("fsdp") // 2
    scratch = scratch_of(planes, chips)
    names = INPUTS + OUTPUTS + tuple(scratch)
    vmem, anywhere = pl.BlockSpec(memory_space=pltpu.VMEM), pl.BlockSpec(memory_space=pl.ANY)
    given = dict(zip(INPUTS, args))
    given["depth_kernel"] = given["depth_kernel"].T
    firsts = [shape((1, L, D), BF16), shape((1, L, D))]
    passed = pl.pallas_call(
        lambda *refs: whole_kernel(names, *refs),
        out_shape=firsts + [shape((GRADS, D)), shape((8, 128))],
        in_specs=[vmem] * len(args),
        out_specs=[vmem] * 4,
        scratch_shapes=list(scratch.values()),
        compiler_params=pltpu.CompilerParams(collective_id=0, has_side_effects=True, vmem_limit_bytes=VMEM_BYTES),
        name="layer",
    )(*given.values())
    outs = [
        shape(given[name].shape)
        for name in (
            "ffn_norm", "ffn_in", "ffn_in_bias", "ffn_out", "ffn_out_bias", "attn_norm", "qkv_weight", "attn_out",
            "attn_out_bias", "rel_table", "conv_norm", "glu_weight", "glu_bias", "depth_kernel", "batch_norm", "conv_out",
            "conv_out_bias", "final_norm",
        )
    ]
    grads = pl.pallas_call(
        finish_kernel,
        out_shape=firsts + outs,
        in_specs=[anywhere, anywhere, vmem, vmem],
        out_specs=[vmem] * (2 + len(outs)),
        scratch_shapes=[pltpu.VMEM((128, 128), F32), pltpu.SemaphoreType.DMA((2,))],
        name="unpack",
    )(*passed)
    grads = list(grads)
    grads[15] = grads[15].T
    return tuple(grads)


VMEM_BYTES = 127 * 512 * 1024


highest = lax.Precision.HIGHEST


def layer_norm(values, params):
    center = values - jnp.mean(values, axis=-1, keepdims=True)
    spread = jnp.mean(center * center, axis=-1, keepdims=True)
    return center * lax.rsqrt(spread + epsilon) * (1.0 + params[0]) + params[1]


def silu_slope(values):
    sigma = jax.nn.sigmoid(values)
    return sigma * (1.0 + values * (1.0 - sigma))


def product(left, right):
    return jnp.dot(left, right, preferred_element_type=jnp.float32)


def product_left(left, right):
    return lax.dot_general(
        left, right, (((0,), (0,)), ((), ())), preferred_element_type=jnp.float32
    )


def product_right(left, right):
    return lax.dot_general(
        left, right, (((1,), (1,)), ((), ())), preferred_element_type=jnp.float32
    )


def plain_fetch_feed(norms, inner_weight, inner_bias, outer_weight, outer_bias, layer):
    return (
        lax.all_gather(norms[layer], ("dp", "fsdp"), axis=1, tiled=True),
        lax.all_gather(inner_weight[layer], ("dp", "fsdp"), axis=0, tiled=True),
        lax.all_gather(inner_bias[layer], ("dp", "fsdp"), axis=0, tiled=True),
        lax.all_gather(outer_weight[layer], ("dp", "fsdp"), axis=0, tiled=True),
        lax.all_gather(outer_bias[layer], ("dp", "fsdp"), axis=0, tiled=True),
    )


def plain_reduce_feed(grads):
    return (
        lax.psum_scatter(grads[0], ("dp", "fsdp"), scatter_dimension=1, tiled=True),
        lax.psum_scatter(grads[1], ("dp", "fsdp"), scatter_dimension=0, tiled=True),
        lax.psum_scatter(grads[2], ("dp", "fsdp"), scatter_dimension=0, tiled=True),
        lax.psum_scatter(grads[3], ("dp", "fsdp"), scatter_dimension=0, tiled=True),
        lax.psum_scatter(grads[4], ("dp", "fsdp"), scatter_dimension=0, tiled=True),
    )


def fetch_attention(attn_norm, qkv_weight, attn_out, attn_out_bias, rel_table):
    return (
        lax.all_gather(attn_norm, ("dp", "fsdp"), axis=1, tiled=True),
        lax.all_gather(qkv_weight, ("dp", "fsdp"), axis=0, tiled=True),
        lax.all_gather(attn_out, ("dp", "fsdp"), axis=0, tiled=True),
        lax.all_gather(attn_out_bias, ("dp", "fsdp"), axis=0, tiled=True),
        lax.all_gather(rel_table, ("dp", "fsdp"), axis=0, tiled=True),
    )


def fetch_conv(
    conv_norm, glu_weight, glu_bias, depth_kernel, batch_norm, conv_out, conv_out_bias, final_norm
):
    return (
        lax.all_gather(conv_norm, ("dp", "fsdp"), axis=1, tiled=True),
        lax.all_gather(glu_weight, ("dp", "fsdp"), axis=0, tiled=True),
        lax.all_gather(glu_bias, ("dp", "fsdp"), axis=0, tiled=True),
        lax.all_gather(depth_kernel, ("dp", "fsdp"), axis=1, tiled=True),
        lax.all_gather(batch_norm, ("dp", "fsdp"), axis=1, tiled=True),
        lax.all_gather(conv_out, ("dp", "fsdp"), axis=0, tiled=True),
        lax.all_gather(conv_out_bias, ("dp", "fsdp"), axis=0, tiled=True),
        lax.all_gather(final_norm, ("dp", "fsdp"), axis=1, tiled=True),
    )


def plain_feed_forward(values, weights):
    norm, weight_in, bias_in, weight_out, bias_out = weights
    normed, norm_back = jax.vjp(layer_norm, values, norm.astype(jnp.float32))
    normed_low = normed.astype(jnp.bfloat16)
    inner = product(normed_low, weight_in) + bias_in.astype(jnp.float32)
    active = jax.nn.silu(inner).astype(jnp.bfloat16)
    result = values + 0.5 * (product(active, weight_out) + bias_out.astype(jnp.float32))
    return (result, (normed_low, inner, active, norm_back))


def plain_feed_backward(upstream, weights, saved):
    norm, weight_in, bias_in, weight_out, bias_out = weights
    normed_low, inner, active, norm_back = saved
    branch = 0.5 * upstream
    branch_low = branch.astype(jnp.bfloat16)
    grad_weight_out = product_left(active, branch_low)
    grad_inner = product_right(branch_low, weight_out) * silu_slope(inner)
    inner_low = grad_inner.astype(jnp.bfloat16)
    grad_weight_in = product_left(normed_low, inner_low)
    grad_values, grad_norm = norm_back(product_right(inner_low, weight_in))
    return (
        upstream + grad_values,
        (
            grad_norm,
            grad_weight_in,
            jnp.sum(grad_inner, axis=0),
            grad_weight_out,
            jnp.sum(branch, axis=0),
        ),
    )


def relative_lines(table, buckets):
    choose = (buckets[None, :] == jnp.arange(BUCKETS, dtype=jnp.int32)[:, None]).astype(jnp.float32)
    lines = jnp.dot(table.astype(jnp.float32).reshape(HEADS, BUCKETS), choose, precision=highest)
    return (lines, choose)


def bias_square(line, length):
    tiled = jnp.broadcast_to(line, (length, 2 * length - 1)).reshape(-1)
    tiled = jnp.concatenate([tiled, jnp.zeros((length,), line.dtype)])
    return tiled.reshape(length, 2 * length)[:, :length][::-1]


def diagonal_sums(square):
    length = square.shape[0]
    padded = jnp.concatenate([square[::-1], jnp.zeros_like(square)], axis=1).reshape(-1)
    return jnp.sum(padded[: length * (2 * length - 1)].reshape(length, 2 * length - 1), axis=0)


def head_scores(query, keys_head, line, same):
    raw = product_right(query, keys_head)
    return jnp.where(same, raw * HEAD_DIM ** (-0.5) + bias_square(line, query.shape[0]), -1e30)


def plain_attention_forward(values, weights, marks, buckets):
    norm, mixer, weight_out, bias_out, table = weights
    length = values.shape[0]
    normed, norm_back = jax.vjp(layer_norm, values, norm.astype(jnp.float32))
    normed_low = normed.astype(jnp.bfloat16)
    mixed = (
        product(normed_low, mixer)
        .astype(jnp.bfloat16)
        .reshape(length, 3, HEADS, HEAD_DIM)
        .transpose(1, 2, 0, 3)
    )
    lines, choose = relative_lines(table, buckets)
    same = marks[:, None] == marks[None, :]

    def head_forward(items):
        query, keys_head, contents, line = items
        scores = head_scores(query, keys_head, line, same)
        peak = jnp.max(scores, axis=1, keepdims=True)
        raised = jnp.exp(scores - peak)
        total = jnp.sum(raised, axis=1, keepdims=True)
        probs = (raised / total).astype(jnp.bfloat16)
        return (product(probs, contents).astype(jnp.bfloat16), (peak + jnp.log(total))[:, 0])

    attended, logsum = lax.map(head_forward, (mixed[0], mixed[1], mixed[2], lines))
    joined = attended.transpose(1, 0, 2).reshape(length, D)
    result = values + product(joined, weight_out) + bias_out.astype(jnp.float32)
    return (result, (normed_low, mixed, lines, choose, same, joined, logsum, norm_back))


def plain_attention_backward(upstream, weights, saved):
    norm, mixer, weight_out, bias_out, table = weights
    normed_low, mixed, lines, choose, same, joined, logsum, norm_back = saved
    length = upstream.shape[0]
    upstream_low = upstream.astype(jnp.bfloat16)
    grad_weight_out = product_left(joined, upstream_low)
    grad_joined = (
        product_right(upstream_low, weight_out)
        .astype(jnp.bfloat16)
        .reshape(length, HEADS, HEAD_DIM)
        .transpose(1, 0, 2)
    )

    def head_backward(items):
        query, keys_head, contents, line, incoming, logs = items
        scores = head_scores(query, keys_head, line, same)
        probs = jnp.exp(scores - logs[:, None])
        grad_contents = product_left(probs.astype(jnp.bfloat16), incoming)
        grad_probs = product_right(incoming, contents)
        grad_scores = probs * (grad_probs - jnp.sum(grad_probs * probs, axis=1, keepdims=True))
        scaled = (grad_scores * HEAD_DIM ** (-0.5)).astype(jnp.bfloat16)
        grad_query = product(scaled, keys_head)
        grad_keys = product_left(scaled, query)
        return (
            jnp.stack([grad_query, grad_keys, grad_contents]).astype(jnp.bfloat16),
            diagonal_sums(grad_scores),
        )

    grad_mixed, grad_lines = lax.map(
        head_backward, (mixed[0], mixed[1], mixed[2], lines, grad_joined, logsum)
    )
    grad_flat = grad_mixed.transpose(2, 1, 0, 3).reshape(length, 3 * D)
    grad_mixer = product_left(normed_low, grad_flat)
    grad_values, grad_norm = norm_back(product_right(grad_flat, mixer))
    grad_table = jnp.dot(grad_lines, choose.T, precision=highest).reshape(-1)
    return (
        upstream + grad_values,
        (grad_norm, grad_mixer, grad_weight_out, jnp.sum(upstream, axis=0), grad_table),
    )


def gate_unit(joined):
    width = joined.shape[1] // 2
    return joined[:, :width] * jax.nn.sigmoid(joined[:, width:])


def plain_depthwise(gated, kernel, marks):
    length = gated.shape[0]
    half = kernel.shape[0] // 2
    padded = jnp.pad(gated, ((half, half), (0, 0)))
    bounds = jnp.pad(marks, (half, half), constant_values=-1)
    total = jnp.zeros(gated.shape, gated.dtype)
    for step in range(kernel.shape[0]):
        same = (bounds[step : step + length] == marks)[:, None]
        total = total + jnp.where(same, padded[step : step + length], 0.0) * kernel[step]
    return total


def plain_conv_forward(values, weights, marks, frames):
    norm, weight_glu, bias_glu, kernel, batch, weight_out, bias_out, final = weights
    normed, norm_back = jax.vjp(layer_norm, values, norm.astype(jnp.float32))
    normed_low = normed.astype(jnp.bfloat16)
    joined = product(normed_low, weight_glu) + bias_glu.astype(jnp.float32)
    gated, gate_back = jax.vjp(gate_unit, joined)
    middle, depth_back = jax.vjp(
        lambda inner, taps: plain_depthwise(inner, taps, marks), gated, kernel.astype(jnp.float32)
    )
    sums = lax.psum((jnp.sum(middle, axis=0), jnp.sum(middle * middle, axis=0)), ("dp", "fsdp"))
    center = sums[0] / frames
    inverse = lax.rsqrt(sums[1] / frames - center * center + epsilon)
    gain = 1.0 + batch[0].astype(jnp.float32)
    unit = (middle - center) * inverse
    normal = unit * gain + batch[1].astype(jnp.float32)
    active = jax.nn.silu(normal).astype(jnp.bfloat16)
    result = values + product(active, weight_out) + bias_out.astype(jnp.float32)
    return (
        result,
        (normed_low, gate_back, depth_back, inverse, gain, unit, normal, active, norm_back),
    )


def plain_conv_backward(upstream, weights, saved, frames):
    norm, weight_glu, bias_glu, kernel, batch, weight_out, bias_out, final = weights
    normed_low, gate_back, depth_back, inverse, gain, unit, normal, active, norm_back = saved
    upstream_low = upstream.astype(jnp.bfloat16)
    grad_weight_out = product_left(active, upstream_low)
    grad_normal = product_right(upstream_low, weight_out) * silu_slope(normal)
    sums = lax.psum(
        (jnp.sum(grad_normal, axis=0), jnp.sum(grad_normal * unit, axis=0)), ("dp", "fsdp")
    )
    grad_middle = inverse * (
        grad_normal * gain - gain * sums[0] / frames - unit * (gain * sums[1] / frames)
    )
    grad_gated, grad_kernel = depth_back(grad_middle)
    grad_joined = gate_back(grad_gated)[0]
    joined_low = grad_joined.astype(jnp.bfloat16)
    grad_weight_glu = product_left(normed_low, joined_low)
    grad_values, grad_norm = norm_back(product_right(joined_low, weight_glu))
    grad_batch = jnp.stack([sums[1], sums[0]])
    return (
        upstream + grad_values,
        (
            grad_norm,
            grad_weight_glu,
            jnp.sum(grad_joined, axis=0),
            grad_kernel,
            grad_weight_out,
            jnp.sum(upstream, axis=0),
        ),
        grad_batch,
    )


def plain(
    inputs,
    segments,
    buckets,
    cotangent,
    ffn_norm,
    ffn_in,
    ffn_in_bias,
    ffn_out,
    ffn_out_bias,
    attn_norm,
    qkv_weight,
    attn_out,
    attn_out_bias,
    rel_table,
    conv_norm,
    glu_weight,
    glu_bias,
    depth_kernel,
    batch_norm,
    conv_out,
    conv_out_bias,
    final_norm,
):
    values = inputs[0].astype(jnp.float32)
    marks = segments[0]
    devices = lax.axis_size(("dp", "fsdp"))
    frames = values.shape[0] * devices
    feed_first = plain_fetch_feed(ffn_norm, ffn_in, ffn_in_bias, ffn_out, ffn_out_bias, 0)
    first, first_saved = plain_feed_forward(values, feed_first)
    attn_weights = fetch_attention(attn_norm, qkv_weight, attn_out, attn_out_bias, rel_table)
    second, attn_saved = plain_attention_forward(first, attn_weights, marks, buckets)
    conv_weights = fetch_conv(
        conv_norm,
        glu_weight,
        glu_bias,
        depth_kernel,
        batch_norm,
        conv_out,
        conv_out_bias,
        final_norm,
    )
    third, conv_saved = plain_conv_forward(second, conv_weights, marks, frames)
    feed_second = plain_fetch_feed(ffn_norm, ffn_in, ffn_in_bias, ffn_out, ffn_out_bias, 1)
    fourth, second_saved = plain_feed_forward(third, feed_second)
    result, final_back = jax.vjp(layer_norm, fourth, conv_weights[7].astype(jnp.float32))
    grad_fourth, grad_final = final_back(cotangent[0].astype(jnp.float32))
    second_back = plain_fetch_feed(ffn_norm, ffn_in, ffn_in_bias, ffn_out, ffn_out_bias, 1)
    grad_third, second_grads = plain_feed_backward(grad_fourth, second_back, second_saved)
    conv_back = fetch_conv(
        conv_norm,
        glu_weight,
        glu_bias,
        depth_kernel,
        batch_norm,
        conv_out,
        conv_out_bias,
        final_norm,
    )
    grad_second, conv_grads, grad_batch = plain_conv_backward(grad_third, conv_back, conv_saved, frames)
    attn_back = fetch_attention(attn_norm, qkv_weight, attn_out, attn_out_bias, rel_table)
    grad_first, attn_grads = plain_attention_backward(grad_second, attn_back, attn_saved)
    first_back = plain_fetch_feed(ffn_norm, ffn_in, ffn_in_bias, ffn_out, ffn_out_bias, 0)
    grad_start, first_grads = plain_feed_backward(grad_first, first_back, first_saved)
    first_shards = plain_reduce_feed(first_grads)
    second_shards = plain_reduce_feed(second_grads)
    attn_shards = (
        lax.psum_scatter(attn_grads[0], ("dp", "fsdp"), scatter_dimension=1, tiled=True),
        lax.psum_scatter(attn_grads[1], ("dp", "fsdp"), scatter_dimension=0, tiled=True),
        lax.psum_scatter(attn_grads[2], ("dp", "fsdp"), scatter_dimension=0, tiled=True),
        lax.psum_scatter(attn_grads[3], ("dp", "fsdp"), scatter_dimension=0, tiled=True),
        lax.psum_scatter(attn_grads[4], ("dp", "fsdp"), scatter_dimension=0, tiled=True),
    )
    conv_shards = (
        lax.psum_scatter(conv_grads[0], ("dp", "fsdp"), scatter_dimension=1, tiled=True),
        lax.psum_scatter(conv_grads[1], ("dp", "fsdp"), scatter_dimension=0, tiled=True),
        lax.psum_scatter(conv_grads[2], ("dp", "fsdp"), scatter_dimension=0, tiled=True),
        lax.psum_scatter(conv_grads[3], ("dp", "fsdp"), scatter_dimension=1, tiled=True),
        lax.psum_scatter(conv_grads[4], ("dp", "fsdp"), scatter_dimension=0, tiled=True),
        lax.psum_scatter(conv_grads[5], ("dp", "fsdp"), scatter_dimension=0, tiled=True),
        lax.psum_scatter(grad_final, ("dp", "fsdp"), scatter_dimension=1, tiled=True),
    )
    width = D // devices
    batch_shard = lax.dynamic_slice_in_dim(
        grad_batch, lax.axis_index(("dp", "fsdp")) * width, width, 1
    )
    return (
        result[None].astype(jnp.bfloat16),
        grad_start[None],
        jnp.stack([first_shards[0], second_shards[0]]),
        jnp.stack([first_shards[1], second_shards[1]]),
        jnp.stack([first_shards[2], second_shards[2]]),
        jnp.stack([first_shards[3], second_shards[3]]),
        jnp.stack([first_shards[4], second_shards[4]]),
        attn_shards[0],
        attn_shards[1],
        attn_shards[2],
        attn_shards[3],
        attn_shards[4],
        conv_shards[0],
        conv_shards[1],
        conv_shards[2],
        conv_shards[3],
        batch_shard,
        conv_shards[4],
        conv_shards[5],
        conv_shards[6],
    )


def solution(mesh):
    in_specs = (
        P(("dp", "fsdp"), None, None),
        P(("dp", "fsdp"), None),
        P(),
        P(("dp", "fsdp"), None, None),
        P(None, None, ("dp", "fsdp")),
        P(None, ("dp", "fsdp"), None),
        P(None, ("dp", "fsdp")),
        P(None, ("dp", "fsdp"), None),
        P(None, ("dp", "fsdp")),
        P(None, ("dp", "fsdp")),
        P(("dp", "fsdp"), None),
        P(("dp", "fsdp"), None),
        P(("dp", "fsdp")),
        P(("dp", "fsdp")),
        P(None, ("dp", "fsdp")),
        P(("dp", "fsdp"), None),
        P(("dp", "fsdp")),
        P(None, ("dp", "fsdp")),
        P(None, ("dp", "fsdp")),
        P(("dp", "fsdp"), None),
        P(("dp", "fsdp")),
        P(None, ("dp", "fsdp")),
    )
    out_specs = (
        P(("dp", "fsdp"), None, None),
        P(("dp", "fsdp"), None, None),
        P(None, None, ("dp", "fsdp")),
        P(None, ("dp", "fsdp"), None),
        P(None, ("dp", "fsdp")),
        P(None, ("dp", "fsdp"), None),
        P(None, ("dp", "fsdp")),
        P(None, ("dp", "fsdp")),
        P(("dp", "fsdp"), None),
        P(("dp", "fsdp"), None),
        P(("dp", "fsdp")),
        P(("dp", "fsdp")),
        P(None, ("dp", "fsdp")),
        P(("dp", "fsdp"), None),
        P(("dp", "fsdp")),
        P(None, ("dp", "fsdp")),
        P(None, ("dp", "fsdp")),
        P(("dp", "fsdp"), None),
        P(("dp", "fsdp")),
        P(None, ("dp", "fsdp")),
    )
    fast = mesh.shape["dp"] == 4 and mesh.shape["fsdp"] == 8
    return jax.shard_map(local if fast else plain, mesh=mesh, in_specs=in_specs, out_specs=out_specs, check_vma=False)
```

```python
import jax
import jax.numpy as jnp
from jax import lax
from jax.experimental import pallas as pl
from jax.experimental.pallas import tpu as pltpu
from jax.sharding import PartitionSpec as P

D = 512
FF = 2048
HEADS = 8
HEAD_DIM = 64
BUCKETS = 32
L = 512
TAPS = 32
PAD = 16
epsilon = 1e-05
F32, BF16 = jnp.float32, jnp.bfloat16
MESH = pl.DeviceIdType.MESH

SMALL, IN0, OUT0, QKV, ATT, GLU, CONV, IN1, OUT1, ROWS = 0, 16, 80, 144, 192, 208, 240, 256, 320, 384
GRADS = ROWS - IN0
(S_FFN, S_FOB, S_ATTN, S_AOB, S_CONV, S_BATCH, S_COB, S_FINAL, S_TAPS, S_ROWS) = (0, 4, 6, 8, 9, 11, 13, 14, 16, 48)
CHUNK = 64
BLOCK = 128
SOFT = 32
UNROLL = True


def dot(a, b):
    return jnp.dot(a, b, preferred_element_type=F32)


def dot_nt(a, b):
    return lax.dot_general(a, b, (((1,), (1,)), ((), ())), preferred_element_type=F32)


def dot_tn(a, b):
    return lax.dot_general(a, b, (((0,), (0,)), ((), ())), preferred_element_type=F32)


def chunks(body, carry=None, size=CHUNK):
    def step(i, carry):
        return body(pl.ds(pl.multiple_of(i * size, size), size), carry)

    return lax.fori_loop(0, L // size, step, carry, unroll=True)


def fold(values):
    return jnp.sum(values.reshape(values.shape[0] // 8, 8, values.shape[1]), axis=0)


def zeros8(width=D):
    return jnp.zeros((8, width), F32)


def total_row(values):
    return jnp.sum(values, axis=0, keepdims=True)


class Bag:
    pass


class Place:
    def __init__(self):
        self.planes = lax.axis_size("dp")
        self.chips = lax.axis_size("fsdp") // 2
        self.plane, inner = lax.axis_index("dp"), lax.axis_index("fsdp")
        self.z, self.core = inner // 2, inner % 2
        y, x = self.plane // 2, self.plane % 2
        self.plane_x, self.plane_y, self.plane_d = y * 2 + 1 - x, (1 - y) * 2 + x, (1 - y) * 2 + 1 - x
        self.twin = (self.plane, 2 * self.z + 1 - self.core)
        self.over_x = (self.plane_x, inner)
        self.over_y = (self.plane_y, inner)
        self.chip = [lax.rem(self.z + step, self.chips) for step in range(self.chips)]
        self.along = [(self.plane, 2 * chip + self.core) for chip in self.chip]
        self.rank = self.plane * 2 + self.core
        self.members = []
        for step in range(self.planes):
            for flip in range(2):
                if step or flip:
                    plane, core = lax.rem(self.plane + step, self.planes), lax.rem(self.core + flip, 2)
                    self.members.append(((plane, 2 * self.z + core), plane * 2 + core))


class Copies:
    def __init__(self, sends, receives, place):
        self.sends, self.receives, self.place = sends, receives, place
        self.begun = []

    def start(self, number, make, receive=None):
        def copy():
            source, target, device = make()
            return pltpu.make_async_remote_copy(
                source, target, self.sends.at[number], self.receives.at[number if receive is None else receive],
                device_id=device, device_id_type=MESH,
            )

        copy().start()
        self.begun.append(copy)

    def arrived(self, number, target):
        pltpu.make_async_remote_copy(
            target, target, self.sends.at[number], self.receives.at[number],
            device_id=self.place.twin, device_id_type=MESH,
        ).wait_recv()

    def sent(self):
        for copy in self.begun:
            copy().wait_send()
        self.begun = []


class Gather:
    def __init__(self, place, weights, copies, first, begin, size, split):
        self.place, self.weights, self.copies, self.first = place, weights, copies, first
        self.rows = pl.ds(begin, size)
        self.parts = (pl.ds(begin, split), pl.ds(begin + split, size - split))
        chips = place.chips
        self.x, self.y, self.d, self.t = chips, 2 * chips, 3 * chips, 3 * chips + 2

    @staticmethod
    def semaphores(chips):
        return 3 * chips + 6

    def column(self, plane, side, which):
        return self.weights.at[plane, :, side, which]

    def slot(self, plane, step):
        p = self.place
        return self.weights.at[plane, p.chip[(p.chips - step) % p.chips], p.core, self.rows]

    def move(self, number, ref, device):
        self.copies.start(self.first + number, lambda: (ref(), ref(), device))

    def arrived(self, number, ref):
        self.copies.arrived(self.first + number, ref)

    def along_z(self):
        p = self.place
        for d in range(1, p.chips):
            self.move(d, lambda: self.slot(p.plane, 0), p.along[d])

    def beside(self, step):
        p = self.place
        self.move(self.x + step, lambda: self.slot(p.plane, step), p.over_x)
        self.move(self.y + step, lambda: self.slot(p.plane, step), p.over_y)

    def own(self):
        self.beside(0)

    def forward(self):
        p = self.place
        for d in range(1, p.chips):
            self.arrived(d, self.slot(p.plane, d))
            self.beside(d)
        self.move(self.t, lambda: self.column(p.plane, p.core, self.rows), p.twin)

    def turn(self):
        p = self.place
        for d in range(p.chips):
            self.arrived(self.x + d, self.slot(p.plane_x, d))
        self.move(self.d, lambda: self.column(p.plane_x, p.core, self.parts[0]), p.over_y)
        for d in range(p.chips):
            self.arrived(self.y + d, self.slot(p.plane_y, d))
        self.move(self.d + 1, lambda: self.column(p.plane_y, p.core, self.parts[1]), p.over_x)
        self.move(self.t + 1, lambda: self.column(p.plane_x, p.core, self.rows), p.twin)
        self.move(self.t + 2, lambda: self.column(p.plane_y, p.core, self.rows), p.twin)

    def across(self):
        p = self.place
        self.arrived(self.d, self.column(p.plane_d, p.core, self.parts[0]))
        self.arrived(self.d + 1, self.column(p.plane_d, p.core, self.parts[1]))
        self.move(self.t + 3, lambda: self.column(p.plane_d, p.core, self.rows), p.twin)

    def done(self):
        p = self.place
        for number, plane in enumerate((p.plane, p.plane_x, p.plane_y, p.plane_d)):
            self.arrived(self.t + number, self.column(plane, 1 - p.core, self.rows))


def reduce_steps(place, data, twin, diagonal, from_x, from_y, from_z, copies, first, begin, size, split, landing, finish):
    p, core, chips = place, place.core, place.chips
    rows, lands = pl.ds(begin, size), pl.ds(landing, size)
    parts = (pl.ds(begin, split), pl.ds(begin + split, size - split))
    parts_land = (pl.ds(landing, split), pl.ds(landing + split, size - split))

    def column(plane, side, which):
        return data.at[plane, :, side, which]

    def add(plane, which, *sources):
        def step(zz, carry):
            value = data[plane, zz, core, which, :]
            for ref in sources:
                value = value + ref(zz)
            data[plane, zz, core, which, :] = value
            return carry

        lax.fori_loop(0, chips, step, 0)

    def read(ref, which, *lead):
        return lambda zz: ref[lead + (zz, which, slice(None))]

    def to_twin():
        for number, plane in enumerate((p.plane_d, p.plane_y, p.plane_x, p.plane)):
            copies.start(
                first + number, lambda plane=plane: (column(plane, 1 - core, rows), twin.at[plane, :, lands], p.twin)
            )

    def across():
        copies.arrived(first, twin.at[p.plane_d, :, lands])
        add(p.plane_d, rows, read(twin, lands, p.plane_d))
        copies.start(first + 4, lambda: (column(p.plane_d, core, parts[0]), diagonal.at[:, parts_land[0]], p.over_y))
        if split < size:
            copies.start(first + 5, lambda: (column(p.plane_d, core, parts[1]), diagonal.at[:, parts_land[1]], p.over_x))

    def beside():
        copies.arrived(first + 2, twin.at[p.plane_x, :, lands])
        copies.arrived(first + 4, diagonal.at[:, parts_land[0]])
        add(p.plane_x, rows, read(twin, lands, p.plane_x))
        add(p.plane_x, parts[0], read(diagonal, parts_land[0]))
        copies.start(first + 7, lambda: (column(p.plane_x, core, rows), from_x.at[:, lands], p.over_x))
        copies.arrived(first + 1, twin.at[p.plane_y, :, lands])
        add(p.plane_y, rows, read(twin, lands, p.plane_y))
        if split < size:
            copies.arrived(first + 5, diagonal.at[:, parts_land[1]])
            add(p.plane_y, parts[1], read(diagonal, parts_land[1]))
        copies.start(first + 6, lambda: (column(p.plane_y, core, rows), from_y.at[:, lands], p.over_y))

    def own_column():
        copies.arrived(first + 3, twin.at[p.plane, :, lands])
        copies.arrived(first + 6, from_y.at[:, lands])
        copies.arrived(first + 7, from_x.at[:, lands])
        add(p.plane, rows, read(twin, lands, p.plane), read(from_x, lands), read(from_y, lands))
        for d in range(1, chips):
            copies.start(
                first + 7 + d,
                lambda d=d: (data.at[p.plane, p.chip[d], core, rows], from_z.at[d - 1, lands], p.along[d]),
            )

    def along_z():
        for d in range(1, chips):
            copies.arrived(first + 7 + d, from_z.at[d - 1, lands])
        value = data[p.plane, p.z, core, rows, :].astype(F32)
        for d in range(1, chips):
            value = value + from_z[d - 1, lands, :].astype(F32)
        finish(value)

    return [to_twin, across, beside, own_column, along_z]


class Thin:
    def __init__(self, place, tiles, near, part, far, result, copies, first):
        self.place, self.tiles, self.near, self.part, self.far, self.result = place, tiles, near, part, far, result
        self.copies, self.first = copies, first

    def start(self):
        p = self.place
        for i, (device, rank) in enumerate(p.members):
            self.copies.start(
                self.first + i,
                lambda device=device: (self.tiles.at[device[0], :, lax.rem(device[1], 2)], self.near.at[p.rank], device),
                self.first + p.rank,
            )
        self.near[p.rank] = self.tiles[p.plane, :, p.core]

    def turn(self):
        p = self.place
        for device, rank in p.members:
            self.copies.arrived(self.first + rank, self.near.at[rank])
        value = self.near[0]
        for i in range(1, 2 * p.planes):
            value = value + self.near[i]
        self.part[...] = value
        base = self.first + 2 * p.planes
        for d in range(1, p.chips):
            self.copies.start(base + d, lambda d=d: (self.part.at[p.chip[d]], self.far.at[d], p.along[d]))

    def finish(self):
        p = self.place
        base = self.first + 2 * p.planes
        value = self.part[p.z]
        for d in range(1, p.chips):
            self.copies.arrived(base + d, self.far.at[d])
            value = value + self.far[d]
        self.result[...] = value


class Total:
    def __init__(self, place, own, near, part, far, result, copies, first):
        self.place, self.own, self.near, self.part, self.far, self.result = place, own, near, part, far, result
        self.copies, self.first = copies, first

    def start(self):
        p = self.place
        me = p.rank
        for i, (device, rank) in enumerate(p.members):
            self.copies.start(self.first + i, lambda device=device: (self.own, self.near.at[me], device), self.first + me)
        self.near[me] = self.own[...]

    def turn(self):
        p = self.place
        for device, rank in p.members:
            self.copies.arrived(self.first + rank, self.near.at[rank])
        value = self.near[0]
        for i in range(1, 2 * p.planes):
            value = value + self.near[i]
        self.part[...] = value
        base = self.first + 2 * p.planes
        for d in range(1, p.chips):
            self.copies.start(base + d, lambda d=d: (self.part, self.far.at[d], p.along[d]))

    def finish(self):
        p = self.place
        base = self.first + 2 * p.planes
        value = self.part[...]
        for d in range(1, p.chips):
            self.copies.arrived(base + d, self.far.at[d])
            value = value + self.far[d]
        self.result[...] = value


def at_points(table):
    def pump(index, place=0):
        for (iteration, where), steps in table.items():
            if where != place or (isinstance(index, int) and index != iteration):
                continue

            def act(steps=steps):
                for step in steps:
                    step()

            if isinstance(index, int):
                act()
            else:
                pl.when(index == iteration)(act)

    return pump


def still(index, place=0):
    pass


def standard(values):
    values = values.astype(F32)
    center = values - jnp.mean(values, axis=-1, keepdims=True)
    inverse = lax.rsqrt(jnp.mean(center * center, axis=-1, keepdims=True) + epsilon)
    return center * inverse, inverse


def norm_rows(source, target, small, row):
    gain, shift = 1.0 + small[row : row + 1, :], small[row + 1 : row + 2, :]

    def body(rows, carry):
        target[rows, :] = (standard(source[rows, :])[0] * gain + shift).astype(target.dtype)
        return carry

    chunks(body, 0)


def norm_back(source, grad, upstream, result, small, row, grads):
    gain = 1.0 + small[row : row + 1, :]

    def body(rows, carry):
        unit, inverse = standard(source[rows, :])
        given = grad[rows, :].astype(F32)
        inner = given * gain
        back = inverse * (
            inner
            - jnp.mean(inner, axis=-1, keepdims=True)
            - unit * jnp.mean(inner * unit, axis=-1, keepdims=True)
        )
        result[rows, :] = back if upstream is None else upstream[rows, :] + back
        return carry[0] + fold(given * unit), carry[1] + fold(given)

    first, second = chunks(body, (zeros8(), zeros8()))
    grads[row : row + 1, :] = total_row(first)
    grads[row + 1 : row + 2, :] = total_row(second)


def block_cols(c):
    return pl.ds(c * D if isinstance(c, int) else pl.multiple_of(c * D, D), D)


def columns(weights, start, block):
    return weights[:, :, :, start + 16 * block : start + 16 * block + 16, :].reshape(D, D)


def put_columns(weights, start, block, value):
    rows = pl.ds(start + 16 * block, 16)
    weights[:, :, :, rows, :] = value.astype(BF16).reshape(weights.shape[:3] + (16, D))


def lines_of(weights, start, block):
    return weights[block, :, :, start : start + 64, :].reshape(D, D)


def put_lines(weights, start, block, value):
    weights[block, :, :, start : start + 64, :] = value.astype(BF16).reshape(weights.shape[1:3] + (64, D))


def feed_inner(source, normed, active, slope, raws, weights, small, inner_bias, layer, pump):
    norm_rows(source, normed, small, S_FFN + 2 * layer)
    for c in range(FF // D):
        pump(c)
        cols, raw = block_cols(c), raws[c % 2]
        raw[...] = dot(normed[...], columns(weights, (IN0, IN1)[layer], c))
        bias = inner_bias[layer : layer + 1, cols]

        def body(rows, carry, cols=cols, raw=raw, bias=bias):
            inner = raw[rows, :] + bias
            sigma = jax.nn.sigmoid(inner)
            value = inner * sigma
            active[rows, cols] = value.astype(BF16)
            slope[rows, cols] = (sigma + value * (1.0 - sigma)).astype(BF16)
            return carry

        chunks(body, 0)


def feed_outer(source, active, result, hold, weights, small, layer):
    begin = (OUT0, OUT1)[layer]
    hold[...] = dot(active[...], weights[:, :, :, begin : begin + 64, :].reshape(FF, D))
    bias = small[S_FOB + layer : S_FOB + layer + 1, :]

    def body(rows, carry):
        result[rows, :] = source[rows, :].astype(F32) + 0.5 * (hold[rows, :] + bias)
        return carry

    chunks(body, 0)


def feed_back_start(upstream, low, grads, layer):
    def start(rows, carry):
        half = 0.5 * upstream[rows, :]
        low[rows, :] = half.astype(BF16)
        return carry + fold(half)

    grads[S_FOB + layer : S_FOB + layer + 1, :] = total_row(chunks(start, zeros8()))


def feed_back_outer(active, low, weights, begin, pump):
    for c in range(FF // D):
        put_lines(weights, begin, c, dot_tn(active[:, block_cols(c)], low[...]))
        pump(c)


def feed_back_inner(normed, slope, low, raws, weights, target, inner_grads, layer, pump):
    begin = (OUT0, OUT1)[layer]
    for c in range(FF // D):
        cols, raw = block_cols(c), raws[c % 2]
        raw[...] = dot_nt(low[...], lines_of(weights, begin, c))

        def body(rows, carry, cols=cols, raw=raw):
            grad = raw[rows, :] * slope[rows, cols].astype(F32)
            slope[rows, cols] = grad.astype(BF16)
            return carry + fold(grad)

        inner_grads[layer : layer + 1, cols] = total_row(chunks(body, zeros8()))
        if target is not None:
            put_columns(weights, target, c, dot_tn(normed[...], slope[:, cols]))
        pump(c)


def product_back(grad, normed, total, weights, begin, blocks, pump):
    value = None
    for c in range(blocks):
        part = dot_nt(grad[:, block_cols(c)], columns(weights, begin, c))
        value = part if value is None else value + part
    total[...] = value
    for c in range(blocks):
        if normed is not None:
            put_columns(weights, begin, c, dot_tn(normed[...], grad[:, block_cols(c)]))
        pump(c)


def bucket_choice(buckets):
    return (lax.broadcasted_iota(jnp.int32, (BUCKETS, 2 * L), 0) == buckets[...]).astype(F32)


def attention_mix(source, normed, mixed, weights, small):
    norm_rows(source, normed, small, S_ATTN)

    for c in range(3):
        mixed[:, block_cols(c)] = dot(normed[...], columns(weights, QKV, c)).astype(BF16)


def attention_mask(mask, bounds, marks):
    def body(rows, carry):
        same = bounds[pl.ds(rows.start + PAD, CHUNK), 0:1] == marks[...]
        mask[rows, :] = jnp.where(same, 3e38, -1e30)
        return carry

    chunks(body, 0)


def attention_squares(lines, squares, table, buckets):
    lines[...] = dot(table[...].astype(BF16), bucket_choice(buckets).astype(BF16))

    def head(h, carry):
        line = jnp.broadcast_to(lines[pl.ds(h, 1), :], (BLOCK, 2 * L))
        square = pltpu.roll(line, 2 * L - BLOCK + 1, 1, stride=1, stride_axis=0).astype(BF16)
        for part in range(2):
            squares[lax.rem(h, 4), lax.div(h, 4), part * BLOCK : (part + 1) * BLOCK, :] = square[:, part * L : (part + 1) * L]
        return carry

    lax.fori_loop(0, HEADS, head, 0)


def attention_forward(source, mixed, probs, joined, recips, result, squares, mask, hold, hold2, weights, small, pump):
    lane = lax.broadcasted_iota(jnp.int32, (1, 128), 1)

    def pair(index, carry):
        begin = pl.multiple_of(128 * index, 128)
        query = mixed[:, pl.ds(begin, 128)] * HEAD_DIM ** (-0.5)
        keys = mixed[:, pl.ds(D + begin, 128)]
        contents = mixed[:, pl.ds(2 * D + begin, 128)]
        parts = []
        for half, raw in enumerate((hold, hold2)):
            here = (lane // HEAD_DIM) == half
            raw[...] = dot_nt(jnp.where(here, query, jnp.zeros_like(query)), keys)
        for half, raw in enumerate((hold, hold2)):
            head = 2 * index + half
            here = (lane // HEAD_DIM) == half
            for block in range(L // BLOCK):

                def body(i, carry, block=block, raw=raw, head=head):
                    at = pl.multiple_of(i * SOFT, SOFT)
                    rows = pl.ds(block * BLOCK + at, SOFT)
                    square = squares[lax.rem(head, 4), lax.div(head, 4), pl.ds(at, SOFT), 384 - block * BLOCK : L]
                    if block < L // BLOCK - 1:
                        more = squares[lax.rem(head, 4), lax.div(head, 4), pl.ds(BLOCK + at, SOFT), 0 : 384 - block * BLOCK]
                        square = jnp.concatenate([square, more], axis=1)
                    scores = jnp.minimum(raw[rows, :] + square.astype(F32), mask[rows, :])
                    probs[head, rows, :] = jnp.exp(scores - jnp.max(scores, axis=1, keepdims=True)).astype(BF16)
                    return carry

                lax.fori_loop(0, BLOCK // SOFT, body, 0, unroll=UNROLL)
                if half:
                    pump(index, block)
            parts.append(dot(probs[head], jnp.where(here, contents, jnp.ones_like(contents))))
        value = jnp.where(lane < HEAD_DIM, parts[0], parts[1])
        sums = jnp.where(lane < HEAD_DIM, pltpu.roll(parts[0], HEAD_DIM, 1), pltpu.roll(parts[1], HEAD_DIM, 1))
        recip = 1.0 / sums
        recips[:, pl.ds(begin, 128)] = recip
        joined[:, pl.ds(begin, 128)] = value * recip
        return carry

    lax.fori_loop(0, HEADS // 2, pair, 0)
    hold[...] = dot(joined[...].astype(BF16), columns(weights, ATT, 0))
    bias = small[S_AOB : S_AOB + 1, :]

    def body(rows, carry):
        result[rows, :] = source[rows, :] + hold[rows, :] + bias
        return carry

    chunks(body, 0)


def attention_back_start(upstream, joined, recips, low, spread, hold, weights, grads):
    def start(rows, carry):
        given = upstream[rows, :]
        low[rows, :] = given.astype(BF16)
        return carry + fold(given)

    grads[S_AOB : S_AOB + 1, :] = total_row(chunks(start, zeros8()))
    hold[...] = dot_nt(low[...], columns(weights, ATT, 0))

    def body(rows, carry):
        spread[rows, :] = (hold[rows, :] * recips[rows, :]).astype(BF16)
        return carry

    chunks(body, 0)
    put_columns(weights, ATT, 0, dot_tn(joined[...].astype(BF16), low[...]))


def attention_backward(mixed, probs, spread, joined, grad_mixed, scaled, hold, hold2, means, diagonals, lines, buckets, table_grad, pump):
    lane = lax.broadcasted_iota(jnp.int32, (1, 128), 1)
    sides = lax.broadcasted_iota(jnp.int32, (256, 256), 0) // HEAD_DIM % 2 == lax.broadcasted_iota(jnp.int32, (256, 256), 1) // 128
    sides = jnp.where(sides, 1.0, 0.0).astype(BF16)

    def pair(index, carry):
        begin = pl.multiple_of(128 * index, 128)
        query = mixed[:, pl.ds(begin, 128)]
        keys = mixed[:, pl.ds(D + begin, 128)]
        contents = mixed[:, pl.ds(2 * D + begin, 128)]
        incoming = spread[:, pl.ds(begin, 128)]
        for half, raw in enumerate((hold, hold2)):
            here = (lane // HEAD_DIM) == half
            raw[...] = dot_nt(jnp.where(here, incoming, jnp.zeros_like(incoming)), contents)
        both = incoming.astype(F32) * joined[:, pl.ds(begin, 128)]
        upper = both.astype(BF16)
        lower = (both - upper.astype(F32)).astype(BF16)
        means[:, 0:256] = dot(jnp.concatenate([upper, lower], axis=1), sides)
        turned_query, turned_incoming = query.T, incoming.T
        grads_query, grads_keys, grads_contents = [], [], []
        for half, raw in enumerate((hold, hold2)):
            head = 2 * index + half
            side = slice(half * HEAD_DIM, (half + 1) * HEAD_DIM)
            cols = pl.ds(half * L, L)
            part = zeros8(2 * L)
            for u in range(BLOCK // 16):
                tiles = [None] * 7 + [jnp.zeros((16, 128), F32)]
                for block in range(L // BLOCK):
                    rows = pl.ds(block * BLOCK + 16 * u, 16)
                    mean = means[rows, 128 * half : 128 * half + 128]
                    slant = probs[head, rows, :].astype(F32) * (raw[rows, :] - jnp.concatenate([mean] * 4, axis=1))
                    scaled[rows, cols] = slant.astype(BF16)
                    for j in range(4):
                        piece = slant[:, 128 * j : 128 * j + 128]
                        at = 3 - block + j
                        tiles[at] = piece if tiles[at] is None else tiles[at] + piece
                full = jnp.concatenate(tiles, axis=1)
                part = part + pltpu.roll(full[0:8], BLOCK - 8 - 16 * u, 1) + pltpu.roll(full[8:16], BLOCK - 16 - 16 * u, 1)
            diagonals[:, pl.ds(head, 1), :] = part.reshape(8, 1, 2 * L)
            grads_query.append(dot(scaled[:, cols], keys))
            grads_keys.append(dot(turned_query[side], scaled[:, cols]))
            grads_contents.append(dot(turned_incoming[side], probs[head]))
            pump(index, half)
        scale = HEAD_DIM ** (-0.5)
        grad_mixed[:, pl.ds(begin, 128)] = (jnp.where(lane < HEAD_DIM, *grads_query) * scale).astype(BF16)
        grad_mixed[:, pl.ds(D + begin, 128)] = (jnp.concatenate(grads_keys, axis=0).T * scale).astype(BF16)
        grad_mixed[:, pl.ds(2 * D + begin, 128)] = jnp.concatenate(grads_contents, axis=0).T.astype(BF16)
        return carry

    lax.fori_loop(0, HEADS // 2, pair, 0)
    line = diagonals[7]
    for r in range(7):
        line = line + pltpu.roll(diagonals[r], 7 - r, 1)
    table_grad[...] = lax.dot_general(
        line, bucket_choice(buckets), (((1,), (1,)), ((), ())),
        precision=lax.Precision.HIGHEST, preferred_element_type=F32,
    )


def clear_pads(padded):
    edge = jnp.zeros((4, PAD, 128), F32)
    padded[:, 0:PAD, :] = edge
    padded[:, PAD + L : 2 * PAD + L, :] = edge


def conv_front(source, normed, sigma, tilt, gated, middle, sums, hold, spare, weights, small, gate_bias, bounds, pump):
    norm_rows(source, normed, small, S_CONV)
    clear_pads(gated)
    hold[...] = dot(normed[...], columns(weights, GLU, 1))
    bias = gate_bias[0:1, D:]

    def gate(rows, carry):
        gate = jax.nn.sigmoid(hold[rows, :] + bias)
        spare[rows, :] = gate
        sigma[rows, :] = gate.astype(BF16)
        return carry

    chunks(gate, 0)
    hold[...] = dot(normed[...], columns(weights, GLU, 0))
    bias = gate_bias[0:1, :D]

    def unit(rows, carry):
        gate = spare[rows, :]
        values = (hold[rows, :] + bias) * gate
        tilt[rows, :] = (values * (1.0 - gate)).astype(BF16)
        for j in range(4):
            gated[j, pl.ds(rows.start + PAD, CHUNK), :] = values[:, 128 * j : 128 * j + 128]
        return carry

    chunks(unit, 0)
    size = 32

    def slide(i, carry):
        begin = pl.multiple_of(i * size, size)
        marks = bounds[pl.ds(begin + PAD, size), :]
        accs = [jnp.zeros((size, 128), F32) for _ in range(4)]
        for k in range(TAPS):
            same = bounds[pl.ds(begin + k, size), :] == marks
            for j in range(4):
                tap = small[S_TAPS + k : S_TAPS + k + 1, 128 * j : 128 * j + 128]
                accs[j] += jnp.where(same, gated[j, pl.ds(begin + k, size), :], 0.0) * tap
        result = []
        for j in range(4):
            middle[pl.ds(begin, size), 128 * j : 128 * j + 128] = accs[j]
            result.append(carry[j] + fold(accs[j]))
            result.append(carry[4 + j] + fold(accs[j] * accs[j]))
        pump(i)
        return result[0::2] + result[1::2]

    ends = lax.fori_loop(0, L // size, slide, [zeros8(128)] * 8, unroll=2)
    for j in range(4):
        sums[0:1, 128 * j : 128 * j + 128] = total_row(ends[j])
        sums[1:2, 128 * j : 128 * j + 128] = total_row(ends[4 + j])


def conv_rest(source, middle, sums, unit, active, slope, result, hold, weights, small, frames):
    center = sums[0:1, :] * (1.0 / frames)
    inverse = lax.rsqrt(sums[1:2, :] * (1.0 / frames) - center * center + epsilon)
    gain, shift = 1.0 + small[S_BATCH : S_BATCH + 1, :], small[S_BATCH + 1 : S_BATCH + 2, :]

    def body(rows, carry):
        values = (middle[rows, :] - center) * inverse
        unit[rows, :] = values
        normal = values * gain + shift
        sigma = jax.nn.sigmoid(normal)
        value = normal * sigma
        active[rows, :] = value.astype(BF16)
        slope[rows, :] = (sigma + value * (1.0 - sigma)).astype(slope.dtype)
        return carry

    chunks(body, 0)
    hold[...] = dot(active[...], columns(weights, CONV, 0))
    bias = small[S_COB : S_COB + 1, :]

    def add(rows, carry):
        result[rows, :] = source[rows, :] + hold[rows, :] + bias
        return carry

    chunks(add, 0)


def conv_back_rest(upstream, unit, slope, grad_normal, low, hold, weights, grads, sums):
    def start(rows, carry):
        given = upstream[rows, :]
        low[rows, :] = given.astype(BF16)
        return carry + fold(given)

    grads[S_COB : S_COB + 1, :] = total_row(chunks(start, zeros8()))
    hold[...] = dot_nt(low[...], columns(weights, CONV, 0))

    def body(rows, carry):
        grad = hold[rows, :] * slope[rows, :].astype(F32)
        grad_normal[rows, :] = grad
        return carry[0] + fold(grad), carry[1] + fold(grad * unit[rows, :])

    first, second = chunks(body, (zeros8(), zeros8()))
    sums[0:1, :] = total_row(first)
    sums[1:2, :] = total_row(second)
    grads[S_BATCH : S_BATCH + 1, :] = total_row(second)
    grads[S_BATCH + 1 : S_BATCH + 2, :] = total_row(first)


def conv_back_front(
    sigma, tilt, gated, unit, grad_normal, front_sums, sums, padded, grad_joined, hold, tap_sums, small, bounds, grads, gate_grads,
    frames, pump,
):
    center = front_sums[0:1, :] * (1.0 / frames)
    inverse = lax.rsqrt(front_sums[1:2, :] * (1.0 / frames) - center * center + epsilon)
    gain = 1.0 + small[S_BATCH : S_BATCH + 1, :]
    mean0, mean1 = gain * sums[0:1, :] * (1.0 / frames), gain * sums[1:2, :] * (1.0 / frames)
    clear_pads(padded)

    def start(rows, carry):
        grad = inverse * (gain * grad_normal[rows, :] - mean0 - unit[rows, :] * mean1)
        for j in range(4):
            padded[j, pl.ds(rows.start + PAD, CHUNK), :] = grad[:, 128 * j : 128 * j + 128]
        return carry

    chunks(start, 0)
    tap_sums[...] = jnp.zeros_like(tap_sums)
    size = 32

    def slide(i, carry):
        begin = pl.multiple_of(i * size, size)
        marks = bounds[pl.ds(begin + PAD, size), :]
        accs = [jnp.zeros((size, 128), F32) for _ in range(4)]
        for k in range(TAPS):
            same = bounds[pl.ds(begin + 2 * PAD - k, size), :] == marks
            for j in range(4):
                tap = small[S_TAPS + k : S_TAPS + k + 1, 128 * j : 128 * j + 128]
                accs[j] += jnp.where(same, padded[j, pl.ds(begin + 2 * PAD - k, size), :], 0.0) * tap
        for j in range(4):
            hold[pl.ds(begin, size), 128 * j : 128 * j + 128] = accs[j]
        grads_here = [padded[j, pl.ds(begin + PAD, size), :] for j in range(4)]
        for k in range(TAPS):
            same = bounds[pl.ds(begin + k, size), :] == marks
            for j in range(4):
                term = jnp.where(same, gated[j, pl.ds(begin + k, size), :], 0.0) * grads_here[j]
                tap_sums[k, :, 128 * j : 128 * j + 128] += fold(term)
        pump(i)
        return carry

    lax.fori_loop(0, L // size, slide, 0, unroll=2)
    grads[S_TAPS : S_TAPS + TAPS, :] = jnp.sum(tap_sums[...], axis=1)

    def split(rows, carry):
        grad = hold[rows, :]
        first = grad * sigma[rows, :].astype(F32)
        second = grad * tilt[rows, :].astype(F32)
        grad_joined[rows, :D] = first.astype(BF16)
        grad_joined[rows, D : 2 * D] = second.astype(BF16)
        return carry[0] + fold(first), carry[1] + fold(second)

    first, second = chunks(split, (zeros8(), zeros8()))
    gate_grads[0:1, :D] = total_row(first)
    gate_grads[0:1, D:] = total_row(second)


THIN = (
    ("ffn_norm", S_FFN), ("ffn_out_bias", S_FOB), ("attn_norm", S_ATTN), ("attn_out_bias", S_AOB), ("conv_norm", S_CONV),
    ("batch_norm", S_BATCH), ("conv_out_bias", S_COB), ("final_norm", S_FINAL), ("depth_kernel", S_TAPS),
)


def turned(value):
    rows, lanes = value.shape
    value = jnp.concatenate([value, jnp.zeros((rows, 128 - lanes), F32)], axis=1)
    return jnp.concatenate([value, jnp.zeros((128 - rows, 128), F32)], axis=0).T[:lanes, :rows]


def pack_small(b, tile):
    tile[...] = jnp.zeros_like(tile)
    for name, row in THIN:
        value = getattr(b, name)[...].astype(F32)
        if name == "depth_kernel":
            value = turned(value)
        value = value.reshape(-1, value.shape[-1])
        for r in range(0, value.shape[0], 16):
            part = value[r : r + 16]
            begin = (row + r) % 16
            at = 128 * ((row + r) // 16)
            tile[begin : begin + part.shape[0], at : at + part.shape[1]] = part
    tile[0:2, 384 : 384 + b.ffn_in_bias.shape[1]] = b.ffn_in_bias[...].astype(F32)
    wide, few = b.glu_bias.shape[0], b.rel_table.shape[0]
    tile[2:3, 384 : 384 + wide] = b.glu_bias[...].astype(F32).reshape(1, wide)
    tile[3:4, 384 : 384 + few] = b.rel_table[...].astype(F32).reshape(1, few)


def load_weights(b, place):
    copies = {}

    def load(row, source):
        target = b.weights.at[place.plane, place.z, place.core, pl.ds(row, source.shape[0])]
        copies[row] = pltpu.make_async_copy(source, target, b.load_sems.at[len(copies)])
        copies[row].start()

    for layer in range(2):
        for c in range(FF // D):
            load((IN0, IN1)[layer] + 16 * c, b.ffn_in.at[layer, :, pl.ds(D * c, D)])
        load((OUT0, OUT1)[layer], b.ffn_out.at[layer])
        if layer == 0:
            for c in range(3):
                load(QKV + 16 * c, b.qkv_weight.at[:, pl.ds(D * c, D)])
            load(ATT, b.attn_out.at[:, :])
            for c in range(2):
                load(GLU + 16 * c, b.glu_weight.at[:, pl.ds(D * c, D)])
            load(CONV, b.conv_out.at[:, :])
    return copies


def unpack_small(b, place):
    per = 2 * place.chips
    count = place.planes * per
    width = D // count
    for device in range(count):
        tile = b.weights[device // per, (device % per) // 2, device % 2, 0:16, :].astype(F32)
        for q in range(3):
            b.small[16 * q : 16 * q + 16, width * device : width * device + width] = tile[:, 128 * q : 128 * q + width]
        b.inner_bias[:, 4 * width * device : 4 * width * (device + 1)] = tile[0:2, 384 : 384 + 4 * width]
        b.gate_bias[:, 2 * width * device : 2 * width * (device + 1)] = tile[2:3, 384 : 384 + 2 * width]
        few = HEADS * BUCKETS // count
        head, at = few * device // BUCKETS, few * device % BUCKETS
        b.table[head : head + 1, at : at + few] = tile[3:4, 384 : 384 + few]


def pack_small_grads(b, place):
    per = 2 * place.chips
    count = place.planes * per
    width = D // count
    few = HEADS * BUCKETS // count
    for device in range(count):
        tile = b.edges.at[device // per, (device % per) // 2, device % 2]
        for g in range(8):
            tile[0:6, 16 * g : 16 * g + width] = b.grads[6 * g : 6 * g + 6, width * device : width * device + width]
        for m in range(2):
            tile[6:7, 64 * m : 64 * m + 4 * width] = b.inner_grads[m : m + 1, 4 * width * device : 4 * width * (device + 1)]
        tile[7:8, 0 : 2 * width] = b.gate_grads[:, 2 * width * device : 2 * width * (device + 1)]
        head, at = few * device // BUCKETS, few * device % BUCKETS
        tile[7:8, 64 : 64 + few] = b.table_grad[head : head + 1, at : at + few]


INPUTS = (
    "inputs", "segments", "buckets", "cotangent", "ffn_norm", "ffn_in", "ffn_in_bias", "ffn_out", "ffn_out_bias", "attn_norm",
    "qkv_weight", "attn_out", "attn_out_bias", "rel_table", "conv_norm", "glu_weight", "glu_bias", "depth_kernel", "batch_norm",
    "conv_out", "conv_out_bias", "final_norm",
)
LOADED = ("inputs", "cotangent", "ffn_in", "ffn_out", "qkv_weight", "attn_out", "glu_weight", "conv_out")
OUTPUTS = ("output", "grad_x", "shard", "thin")
GATHERS = ((SMALL, 48, 32), (IN0 + 32, 32, 16), (OUT0, 64, 32), (QKV, 64, 32), (GLU, 48, 32), (IN1, 64, 32), (OUT1, 64, 32))
REDUCES = (
    (OUT1, OUT1, 64, 32), (IN1, IN1, 64, 32), (CONV, CONV, 16, 16), (GLU, GLU, 32, 16),
    (ATT, ATT, 16, 16), (QKV, QKV, 48, 32), (OUT1, OUT0, 32, 16),
    (OUT1 + 32, OUT0 + 32, 32, 16), (IN1, IN0, 32, 16), (IN1 + 32, IN0 + 32, 32, 16),
)


def scratch_of(planes, chips):
    wide, low, big = pltpu.VMEM((L, D), F32), pltpu.VMEM((L, D), BF16), pltpu.VMEM((L, FF), BF16)
    pads = pltpu.VMEM((4, L + 2 * PAD, 128), F32)
    stats = pltpu.VMEM((2, D), F32)
    return dict(
        weights=pltpu.VMEM((planes, chips, 2, ROWS, D), BF16),
        twin=pltpu.VMEM((planes, chips, GRADS, D), BF16),
        diagonal=pltpu.VMEM((chips, GRADS, D), BF16),
        from_x=pltpu.VMEM((chips, GRADS, D), BF16),
        from_y=pltpu.VMEM((chips, GRADS, D), BF16),
        from_z=pltpu.VMEM((chips - 1, GRADS, D), BF16),
        edges=pltpu.VMEM((planes, chips, 2, 8, 128), F32),
        edge_near=pltpu.VMEM((2 * planes, chips, 8, 128), F32),
        edge_part=pltpu.VMEM((chips, 8, 128), F32),
        edge_far=pltpu.VMEM((chips, 8, 128), F32),
        small=pltpu.VMEM((S_ROWS, D), F32),
        inner_bias=pltpu.VMEM((2, FF), F32),
        gate_bias=pltpu.VMEM((1, 2 * D), F32),
        table=pltpu.VMEM((HEADS, BUCKETS), F32),
        tile=pltpu.VMEM((16, D), F32),
        grads=pltpu.VMEM((S_ROWS, D), F32),
        inner_grads=pltpu.VMEM((2, FF), F32),
        gate_grads=pltpu.VMEM((1, 2 * D), F32),
        table_grad=pltpu.VMEM((HEADS, BUCKETS), F32),
        lines=pltpu.VMEM((HEADS, 2 * L), F32),
        choice=pltpu.VMEM((1, 2 * L), jnp.int32),
        bounds=pltpu.VMEM((L + 2 * PAD, 128), F32),
        marks=pltpu.VMEM((1, L), F32),
        front_own=stats, back_own=stats, front_sums=stats, back_sums=stats, front_part=stats, back_part=stats,
        front_near=pltpu.VMEM((2 * planes, 2, D), F32), back_near=pltpu.VMEM((2 * planes, 2, D), F32),
        front_far=pltpu.VMEM((chips, 2, D), F32), back_far=pltpu.VMEM((chips, 2, D), F32),
        x1=wide, x2=wide, x3=wide, x4=wide, normed_a=low, normed_c=low, normed1=low,
        active0=big, slope0=big, active1=big, slope1=big, mixed=pltpu.VMEM((L, 3 * D), BF16),
        probs=pltpu.VMEM((HEADS, L, L), BF16), joined=wide, recips=wide, diagonals=pltpu.VMEM((8, HEADS, 2 * L), F32), sigma=low, tilt=low, gated=pads, middle=wide, active_c=low, slope_c=low,
        padded=pads, low=low, hold=wide, total=wide, taps=pltpu.VMEM((TAPS, 8, D), F32),
        x0=low, given=low, result=low,
        load_sems=pltpu.SemaphoreType.DMA((17,)),
        edge_sems=pltpu.SemaphoreType.DMA((4,)),
        gather_sends=pltpu.SemaphoreType.DMA((len(GATHERS) * Gather.semaphores(chips),)),
        gather_receives=pltpu.SemaphoreType.DMA((len(GATHERS) * Gather.semaphores(chips),)),
        reduce_sends=pltpu.SemaphoreType.DMA((len(REDUCES) * (chips + 7),)),
        reduce_receives=pltpu.SemaphoreType.DMA((len(REDUCES) * (chips + 7),)),
        total_sends=pltpu.SemaphoreType.DMA((3 * (2 * planes + chips),)),
        total_receives=pltpu.SemaphoreType.DMA((3 * (2 * planes + chips),)),
    )


def whole_kernel(names, *refs):
    b = Bag()
    for name, ref in zip(names, refs):
        setattr(b, name, ref)
    place = Place()
    planes, chips = place.planes, place.chips
    frames = L * planes * chips * 2
    barrier = pltpu.get_barrier_semaphore()
    near = [device for device, rank in place.members] + [place.along[d] for d in range(1, chips)]
    for device in near:
        pl.semaphore_signal(barrier, inc=1, device_id=device, device_id_type=MESH)
    loads = load_weights(b, place)
    load_x = pltpu.make_async_copy(b.inputs.at[0], b.x0, b.edge_sems.at[0])
    load_cotangent = pltpu.make_async_copy(b.cotangent.at[0], b.given, b.edge_sems.at[1])
    load_x.start()
    load_cotangent.start()
    pack_small(b, b.tile)
    b.weights[place.plane, place.z, place.core, 0:16, :] = b.tile[...].astype(BF16)
    pl.semaphore_wait(barrier, len(near))

    gathers = Copies(b.gather_sends, b.gather_receives, place)
    rounds = [
        Gather(place, b.weights, gathers, i * Gather.semaphores(chips), begin, size, split)
        for i, (begin, size, split) in enumerate(GATHERS)
    ]
    r0, r1, r2, r3, r4, r5, r6 = rounds
    for r, (begin, size, _) in zip(rounds, GATHERS):
        for row, copy in loads.items():
            if begin <= row < begin + size:
                copy.wait()
        r.along_z()
        if r in rounds[:5]:
            r.own()
    b.marks[...] = b.segments[...].astype(F32)
    b.bounds[...] = jnp.full(b.bounds.shape, -1.0, F32)
    b.bounds[PAD : PAD + L, :] = jnp.broadcast_to(b.marks[...], (128, L)).T
    b.choice[...] = jnp.full(b.choice.shape, -1, jnp.int32)
    b.choice[:, 0 : 2 * L - 1] = b.buckets[...].reshape(1, 2 * L - 1)
    attention_mask(b.x4, b.bounds, b.marks)
    for step in (r0.forward, r1.forward, r0.turn, r1.turn, r2.forward, r0.across, r0.done):
        step()
    unpack_small(b, place)

    x0 = b.x0
    load_x.wait()
    raws = (b.hold, b.total)
    feed_inner(
        x0, b.normed_c, b.active0, b.slope0, raws, b.weights, b.small, b.inner_bias, 0,
        at_points({(2, 0): (r1.across, r1.done, r3.forward)}),
    )
    attention_squares(b.lines, b.twin, b.table, b.choice)
    for step in (r2.turn, r3.turn, r4.forward, r5.own, r2.across, r2.done):
        step()
    feed_outer(x0, b.active0, b.x1, b.hold, b.weights, b.small, 0)
    r3.across()
    r3.done()
    attention_mix(b.x1, b.normed_a, b.mixed, b.weights, b.small)
    for step in (r4.turn, r5.forward, r6.own, r6.forward):
        step()
    attention_forward(
        b.x1, b.mixed, b.probs, b.joined, b.recips, b.x2, b.twin, b.x4, b.hold, b.x3, b.weights, b.small, still
    )
    r4.across()
    r4.done()
    conv_front(
        b.x2, b.normed_c, b.sigma, b.tilt, b.gated, b.middle, b.front_own, b.hold, b.total, b.weights, b.small, b.gate_bias, b.bounds,
        at_points({(5, 0): (r5.turn,)}),
    )
    totals = Copies(b.total_sends, b.total_receives, place)
    front = Total(place, b.front_own, b.front_near, b.front_part, b.front_far, b.front_sums, totals, 0)
    front.start()
    r6.turn()
    front.turn()
    front.finish()
    conv_rest(b.x2, b.middle, b.front_sums, b.middle, b.active_c, b.slope_c, b.x3, b.hold, b.weights, b.small, frames)
    r5.across()
    r5.done()
    feed_inner(b.x3, b.normed1, b.active1, b.slope1, raws, b.weights, b.small, b.inner_bias, 1, still)
    r6.across()
    r6.done()
    feed_outer(b.x3, b.active1, b.x4, b.hold, b.weights, b.small, 1)
    norm_rows(b.x4, b.result, b.small, S_FINAL)
    save_output = pltpu.make_async_copy(b.result, b.output.at[0], b.edge_sems.at[2])
    save_output.start()
    load_cotangent.wait()
    flow = b.x4
    norm_back(b.x4, b.given, None, flow, b.small, S_FINAL, b.grads)
    gathers.sent()

    early = Copies(b.reduce_sends, b.reduce_receives, place)
    reduces = Copies(b.reduce_sends, b.reduce_receives, place)
    landings = (b.twin, b.diagonal, b.from_x, b.from_y, b.from_z)

    def finish(begin, size):
        def act(value):
            b.shard[begin - IN0 : begin - IN0 + size, :] = value

        return act

    backs = [
        reduce_steps(
            place, b.weights, *landings, early if i < 2 else reduces, i * (chips + 7), begin, size, split, owner - IN0,
            finish(owner, size),
        )
        for i, (begin, owner, size, split) in enumerate(REDUCES)
    ]
    out1, in1, tip, glu, att, mix, out0, out0_end, in0, in0_end = backs
    feed_back_start(flow, b.low, b.grads, 1)
    feed_back_inner(b.normed1, b.slope1, b.low, raws, b.weights, None, b.inner_grads, 1, still)
    feed_back_outer(b.active1, b.low, b.weights, OUT1, still)
    out1[0]()
    product_back(b.slope1, b.normed1, b.total, b.weights, IN1, 4, still)
    in1[0]()
    out1[1]()
    norm_back(b.x3, b.total, flow, flow, b.small, S_FFN + 2, b.grads)
    in1[1]()
    grad_normal = b.x3
    conv_back_rest(flow, b.middle, b.slope_c, grad_normal, b.low, b.hold, b.weights, b.grads, b.back_own)
    back = Total(place, b.back_own, b.back_near, b.back_part, b.back_far, b.back_sums, totals, 2 * planes + chips)
    back.start()
    put_columns(b.weights, CONV, 0, dot_tn(b.active_c[...], b.low[...]))
    tip[0]()
    back.turn()
    out1[2]()
    tip[1]()
    back.finish()
    conv_back_front(
        b.sigma, b.tilt, b.gated, b.middle, grad_normal, b.front_sums, b.back_sums, b.padded, b.active1, b.hold, b.taps, b.small,
        b.bounds, b.grads, b.gate_grads, frames, at_points({(4, 0): (in1[2],), (8, 0): (tip[2],), (14, 0): (out1[3],)}),
    )
    product_back(b.active1, b.normed_c, b.total, b.weights, GLU, 2, still)
    glu[0]()
    norm_back(b.x2, b.total, flow, flow, b.small, S_CONV, b.grads)
    attention_back_start(flow, b.joined, b.recips, b.low, b.normed1, b.hold, b.weights, b.grads)
    att[0]()
    glu[1]()
    attention_backward(
        b.mixed, b.probs, b.normed1, b.joined, b.active1, b.slope1, b.hold, b.x3, b.total, b.diagonals, b.lines, b.choice,
        b.table_grad, at_points({(0, 1): (in1[3], att[1]), (2, 0): (tip[3],), (2, 1): (glu[2],), (3, 0): (out1[4],), (3, 1): (att[2],)}),
    )
    product_back(b.active1, b.normed_a, b.total, b.weights, QKV, 3, still)
    mix[0]()
    norm_back(b.x1, b.total, flow, flow, b.small, S_ATTN, b.grads)
    in1[4]()
    tip[4]()
    early.sent()
    norm_rows(x0, b.normed_c, b.small, S_FFN)
    feed_back_start(flow, b.low, b.grads, 0)
    feed_back_outer(b.active0, b.low, b.weights, OUT1, still)
    out0[0]()
    out0_end[0]()
    mix[1]()
    glu[3]()
    att[3]()
    feed_back_inner(
        b.normed_c, b.slope0, b.low, raws, b.weights, IN1, b.inner_grads, 0,
        at_points({(1, 0): (in0[0], out0[1]), (2, 0): (out0_end[1],)}),
    )
    in0_end[0]()
    in0[1]()
    product_back(b.slope0, None, b.total, b.weights, IN0, 4, still)
    in0_end[1]()
    norm_back(x0, b.total, flow, b.x3, b.small, S_FFN, b.grads)
    save_grad_x = pltpu.make_async_copy(b.x3, b.grad_x.at[0], b.edge_sems.at[3])
    save_grad_x.start()
    pack_small_grads(b, place)
    thin = Thin(place, b.edges, b.edge_near, b.edge_part, b.edge_far, b.thin, totals, 2 * (2 * planes + chips))
    thin.start()
    for step in (
        mix[2], thin.turn, out0[2], out0_end[2], in0[2], in0_end[2], glu[4], att[4], thin.finish, mix[3], out0[3], out0_end[3],
        mix[4], in0[3], out0[4], in0_end[3], out0_end[4], in0[4], in0_end[4],
    ):
        step()
    early.sent()
    reduces.sent()
    totals.sent()
    save_output.wait()
    save_grad_x.wait()


def finish_kernel(*refs):
    (
        output_in, grad_x_in, shard, thin, output, grad_x, grad_ffn_norm, grad_ffn_in, grad_ffn_in_bias, grad_ffn_out,
        grad_ffn_out_bias, grad_attn_norm, grad_qkv, grad_attn_out, grad_attn_out_bias, grad_rel, grad_conv_norm, grad_glu,
        grad_glu_bias, grad_depth, grad_batch, grad_conv_out, grad_conv_out_bias, grad_final, taps, semaphores,
    ) = refs
    copies = [
        pltpu.make_async_copy(output_in, output, semaphores.at[0]), pltpu.make_async_copy(grad_x_in, grad_x, semaphores.at[1])
    ]
    for copy in copies:
        copy.start()
    cut = lambda begin, size: shard[begin - IN0 : begin - IN0 + size, :]
    width = grad_final.shape[-1]

    def thin_rows(begin, count):
        rows = []
        for p in range(begin, begin + count):
            rows.append(thin[p % 6 : p % 6 + 1, 16 * (p // 6) : 16 * (p // 6) + width])
        return rows

    for layer in range(2):
        for c in range(FF // D):
            grad_ffn_in[layer, :, D * c : D * c + D] = cut((IN0, IN1)[layer] + 16 * c, 16)
        grad_ffn_out[layer] = cut((OUT0, OUT1)[layer], 64)
        grad_ffn_in_bias[layer : layer + 1, :] = thin[6:7, 64 * layer : 64 * layer + 4 * width]
        for r, row in enumerate(thin_rows(S_FFN + 2 * layer, 2)):
            grad_ffn_norm[layer, r : r + 1, :] = row
    for c in range(3):
        grad_qkv[:, D * c : D * c + D] = cut(QKV + 16 * c, 16)
    grad_attn_out[...] = cut(ATT, 16)
    for c in range(2):
        grad_glu[:, D * c : D * c + D] = cut(GLU + 16 * c, 16)
    grad_conv_out[...] = cut(CONV, 16)
    for ref, begin in (
        (grad_ffn_out_bias, S_FOB), (grad_attn_norm, S_ATTN), (grad_conv_norm, S_CONV), (grad_batch, S_BATCH),
        (grad_final, S_FINAL),
    ):
        for r, row in enumerate(thin_rows(begin, ref.shape[0])):
            ref[r : r + 1, :] = row
    for r, row in enumerate(thin_rows(S_TAPS, TAPS)):
        taps[r : r + 1, 0:width] = row
    grad_depth[...] = taps[...].T[0:width, 0:TAPS]
    grad_attn_out_bias[...] = thin_rows(S_AOB, 1)[0][0]
    grad_conv_out_bias[...] = thin_rows(S_COB, 1)[0][0]
    grad_glu_bias[...] = thin[7:8, 0 : 2 * width][0]
    grad_rel[...] = thin[7:8, 64 : 64 + grad_rel.shape[0]][0]
    for copy in copies:
        copy.wait()


def shape(dims, kind=F32):
    return jax.ShapeDtypeStruct(dims, kind)


def local(*args):
    planes, chips = lax.axis_size("dp"), lax.axis_size("fsdp") // 2
    scratch = scratch_of(planes, chips)
    names = INPUTS + OUTPUTS + tuple(scratch)
    vmem, anywhere = pl.BlockSpec(memory_space=pltpu.VMEM), pl.BlockSpec(memory_space=pl.ANY)
    given = dict(zip(INPUTS, args))
    given["depth_kernel"] = given["depth_kernel"].T
    firsts = [shape((1, L, D), BF16), shape((1, L, D))]
    passed = pl.pallas_call(
        lambda *refs: whole_kernel(names, *refs),
        out_shape=firsts + [shape((GRADS, D)), shape((8, 128))],
        in_specs=[anywhere if name in LOADED else vmem for name in INPUTS],
        out_specs=[anywhere, anywhere, vmem, vmem],
        scratch_shapes=list(scratch.values()),
        compiler_params=pltpu.CompilerParams(collective_id=0, has_side_effects=True, vmem_limit_bytes=VMEM_BYTES),
        name="layer",
    )(*given.values())
    outs = [
        shape(given[name].shape)
        for name in (
            "ffn_norm", "ffn_in", "ffn_in_bias", "ffn_out", "ffn_out_bias", "attn_norm", "qkv_weight", "attn_out",
            "attn_out_bias", "rel_table", "conv_norm", "glu_weight", "glu_bias", "depth_kernel", "batch_norm", "conv_out",
            "conv_out_bias", "final_norm",
        )
    ]
    grads = pl.pallas_call(
        finish_kernel,
        out_shape=firsts + outs,
        in_specs=[anywhere, anywhere, vmem, vmem],
        out_specs=[vmem] * (2 + len(outs)),
        scratch_shapes=[pltpu.VMEM((128, 128), F32), pltpu.SemaphoreType.DMA((2,))],
        name="unpack",
    )(*passed)
    grads = list(grads)
    grads[15] = grads[15].T
    return tuple(grads)


VMEM_BYTES = 127 * 512 * 1024


highest = lax.Precision.HIGHEST


def layer_norm(values, params):
    center = values - jnp.mean(values, axis=-1, keepdims=True)
    spread = jnp.mean(center * center, axis=-1, keepdims=True)
    return center * lax.rsqrt(spread + epsilon) * (1.0 + params[0]) + params[1]


def silu_slope(values):
    sigma = jax.nn.sigmoid(values)
    return sigma * (1.0 + values * (1.0 - sigma))


def product(left, right):
    return jnp.dot(left, right, preferred_element_type=jnp.float32)


def product_left(left, right):
    return lax.dot_general(
        left, right, (((0,), (0,)), ((), ())), preferred_element_type=jnp.float32
    )


def product_right(left, right):
    return lax.dot_general(
        left, right, (((1,), (1,)), ((), ())), preferred_element_type=jnp.float32
    )


def plain_fetch_feed(norms, inner_weight, inner_bias, outer_weight, outer_bias, layer):
    return (
        lax.all_gather(norms[layer], ("dp", "fsdp"), axis=1, tiled=True),
        lax.all_gather(inner_weight[layer], ("dp", "fsdp"), axis=0, tiled=True),
        lax.all_gather(inner_bias[layer], ("dp", "fsdp"), axis=0, tiled=True),
        lax.all_gather(outer_weight[layer], ("dp", "fsdp"), axis=0, tiled=True),
        lax.all_gather(outer_bias[layer], ("dp", "fsdp"), axis=0, tiled=True),
    )


def plain_reduce_feed(grads):
    return (
        lax.psum_scatter(grads[0], ("dp", "fsdp"), scatter_dimension=1, tiled=True),
        lax.psum_scatter(grads[1], ("dp", "fsdp"), scatter_dimension=0, tiled=True),
        lax.psum_scatter(grads[2], ("dp", "fsdp"), scatter_dimension=0, tiled=True),
        lax.psum_scatter(grads[3], ("dp", "fsdp"), scatter_dimension=0, tiled=True),
        lax.psum_scatter(grads[4], ("dp", "fsdp"), scatter_dimension=0, tiled=True),
    )


def fetch_attention(attn_norm, qkv_weight, attn_out, attn_out_bias, rel_table):
    return (
        lax.all_gather(attn_norm, ("dp", "fsdp"), axis=1, tiled=True),
        lax.all_gather(qkv_weight, ("dp", "fsdp"), axis=0, tiled=True),
        lax.all_gather(attn_out, ("dp", "fsdp"), axis=0, tiled=True),
        lax.all_gather(attn_out_bias, ("dp", "fsdp"), axis=0, tiled=True),
        lax.all_gather(rel_table, ("dp", "fsdp"), axis=0, tiled=True),
    )


def fetch_conv(
    conv_norm, glu_weight, glu_bias, depth_kernel, batch_norm, conv_out, conv_out_bias, final_norm
):
    return (
        lax.all_gather(conv_norm, ("dp", "fsdp"), axis=1, tiled=True),
        lax.all_gather(glu_weight, ("dp", "fsdp"), axis=0, tiled=True),
        lax.all_gather(glu_bias, ("dp", "fsdp"), axis=0, tiled=True),
        lax.all_gather(depth_kernel, ("dp", "fsdp"), axis=1, tiled=True),
        lax.all_gather(batch_norm, ("dp", "fsdp"), axis=1, tiled=True),
        lax.all_gather(conv_out, ("dp", "fsdp"), axis=0, tiled=True),
        lax.all_gather(conv_out_bias, ("dp", "fsdp"), axis=0, tiled=True),
        lax.all_gather(final_norm, ("dp", "fsdp"), axis=1, tiled=True),
    )


def plain_feed_forward(values, weights):
    norm, weight_in, bias_in, weight_out, bias_out = weights
    normed, norm_back = jax.vjp(layer_norm, values, norm.astype(jnp.float32))
    normed_low = normed.astype(jnp.bfloat16)
    inner = product(normed_low, weight_in) + bias_in.astype(jnp.float32)
    active = jax.nn.silu(inner).astype(jnp.bfloat16)
    result = values + 0.5 * (product(active, weight_out) + bias_out.astype(jnp.float32))
    return (result, (normed_low, inner, active, norm_back))


def plain_feed_backward(upstream, weights, saved):
    norm, weight_in, bias_in, weight_out, bias_out = weights
    normed_low, inner, active, norm_back = saved
    branch = 0.5 * upstream
    branch_low = branch.astype(jnp.bfloat16)
    grad_weight_out = product_left(active, branch_low)
    grad_inner = product_right(branch_low, weight_out) * silu_slope(inner)
    inner_low = grad_inner.astype(jnp.bfloat16)
    grad_weight_in = product_left(normed_low, inner_low)
    grad_values, grad_norm = norm_back(product_right(inner_low, weight_in))
    return (
        upstream + grad_values,
        (
            grad_norm,
            grad_weight_in,
            jnp.sum(grad_inner, axis=0),
            grad_weight_out,
            jnp.sum(branch, axis=0),
        ),
    )


def relative_lines(table, buckets):
    choose = (buckets[None, :] == jnp.arange(BUCKETS, dtype=jnp.int32)[:, None]).astype(jnp.float32)
    lines = jnp.dot(table.astype(jnp.float32).reshape(HEADS, BUCKETS), choose, precision=highest)
    return (lines, choose)


def bias_square(line, length):
    tiled = jnp.broadcast_to(line, (length, 2 * length - 1)).reshape(-1)
    tiled = jnp.concatenate([tiled, jnp.zeros((length,), line.dtype)])
    return tiled.reshape(length, 2 * length)[:, :length][::-1]


def diagonal_sums(square):
    length = square.shape[0]
    padded = jnp.concatenate([square[::-1], jnp.zeros_like(square)], axis=1).reshape(-1)
    return jnp.sum(padded[: length * (2 * length - 1)].reshape(length, 2 * length - 1), axis=0)


def head_scores(query, keys_head, line, same):
    raw = product_right(query, keys_head)
    return jnp.where(same, raw * HEAD_DIM ** (-0.5) + bias_square(line, query.shape[0]), -1e30)


def plain_attention_forward(values, weights, marks, buckets):
    norm, mixer, weight_out, bias_out, table = weights
    length = values.shape[0]
    normed, norm_back = jax.vjp(layer_norm, values, norm.astype(jnp.float32))
    normed_low = normed.astype(jnp.bfloat16)
    mixed = (
        product(normed_low, mixer)
        .astype(jnp.bfloat16)
        .reshape(length, 3, HEADS, HEAD_DIM)
        .transpose(1, 2, 0, 3)
    )
    lines, choose = relative_lines(table, buckets)
    same = marks[:, None] == marks[None, :]

    def head_forward(items):
        query, keys_head, contents, line = items
        scores = head_scores(query, keys_head, line, same)
        peak = jnp.max(scores, axis=1, keepdims=True)
        raised = jnp.exp(scores - peak)
        total = jnp.sum(raised, axis=1, keepdims=True)
        probs = (raised / total).astype(jnp.bfloat16)
        return (product(probs, contents).astype(jnp.bfloat16), (peak + jnp.log(total))[:, 0])

    attended, logsum = lax.map(head_forward, (mixed[0], mixed[1], mixed[2], lines))
    joined = attended.transpose(1, 0, 2).reshape(length, D)
    result = values + product(joined, weight_out) + bias_out.astype(jnp.float32)
    return (result, (normed_low, mixed, lines, choose, same, joined, logsum, norm_back))


def plain_attention_backward(upstream, weights, saved):
    norm, mixer, weight_out, bias_out, table = weights
    normed_low, mixed, lines, choose, same, joined, logsum, norm_back = saved
    length = upstream.shape[0]
    upstream_low = upstream.astype(jnp.bfloat16)
    grad_weight_out = product_left(joined, upstream_low)
    grad_joined = (
        product_right(upstream_low, weight_out)
        .astype(jnp.bfloat16)
        .reshape(length, HEADS, HEAD_DIM)
        .transpose(1, 0, 2)
    )

    def head_backward(items):
        query, keys_head, contents, line, incoming, logs = items
        scores = head_scores(query, keys_head, line, same)
        probs = jnp.exp(scores - logs[:, None])
        grad_contents = product_left(probs.astype(jnp.bfloat16), incoming)
        grad_probs = product_right(incoming, contents)
        grad_scores = probs * (grad_probs - jnp.sum(grad_probs * probs, axis=1, keepdims=True))
        scaled = (grad_scores * HEAD_DIM ** (-0.5)).astype(jnp.bfloat16)
        grad_query = product(scaled, keys_head)
        grad_keys = product_left(scaled, query)
        return (
            jnp.stack([grad_query, grad_keys, grad_contents]).astype(jnp.bfloat16),
            diagonal_sums(grad_scores),
        )

    grad_mixed, grad_lines = lax.map(
        head_backward, (mixed[0], mixed[1], mixed[2], lines, grad_joined, logsum)
    )
    grad_flat = grad_mixed.transpose(2, 1, 0, 3).reshape(length, 3 * D)
    grad_mixer = product_left(normed_low, grad_flat)
    grad_values, grad_norm = norm_back(product_right(grad_flat, mixer))
    grad_table = jnp.dot(grad_lines, choose.T, precision=highest).reshape(-1)
    return (
        upstream + grad_values,
        (grad_norm, grad_mixer, grad_weight_out, jnp.sum(upstream, axis=0), grad_table),
    )


def gate_unit(joined):
    width = joined.shape[1] // 2
    return joined[:, :width] * jax.nn.sigmoid(joined[:, width:])


def plain_depthwise(gated, kernel, marks):
    length = gated.shape[0]
    half = kernel.shape[0] // 2
    padded = jnp.pad(gated, ((half, half), (0, 0)))
    bounds = jnp.pad(marks, (half, half), constant_values=-1)
    total = jnp.zeros(gated.shape, gated.dtype)
    for step in range(kernel.shape[0]):
        same = (bounds[step : step + length] == marks)[:, None]
        total = total + jnp.where(same, padded[step : step + length], 0.0) * kernel[step]
    return total


def plain_conv_forward(values, weights, marks, frames):
    norm, weight_glu, bias_glu, kernel, batch, weight_out, bias_out, final = weights
    normed, norm_back = jax.vjp(layer_norm, values, norm.astype(jnp.float32))
    normed_low = normed.astype(jnp.bfloat16)
    joined = product(normed_low, weight_glu) + bias_glu.astype(jnp.float32)
    gated, gate_back = jax.vjp(gate_unit, joined)
    middle, depth_back = jax.vjp(
        lambda inner, taps: plain_depthwise(inner, taps, marks), gated, kernel.astype(jnp.float32)
    )
    sums = lax.psum((jnp.sum(middle, axis=0), jnp.sum(middle * middle, axis=0)), ("dp", "fsdp"))
    center = sums[0] / frames
    inverse = lax.rsqrt(sums[1] / frames - center * center + epsilon)
    gain = 1.0 + batch[0].astype(jnp.float32)
    unit = (middle - center) * inverse
    normal = unit * gain + batch[1].astype(jnp.float32)
    active = jax.nn.silu(normal).astype(jnp.bfloat16)
    result = values + product(active, weight_out) + bias_out.astype(jnp.float32)
    return (
        result,
        (normed_low, gate_back, depth_back, inverse, gain, unit, normal, active, norm_back),
    )


def plain_conv_backward(upstream, weights, saved, frames):
    norm, weight_glu, bias_glu, kernel, batch, weight_out, bias_out, final = weights
    normed_low, gate_back, depth_back, inverse, gain, unit, normal, active, norm_back = saved
    upstream_low = upstream.astype(jnp.bfloat16)
    grad_weight_out = product_left(active, upstream_low)
    grad_normal = product_right(upstream_low, weight_out) * silu_slope(normal)
    sums = lax.psum(
        (jnp.sum(grad_normal, axis=0), jnp.sum(grad_normal * unit, axis=0)), ("dp", "fsdp")
    )
    grad_middle = inverse * (
        grad_normal * gain - gain * sums[0] / frames - unit * (gain * sums[1] / frames)
    )
    grad_gated, grad_kernel = depth_back(grad_middle)
    grad_joined = gate_back(grad_gated)[0]
    joined_low = grad_joined.astype(jnp.bfloat16)
    grad_weight_glu = product_left(normed_low, joined_low)
    grad_values, grad_norm = norm_back(product_right(joined_low, weight_glu))
    grad_batch = jnp.stack([sums[1], sums[0]])
    return (
        upstream + grad_values,
        (
            grad_norm,
            grad_weight_glu,
            jnp.sum(grad_joined, axis=0),
            grad_kernel,
            grad_weight_out,
            jnp.sum(upstream, axis=0),
        ),
        grad_batch,
    )


def plain(
    inputs,
    segments,
    buckets,
    cotangent,
    ffn_norm,
    ffn_in,
    ffn_in_bias,
    ffn_out,
    ffn_out_bias,
    attn_norm,
    qkv_weight,
    attn_out,
    attn_out_bias,
    rel_table,
    conv_norm,
    glu_weight,
    glu_bias,
    depth_kernel,
    batch_norm,
    conv_out,
    conv_out_bias,
    final_norm,
):
    values = inputs[0].astype(jnp.float32)
    marks = segments[0]
    devices = lax.axis_size(("dp", "fsdp"))
    frames = values.shape[0] * devices
    feed_first = plain_fetch_feed(ffn_norm, ffn_in, ffn_in_bias, ffn_out, ffn_out_bias, 0)
    first, first_saved = plain_feed_forward(values, feed_first)
    attn_weights = fetch_attention(attn_norm, qkv_weight, attn_out, attn_out_bias, rel_table)
    second, attn_saved = plain_attention_forward(first, attn_weights, marks, buckets)
    conv_weights = fetch_conv(
        conv_norm,
        glu_weight,
        glu_bias,
        depth_kernel,
        batch_norm,
        conv_out,
        conv_out_bias,
        final_norm,
    )
    third, conv_saved = plain_conv_forward(second, conv_weights, marks, frames)
    feed_second = plain_fetch_feed(ffn_norm, ffn_in, ffn_in_bias, ffn_out, ffn_out_bias, 1)
    fourth, second_saved = plain_feed_forward(third, feed_second)
    result, final_back = jax.vjp(layer_norm, fourth, conv_weights[7].astype(jnp.float32))
    grad_fourth, grad_final = final_back(cotangent[0].astype(jnp.float32))
    second_back = plain_fetch_feed(ffn_norm, ffn_in, ffn_in_bias, ffn_out, ffn_out_bias, 1)
    grad_third, second_grads = plain_feed_backward(grad_fourth, second_back, second_saved)
    conv_back = fetch_conv(
        conv_norm,
        glu_weight,
        glu_bias,
        depth_kernel,
        batch_norm,
        conv_out,
        conv_out_bias,
        final_norm,
    )
    grad_second, conv_grads, grad_batch = plain_conv_backward(grad_third, conv_back, conv_saved, frames)
    attn_back = fetch_attention(attn_norm, qkv_weight, attn_out, attn_out_bias, rel_table)
    grad_first, attn_grads = plain_attention_backward(grad_second, attn_back, attn_saved)
    first_back = plain_fetch_feed(ffn_norm, ffn_in, ffn_in_bias, ffn_out, ffn_out_bias, 0)
    grad_start, first_grads = plain_feed_backward(grad_first, first_back, first_saved)
    first_shards = plain_reduce_feed(first_grads)
    second_shards = plain_reduce_feed(second_grads)
    attn_shards = (
        lax.psum_scatter(attn_grads[0], ("dp", "fsdp"), scatter_dimension=1, tiled=True),
        lax.psum_scatter(attn_grads[1], ("dp", "fsdp"), scatter_dimension=0, tiled=True),
        lax.psum_scatter(attn_grads[2], ("dp", "fsdp"), scatter_dimension=0, tiled=True),
        lax.psum_scatter(attn_grads[3], ("dp", "fsdp"), scatter_dimension=0, tiled=True),
        lax.psum_scatter(attn_grads[4], ("dp", "fsdp"), scatter_dimension=0, tiled=True),
    )
    conv_shards = (
        lax.psum_scatter(conv_grads[0], ("dp", "fsdp"), scatter_dimension=1, tiled=True),
        lax.psum_scatter(conv_grads[1], ("dp", "fsdp"), scatter_dimension=0, tiled=True),
        lax.psum_scatter(conv_grads[2], ("dp", "fsdp"), scatter_dimension=0, tiled=True),
        lax.psum_scatter(conv_grads[3], ("dp", "fsdp"), scatter_dimension=1, tiled=True),
        lax.psum_scatter(conv_grads[4], ("dp", "fsdp"), scatter_dimension=0, tiled=True),
        lax.psum_scatter(conv_grads[5], ("dp", "fsdp"), scatter_dimension=0, tiled=True),
        lax.psum_scatter(grad_final, ("dp", "fsdp"), scatter_dimension=1, tiled=True),
    )
    width = D // devices
    batch_shard = lax.dynamic_slice_in_dim(
        grad_batch, lax.axis_index(("dp", "fsdp")) * width, width, 1
    )
    return (
        result[None].astype(jnp.bfloat16),
        grad_start[None],
        jnp.stack([first_shards[0], second_shards[0]]),
        jnp.stack([first_shards[1], second_shards[1]]),
        jnp.stack([first_shards[2], second_shards[2]]),
        jnp.stack([first_shards[3], second_shards[3]]),
        jnp.stack([first_shards[4], second_shards[4]]),
        attn_shards[0],
        attn_shards[1],
        attn_shards[2],
        attn_shards[3],
        attn_shards[4],
        conv_shards[0],
        conv_shards[1],
        conv_shards[2],
        conv_shards[3],
        batch_shard,
        conv_shards[4],
        conv_shards[5],
        conv_shards[6],
    )


def solution(mesh):
    in_specs = (
        P(("dp", "fsdp"), None, None),
        P(("dp", "fsdp"), None),
        P(),
        P(("dp", "fsdp"), None, None),
        P(None, None, ("dp", "fsdp")),
        P(None, ("dp", "fsdp"), None),
        P(None, ("dp", "fsdp")),
        P(None, ("dp", "fsdp"), None),
        P(None, ("dp", "fsdp")),
        P(None, ("dp", "fsdp")),
        P(("dp", "fsdp"), None),
        P(("dp", "fsdp"), None),
        P(("dp", "fsdp")),
        P(("dp", "fsdp")),
        P(None, ("dp", "fsdp")),
        P(("dp", "fsdp"), None),
        P(("dp", "fsdp")),
        P(None, ("dp", "fsdp")),
        P(None, ("dp", "fsdp")),
        P(("dp", "fsdp"), None),
        P(("dp", "fsdp")),
        P(None, ("dp", "fsdp")),
    )
    out_specs = (
        P(("dp", "fsdp"), None, None),
        P(("dp", "fsdp"), None, None),
        P(None, None, ("dp", "fsdp")),
        P(None, ("dp", "fsdp"), None),
        P(None, ("dp", "fsdp")),
        P(None, ("dp", "fsdp"), None),
        P(None, ("dp", "fsdp")),
        P(None, ("dp", "fsdp")),
        P(("dp", "fsdp"), None),
        P(("dp", "fsdp"), None),
        P(("dp", "fsdp")),
        P(("dp", "fsdp")),
        P(None, ("dp", "fsdp")),
        P(("dp", "fsdp"), None),
        P(("dp", "fsdp")),
        P(None, ("dp", "fsdp")),
        P(None, ("dp", "fsdp")),
        P(("dp", "fsdp"), None),
        P(("dp", "fsdp")),
        P(None, ("dp", "fsdp")),
    )
    fast = mesh.shape["dp"] == 4 and mesh.shape["fsdp"] == 8
    return jax.shard_map(local if fast else plain, mesh=mesh, in_specs=in_specs, out_specs=out_specs, check_vma=False)
```

```python
import math

import jax
import jax.numpy as jnp
from jax import lax
from jax.experimental import pallas as pl
from jax.experimental.pallas import tpu as pltpu
from jax.sharding import PartitionSpec as P

D = 512
FF = 2048
HEADS = 8
HEAD_DIM = 64
BUCKETS = 32
L = 512
TAPS = 32
PAD = 16
epsilon = 1e-05
F32, BF16 = jnp.float32, jnp.bfloat16
MESH = pl.DeviceIdType.MESH

SMALL, IN0, OUT0, QKV, ATT, GLU, CONV, IN1, OUT1, ROWS = 0, 16, 80, 144, 192, 208, 240, 256, 320, 384
GRADS = ROWS - IN0
(S_FFN, S_FOB, S_ATTN, S_AOB, S_CONV, S_BATCH, S_COB, S_FINAL, S_TAPS, S_ROWS) = (0, 4, 6, 8, 9, 11, 13, 14, 16, 48)
CHUNK = 64
BLOCK = 128
SOFT = 32
UNROLL = True


def dot(a, b):
    return jnp.dot(a, b, preferred_element_type=F32)


def dot_nt(a, b):
    return lax.dot_general(a, b, (((1,), (1,)), ((), ())), preferred_element_type=F32)


def dot_tn(a, b):
    return lax.dot_general(a, b, (((0,), (0,)), ((), ())), preferred_element_type=F32)


def chunks(body, carry=None, size=CHUNK):
    def step(i, carry):
        return body(pl.ds(pl.multiple_of(i * size, size), size), carry)

    return lax.fori_loop(0, L // size, step, carry, unroll=True)


def fold(values):
    return jnp.sum(values.reshape(values.shape[0] // 8, 8, values.shape[1]), axis=0)


def zeros8(width=D):
    return jnp.zeros((8, width), F32)


def total_row(values):
    return jnp.sum(values, axis=0, keepdims=True)


class Bag:
    pass


class Place:
    def __init__(self):
        self.planes = lax.axis_size("dp")
        self.chips = lax.axis_size("fsdp") // 2
        self.plane, inner = lax.axis_index("dp"), lax.axis_index("fsdp")
        self.z, self.core = inner // 2, inner % 2
        y, x = self.plane // 2, self.plane % 2
        self.plane_x, self.plane_y, self.plane_d = y * 2 + 1 - x, (1 - y) * 2 + x, (1 - y) * 2 + 1 - x
        self.twin = (self.plane, 2 * self.z + 1 - self.core)
        self.over_x = (self.plane_x, inner)
        self.over_y = (self.plane_y, inner)
        self.chip = [lax.rem(self.z + step, self.chips) for step in range(self.chips)]
        self.along = [(self.plane, 2 * chip + self.core) for chip in self.chip]
        self.rank = self.plane * 2 + self.core
        self.members = []
        for step in range(self.planes):
            for flip in range(2):
                if step or flip:
                    plane, core = lax.rem(self.plane + step, self.planes), lax.rem(self.core + flip, 2)
                    self.members.append(((plane, 2 * self.z + core), plane * 2 + core))


class Copies:
    def __init__(self, sends, receives, place):
        self.sends, self.receives, self.place = sends, receives, place
        self.begun = []

    def start(self, number, make, receive=None):
        def copy():
            source, target, device = make()
            return pltpu.make_async_remote_copy(
                source, target, self.sends.at[number], self.receives.at[number if receive is None else receive],
                device_id=device, device_id_type=MESH,
            )

        copy().start()
        self.begun.append(copy)

    def arrived(self, number, target):
        pltpu.make_async_remote_copy(
            target, target, self.sends.at[number], self.receives.at[number],
            device_id=self.place.twin, device_id_type=MESH,
        ).wait_recv()

    def sent(self):
        for copy in self.begun:
            copy().wait_send()
        self.begun = []


class Gather:
    def __init__(self, place, weights, copies, first, begin, size, split):
        self.place, self.weights, self.copies, self.first = place, weights, copies, first
        self.rows = pl.ds(begin, size)
        self.parts = (pl.ds(begin, split), pl.ds(begin + split, size - split))
        chips = place.chips
        self.x, self.y, self.d, self.t = chips, 2 * chips, 3 * chips, 3 * chips + 2

    @staticmethod
    def semaphores(chips):
        return 3 * chips + 6

    def column(self, plane, side, which):
        return self.weights.at[plane, :, side, which]

    def slot(self, plane, step):
        p = self.place
        return self.weights.at[plane, p.chip[(p.chips - step) % p.chips], p.core, self.rows]

    def move(self, number, ref, device):
        self.copies.start(self.first + number, lambda: (ref(), ref(), device))

    def arrived(self, number, ref):
        self.copies.arrived(self.first + number, ref)

    def along_z(self):
        p = self.place
        for d in range(1, p.chips):
            self.move(d, lambda: self.slot(p.plane, 0), p.along[d])

    def beside(self, step):
        p = self.place
        self.move(self.x + step, lambda: self.slot(p.plane, step), p.over_x)
        self.move(self.y + step, lambda: self.slot(p.plane, step), p.over_y)

    def own(self):
        self.beside(0)

    def forward(self):
        p = self.place
        for d in range(1, p.chips):
            self.arrived(d, self.slot(p.plane, d))
            self.beside(d)
        self.move(self.t, lambda: self.column(p.plane, p.core, self.rows), p.twin)

    def turn(self):
        p = self.place
        for d in range(p.chips):
            self.arrived(self.x + d, self.slot(p.plane_x, d))
        self.move(self.d, lambda: self.column(p.plane_x, p.core, self.parts[0]), p.over_y)
        for d in range(p.chips):
            self.arrived(self.y + d, self.slot(p.plane_y, d))
        self.move(self.d + 1, lambda: self.column(p.plane_y, p.core, self.parts[1]), p.over_x)
        self.move(self.t + 1, lambda: self.column(p.plane_x, p.core, self.rows), p.twin)
        self.move(self.t + 2, lambda: self.column(p.plane_y, p.core, self.rows), p.twin)

    def across(self):
        p = self.place
        self.arrived(self.d, self.column(p.plane_d, p.core, self.parts[0]))
        self.arrived(self.d + 1, self.column(p.plane_d, p.core, self.parts[1]))
        self.move(self.t + 3, lambda: self.column(p.plane_d, p.core, self.rows), p.twin)

    def done(self):
        p = self.place
        for number, plane in enumerate((p.plane, p.plane_x, p.plane_y, p.plane_d)):
            self.arrived(self.t + number, self.column(plane, 1 - p.core, self.rows))


def reduce_steps(place, data, twin, diagonal, from_x, from_y, from_z, copies, first, begin, size, split, landing, finish):
    p, core, chips = place, place.core, place.chips
    rows, lands = pl.ds(begin, size), pl.ds(landing, size)
    parts = (pl.ds(begin, split), pl.ds(begin + split, size - split))
    parts_land = (pl.ds(landing, split), pl.ds(landing + split, size - split))

    def column(plane, side, which):
        return data.at[plane, :, side, which]

    def add(plane, which, *sources):
        def step(zz, carry):
            value = data[plane, zz, core, which, :]
            for ref in sources:
                value = value + ref(zz)
            data[plane, zz, core, which, :] = value
            return carry

        lax.fori_loop(0, chips, step, 0, unroll=True)

    def read(ref, which, *lead):
        return lambda zz: ref[lead + (zz, which, slice(None))]

    def to_twin():
        for number, plane in enumerate((p.plane_d, p.plane_y, p.plane_x, p.plane)):
            copies.start(
                first + number, lambda plane=plane: (column(plane, 1 - core, rows), twin.at[plane, :, lands], p.twin)
            )

    def across():
        copies.arrived(first, twin.at[p.plane_d, :, lands])
        add(p.plane_d, rows, read(twin, lands, p.plane_d))
        copies.start(first + 4, lambda: (column(p.plane_d, core, parts[0]), diagonal.at[:, parts_land[0]], p.over_y))
        if split < size:
            copies.start(first + 5, lambda: (column(p.plane_d, core, parts[1]), diagonal.at[:, parts_land[1]], p.over_x))

    def beside():
        copies.arrived(first + 2, twin.at[p.plane_x, :, lands])
        copies.arrived(first + 4, diagonal.at[:, parts_land[0]])
        add(p.plane_x, rows, read(twin, lands, p.plane_x))
        add(p.plane_x, parts[0], read(diagonal, parts_land[0]))
        copies.start(first + 7, lambda: (column(p.plane_x, core, rows), from_x.at[:, lands], p.over_x))
        copies.arrived(first + 1, twin.at[p.plane_y, :, lands])
        add(p.plane_y, rows, read(twin, lands, p.plane_y))
        if split < size:
            copies.arrived(first + 5, diagonal.at[:, parts_land[1]])
            add(p.plane_y, parts[1], read(diagonal, parts_land[1]))
        copies.start(first + 6, lambda: (column(p.plane_y, core, rows), from_y.at[:, lands], p.over_y))

    def own_column():
        copies.arrived(first + 3, twin.at[p.plane, :, lands])
        copies.arrived(first + 6, from_y.at[:, lands])
        copies.arrived(first + 7, from_x.at[:, lands])
        add(p.plane, rows, read(twin, lands, p.plane), read(from_x, lands), read(from_y, lands))
        for d in range(1, chips):
            copies.start(
                first + 7 + d,
                lambda d=d: (data.at[p.plane, p.chip[d], core, rows], from_z.at[d - 1, lands], p.along[d]),
            )

    def along_z():
        for d in range(1, chips):
            copies.arrived(first + 7 + d, from_z.at[d - 1, lands])
        value = data[p.plane, p.z, core, rows, :].astype(F32)
        for d in range(1, chips):
            value = value + from_z[d - 1, lands, :].astype(F32)
        finish(value)

    return [to_twin, across, beside, own_column, along_z]


class Thin:
    def __init__(self, place, tiles, near, part, far, result, copies, first):
        self.place, self.tiles, self.near, self.part, self.far, self.result = place, tiles, near, part, far, result
        self.copies, self.first = copies, first

    def start(self):
        p = self.place
        for i, (device, rank) in enumerate(p.members):
            self.copies.start(
                self.first + i,
                lambda device=device: (self.tiles.at[device[0], :, lax.rem(device[1], 2)], self.near.at[p.rank], device),
                self.first + p.rank,
            )
        self.near[p.rank] = self.tiles[p.plane, :, p.core]

    def turn(self):
        p = self.place
        for device, rank in p.members:
            self.copies.arrived(self.first + rank, self.near.at[rank])
        value = self.near[0]
        for i in range(1, 2 * p.planes):
            value = value + self.near[i]
        self.part[...] = value
        base = self.first + 2 * p.planes
        for d in range(1, p.chips):
            self.copies.start(base + d, lambda d=d: (self.part.at[p.chip[d]], self.far.at[d], p.along[d]))

    def finish(self):
        p = self.place
        base = self.first + 2 * p.planes
        value = self.part[p.z]
        for d in range(1, p.chips):
            self.copies.arrived(base + d, self.far.at[d])
            value = value + self.far[d]
        self.result[...] = value


class Total:
    def __init__(self, place, own, near, part, far, result, copies, first):
        self.place, self.own, self.near, self.part, self.far, self.result = place, own, near, part, far, result
        self.copies, self.first = copies, first

    def start(self):
        p = self.place
        me = p.rank
        for i, (device, rank) in enumerate(p.members):
            self.copies.start(self.first + i, lambda device=device: (self.own, self.near.at[me], device), self.first + me)
        self.near[me] = self.own[...]

    def turn(self):
        p = self.place
        for device, rank in p.members:
            self.copies.arrived(self.first + rank, self.near.at[rank])
        value = self.near[0]
        for i in range(1, 2 * p.planes):
            value = value + self.near[i]
        self.part[...] = value
        base = self.first + 2 * p.planes
        for d in range(1, p.chips):
            self.copies.start(base + d, lambda d=d: (self.part, self.far.at[d], p.along[d]))

    def finish(self):
        p = self.place
        base = self.first + 2 * p.planes
        value = self.part[...]
        for d in range(1, p.chips):
            self.copies.arrived(base + d, self.far.at[d])
            value = value + self.far[d]
        self.result[...] = value


def at_points(table):
    def pump(index, place=0):
        for (iteration, where), steps in table.items():
            if where != place or (isinstance(index, int) and index != iteration):
                continue

            def act(steps=steps):
                for step in steps:
                    step()

            if isinstance(index, int):
                act()
            else:
                pl.when(index == iteration)(act)

    return pump


def still(index, place=0):
    pass


def standard(values):
    values = values.astype(F32)
    center = values - jnp.mean(values, axis=-1, keepdims=True)
    inverse = lax.rsqrt(jnp.mean(center * center, axis=-1, keepdims=True) + epsilon)
    return center * inverse, inverse


def norm_rows(source, target, small, row):
    gain, shift = 1.0 + small[row : row + 1, :], small[row + 1 : row + 2, :]

    def body(rows, carry):
        target[rows, :] = (standard(source[rows, :])[0] * gain + shift).astype(target.dtype)
        return carry

    chunks(body, 0)


def norm_back(source, grad, upstream, result, small, row, grads):
    gain = 1.0 + small[row : row + 1, :]

    def body(rows, carry):
        unit, inverse = standard(source[rows, :])
        given = grad[rows, :].astype(F32)
        inner = given * gain
        back = inverse * (
            inner
            - jnp.mean(inner, axis=-1, keepdims=True)
            - unit * jnp.mean(inner * unit, axis=-1, keepdims=True)
        )
        result[rows, :] = back if upstream is None else upstream[rows, :] + back
        return carry[0] + fold(given * unit), carry[1] + fold(given)

    first, second = chunks(body, (zeros8(), zeros8()))
    grads[row : row + 1, :] = total_row(first)
    grads[row + 1 : row + 2, :] = total_row(second)


def block_cols(c):
    return pl.ds(c * D if isinstance(c, int) else pl.multiple_of(c * D, D), D)


def columns(weights, start, block):
    return weights[:, :, :, start + 16 * block : start + 16 * block + 16, :].reshape(D, D)


def put_columns(weights, start, block, value):
    rows = pl.ds(start + 16 * block, 16)
    weights[:, :, :, rows, :] = value.astype(BF16).reshape(weights.shape[:3] + (16, D))


def lines_of(weights, start, block):
    return weights[block, :, :, start : start + 64, :].reshape(D, D)


def put_lines(weights, start, block, value):
    weights[block, :, :, start : start + 64, :] = value.astype(BF16).reshape(weights.shape[1:3] + (64, D))


def feed_inner(source, normed, active, slope, raws, weights, small, inner_bias, layer, pump):
    norm_rows(source, normed, small, S_FFN + 2 * layer)
    for c in range(FF // D):
        pump(c)
        cols, raw = block_cols(c), raws[c % 2]
        raw[...] = dot(normed[...], columns(weights, (IN0, IN1)[layer], c))
        bias = inner_bias[layer : layer + 1, cols]

        def body(rows, carry, cols=cols, raw=raw, bias=bias):
            inner = raw[rows, :] + bias
            sigma = jax.nn.sigmoid(inner)
            value = inner * sigma
            active[rows, cols] = value.astype(BF16)
            slope[rows, cols] = (sigma + value * (1.0 - sigma)).astype(BF16)
            return carry

        chunks(body, 0)


def feed_outer(source, active, result, hold, weights, small, layer):
    begin = (OUT0, OUT1)[layer]
    hold[...] = dot(active[...], weights[:, :, :, begin : begin + 64, :].reshape(FF, D))
    bias = small[S_FOB + layer : S_FOB + layer + 1, :]

    def body(rows, carry):
        result[rows, :] = source[rows, :].astype(F32) + 0.5 * (hold[rows, :] + bias)
        return carry

    chunks(body, 0)


def feed_back_start(upstream, low, grads, layer):
    def start(rows, carry):
        half = 0.5 * upstream[rows, :]
        low[rows, :] = half.astype(BF16)
        return carry + fold(half)

    grads[S_FOB + layer : S_FOB + layer + 1, :] = total_row(chunks(start, zeros8()))


def feed_back_outer(active, low, weights, begin, pump):
    for c in range(FF // D):
        put_lines(weights, begin, c, dot_tn(active[:, block_cols(c)], low[...]))
        pump(c)


def feed_back_inner(normed, slope, low, raws, weights, target, inner_grads, layer, pump):
    begin = (OUT0, OUT1)[layer]
    for c in range(FF // D):
        cols, raw = block_cols(c), raws[c % 2]
        raw[...] = dot_nt(low[...], lines_of(weights, begin, c))

        def body(rows, carry, cols=cols, raw=raw):
            grad = raw[rows, :] * slope[rows, cols].astype(F32)
            slope[rows, cols] = grad.astype(BF16)
            return carry + fold(grad)

        inner_grads[layer : layer + 1, cols] = total_row(chunks(body, zeros8()))
        if target is not None:
            put_columns(weights, target, c, dot_tn(normed[...], slope[:, cols]))
        pump(c)


def product_back(grad, normed, total, weights, begin, blocks, pump):
    value = None
    for c in range(blocks):
        part = dot_nt(grad[:, block_cols(c)], columns(weights, begin, c))
        value = part if value is None else value + part
    total[...] = value
    for c in range(blocks):
        if normed is not None:
            put_columns(weights, begin, c, dot_tn(normed[...], grad[:, block_cols(c)]))
        pump(c)


def bucket_choice(buckets):
    return (lax.broadcasted_iota(jnp.int32, (BUCKETS, 2 * L), 0) == buckets[...]).astype(F32)


def attention_mix(source, normed, mixed, weights, small):
    norm_rows(source, normed, small, S_ATTN)

    for c in range(3):
        mixed[:, block_cols(c)] = dot(normed[...], columns(weights, QKV, c)).astype(BF16)


def attention_mask(mask, bounds, marks):
    def body(rows, carry):
        same = bounds[pl.ds(rows.start + PAD, CHUNK), 0:1] == marks[...]
        mask[rows, :] = jnp.where(same, 3e38, -1e30)
        return carry

    chunks(body, 0)


def attention_squares(lines, squares, table, buckets):
    lines[...] = dot(table[...].astype(BF16), bucket_choice(buckets).astype(BF16))

    def head(h, carry):
        line = jnp.broadcast_to(lines[pl.ds(h, 1), :], (BLOCK, 2 * L))
        square = pltpu.roll(line, 2 * L - BLOCK + 1, 1, stride=1, stride_axis=0).astype(BF16)
        for part in range(2):
            squares[lax.rem(h, 4), lax.div(h, 4), part * BLOCK : (part + 1) * BLOCK, :] = square[:, part * L : (part + 1) * L]
        return carry

    lax.fori_loop(0, HEADS, head, 0)


def attention_forward(source, mixed, probs, joined, recips, result, squares, mask, hold, hold2, weights, small, pump):
    lane = lax.broadcasted_iota(jnp.int32, (1, 128), 1)

    def pair(index, carry):
        begin = pl.multiple_of(128 * index, 128)
        query = mixed[:, pl.ds(begin, 128)] * HEAD_DIM ** (-0.5)
        keys = mixed[:, pl.ds(D + begin, 128)]
        contents = mixed[:, pl.ds(2 * D + begin, 128)]
        parts = []
        for half, raw in enumerate((hold, hold2)):
            here = (lane // HEAD_DIM) == half
            raw[...] = dot_nt(jnp.where(here, query, jnp.zeros_like(query)), keys)
        for half, raw in enumerate((hold, hold2)):
            head = 2 * index + half
            here = (lane // HEAD_DIM) == half
            for block in range(L // BLOCK):

                def body(i, carry, block=block, raw=raw, head=head):
                    at = pl.multiple_of(i * SOFT, SOFT)
                    rows = pl.ds(block * BLOCK + at, SOFT)
                    square = squares[lax.rem(head, 4), lax.div(head, 4), pl.ds(at, SOFT), 384 - block * BLOCK : L]
                    if block < L // BLOCK - 1:
                        more = squares[lax.rem(head, 4), lax.div(head, 4), pl.ds(BLOCK + at, SOFT), 0 : 384 - block * BLOCK]
                        square = jnp.concatenate([square, more], axis=1)
                    scores = jnp.minimum(raw[rows, :] + square.astype(F32), mask[rows, :])
                    probs[head, rows, :] = jnp.exp(scores - jnp.max(scores, axis=1, keepdims=True)).astype(BF16)
                    return carry

                lax.fori_loop(0, BLOCK // SOFT, body, 0, unroll=UNROLL)
                if half:
                    pump(index, block)
            parts.append(dot(probs[head], jnp.where(here, contents, jnp.ones_like(contents))))
        value = jnp.where(lane < HEAD_DIM, parts[0], parts[1])
        sums = jnp.where(lane < HEAD_DIM, pltpu.roll(parts[0], HEAD_DIM, 1), pltpu.roll(parts[1], HEAD_DIM, 1))
        recip = 1.0 / sums
        recips[:, pl.ds(begin, 128)] = recip
        joined[:, pl.ds(begin, 128)] = value * recip
        return carry

    lax.fori_loop(0, HEADS // 2, pair, 0)
    hold[...] = dot(joined[...].astype(BF16), columns(weights, ATT, 0))
    bias = small[S_AOB : S_AOB + 1, :]

    def body(rows, carry):
        result[rows, :] = source[rows, :] + hold[rows, :] + bias
        return carry

    chunks(body, 0)


def attention_back_start(upstream, joined, recips, low, spread, hold, weights, grads):
    def start(rows, carry):
        given = upstream[rows, :]
        low[rows, :] = given.astype(BF16)
        return carry + fold(given)

    grads[S_AOB : S_AOB + 1, :] = total_row(chunks(start, zeros8()))
    hold[...] = dot_nt(low[...], columns(weights, ATT, 0))

    def body(rows, carry):
        spread[rows, :] = (hold[rows, :] * recips[rows, :]).astype(BF16)
        return carry

    chunks(body, 0)
    put_columns(weights, ATT, 0, dot_tn(joined[...].astype(BF16), low[...]))


def attention_backward(mixed, probs, spread, joined, grad_mixed, scaled, hold, hold2, means, diagonals, lines, buckets, table_grad, pump):
    lane = lax.broadcasted_iota(jnp.int32, (1, 128), 1)
    sides = lax.broadcasted_iota(jnp.int32, (256, 256), 0) // HEAD_DIM % 2 == lax.broadcasted_iota(jnp.int32, (256, 256), 1) // 128
    sides = jnp.where(sides, 1.0, 0.0).astype(BF16)

    def pair(index, carry):
        begin = pl.multiple_of(128 * index, 128)
        query = mixed[:, pl.ds(begin, 128)]
        keys = mixed[:, pl.ds(D + begin, 128)]
        contents = mixed[:, pl.ds(2 * D + begin, 128)]
        incoming = spread[:, pl.ds(begin, 128)]
        for half, raw in enumerate((hold, hold2)):
            here = (lane // HEAD_DIM) == half
            raw[...] = dot_nt(jnp.where(here, incoming, jnp.zeros_like(incoming)), contents)
        both = incoming.astype(F32) * joined[:, pl.ds(begin, 128)]
        upper = both.astype(BF16)
        lower = (both - upper.astype(F32)).astype(BF16)
        means[:, 0:256] = dot(jnp.concatenate([upper, lower], axis=1), sides)
        turned_query, turned_incoming = query.T, incoming.T
        grads_query, grads_keys, grads_contents = [], [], []
        for half, raw in enumerate((hold, hold2)):
            head = 2 * index + half
            side = slice(half * HEAD_DIM, (half + 1) * HEAD_DIM)
            cols = pl.ds(half * L, L)
            part = zeros8(2 * L)
            for u in range(BLOCK // 16):
                tiles = [None] * 7 + [jnp.zeros((16, 128), F32)]
                for block in range(L // BLOCK):
                    rows = pl.ds(block * BLOCK + 16 * u, 16)
                    mean = means[rows, 128 * half : 128 * half + 128]
                    slant = probs[head, rows, :].astype(F32) * (raw[rows, :] - jnp.concatenate([mean] * 4, axis=1))
                    scaled[rows, cols] = slant.astype(BF16)
                    for j in range(4):
                        piece = slant[:, 128 * j : 128 * j + 128]
                        at = 3 - block + j
                        tiles[at] = piece if tiles[at] is None else tiles[at] + piece
                full = jnp.concatenate(tiles, axis=1)
                part = part + pltpu.roll(full[0:8], BLOCK - 8 - 16 * u, 1) + pltpu.roll(full[8:16], BLOCK - 16 - 16 * u, 1)
            diagonals[:, pl.ds(head, 1), :] = part.reshape(8, 1, 2 * L)
            grads_query.append(dot(scaled[:, cols], keys))
            grads_keys.append(dot(turned_query[side], scaled[:, cols]))
            grads_contents.append(dot(turned_incoming[side], probs[head]))
            pump(index, half)
        scale = HEAD_DIM ** (-0.5)
        grad_mixed[:, pl.ds(begin, 128)] = (jnp.where(lane < HEAD_DIM, *grads_query) * scale).astype(BF16)
        grad_mixed[:, pl.ds(D + begin, 128)] = (jnp.concatenate(grads_keys, axis=0).T * scale).astype(BF16)
        grad_mixed[:, pl.ds(2 * D + begin, 128)] = jnp.concatenate(grads_contents, axis=0).T.astype(BF16)
        return carry

    lax.fori_loop(0, HEADS // 2, pair, 0)
    line = diagonals[7]
    for r in range(7):
        line = line + pltpu.roll(diagonals[r], 7 - r, 1)
    table_grad[...] = lax.dot_general(
        line, bucket_choice(buckets), (((1,), (1,)), ((), ())),
        precision=lax.Precision.HIGHEST, preferred_element_type=F32,
    )


def clear_pads(padded):
    edge = jnp.zeros((4, PAD, 128), F32)
    padded[:, 0:PAD, :] = edge
    padded[:, PAD + L : 2 * PAD + L, :] = edge


def conv_front(source, normed, sigma, tilt, gated, middle, sums, hold, spare, weights, small, gate_bias, bounds, pump):
    norm_rows(source, normed, small, S_CONV)
    clear_pads(gated)
    hold[...] = dot(normed[...], columns(weights, GLU, 1))
    bias = gate_bias[0:1, D:]

    def gate(rows, carry):
        gate = jax.nn.sigmoid(hold[rows, :] + bias)
        spare[rows, :] = gate
        sigma[rows, :] = gate.astype(BF16)
        return carry

    chunks(gate, 0)
    hold[...] = dot(normed[...], columns(weights, GLU, 0))
    bias = gate_bias[0:1, :D]

    def unit(rows, carry):
        gate = spare[rows, :]
        values = (hold[rows, :] + bias) * gate
        tilt[rows, :] = (values * (1.0 - gate)).astype(BF16)
        for j in range(4):
            gated[j, pl.ds(rows.start + PAD, CHUNK), :] = values[:, 128 * j : 128 * j + 128]
        return carry

    chunks(unit, 0)
    size = 32

    def slide(i, carry):
        begin = pl.multiple_of(i * size, size)
        marks = bounds[pl.ds(begin + PAD, size), :]
        accs = [jnp.zeros((size, 128), F32) for _ in range(4)]
        for k in range(TAPS):
            same = bounds[pl.ds(begin + k, size), :] == marks
            for j in range(4):
                tap = small[S_TAPS + k : S_TAPS + k + 1, 128 * j : 128 * j + 128]
                accs[j] += jnp.where(same, gated[j, pl.ds(begin + k, size), :], 0.0) * tap
        result = []
        for j in range(4):
            middle[pl.ds(begin, size), 128 * j : 128 * j + 128] = accs[j]
            result.append(carry[j] + fold(accs[j]))
            result.append(carry[4 + j] + fold(accs[j] * accs[j]))
        pump(i)
        return result[0::2] + result[1::2]

    ends = lax.fori_loop(0, L // size, slide, [zeros8(128)] * 8, unroll=2)
    for j in range(4):
        sums[0:1, 128 * j : 128 * j + 128] = total_row(ends[j])
        sums[1:2, 128 * j : 128 * j + 128] = total_row(ends[4 + j])


def conv_rest(source, middle, sums, unit, active, slope, result, hold, weights, small, frames):
    center = sums[0:1, :] * (1.0 / frames)
    inverse = lax.rsqrt(sums[1:2, :] * (1.0 / frames) - center * center + epsilon)
    gain, shift = 1.0 + small[S_BATCH : S_BATCH + 1, :], small[S_BATCH + 1 : S_BATCH + 2, :]

    def body(rows, carry):
        values = (middle[rows, :] - center) * inverse
        unit[rows, :] = values
        normal = values * gain + shift
        sigma = jax.nn.sigmoid(normal)
        value = normal * sigma
        active[rows, :] = value.astype(BF16)
        slope[rows, :] = (sigma + value * (1.0 - sigma)).astype(slope.dtype)
        return carry

    chunks(body, 0)
    hold[...] = dot(active[...], columns(weights, CONV, 0))
    bias = small[S_COB : S_COB + 1, :]

    def add(rows, carry):
        result[rows, :] = source[rows, :] + hold[rows, :] + bias
        return carry

    chunks(add, 0)


def conv_back_rest(upstream, unit, slope, grad_normal, low, hold, weights, grads, sums):
    def start(rows, carry):
        given = upstream[rows, :]
        low[rows, :] = given.astype(BF16)
        return carry + fold(given)

    grads[S_COB : S_COB + 1, :] = total_row(chunks(start, zeros8()))
    hold[...] = dot_nt(low[...], columns(weights, CONV, 0))

    def body(rows, carry):
        grad = hold[rows, :] * slope[rows, :].astype(F32)
        grad_normal[rows, :] = grad
        return carry[0] + fold(grad), carry[1] + fold(grad * unit[rows, :])

    first, second = chunks(body, (zeros8(), zeros8()))
    sums[0:1, :] = total_row(first)
    sums[1:2, :] = total_row(second)
    grads[S_BATCH : S_BATCH + 1, :] = total_row(second)
    grads[S_BATCH + 1 : S_BATCH + 2, :] = total_row(first)


def conv_back_front(
    sigma, tilt, gated, unit, grad_normal, front_sums, sums, padded, grad_joined, hold, tap_sums, small, bounds, grads, gate_grads,
    frames, pump,
):
    center = front_sums[0:1, :] * (1.0 / frames)
    inverse = lax.rsqrt(front_sums[1:2, :] * (1.0 / frames) - center * center + epsilon)
    gain = 1.0 + small[S_BATCH : S_BATCH + 1, :]
    mean0, mean1 = gain * sums[0:1, :] * (1.0 / frames), gain * sums[1:2, :] * (1.0 / frames)
    clear_pads(padded)

    def start(rows, carry):
        grad = inverse * (gain * grad_normal[rows, :] - mean0 - unit[rows, :] * mean1)
        for j in range(4):
            padded[j, pl.ds(rows.start + PAD, CHUNK), :] = grad[:, 128 * j : 128 * j + 128]
        return carry

    chunks(start, 0)
    tap_sums[...] = jnp.zeros_like(tap_sums)
    size = 32

    def slide(i, carry):
        begin = pl.multiple_of(i * size, size)
        marks = bounds[pl.ds(begin + PAD, size), :]
        accs = [jnp.zeros((size, 128), F32) for _ in range(4)]
        here = [gated[j, pl.ds(begin + PAD, size), :] for j in range(4)]
        for k in range(TAPS):
            same = bounds[pl.ds(begin + 2 * PAD - k, size), :] == marks
            for j in range(4):
                tap = small[S_TAPS + k : S_TAPS + k + 1, 128 * j : 128 * j + 128]
                grad = jnp.where(same, padded[j, pl.ds(begin + 2 * PAD - k, size), :], 0.0)
                accs[j] += grad * tap
                tap_sums[k, :, 128 * j : 128 * j + 128] += fold(grad * here[j])
        for j in range(4):
            hold[pl.ds(begin, size), 128 * j : 128 * j + 128] = accs[j]
        pump(i)
        return carry

    lax.fori_loop(0, L // size, slide, 0, unroll=2)
    grads[S_TAPS : S_TAPS + TAPS, :] = jnp.sum(tap_sums[...], axis=1)

    def split(rows, carry):
        grad = hold[rows, :]
        first = grad * sigma[rows, :].astype(F32)
        second = grad * tilt[rows, :].astype(F32)
        grad_joined[rows, :D] = first.astype(BF16)
        grad_joined[rows, D : 2 * D] = second.astype(BF16)
        return carry[0] + fold(first), carry[1] + fold(second)

    first, second = chunks(split, (zeros8(), zeros8()))
    gate_grads[0:1, :D] = total_row(first)
    gate_grads[0:1, D:] = total_row(second)


THIN = (
    ("ffn_norm", S_FFN), ("ffn_out_bias", S_FOB), ("attn_norm", S_ATTN), ("attn_out_bias", S_AOB), ("conv_norm", S_CONV),
    ("batch_norm", S_BATCH), ("conv_out_bias", S_COB), ("final_norm", S_FINAL), ("depth_kernel", S_TAPS),
)


def turned(value):
    rows, lanes = value.shape
    value = jnp.concatenate([value, jnp.zeros((rows, 128 - lanes), F32)], axis=1)
    return jnp.concatenate([value, jnp.zeros((128 - rows, 128), F32)], axis=0).T[:lanes, :rows]


def pack_small(b, tile):
    tile[...] = jnp.zeros_like(tile)
    for name, row in THIN:
        value = getattr(b, name)[...].astype(F32)
        if name == "depth_kernel":
            value = turned(value)
        value = value.reshape(-1, value.shape[-1])
        for r in range(0, value.shape[0], 16):
            part = value[r : r + 16]
            begin = (row + r) % 16
            at = 128 * ((row + r) // 16)
            tile[begin : begin + part.shape[0], at : at + part.shape[1]] = part
    tile[0:2, 384 : 384 + b.ffn_in_bias.shape[1]] = b.ffn_in_bias[...].astype(F32)
    wide, few = b.glu_bias.shape[0], b.rel_table.shape[0]
    tile[2:3, 384 : 384 + wide] = b.glu_bias[...].astype(F32).reshape(1, wide)
    tile[3:4, 384 : 384 + few] = b.rel_table[...].astype(F32).reshape(1, few)


def load_weights(b, place):
    copies = {}

    def load(row, source):
        target = b.weights.at[place.plane, place.z, place.core, pl.ds(row, source.shape[0])]
        copies[row] = pltpu.make_async_copy(source, target, b.load_sems.at[len(copies)])
        copies[row].start()

    for layer in range(2):
        for c in range(FF // D):
            load((IN0, IN1)[layer] + 16 * c, b.ffn_in.at[layer, :, pl.ds(D * c, D)])
        load((OUT0, OUT1)[layer], b.ffn_out.at[layer])
        if layer == 0:
            for c in range(3):
                load(QKV + 16 * c, b.qkv_weight.at[:, pl.ds(D * c, D)])
            load(ATT, b.attn_out.at[:, :])
            for c in range(2):
                load(GLU + 16 * c, b.glu_weight.at[:, pl.ds(D * c, D)])
            load(CONV, b.conv_out.at[:, :])
    return copies


def unpack_small(b, place):
    per = 2 * place.chips
    count = place.planes * per
    width = D // count
    for device in range(count):
        tile = b.weights[device // per, (device % per) // 2, device % 2, 0:16, :].astype(F32)
        for q in range(3):
            b.small[16 * q : 16 * q + 16, width * device : width * device + width] = tile[:, 128 * q : 128 * q + width]
        b.inner_bias[:, 4 * width * device : 4 * width * (device + 1)] = tile[0:2, 384 : 384 + 4 * width]
        b.gate_bias[:, 2 * width * device : 2 * width * (device + 1)] = tile[2:3, 384 : 384 + 2 * width]
        few = HEADS * BUCKETS // count
        head, at = few * device // BUCKETS, few * device % BUCKETS
        b.table[head : head + 1, at : at + few] = tile[3:4, 384 : 384 + few]


def pack_small_grads(b, place):
    per = 2 * place.chips
    count = place.planes * per
    width = D // count
    few = HEADS * BUCKETS // count
    for device in range(count):
        tile = b.edges.at[device // per, (device % per) // 2, device % 2]
        for g in range(8):
            tile[0:6, 16 * g : 16 * g + width] = b.grads[6 * g : 6 * g + 6, width * device : width * device + width]
        for m in range(2):
            tile[6:7, 64 * m : 64 * m + 4 * width] = b.inner_grads[m : m + 1, 4 * width * device : 4 * width * (device + 1)]
        tile[7:8, 0 : 2 * width] = b.gate_grads[:, 2 * width * device : 2 * width * (device + 1)]
        head, at = few * device // BUCKETS, few * device % BUCKETS
        tile[7:8, 64 : 64 + few] = b.table_grad[head : head + 1, at : at + few]


INPUTS = (
    "inputs", "segments", "buckets", "cotangent", "ffn_norm", "ffn_in", "ffn_in_bias", "ffn_out", "ffn_out_bias", "attn_norm",
    "qkv_weight", "attn_out", "attn_out_bias", "rel_table", "conv_norm", "glu_weight", "glu_bias", "depth_kernel", "batch_norm",
    "conv_out", "conv_out_bias", "final_norm",
)
LOADED = ("inputs", "cotangent", "ffn_in", "ffn_out", "qkv_weight", "attn_out", "glu_weight", "conv_out")
OUTPUTS = ("output", "grad_x", "shard", "thin")
GATHERS = ((SMALL, 48, 32), (IN0 + 32, 32, 16), (OUT0, 64, 32), (QKV, 64, 32), (GLU, 48, 32), (IN1, 64, 32), (OUT1, 64, 32))
REDUCES = (
    (OUT1, OUT1, 64, 32), (IN1, IN1, 64, 32), (CONV, CONV, 16, 16), (GLU, GLU, 32, 16),
    (ATT, ATT, 16, 16), (QKV, QKV, 48, 32), (OUT1, OUT0, 32, 16),
    (OUT1 + 32, OUT0 + 32, 32, 16), (IN1, IN0, 32, 16), (IN1 + 32, IN0 + 32, 32, 16),
)


def scratch_of(planes, chips):
    wide, low, big = pltpu.VMEM((L, D), F32), pltpu.VMEM((L, D), BF16), pltpu.VMEM((L, FF), BF16)
    pads = pltpu.VMEM((4, L + 2 * PAD, 128), F32)
    stats = pltpu.VMEM((2, D), F32)
    return dict(
        weights=pltpu.VMEM((planes, chips, 2, ROWS, D), BF16),
        twin=pltpu.VMEM((planes, chips, GRADS, D), BF16),
        diagonal=pltpu.VMEM((chips, GRADS, D), BF16),
        from_x=pltpu.VMEM((chips, GRADS, D), BF16),
        from_y=pltpu.VMEM((chips, GRADS, D), BF16),
        from_z=pltpu.VMEM((chips - 1, GRADS, D), BF16),
        edges=pltpu.VMEM((planes, chips, 2, 8, 128), F32),
        edge_near=pltpu.VMEM((2 * planes, chips, 8, 128), F32),
        edge_part=pltpu.VMEM((chips, 8, 128), F32),
        edge_far=pltpu.VMEM((chips, 8, 128), F32),
        small=pltpu.VMEM((S_ROWS, D), F32),
        inner_bias=pltpu.VMEM((2, FF), F32),
        gate_bias=pltpu.VMEM((1, 2 * D), F32),
        table=pltpu.VMEM((HEADS, BUCKETS), F32),
        tile=pltpu.VMEM((16, D), F32),
        grads=pltpu.VMEM((S_ROWS, D), F32),
        inner_grads=pltpu.VMEM((2, FF), F32),
        gate_grads=pltpu.VMEM((1, 2 * D), F32),
        table_grad=pltpu.VMEM((HEADS, BUCKETS), F32),
        lines=pltpu.VMEM((HEADS, 2 * L), F32),
        choice=pltpu.VMEM((1, 2 * L), jnp.int32),
        bounds=pltpu.VMEM((L + 2 * PAD, 128), F32),
        marks=pltpu.VMEM((1, L), F32),
        front_own=stats, back_own=stats, front_sums=stats, back_sums=stats, front_part=stats, back_part=stats,
        front_near=pltpu.VMEM((2 * planes, 2, D), F32), back_near=pltpu.VMEM((2 * planes, 2, D), F32),
        front_far=pltpu.VMEM((chips, 2, D), F32), back_far=pltpu.VMEM((chips, 2, D), F32),
        x1=wide, x2=wide, x3=wide, x4=wide, normed_a=low, normed_c=low, normed1=low,
        active0=big, slope0=big, active1=big, slope1=big, mixed=pltpu.VMEM((L, 3 * D), BF16),
        probs=pltpu.VMEM((HEADS, L, L), BF16), joined=wide, recips=wide, diagonals=pltpu.VMEM((8, HEADS, 2 * L), F32), sigma=low, tilt=low, gated=pads, middle=wide, active_c=low, slope_c=low,
        padded=pads, low=low, hold=wide, total=wide, taps=pltpu.VMEM((TAPS, 8, D), F32),
        x0=low, given=low, result=low,
        load_sems=pltpu.SemaphoreType.DMA((17,)),
        edge_sems=pltpu.SemaphoreType.DMA((4,)),
        gather_sends=pltpu.SemaphoreType.DMA((len(GATHERS) * Gather.semaphores(chips),)),
        gather_receives=pltpu.SemaphoreType.DMA((len(GATHERS) * Gather.semaphores(chips),)),
        reduce_sends=pltpu.SemaphoreType.DMA((len(REDUCES) * (chips + 7),)),
        reduce_receives=pltpu.SemaphoreType.DMA((len(REDUCES) * (chips + 7),)),
        total_sends=pltpu.SemaphoreType.DMA((3 * (2 * planes + chips),)),
        total_receives=pltpu.SemaphoreType.DMA((3 * (2 * planes + chips),)),
    )


def whole_kernel(names, *refs):
    b = Bag()
    for name, ref in zip(names, refs):
        setattr(b, name, ref)
    place = Place()
    planes, chips = place.planes, place.chips
    frames = L * planes * chips * 2
    barrier = pltpu.get_barrier_semaphore()
    near = [device for device, rank in place.members] + [place.along[d] for d in range(1, chips)]
    for device in near:
        pl.semaphore_signal(barrier, inc=1, device_id=device, device_id_type=MESH)
    loads = load_weights(b, place)
    load_x = pltpu.make_async_copy(b.inputs.at[0], b.x0, b.edge_sems.at[0])
    load_cotangent = pltpu.make_async_copy(b.cotangent.at[0], b.given, b.edge_sems.at[1])
    load_x.start()
    load_cotangent.start()
    pack_small(b, b.tile)
    b.weights[place.plane, place.z, place.core, 0:16, :] = b.tile[...].astype(BF16)
    pl.semaphore_wait(barrier, len(near))

    gathers = Copies(b.gather_sends, b.gather_receives, place)
    rounds = [
        Gather(place, b.weights, gathers, i * Gather.semaphores(chips), begin, size, split)
        for i, (begin, size, split) in enumerate(GATHERS)
    ]
    r0, r1, r2, r3, r4, r5, r6 = rounds
    for r, (begin, size, _) in zip(rounds, GATHERS):
        for row, copy in loads.items():
            if begin <= row < begin + size:
                copy.wait()
        r.along_z()
        if r in rounds[:5]:
            r.own()
    b.marks[...] = b.segments[...].astype(F32)
    b.bounds[...] = jnp.full(b.bounds.shape, -1.0, F32)
    b.bounds[PAD : PAD + L, :] = jnp.broadcast_to(b.marks[...], (128, L)).T
    b.choice[...] = jnp.full(b.choice.shape, -1, jnp.int32)
    b.choice[:, 0 : 2 * L - 1] = b.buckets[...].reshape(1, 2 * L - 1)
    attention_mask(b.x4, b.bounds, b.marks)
    for step in (r0.forward, r1.forward, r0.turn, r1.turn, r2.forward, r0.across, r0.done):
        step()
    unpack_small(b, place)

    x0 = b.x0
    load_x.wait()
    raws = (b.hold, b.total)
    feed_inner(
        x0, b.normed_c, b.active0, b.slope0, raws, b.weights, b.small, b.inner_bias, 0,
        at_points({(2, 0): (r1.across, r1.done, r3.forward)}),
    )
    attention_squares(b.lines, b.twin, b.table, b.choice)
    for step in (r2.turn, r3.turn, r4.forward, r5.own, r2.across, r2.done):
        step()
    feed_outer(x0, b.active0, b.x1, b.hold, b.weights, b.small, 0)
    r3.across()
    r3.done()
    attention_mix(b.x1, b.normed_a, b.mixed, b.weights, b.small)
    for step in (r4.turn, r5.forward, r6.own, r6.forward):
        step()
    attention_forward(
        b.x1, b.mixed, b.probs, b.joined, b.recips, b.x2, b.twin, b.x4, b.hold, b.x3, b.weights, b.small, still
    )
    r4.across()
    r4.done()
    conv_front(
        b.x2, b.normed_c, b.sigma, b.tilt, b.gated, b.middle, b.front_own, b.hold, b.total, b.weights, b.small, b.gate_bias, b.bounds,
        at_points({(5, 0): (r5.turn,)}),
    )
    totals = Copies(b.total_sends, b.total_receives, place)
    front = Total(place, b.front_own, b.front_near, b.front_part, b.front_far, b.front_sums, totals, 0)
    front.start()
    r6.turn()
    front.turn()
    front.finish()
    conv_rest(b.x2, b.middle, b.front_sums, b.middle, b.active_c, b.slope_c, b.x3, b.hold, b.weights, b.small, frames)
    r5.across()
    r5.done()
    feed_inner(b.x3, b.normed1, b.active1, b.slope1, raws, b.weights, b.small, b.inner_bias, 1, still)
    r6.across()
    r6.done()
    feed_outer(b.x3, b.active1, b.x4, b.hold, b.weights, b.small, 1)
    norm_rows(b.x4, b.result, b.small, S_FINAL)
    save_output = pltpu.make_async_copy(b.result, b.output.at[0], b.edge_sems.at[2])
    save_output.start()
    load_cotangent.wait()
    flow = b.x4
    norm_back(b.x4, b.given, None, flow, b.small, S_FINAL, b.grads)
    gathers.sent()

    early = Copies(b.reduce_sends, b.reduce_receives, place)
    reduces = Copies(b.reduce_sends, b.reduce_receives, place)
    landings = (b.twin, b.diagonal, b.from_x, b.from_y, b.from_z)

    def finish(begin, size):
        def act(value):
            b.shard[begin - IN0 : begin - IN0 + size, :] = value

        return act

    backs = [
        reduce_steps(
            place, b.weights, *landings, early if i < 2 else reduces, i * (chips + 7), begin, size, split, owner - IN0,
            finish(owner, size),
        )
        for i, (begin, owner, size, split) in enumerate(REDUCES)
    ]
    out1, in1, tip, glu, att, mix, out0, out0_end, in0, in0_end = backs
    feed_back_start(flow, b.low, b.grads, 1)
    feed_back_inner(b.normed1, b.slope1, b.low, raws, b.weights, None, b.inner_grads, 1, still)
    feed_back_outer(b.active1, b.low, b.weights, OUT1, still)
    out1[0]()
    product_back(b.slope1, b.normed1, b.total, b.weights, IN1, 4, still)
    in1[0]()
    out1[1]()
    norm_back(b.x3, b.total, flow, flow, b.small, S_FFN + 2, b.grads)
    in1[1]()
    grad_normal = b.x3
    conv_back_rest(flow, b.middle, b.slope_c, grad_normal, b.low, b.hold, b.weights, b.grads, b.back_own)
    back = Total(place, b.back_own, b.back_near, b.back_part, b.back_far, b.back_sums, totals, 2 * planes + chips)
    back.start()
    put_columns(b.weights, CONV, 0, dot_tn(b.active_c[...], b.low[...]))
    tip[0]()
    back.turn()
    out1[2]()
    tip[1]()
    back.finish()
    conv_back_front(
        b.sigma, b.tilt, b.gated, b.middle, grad_normal, b.front_sums, b.back_sums, b.padded, b.active1, b.hold, b.taps, b.small,
        b.bounds, b.grads, b.gate_grads, frames, at_points({(4, 0): (in1[2],), (8, 0): (tip[2],), (14, 0): (out1[3],)}),
    )
    product_back(b.active1, b.normed_c, b.total, b.weights, GLU, 2, still)
    glu[0]()
    norm_back(b.x2, b.total, flow, flow, b.small, S_CONV, b.grads)
    attention_back_start(flow, b.joined, b.recips, b.low, b.normed1, b.hold, b.weights, b.grads)
    att[0]()
    glu[1]()
    attention_backward(
        b.mixed, b.probs, b.normed1, b.joined, b.active1, b.slope1, b.hold, b.x3, b.total, b.diagonals, b.lines, b.choice,
        b.table_grad, at_points({(0, 1): (in1[3], att[1]), (2, 0): (tip[3],), (2, 1): (glu[2],), (3, 0): (out1[4],), (3, 1): (att[2],)}),
    )
    product_back(b.active1, b.normed_a, b.total, b.weights, QKV, 3, still)
    mix[0]()
    norm_back(b.x1, b.total, flow, flow, b.small, S_ATTN, b.grads)
    in1[4]()
    tip[4]()
    early.sent()
    norm_rows(x0, b.normed_c, b.small, S_FFN)
    feed_back_start(flow, b.low, b.grads, 0)
    feed_back_outer(b.active0, b.low, b.weights, OUT1, still)
    out0[0]()
    out0_end[0]()
    mix[1]()
    glu[3]()
    att[3]()
    feed_back_inner(
        b.normed_c, b.slope0, b.low, raws, b.weights, IN1, b.inner_grads, 0,
        at_points({(1, 0): (in0[0], out0[1]), (2, 0): (out0_end[1],)}),
    )
    in0_end[0]()
    in0[1]()
    product_back(b.slope0, None, b.total, b.weights, IN0, 4, still)
    in0_end[1]()
    norm_back(x0, b.total, flow, b.x3, b.small, S_FFN, b.grads)
    save_grad_x = pltpu.make_async_copy(b.x3, b.grad_x.at[0], b.edge_sems.at[3])
    save_grad_x.start()
    pack_small_grads(b, place)
    thin = Thin(place, b.edges, b.edge_near, b.edge_part, b.edge_far, b.thin, totals, 2 * (2 * planes + chips))
    thin.start()
    for step in (
        mix[2], thin.turn, out0[2], out0_end[2], in0[2], in0_end[2], glu[4], att[4], thin.finish, mix[3], out0[3], out0_end[3],
        mix[4], in0[3], out0[4], in0_end[3], out0_end[4], in0[4], in0_end[4],
    ):
        step()
    early.sent()
    reduces.sent()
    totals.sent()
    save_output.wait()
    save_grad_x.wait()


def finish_kernel(*refs):
    (
        output_in, grad_x_in, shard, thin, output, grad_x, grad_ffn_norm, grad_ffn_in, grad_ffn_in_bias, grad_ffn_out,
        grad_ffn_out_bias, grad_attn_norm, grad_qkv, grad_attn_out, grad_attn_out_bias, grad_rel, grad_conv_norm, grad_glu,
        grad_glu_bias, grad_depth, grad_batch, grad_conv_out, grad_conv_out_bias, grad_final, taps, semaphores,
    ) = refs
    copies = [
        pltpu.make_async_copy(output_in, output, semaphores.at[0]), pltpu.make_async_copy(grad_x_in, grad_x, semaphores.at[1])
    ]
    for copy in copies:
        copy.start()
    cut = lambda begin, size: shard[begin - IN0 : begin - IN0 + size, :]
    width = grad_final.shape[-1]

    def thin_rows(begin, count):
        rows = []
        for p in range(begin, begin + count):
            rows.append(thin[p % 6 : p % 6 + 1, 16 * (p // 6) : 16 * (p // 6) + width])
        return rows

    for layer in range(2):
        for c in range(FF // D):
            grad_ffn_in[layer, :, D * c : D * c + D] = cut((IN0, IN1)[layer] + 16 * c, 16)
        grad_ffn_out[layer] = cut((OUT0, OUT1)[layer], 64)
        grad_ffn_in_bias[layer : layer + 1, :] = thin[6:7, 64 * layer : 64 * layer + 4 * width]
        for r, row in enumerate(thin_rows(S_FFN + 2 * layer, 2)):
            grad_ffn_norm[layer, r : r + 1, :] = row
    for c in range(3):
        grad_qkv[:, D * c : D * c + D] = cut(QKV + 16 * c, 16)
    grad_attn_out[...] = cut(ATT, 16)
    for c in range(2):
        grad_glu[:, D * c : D * c + D] = cut(GLU + 16 * c, 16)
    grad_conv_out[...] = cut(CONV, 16)
    for ref, begin in (
        (grad_ffn_out_bias, S_FOB), (grad_attn_norm, S_ATTN), (grad_conv_norm, S_CONV), (grad_batch, S_BATCH),
        (grad_final, S_FINAL),
    ):
        for r, row in enumerate(thin_rows(begin, ref.shape[0])):
            ref[r : r + 1, :] = row
    for r, row in enumerate(thin_rows(S_TAPS, TAPS)):
        taps[r : r + 1, 0:width] = row
    grad_depth[...] = taps[...].T[0:width, 0:TAPS]
    grad_attn_out_bias[...] = thin_rows(S_AOB, 1)[0][0]
    grad_conv_out_bias[...] = thin_rows(S_COB, 1)[0][0]
    grad_glu_bias[...] = thin[7:8, 0 : 2 * width][0]
    grad_rel[...] = thin[7:8, 64 : 64 + grad_rel.shape[0]][0]
    for copy in copies:
        copy.wait()


def shape(dims, kind=F32):
    return jax.ShapeDtypeStruct(dims, kind)


def local(*args):
    planes, chips = lax.axis_size("dp"), lax.axis_size("fsdp") // 2
    scratch = scratch_of(planes, chips)
    names = INPUTS + OUTPUTS + tuple(scratch)
    vmem, anywhere = pl.BlockSpec(memory_space=pltpu.VMEM), pl.BlockSpec(memory_space=pl.ANY)
    given = dict(zip(INPUTS, args))
    given["depth_kernel"] = given["depth_kernel"].T
    firsts = [shape((1, L, D), BF16), shape((1, L, D))]
    passed = pl.pallas_call(
        lambda *refs: whole_kernel(names, *refs),
        out_shape=firsts + [shape((GRADS, D)), shape((8, 128))],
        in_specs=[anywhere if name in LOADED else vmem for name in INPUTS],
        out_specs=[anywhere, anywhere, vmem, vmem],
        scratch_shapes=list(scratch.values()),
        compiler_params=pltpu.CompilerParams(collective_id=0, has_side_effects=True, vmem_limit_bytes=VMEM_BYTES),
        name="layer",
    )(*given.values())
    outs = [
        shape(given[name].shape)
        for name in (
            "ffn_norm", "ffn_in", "ffn_in_bias", "ffn_out", "ffn_out_bias", "attn_norm", "qkv_weight", "attn_out",
            "attn_out_bias", "rel_table", "conv_norm", "glu_weight", "glu_bias", "depth_kernel", "batch_norm", "conv_out",
            "conv_out_bias", "final_norm",
        )
    ]
    grads = pl.pallas_call(
        finish_kernel,
        out_shape=firsts + outs,
        in_specs=[anywhere, anywhere, vmem, vmem],
        out_specs=[vmem] * (2 + len(outs)),
        scratch_shapes=[pltpu.VMEM((128, 128), F32), pltpu.SemaphoreType.DMA((2,))],
        name="unpack",
    )(*passed)
    grads = list(grads)
    grads[15] = grads[15].T
    return tuple(grads)


VMEM_BYTES = 127 * 512 * 1024


highest = lax.Precision.HIGHEST


def layer_norm(values, params):
    center = values - jnp.mean(values, axis=-1, keepdims=True)
    spread = jnp.mean(center * center, axis=-1, keepdims=True)
    return center * lax.rsqrt(spread + epsilon) * (1.0 + params[0]) + params[1]


def silu_slope(values):
    sigma = jax.nn.sigmoid(values)
    return sigma * (1.0 + values * (1.0 - sigma))


def product(left, right):
    return jnp.dot(left, right, preferred_element_type=jnp.float32)


def product_left(left, right):
    return lax.dot_general(
        left, right, (((0,), (0,)), ((), ())), preferred_element_type=jnp.float32
    )


def product_right(left, right):
    return lax.dot_general(
        left, right, (((1,), (1,)), ((), ())), preferred_element_type=jnp.float32
    )


def plain_fetch_feed(norms, inner_weight, inner_bias, outer_weight, outer_bias, layer):
    return (
        lax.all_gather(norms[layer], ("dp", "fsdp"), axis=1, tiled=True),
        lax.all_gather(inner_weight[layer], ("dp", "fsdp"), axis=0, tiled=True),
        lax.all_gather(inner_bias[layer], ("dp", "fsdp"), axis=0, tiled=True),
        lax.all_gather(outer_weight[layer], ("dp", "fsdp"), axis=0, tiled=True),
        lax.all_gather(outer_bias[layer], ("dp", "fsdp"), axis=0, tiled=True),
    )


def plain_reduce_feed(grads):
    return (
        lax.psum_scatter(grads[0], ("dp", "fsdp"), scatter_dimension=1, tiled=True),
        lax.psum_scatter(grads[1], ("dp", "fsdp"), scatter_dimension=0, tiled=True),
        lax.psum_scatter(grads[2], ("dp", "fsdp"), scatter_dimension=0, tiled=True),
        lax.psum_scatter(grads[3], ("dp", "fsdp"), scatter_dimension=0, tiled=True),
        lax.psum_scatter(grads[4], ("dp", "fsdp"), scatter_dimension=0, tiled=True),
    )


def fetch_attention(attn_norm, qkv_weight, attn_out, attn_out_bias, rel_table):
    return (
        lax.all_gather(attn_norm, ("dp", "fsdp"), axis=1, tiled=True),
        lax.all_gather(qkv_weight, ("dp", "fsdp"), axis=0, tiled=True),
        lax.all_gather(attn_out, ("dp", "fsdp"), axis=0, tiled=True),
        lax.all_gather(attn_out_bias, ("dp", "fsdp"), axis=0, tiled=True),
        lax.all_gather(rel_table, ("dp", "fsdp"), axis=0, tiled=True),
    )


def fetch_conv(
    conv_norm, glu_weight, glu_bias, depth_kernel, batch_norm, conv_out, conv_out_bias, final_norm
):
    return (
        lax.all_gather(conv_norm, ("dp", "fsdp"), axis=1, tiled=True),
        lax.all_gather(glu_weight, ("dp", "fsdp"), axis=0, tiled=True),
        lax.all_gather(glu_bias, ("dp", "fsdp"), axis=0, tiled=True),
        lax.all_gather(depth_kernel, ("dp", "fsdp"), axis=1, tiled=True),
        lax.all_gather(batch_norm, ("dp", "fsdp"), axis=1, tiled=True),
        lax.all_gather(conv_out, ("dp", "fsdp"), axis=0, tiled=True),
        lax.all_gather(conv_out_bias, ("dp", "fsdp"), axis=0, tiled=True),
        lax.all_gather(final_norm, ("dp", "fsdp"), axis=1, tiled=True),
    )


def plain_feed_forward(values, weights):
    norm, weight_in, bias_in, weight_out, bias_out = weights
    normed, norm_back = jax.vjp(layer_norm, values, norm.astype(jnp.float32))
    normed_low = normed.astype(jnp.bfloat16)
    inner = product(normed_low, weight_in) + bias_in.astype(jnp.float32)
    active = jax.nn.silu(inner).astype(jnp.bfloat16)
    result = values + 0.5 * (product(active, weight_out) + bias_out.astype(jnp.float32))
    return (result, (normed_low, inner, active, norm_back))


def plain_feed_backward(upstream, weights, saved):
    norm, weight_in, bias_in, weight_out, bias_out = weights
    normed_low, inner, active, norm_back = saved
    branch = 0.5 * upstream
    branch_low = branch.astype(jnp.bfloat16)
    grad_weight_out = product_left(active, branch_low)
    grad_inner = product_right(branch_low, weight_out) * silu_slope(inner)
    inner_low = grad_inner.astype(jnp.bfloat16)
    grad_weight_in = product_left(normed_low, inner_low)
    grad_values, grad_norm = norm_back(product_right(inner_low, weight_in))
    return (
        upstream + grad_values,
        (
            grad_norm,
            grad_weight_in,
            jnp.sum(grad_inner, axis=0),
            grad_weight_out,
            jnp.sum(branch, axis=0),
        ),
    )


def relative_lines(table, buckets):
    choose = (buckets[None, :] == jnp.arange(BUCKETS, dtype=jnp.int32)[:, None]).astype(jnp.float32)
    lines = jnp.dot(table.astype(jnp.float32).reshape(HEADS, BUCKETS), choose, precision=highest)
    return (lines, choose)


def bias_square(line, length):
    tiled = jnp.broadcast_to(line, (length, 2 * length - 1)).reshape(-1)
    tiled = jnp.concatenate([tiled, jnp.zeros((length,), line.dtype)])
    return tiled.reshape(length, 2 * length)[:, :length][::-1]


def diagonal_sums(square):
    length = square.shape[0]
    padded = jnp.concatenate([square[::-1], jnp.zeros_like(square)], axis=1).reshape(-1)
    return jnp.sum(padded[: length * (2 * length - 1)].reshape(length, 2 * length - 1), axis=0)


def head_scores(query, keys_head, line, same):
    raw = product_right(query, keys_head)
    return jnp.where(same, raw * HEAD_DIM ** (-0.5) + bias_square(line, query.shape[0]), -1e30)


def plain_attention_forward(values, weights, marks, buckets):
    norm, mixer, weight_out, bias_out, table = weights
    length = values.shape[0]
    normed, norm_back = jax.vjp(layer_norm, values, norm.astype(jnp.float32))
    normed_low = normed.astype(jnp.bfloat16)
    mixed = (
        product(normed_low, mixer)
        .astype(jnp.bfloat16)
        .reshape(length, 3, HEADS, HEAD_DIM)
        .transpose(1, 2, 0, 3)
    )
    lines, choose = relative_lines(table, buckets)
    same = marks[:, None] == marks[None, :]

    def head_forward(items):
        query, keys_head, contents, line = items
        scores = head_scores(query, keys_head, line, same)
        peak = jnp.max(scores, axis=1, keepdims=True)
        raised = jnp.exp(scores - peak)
        total = jnp.sum(raised, axis=1, keepdims=True)
        probs = (raised / total).astype(jnp.bfloat16)
        return (product(probs, contents).astype(jnp.bfloat16), (peak + jnp.log(total))[:, 0])

    attended, logsum = lax.map(head_forward, (mixed[0], mixed[1], mixed[2], lines))
    joined = attended.transpose(1, 0, 2).reshape(length, D)
    result = values + product(joined, weight_out) + bias_out.astype(jnp.float32)
    return (result, (normed_low, mixed, lines, choose, same, joined, logsum, norm_back))


def plain_attention_backward(upstream, weights, saved):
    norm, mixer, weight_out, bias_out, table = weights
    normed_low, mixed, lines, choose, same, joined, logsum, norm_back = saved
    length = upstream.shape[0]
    upstream_low = upstream.astype(jnp.bfloat16)
    grad_weight_out = product_left(joined, upstream_low)
    grad_joined = (
        product_right(upstream_low, weight_out)
        .astype(jnp.bfloat16)
        .reshape(length, HEADS, HEAD_DIM)
        .transpose(1, 0, 2)
    )

    def head_backward(items):
        query, keys_head, contents, line, incoming, logs = items
        scores = head_scores(query, keys_head, line, same)
        probs = jnp.exp(scores - logs[:, None])
        grad_contents = product_left(probs.astype(jnp.bfloat16), incoming)
        grad_probs = product_right(incoming, contents)
        grad_scores = probs * (grad_probs - jnp.sum(grad_probs * probs, axis=1, keepdims=True))
        scaled = (grad_scores * HEAD_DIM ** (-0.5)).astype(jnp.bfloat16)
        grad_query = product(scaled, keys_head)
        grad_keys = product_left(scaled, query)
        return (
            jnp.stack([grad_query, grad_keys, grad_contents]).astype(jnp.bfloat16),
            diagonal_sums(grad_scores),
        )

    grad_mixed, grad_lines = lax.map(
        head_backward, (mixed[0], mixed[1], mixed[2], lines, grad_joined, logsum)
    )
    grad_flat = grad_mixed.transpose(2, 1, 0, 3).reshape(length, 3 * D)
    grad_mixer = product_left(normed_low, grad_flat)
    grad_values, grad_norm = norm_back(product_right(grad_flat, mixer))
    grad_table = jnp.dot(grad_lines, choose.T, precision=highest).reshape(-1)
    return (
        upstream + grad_values,
        (grad_norm, grad_mixer, grad_weight_out, jnp.sum(upstream, axis=0), grad_table),
    )


def gate_unit(joined):
    width = joined.shape[1] // 2
    return joined[:, :width] * jax.nn.sigmoid(joined[:, width:])


def plain_depthwise(gated, kernel, marks):
    length = gated.shape[0]
    half = kernel.shape[0] // 2
    padded = jnp.pad(gated, ((half, half), (0, 0)))
    bounds = jnp.pad(marks, (half, half), constant_values=-1)
    total = jnp.zeros(gated.shape, gated.dtype)
    for step in range(kernel.shape[0]):
        same = (bounds[step : step + length] == marks)[:, None]
        total = total + jnp.where(same, padded[step : step + length], 0.0) * kernel[step]
    return total


def plain_conv_forward(values, weights, marks, frames):
    norm, weight_glu, bias_glu, kernel, batch, weight_out, bias_out, final = weights
    normed, norm_back = jax.vjp(layer_norm, values, norm.astype(jnp.float32))
    normed_low = normed.astype(jnp.bfloat16)
    joined = product(normed_low, weight_glu) + bias_glu.astype(jnp.float32)
    gated, gate_back = jax.vjp(gate_unit, joined)
    middle, depth_back = jax.vjp(
        lambda inner, taps: plain_depthwise(inner, taps, marks), gated, kernel.astype(jnp.float32)
    )
    sums = lax.psum((jnp.sum(middle, axis=0), jnp.sum(middle * middle, axis=0)), ("dp", "fsdp"))
    center = sums[0] / frames
    inverse = lax.rsqrt(sums[1] / frames - center * center + epsilon)
    gain = 1.0 + batch[0].astype(jnp.float32)
    unit = (middle - center) * inverse
    normal = unit * gain + batch[1].astype(jnp.float32)
    active = jax.nn.silu(normal).astype(jnp.bfloat16)
    result = values + product(active, weight_out) + bias_out.astype(jnp.float32)
    return (
        result,
        (normed_low, gate_back, depth_back, inverse, gain, unit, normal, active, norm_back),
    )


def plain_conv_backward(upstream, weights, saved, frames):
    norm, weight_glu, bias_glu, kernel, batch, weight_out, bias_out, final = weights
    normed_low, gate_back, depth_back, inverse, gain, unit, normal, active, norm_back = saved
    upstream_low = upstream.astype(jnp.bfloat16)
    grad_weight_out = product_left(active, upstream_low)
    grad_normal = product_right(upstream_low, weight_out) * silu_slope(normal)
    sums = lax.psum(
        (jnp.sum(grad_normal, axis=0), jnp.sum(grad_normal * unit, axis=0)), ("dp", "fsdp")
    )
    grad_middle = inverse * (
        grad_normal * gain - gain * sums[0] / frames - unit * (gain * sums[1] / frames)
    )
    grad_gated, grad_kernel = depth_back(grad_middle)
    grad_joined = gate_back(grad_gated)[0]
    joined_low = grad_joined.astype(jnp.bfloat16)
    grad_weight_glu = product_left(normed_low, joined_low)
    grad_values, grad_norm = norm_back(product_right(joined_low, weight_glu))
    grad_batch = jnp.stack([sums[1], sums[0]])
    return (
        upstream + grad_values,
        (
            grad_norm,
            grad_weight_glu,
            jnp.sum(grad_joined, axis=0),
            grad_kernel,
            grad_weight_out,
            jnp.sum(upstream, axis=0),
        ),
        grad_batch,
    )


def plain(
    inputs,
    segments,
    buckets,
    cotangent,
    ffn_norm,
    ffn_in,
    ffn_in_bias,
    ffn_out,
    ffn_out_bias,
    attn_norm,
    qkv_weight,
    attn_out,
    attn_out_bias,
    rel_table,
    conv_norm,
    glu_weight,
    glu_bias,
    depth_kernel,
    batch_norm,
    conv_out,
    conv_out_bias,
    final_norm,
):
    values = inputs[0].astype(jnp.float32)
    marks = segments[0]
    devices = lax.axis_size(("dp", "fsdp"))
    frames = values.shape[0] * devices
    feed_first = plain_fetch_feed(ffn_norm, ffn_in, ffn_in_bias, ffn_out, ffn_out_bias, 0)
    first, first_saved = plain_feed_forward(values, feed_first)
    attn_weights = fetch_attention(attn_norm, qkv_weight, attn_out, attn_out_bias, rel_table)
    second, attn_saved = plain_attention_forward(first, attn_weights, marks, buckets)
    conv_weights = fetch_conv(
        conv_norm,
        glu_weight,
        glu_bias,
        depth_kernel,
        batch_norm,
        conv_out,
        conv_out_bias,
        final_norm,
    )
    third, conv_saved = plain_conv_forward(second, conv_weights, marks, frames)
    feed_second = plain_fetch_feed(ffn_norm, ffn_in, ffn_in_bias, ffn_out, ffn_out_bias, 1)
    fourth, second_saved = plain_feed_forward(third, feed_second)
    result, final_back = jax.vjp(layer_norm, fourth, conv_weights[7].astype(jnp.float32))
    grad_fourth, grad_final = final_back(cotangent[0].astype(jnp.float32))
    second_back = plain_fetch_feed(ffn_norm, ffn_in, ffn_in_bias, ffn_out, ffn_out_bias, 1)
    grad_third, second_grads = plain_feed_backward(grad_fourth, second_back, second_saved)
    conv_back = fetch_conv(
        conv_norm,
        glu_weight,
        glu_bias,
        depth_kernel,
        batch_norm,
        conv_out,
        conv_out_bias,
        final_norm,
    )
    grad_second, conv_grads, grad_batch = plain_conv_backward(grad_third, conv_back, conv_saved, frames)
    attn_back = fetch_attention(attn_norm, qkv_weight, attn_out, attn_out_bias, rel_table)
    grad_first, attn_grads = plain_attention_backward(grad_second, attn_back, attn_saved)
    first_back = plain_fetch_feed(ffn_norm, ffn_in, ffn_in_bias, ffn_out, ffn_out_bias, 0)
    grad_start, first_grads = plain_feed_backward(grad_first, first_back, first_saved)
    first_shards = plain_reduce_feed(first_grads)
    second_shards = plain_reduce_feed(second_grads)
    attn_shards = (
        lax.psum_scatter(attn_grads[0], ("dp", "fsdp"), scatter_dimension=1, tiled=True),
        lax.psum_scatter(attn_grads[1], ("dp", "fsdp"), scatter_dimension=0, tiled=True),
        lax.psum_scatter(attn_grads[2], ("dp", "fsdp"), scatter_dimension=0, tiled=True),
        lax.psum_scatter(attn_grads[3], ("dp", "fsdp"), scatter_dimension=0, tiled=True),
        lax.psum_scatter(attn_grads[4], ("dp", "fsdp"), scatter_dimension=0, tiled=True),
    )
    conv_shards = (
        lax.psum_scatter(conv_grads[0], ("dp", "fsdp"), scatter_dimension=1, tiled=True),
        lax.psum_scatter(conv_grads[1], ("dp", "fsdp"), scatter_dimension=0, tiled=True),
        lax.psum_scatter(conv_grads[2], ("dp", "fsdp"), scatter_dimension=0, tiled=True),
        lax.psum_scatter(conv_grads[3], ("dp", "fsdp"), scatter_dimension=1, tiled=True),
        lax.psum_scatter(conv_grads[4], ("dp", "fsdp"), scatter_dimension=0, tiled=True),
        lax.psum_scatter(conv_grads[5], ("dp", "fsdp"), scatter_dimension=0, tiled=True),
        lax.psum_scatter(grad_final, ("dp", "fsdp"), scatter_dimension=1, tiled=True),
    )
    width = D // devices
    batch_shard = lax.dynamic_slice_in_dim(
        grad_batch, lax.axis_index(("dp", "fsdp")) * width, width, 1
    )
    return (
        result[None].astype(jnp.bfloat16),
        grad_start[None],
        jnp.stack([first_shards[0], second_shards[0]]),
        jnp.stack([first_shards[1], second_shards[1]]),
        jnp.stack([first_shards[2], second_shards[2]]),
        jnp.stack([first_shards[3], second_shards[3]]),
        jnp.stack([first_shards[4], second_shards[4]]),
        attn_shards[0],
        attn_shards[1],
        attn_shards[2],
        attn_shards[3],
        attn_shards[4],
        conv_shards[0],
        conv_shards[1],
        conv_shards[2],
        conv_shards[3],
        batch_shard,
        conv_shards[4],
        conv_shards[5],
        conv_shards[6],
    )


def solution(mesh):
    in_specs = (
        P(("dp", "fsdp"), None, None),
        P(("dp", "fsdp"), None),
        P(),
        P(("dp", "fsdp"), None, None),
        P(None, None, ("dp", "fsdp")),
        P(None, ("dp", "fsdp"), None),
        P(None, ("dp", "fsdp")),
        P(None, ("dp", "fsdp"), None),
        P(None, ("dp", "fsdp")),
        P(None, ("dp", "fsdp")),
        P(("dp", "fsdp"), None),
        P(("dp", "fsdp"), None),
        P(("dp", "fsdp")),
        P(("dp", "fsdp")),
        P(None, ("dp", "fsdp")),
        P(("dp", "fsdp"), None),
        P(("dp", "fsdp")),
        P(None, ("dp", "fsdp")),
        P(None, ("dp", "fsdp")),
        P(("dp", "fsdp"), None),
        P(("dp", "fsdp")),
        P(None, ("dp", "fsdp")),
    )
    out_specs = (
        P(("dp", "fsdp"), None, None),
        P(("dp", "fsdp"), None, None),
        P(None, None, ("dp", "fsdp")),
        P(None, ("dp", "fsdp"), None),
        P(None, ("dp", "fsdp")),
        P(None, ("dp", "fsdp"), None),
        P(None, ("dp", "fsdp")),
        P(None, ("dp", "fsdp")),
        P(("dp", "fsdp"), None),
        P(("dp", "fsdp"), None),
        P(("dp", "fsdp")),
        P(("dp", "fsdp")),
        P(None, ("dp", "fsdp")),
        P(("dp", "fsdp"), None),
        P(("dp", "fsdp")),
        P(None, ("dp", "fsdp")),
        P(None, ("dp", "fsdp")),
        P(("dp", "fsdp"), None),
        P(("dp", "fsdp")),
        P(None, ("dp", "fsdp")),
    )
    fast = mesh.shape["dp"] == 4 and mesh.shape["fsdp"] == 8
    return jax.shard_map(local if fast else plain, mesh=mesh, in_specs=in_specs, out_specs=out_specs, check_vma=False)
```

```python
import math

import jax
import jax.numpy as jnp
from jax import lax
from jax.experimental import pallas as pl
from jax.experimental.pallas import tpu as pltpu
from jax.sharding import PartitionSpec as P

D = 512
FF = 2048
HEADS = 8
HEAD_DIM = 64
BUCKETS = 32
L = 512
TAPS = 32
PAD = 16
epsilon = 1e-05
F32, BF16 = jnp.float32, jnp.bfloat16
MESH = pl.DeviceIdType.MESH

SMALL, IN0, OUT0, QKV, ATT, GLU, CONV, IN1, OUT1, ROWS = 0, 16, 80, 144, 192, 208, 240, 256, 320, 384
GRADS = ROWS - IN0
(S_FFN, S_FOB, S_ATTN, S_AOB, S_CONV, S_BATCH, S_COB, S_FINAL, S_TAPS, S_ROWS) = (0, 4, 6, 8, 9, 11, 13, 14, 16, 48)
CHUNK = 64
BLOCK = 128
SOFT = 32
UNROLL = True


def dot(a, b):
    return jnp.dot(a, b, preferred_element_type=F32)


def dot_nt(a, b):
    return lax.dot_general(a, b, (((1,), (1,)), ((), ())), preferred_element_type=F32)


def dot_tn(a, b):
    return lax.dot_general(a, b, (((0,), (0,)), ((), ())), preferred_element_type=F32)


def chunks(body, carry=None, size=CHUNK):
    def step(i, carry):
        return body(pl.ds(pl.multiple_of(i * size, size), size), carry)

    return lax.fori_loop(0, L // size, step, carry, unroll=True)


def fold(values):
    return jnp.sum(values.reshape(values.shape[0] // 8, 8, values.shape[1]), axis=0)


def zeros8(width=D):
    return jnp.zeros((8, width), F32)


def total_row(values):
    return jnp.sum(values, axis=0, keepdims=True)


class Bag:
    pass


class Place:
    def __init__(self):
        self.planes = lax.axis_size("dp")
        self.chips = lax.axis_size("fsdp") // 2
        self.plane, inner = lax.axis_index("dp"), lax.axis_index("fsdp")
        self.z, self.core = inner // 2, inner % 2
        y, x = self.plane // 2, self.plane % 2
        self.plane_x, self.plane_y, self.plane_d = y * 2 + 1 - x, (1 - y) * 2 + x, (1 - y) * 2 + 1 - x
        self.twin = (self.plane, 2 * self.z + 1 - self.core)
        self.over_x = (self.plane_x, inner)
        self.over_y = (self.plane_y, inner)
        self.chip = [lax.rem(self.z + step, self.chips) for step in range(self.chips)]
        self.along = [(self.plane, 2 * chip + self.core) for chip in self.chip]
        self.rank = self.plane * 2 + self.core
        self.members = []
        for step in range(self.planes):
            for flip in range(2):
                if step or flip:
                    plane, core = lax.rem(self.plane + step, self.planes), lax.rem(self.core + flip, 2)
                    self.members.append(((plane, 2 * self.z + core), plane * 2 + core))


class Copies:
    def __init__(self, sends, receives, place):
        self.sends, self.receives, self.place = sends, receives, place
        self.begun = []

    def start(self, number, make, receive=None):
        def copy():
            source, target, device = make()
            return pltpu.make_async_remote_copy(
                source, target, self.sends.at[number], self.receives.at[number if receive is None else receive],
                device_id=device, device_id_type=MESH,
            )

        copy().start()
        self.begun.append(copy)

    def arrived(self, number, target):
        pltpu.make_async_remote_copy(
            target, target, self.sends.at[number], self.receives.at[number],
            device_id=self.place.twin, device_id_type=MESH,
        ).wait_recv()

    def sent(self):
        for copy in self.begun:
            copy().wait_send()
        self.begun = []


class Gather:
    def __init__(self, place, weights, copies, first, begin, size, split):
        self.place, self.weights, self.copies, self.first = place, weights, copies, first
        self.rows = pl.ds(begin, size)
        self.parts = (pl.ds(begin, split), pl.ds(begin + split, size - split))
        chips = place.chips
        self.x, self.y, self.d, self.t = chips, 2 * chips, 3 * chips, 3 * chips + 2

    @staticmethod
    def semaphores(chips):
        return 3 * chips + 6

    def column(self, plane, side, which):
        return self.weights.at[plane, :, side, which]

    def slot(self, plane, step):
        p = self.place
        return self.weights.at[plane, p.chip[(p.chips - step) % p.chips], p.core, self.rows]

    def move(self, number, ref, device):
        self.copies.start(self.first + number, lambda: (ref(), ref(), device))

    def arrived(self, number, ref):
        self.copies.arrived(self.first + number, ref)

    def along_z(self):
        p = self.place
        for d in range(1, p.chips):
            self.move(d, lambda: self.slot(p.plane, 0), p.along[d])

    def beside(self, step):
        p = self.place
        self.move(self.x + step, lambda: self.slot(p.plane, step), p.over_x)
        self.move(self.y + step, lambda: self.slot(p.plane, step), p.over_y)

    def own(self):
        self.beside(0)

    def forward(self):
        p = self.place
        for d in range(1, p.chips):
            self.arrived(d, self.slot(p.plane, d))
            self.beside(d)
        self.move(self.t, lambda: self.column(p.plane, p.core, self.rows), p.twin)

    def turn(self):
        p = self.place
        for d in range(p.chips):
            self.arrived(self.x + d, self.slot(p.plane_x, d))
        self.move(self.d, lambda: self.column(p.plane_x, p.core, self.parts[0]), p.over_y)
        for d in range(p.chips):
            self.arrived(self.y + d, self.slot(p.plane_y, d))
        self.move(self.d + 1, lambda: self.column(p.plane_y, p.core, self.parts[1]), p.over_x)
        self.move(self.t + 1, lambda: self.column(p.plane_x, p.core, self.rows), p.twin)
        self.move(self.t + 2, lambda: self.column(p.plane_y, p.core, self.rows), p.twin)

    def across(self):
        p = self.place
        self.arrived(self.d, self.column(p.plane_d, p.core, self.parts[0]))
        self.arrived(self.d + 1, self.column(p.plane_d, p.core, self.parts[1]))
        self.move(self.t + 3, lambda: self.column(p.plane_d, p.core, self.rows), p.twin)

    def done(self):
        p = self.place
        for number, plane in enumerate((p.plane, p.plane_x, p.plane_y, p.plane_d)):
            self.arrived(self.t + number, self.column(plane, 1 - p.core, self.rows))


def reduce_steps(place, data, twin, diagonal, from_x, from_y, from_z, copies, first, begin, size, split, landing, finish):
    p, core, chips = place, place.core, place.chips
    rows, lands = pl.ds(begin, size), pl.ds(landing, size)
    parts = (pl.ds(begin, split), pl.ds(begin + split, size - split))
    parts_land = (pl.ds(landing, split), pl.ds(landing + split, size - split))

    def column(plane, side, which):
        return data.at[plane, :, side, which]

    def add(plane, which, *sources):
        def step(zz, carry):
            value = data[plane, zz, core, which, :]
            for ref in sources:
                value = value + ref(zz)
            data[plane, zz, core, which, :] = value
            return carry

        lax.fori_loop(0, chips, step, 0, unroll=True)

    def read(ref, which, *lead):
        return lambda zz: ref[lead + (zz, which, slice(None))]

    def to_twin():
        for number, plane in enumerate((p.plane_d, p.plane_y, p.plane_x, p.plane)):
            copies.start(
                first + number, lambda plane=plane: (column(plane, 1 - core, rows), twin.at[plane, :, lands], p.twin)
            )

    def across():
        copies.arrived(first, twin.at[p.plane_d, :, lands])
        add(p.plane_d, rows, read(twin, lands, p.plane_d))
        copies.start(first + 4, lambda: (column(p.plane_d, core, parts[0]), diagonal.at[:, parts_land[0]], p.over_y))
        if split < size:
            copies.start(first + 5, lambda: (column(p.plane_d, core, parts[1]), diagonal.at[:, parts_land[1]], p.over_x))

    def beside():
        copies.arrived(first + 2, twin.at[p.plane_x, :, lands])
        copies.arrived(first + 4, diagonal.at[:, parts_land[0]])
        add(p.plane_x, rows, read(twin, lands, p.plane_x))
        add(p.plane_x, parts[0], read(diagonal, parts_land[0]))
        copies.start(first + 7, lambda: (column(p.plane_x, core, rows), from_x.at[:, lands], p.over_x))
        copies.arrived(first + 1, twin.at[p.plane_y, :, lands])
        add(p.plane_y, rows, read(twin, lands, p.plane_y))
        if split < size:
            copies.arrived(first + 5, diagonal.at[:, parts_land[1]])
            add(p.plane_y, parts[1], read(diagonal, parts_land[1]))
        copies.start(first + 6, lambda: (column(p.plane_y, core, rows), from_y.at[:, lands], p.over_y))

    def own_column():
        copies.arrived(first + 3, twin.at[p.plane, :, lands])
        copies.arrived(first + 6, from_y.at[:, lands])
        copies.arrived(first + 7, from_x.at[:, lands])
        add(p.plane, rows, read(twin, lands, p.plane), read(from_x, lands), read(from_y, lands))
        for d in range(1, chips):
            copies.start(
                first + 7 + d,
                lambda d=d: (data.at[p.plane, p.chip[d], core, rows], from_z.at[d - 1, lands], p.along[d]),
            )

    def along_z():
        for d in range(1, chips):
            copies.arrived(first + 7 + d, from_z.at[d - 1, lands])
        value = data[p.plane, p.z, core, rows, :].astype(F32)
        for d in range(1, chips):
            value = value + from_z[d - 1, lands, :].astype(F32)
        finish(value)

    return [to_twin, across, beside, own_column, along_z]


class Thin:
    def __init__(self, place, tiles, near, part, far, result, copies, first):
        self.place, self.tiles, self.near, self.part, self.far, self.result = place, tiles, near, part, far, result
        self.copies, self.first = copies, first

    def start(self):
        p = self.place
        for i, (device, rank) in enumerate(p.members):
            self.copies.start(
                self.first + i,
                lambda device=device: (self.tiles.at[device[0], :, lax.rem(device[1], 2)], self.near.at[p.rank], device),
                self.first + p.rank,
            )
        self.near[p.rank] = self.tiles[p.plane, :, p.core]

    def turn(self):
        p = self.place
        for device, rank in p.members:
            self.copies.arrived(self.first + rank, self.near.at[rank])
        value = self.near[0]
        for i in range(1, 2 * p.planes):
            value = value + self.near[i]
        self.part[...] = value
        base = self.first + 2 * p.planes
        for d in range(1, p.chips):
            self.copies.start(base + d, lambda d=d: (self.part.at[p.chip[d]], self.far.at[d], p.along[d]))

    def finish(self):
        p = self.place
        base = self.first + 2 * p.planes
        value = self.part[p.z]
        for d in range(1, p.chips):
            self.copies.arrived(base + d, self.far.at[d])
            value = value + self.far[d]
        self.result[...] = value


class Total:
    def __init__(self, place, own, near, part, far, result, copies, first):
        self.place, self.own, self.near, self.part, self.far, self.result = place, own, near, part, far, result
        self.copies, self.first = copies, first

    def start(self):
        p = self.place
        me = p.rank
        for i, (device, rank) in enumerate(p.members):
            self.copies.start(self.first + i, lambda device=device: (self.own, self.near.at[me], device), self.first + me)
        self.near[me] = self.own[...]

    def turn(self):
        p = self.place
        for device, rank in p.members:
            self.copies.arrived(self.first + rank, self.near.at[rank])
        value = self.near[0]
        for i in range(1, 2 * p.planes):
            value = value + self.near[i]
        self.part[...] = value
        base = self.first + 2 * p.planes
        for d in range(1, p.chips):
            self.copies.start(base + d, lambda d=d: (self.part, self.far.at[d], p.along[d]))

    def finish(self):
        p = self.place
        base = self.first + 2 * p.planes
        value = self.part[...]
        for d in range(1, p.chips):
            self.copies.arrived(base + d, self.far.at[d])
            value = value + self.far[d]
        self.result[...] = value


def at_points(table):
    def pump(index, place=0):
        for (iteration, where), steps in table.items():
            if where != place or (isinstance(index, int) and index != iteration):
                continue

            def act(steps=steps):
                for step in steps:
                    step()

            if isinstance(index, int):
                act()
            else:
                pl.when(index == iteration)(act)

    return pump


def still(index, place=0):
    pass


def standard(values):
    values = values.astype(F32)
    center = values - jnp.mean(values, axis=-1, keepdims=True)
    inverse = lax.rsqrt(jnp.mean(center * center, axis=-1, keepdims=True) + epsilon)
    return center * inverse, inverse


def norm_rows(source, target, small, row):
    gain, shift = 1.0 + small[row : row + 1, :], small[row + 1 : row + 2, :]

    def body(rows, carry):
        target[rows, :] = (standard(source[rows, :])[0] * gain + shift).astype(target.dtype)
        return carry

    chunks(body, 0)


def norm_back(source, grad, upstream, result, small, row, grads):
    gain = 1.0 + small[row : row + 1, :]

    def body(rows, carry):
        unit, inverse = standard(source[rows, :])
        given = grad[rows, :].astype(F32)
        inner = given * gain
        back = inverse * (
            inner
            - jnp.mean(inner, axis=-1, keepdims=True)
            - unit * jnp.mean(inner * unit, axis=-1, keepdims=True)
        )
        result[rows, :] = back if upstream is None else upstream[rows, :] + back
        return carry[0] + fold(given * unit), carry[1] + fold(given)

    first, second = chunks(body, (zeros8(), zeros8()))
    grads[row : row + 1, :] = total_row(first)
    grads[row + 1 : row + 2, :] = total_row(second)


def block_cols(c):
    return pl.ds(c * D if isinstance(c, int) else pl.multiple_of(c * D, D), D)


def columns(weights, start, block):
    return weights[:, :, :, start + 16 * block : start + 16 * block + 16, :].reshape(D, D)


def put_columns(weights, start, block, value):
    rows = pl.ds(start + 16 * block, 16)
    weights[:, :, :, rows, :] = value.astype(BF16).reshape(weights.shape[:3] + (16, D))


def lines_of(weights, start, block):
    return weights[block, :, :, start : start + 64, :].reshape(D, D)


def put_lines(weights, start, block, value):
    weights[block, :, :, start : start + 64, :] = value.astype(BF16).reshape(weights.shape[1:3] + (64, D))


def feed_inner(source, normed, active, slope, raws, weights, small, inner_bias, layer, pump):
    norm_rows(source, normed, small, S_FFN + 2 * layer)
    for c in range(FF // D):
        pump(c)
        cols, raw = block_cols(c), raws[c % 2]
        raw[...] = dot(normed[...], columns(weights, (IN0, IN1)[layer], c))
        bias = inner_bias[layer : layer + 1, cols]

        def body(rows, carry, cols=cols, raw=raw, bias=bias):
            inner = raw[rows, :] + bias
            sigma = jax.nn.sigmoid(inner)
            value = inner * sigma
            active[rows, cols] = value.astype(BF16)
            slope[rows, cols] = (sigma + value * (1.0 - sigma)).astype(BF16)
            return carry

        chunks(body, 0)


def feed_outer(source, active, result, hold, weights, small, layer):
    begin = (OUT0, OUT1)[layer]
    hold[...] = dot(active[...], weights[:, :, :, begin : begin + 64, :].reshape(FF, D))
    bias = small[S_FOB + layer : S_FOB + layer + 1, :]

    def body(rows, carry):
        result[rows, :] = source[rows, :].astype(F32) + 0.5 * (hold[rows, :] + bias)
        return carry

    chunks(body, 0)


def feed_back_start(upstream, low, grads, layer):
    def start(rows, carry):
        half = 0.5 * upstream[rows, :]
        low[rows, :] = half.astype(BF16)
        return carry + fold(half)

    grads[S_FOB + layer : S_FOB + layer + 1, :] = total_row(chunks(start, zeros8()))


def feed_back_outer(active, low, weights, begin, pump):
    for c in range(FF // D):
        put_lines(weights, begin, c, dot_tn(active[:, block_cols(c)], low[...]))
        pump(c)


def feed_back_inner(normed, slope, low, raws, weights, target, inner_grads, layer, pump):
    begin = (OUT0, OUT1)[layer]
    for c in range(FF // D):
        cols, raw = block_cols(c), raws[c % 2]
        raw[...] = dot_nt(low[...], lines_of(weights, begin, c))

        def body(rows, carry, cols=cols, raw=raw):
            grad = raw[rows, :] * slope[rows, cols].astype(F32)
            slope[rows, cols] = grad.astype(BF16)
            return carry + fold(grad)

        inner_grads[layer : layer + 1, cols] = total_row(chunks(body, zeros8()))
        if target is not None:
            put_columns(weights, target, c, dot_tn(normed[...], slope[:, cols]))
        pump(c)


def product_back(grad, normed, total, weights, begin, blocks, pump):
    value = None
    for c in range(blocks):
        part = dot_nt(grad[:, block_cols(c)], columns(weights, begin, c))
        value = part if value is None else value + part
    total[...] = value
    for c in range(blocks):
        if normed is not None:
            put_columns(weights, begin, c, dot_tn(normed[...], grad[:, block_cols(c)]))
        pump(c)


def bucket_choice(buckets):
    return (lax.broadcasted_iota(jnp.int32, (BUCKETS, 2 * L), 0) == buckets[...]).astype(F32)


def attention_mix(source, normed, mixed, weights, small):
    norm_rows(source, normed, small, S_ATTN)

    for c in range(3):
        mixed[:, block_cols(c)] = dot(normed[...], columns(weights, QKV, c)).astype(BF16)


def attention_mask(mask, bounds, marks):
    def body(rows, carry):
        same = bounds[pl.ds(rows.start + PAD, CHUNK), 0:1] == marks[...]
        mask[rows, :] = jnp.where(same, 3e38, -1e30)
        return carry

    chunks(body, 0)


def attention_squares(lines, squares, table, buckets):
    lines[...] = dot(table[...].astype(BF16), bucket_choice(buckets).astype(BF16))

    def head(h, carry):
        line = jnp.broadcast_to(lines[pl.ds(h, 1), :], (BLOCK, 2 * L))
        square = pltpu.roll(line, 2 * L - BLOCK + 1, 1, stride=1, stride_axis=0).astype(BF16)
        for part in range(2):
            squares[lax.rem(h, 4), lax.div(h, 4), part * BLOCK : (part + 1) * BLOCK, :] = square[:, part * L : (part + 1) * L]
        return carry

    lax.fori_loop(0, HEADS, head, 0)


def attention_forward(source, mixed, probs, joined, recips, result, squares, mask, hold, hold2, weights, small, pump):
    lane = lax.broadcasted_iota(jnp.int32, (1, 128), 1)

    def pair(index, carry):
        begin = pl.multiple_of(128 * index, 128)
        query = mixed[:, pl.ds(begin, 128)] * HEAD_DIM ** (-0.5)
        keys = mixed[:, pl.ds(D + begin, 128)]
        contents = mixed[:, pl.ds(2 * D + begin, 128)]
        parts = []
        for half, raw in enumerate((hold, hold2)):
            here = (lane // HEAD_DIM) == half
            raw[...] = dot_nt(jnp.where(here, query, jnp.zeros_like(query)), keys)
        for half, raw in enumerate((hold, hold2)):
            head = 2 * index + half
            here = (lane // HEAD_DIM) == half
            for block in range(L // BLOCK):

                def body(i, carry, block=block, raw=raw, head=head):
                    at = pl.multiple_of(i * SOFT, SOFT)
                    rows = pl.ds(block * BLOCK + at, SOFT)
                    square = squares[lax.rem(head, 4), lax.div(head, 4), pl.ds(at, SOFT), 384 - block * BLOCK : L]
                    if block < L // BLOCK - 1:
                        more = squares[lax.rem(head, 4), lax.div(head, 4), pl.ds(BLOCK + at, SOFT), 0 : 384 - block * BLOCK]
                        square = jnp.concatenate([square, more], axis=1)
                    scores = jnp.minimum(raw[rows, :] + square.astype(F32), mask[rows, :])
                    probs[head, rows, :] = jnp.exp(scores - jnp.max(scores, axis=1, keepdims=True)).astype(BF16)
                    return carry

                lax.fori_loop(0, BLOCK // SOFT, body, 0, unroll=UNROLL)
                if half:
                    pump(index, block)
            parts.append(dot(probs[head], jnp.where(here, contents, jnp.ones_like(contents))))
        value = jnp.where(lane < HEAD_DIM, parts[0], parts[1])
        sums = jnp.where(lane < HEAD_DIM, pltpu.roll(parts[0], HEAD_DIM, 1), pltpu.roll(parts[1], HEAD_DIM, 1))
        recip = 1.0 / sums
        recips[:, pl.ds(begin, 128)] = recip
        joined[:, pl.ds(begin, 128)] = value * recip
        return carry

    lax.fori_loop(0, HEADS // 2, pair, 0)
    hold[...] = dot(joined[...].astype(BF16), columns(weights, ATT, 0))
    bias = small[S_AOB : S_AOB + 1, :]

    def body(rows, carry):
        result[rows, :] = source[rows, :] + hold[rows, :] + bias
        return carry

    chunks(body, 0)


def attention_back_start(upstream, joined, recips, low, spread, hold, weights, grads):
    def start(rows, carry):
        given = upstream[rows, :]
        low[rows, :] = given.astype(BF16)
        return carry + fold(given)

    grads[S_AOB : S_AOB + 1, :] = total_row(chunks(start, zeros8()))
    hold[...] = dot_nt(low[...], columns(weights, ATT, 0))

    def body(rows, carry):
        spread[rows, :] = (hold[rows, :] * recips[rows, :]).astype(BF16)
        return carry

    chunks(body, 0)
    put_columns(weights, ATT, 0, dot_tn(joined[...].astype(BF16), low[...]))


def attention_backward(mixed, probs, spread, joined, grad_mixed, scaled, hold, hold2, means, diagonals, lines, buckets, table_grad, pump):
    lane = lax.broadcasted_iota(jnp.int32, (1, 128), 1)
    sides = lax.broadcasted_iota(jnp.int32, (256, 256), 0) // HEAD_DIM % 2 == lax.broadcasted_iota(jnp.int32, (256, 256), 1) // 128
    sides = jnp.where(sides, 1.0, 0.0).astype(BF16)

    def pair(index, carry):
        begin = pl.multiple_of(128 * index, 128)
        query = mixed[:, pl.ds(begin, 128)]
        keys = mixed[:, pl.ds(D + begin, 128)]
        contents = mixed[:, pl.ds(2 * D + begin, 128)]
        incoming = spread[:, pl.ds(begin, 128)]
        for half, raw in enumerate((hold, hold2)):
            here = (lane // HEAD_DIM) == half
            raw[...] = dot_nt(jnp.where(here, incoming, jnp.zeros_like(incoming)), contents)
        both = incoming.astype(F32) * joined[:, pl.ds(begin, 128)]
        upper = both.astype(BF16)
        lower = (both - upper.astype(F32)).astype(BF16)
        means[:, 0:256] = dot(jnp.concatenate([upper, lower], axis=1), sides)
        turned_query, turned_incoming = query.T, incoming.T
        grads_query, grads_keys, grads_contents = [], [], []
        for half, raw in enumerate((hold, hold2)):
            head = 2 * index + half
            side = slice(half * HEAD_DIM, (half + 1) * HEAD_DIM)
            cols = pl.ds(half * L, L)
            part = zeros8(2 * L)
            for u in range(BLOCK // 16):
                tiles = [None] * 7 + [jnp.zeros((16, 128), F32)]
                for block in range(L // BLOCK):
                    rows = pl.ds(block * BLOCK + 16 * u, 16)
                    mean = means[rows, 128 * half : 128 * half + 128]
                    slant = probs[head, rows, :].astype(F32) * (raw[rows, :] - jnp.concatenate([mean] * 4, axis=1))
                    scaled[rows, cols] = slant.astype(BF16)
                    for j in range(4):
                        piece = slant[:, 128 * j : 128 * j + 128]
                        at = 3 - block + j
                        tiles[at] = piece if tiles[at] is None else tiles[at] + piece
                full = jnp.concatenate(tiles, axis=1)
                part = part + pltpu.roll(full[0:8], BLOCK - 8 - 16 * u, 1) + pltpu.roll(full[8:16], BLOCK - 16 - 16 * u, 1)
            diagonals[:, pl.ds(head, 1), :] = part.reshape(8, 1, 2 * L)
            grads_query.append(dot(scaled[:, cols], keys))
            grads_keys.append(dot(turned_query[side], scaled[:, cols]))
            grads_contents.append(dot(turned_incoming[side], probs[head]))
            pump(index, half)
        scale = HEAD_DIM ** (-0.5)
        grad_mixed[:, pl.ds(begin, 128)] = (jnp.where(lane < HEAD_DIM, *grads_query) * scale).astype(BF16)
        grad_mixed[:, pl.ds(D + begin, 128)] = (jnp.concatenate(grads_keys, axis=0).T * scale).astype(BF16)
        grad_mixed[:, pl.ds(2 * D + begin, 128)] = jnp.concatenate(grads_contents, axis=0).T.astype(BF16)
        return carry

    lax.fori_loop(0, HEADS // 2, pair, 0)
    line = diagonals[7]
    for r in range(7):
        line = line + pltpu.roll(diagonals[r], 7 - r, 1)
    table_grad[...] = lax.dot_general(
        line, bucket_choice(buckets), (((1,), (1,)), ((), ())),
        precision=lax.Precision.HIGHEST, preferred_element_type=F32,
    )


def clear_pads(padded):
    edge = jnp.zeros((4, PAD, 128), F32)
    padded[:, 0:PAD, :] = edge
    padded[:, PAD + L : 2 * PAD + L, :] = edge


def conv_front(source, normed, sigma, tilt, gated, middle, sums, hold, spare, weights, small, gate_bias, bounds, pump):
    norm_rows(source, normed, small, S_CONV)
    clear_pads(gated)
    hold[...] = dot(normed[...], columns(weights, GLU, 1))
    bias = gate_bias[0:1, D:]

    def gate(rows, carry):
        gate = jax.nn.sigmoid(hold[rows, :] + bias)
        spare[rows, :] = gate
        sigma[rows, :] = gate.astype(BF16)
        return carry

    chunks(gate, 0)
    hold[...] = dot(normed[...], columns(weights, GLU, 0))
    bias = gate_bias[0:1, :D]

    def unit(rows, carry):
        gate = spare[rows, :]
        values = (hold[rows, :] + bias) * gate
        tilt[rows, :] = (values * (1.0 - gate)).astype(BF16)
        for j in range(4):
            gated[j, pl.ds(rows.start + PAD, CHUNK), :] = values[:, 128 * j : 128 * j + 128]
        return carry

    chunks(unit, 0)
    size = 32

    def slide(i, carry):
        begin = pl.multiple_of(i * size, size)
        marks = bounds[pl.ds(begin + PAD, size), :]
        accs = [jnp.zeros((size, 128), F32) for _ in range(4)]
        for k in range(TAPS):
            same = bounds[pl.ds(begin + k, size), :] == marks
            for j in range(4):
                tap = small[S_TAPS + k : S_TAPS + k + 1, 128 * j : 128 * j + 128]
                accs[j] += jnp.where(same, gated[j, pl.ds(begin + k, size), :], 0.0) * tap
        result = []
        for j in range(4):
            middle[pl.ds(begin, size), 128 * j : 128 * j + 128] = accs[j]
            result.append(carry[j] + fold(accs[j]))
            result.append(carry[4 + j] + fold(accs[j] * accs[j]))
        pump(i)
        return result[0::2] + result[1::2]

    ends = lax.fori_loop(0, L // size, slide, [zeros8(128)] * 8, unroll=2)
    for j in range(4):
        sums[0:1, 128 * j : 128 * j + 128] = total_row(ends[j])
        sums[1:2, 128 * j : 128 * j + 128] = total_row(ends[4 + j])


def conv_rest(source, middle, sums, unit, active, slope, result, hold, weights, small, frames):
    center = sums[0:1, :] * (1.0 / frames)
    inverse = lax.rsqrt(sums[1:2, :] * (1.0 / frames) - center * center + epsilon)
    gain, shift = 1.0 + small[S_BATCH : S_BATCH + 1, :], small[S_BATCH + 1 : S_BATCH + 2, :]

    def body(rows, carry):
        values = (middle[rows, :] - center) * inverse
        unit[rows, :] = values
        normal = values * gain + shift
        sigma = jax.nn.sigmoid(normal)
        value = normal * sigma
        active[rows, :] = value.astype(BF16)
        slope[rows, :] = (sigma + value * (1.0 - sigma)).astype(slope.dtype)
        return carry

    chunks(body, 0)
    hold[...] = dot(active[...], columns(weights, CONV, 0))
    bias = small[S_COB : S_COB + 1, :]

    def add(rows, carry):
        result[rows, :] = source[rows, :] + hold[rows, :] + bias
        return carry

    chunks(add, 0)


def conv_back_rest(upstream, unit, slope, grad_normal, low, hold, weights, grads, sums):
    def start(rows, carry):
        given = upstream[rows, :]
        low[rows, :] = given.astype(BF16)
        return carry + fold(given)

    grads[S_COB : S_COB + 1, :] = total_row(chunks(start, zeros8()))
    hold[...] = dot_nt(low[...], columns(weights, CONV, 0))

    def body(rows, carry):
        grad = hold[rows, :] * slope[rows, :].astype(F32)
        grad_normal[rows, :] = grad
        return carry[0] + fold(grad), carry[1] + fold(grad * unit[rows, :])

    first, second = chunks(body, (zeros8(), zeros8()))
    sums[0:1, :] = total_row(first)
    sums[1:2, :] = total_row(second)
    grads[S_BATCH : S_BATCH + 1, :] = total_row(second)
    grads[S_BATCH + 1 : S_BATCH + 2, :] = total_row(first)


def conv_back_front(
    sigma, tilt, gated, unit, grad_normal, front_sums, sums, padded, grad_joined, hold, tap_sums, small, bounds, grads, gate_grads,
    frames, pump,
):
    center = front_sums[0:1, :] * (1.0 / frames)
    inverse = lax.rsqrt(front_sums[1:2, :] * (1.0 / frames) - center * center + epsilon)
    gain = 1.0 + small[S_BATCH : S_BATCH + 1, :]
    mean0, mean1 = gain * sums[0:1, :] * (1.0 / frames), gain * sums[1:2, :] * (1.0 / frames)
    clear_pads(padded)

    def start(rows, carry):
        grad = inverse * (gain * grad_normal[rows, :] - mean0 - unit[rows, :] * mean1)
        for j in range(4):
            padded[j, pl.ds(rows.start + PAD, CHUNK), :] = grad[:, 128 * j : 128 * j + 128]
        return carry

    chunks(start, 0)
    tap_sums[...] = jnp.zeros_like(tap_sums)
    size = 32

    def slide(i, carry):
        begin = pl.multiple_of(i * size, size)
        marks = bounds[pl.ds(begin + PAD, size), :]
        accs = [jnp.zeros((size, 128), F32) for _ in range(4)]
        here = [gated[j, pl.ds(begin + PAD, size), :] for j in range(4)]
        for k in range(TAPS):
            same = bounds[pl.ds(begin + 2 * PAD - k, size), :] == marks
            for j in range(4):
                tap = small[S_TAPS + k : S_TAPS + k + 1, 128 * j : 128 * j + 128]
                grad = jnp.where(same, padded[j, pl.ds(begin + 2 * PAD - k, size), :], 0.0)
                accs[j] += grad * tap
                tap_sums[k, :, 128 * j : 128 * j + 128] += fold(grad * here[j])
        for j in range(4):
            hold[pl.ds(begin, size), 128 * j : 128 * j + 128] = accs[j]
        pump(i)
        return carry

    lax.fori_loop(0, L // size, slide, 0, unroll=2)
    grads[S_TAPS : S_TAPS + TAPS, :] = jnp.sum(tap_sums[...], axis=1)

    def split(rows, carry):
        grad = hold[rows, :]
        first = grad * sigma[rows, :].astype(F32)
        second = grad * tilt[rows, :].astype(F32)
        grad_joined[rows, :D] = first.astype(BF16)
        grad_joined[rows, D : 2 * D] = second.astype(BF16)
        return carry[0] + fold(first), carry[1] + fold(second)

    first, second = chunks(split, (zeros8(), zeros8()))
    gate_grads[0:1, :D] = total_row(first)
    gate_grads[0:1, D:] = total_row(second)


THIN = (
    ("ffn_norm", S_FFN), ("ffn_out_bias", S_FOB), ("attn_norm", S_ATTN), ("attn_out_bias", S_AOB), ("conv_norm", S_CONV),
    ("batch_norm", S_BATCH), ("conv_out_bias", S_COB), ("final_norm", S_FINAL), ("depth_kernel", S_TAPS),
)


def turned(value):
    rows, lanes = value.shape
    value = jnp.concatenate([value, jnp.zeros((rows, 128 - lanes), F32)], axis=1)
    return jnp.concatenate([value, jnp.zeros((128 - rows, 128), F32)], axis=0).T[:lanes, :rows]


def pack_small(b, tile):
    tile[...] = jnp.zeros_like(tile)
    for name, row in THIN:
        value = getattr(b, name)[...].astype(F32)
        if name == "depth_kernel":
            value = turned(value)
        value = value.reshape(-1, value.shape[-1])
        for r in range(0, value.shape[0], 16):
            part = value[r : r + 16]
            begin = (row + r) % 16
            at = 128 * ((row + r) // 16)
            tile[begin : begin + part.shape[0], at : at + part.shape[1]] = part
    tile[0:2, 384 : 384 + b.ffn_in_bias.shape[1]] = b.ffn_in_bias[...].astype(F32)
    wide, few = b.glu_bias.shape[0], b.rel_table.shape[0]
    tile[2:3, 384 : 384 + wide] = b.glu_bias[...].astype(F32).reshape(1, wide)
    tile[3:4, 384 : 384 + few] = b.rel_table[...].astype(F32).reshape(1, few)


def load_weights(b, place):
    copies = {}

    def load(row, source):
        target = b.weights.at[place.plane, place.z, place.core, pl.ds(row, source.shape[0])]
        copies[row] = pltpu.make_async_copy(source, target, b.load_sems.at[len(copies)])
        copies[row].start()

    for layer in range(2):
        for c in range(FF // D):
            load((IN0, IN1)[layer] + 16 * c, b.ffn_in.at[layer, :, pl.ds(D * c, D)])
        load((OUT0, OUT1)[layer], b.ffn_out.at[layer])
        if layer == 0:
            for c in range(3):
                load(QKV + 16 * c, b.qkv_weight.at[:, pl.ds(D * c, D)])
            load(ATT, b.attn_out.at[:, :])
            for c in range(2):
                load(GLU + 16 * c, b.glu_weight.at[:, pl.ds(D * c, D)])
            load(CONV, b.conv_out.at[:, :])
    return copies


def unpack_small(b, place):
    per = 2 * place.chips
    count = place.planes * per
    width = D // count
    for device in range(count):
        tile = b.weights[device // per, (device % per) // 2, device % 2, 0:16, :].astype(F32)
        for q in range(3):
            b.small[16 * q : 16 * q + 16, width * device : width * device + width] = tile[:, 128 * q : 128 * q + width]
        b.inner_bias[:, 4 * width * device : 4 * width * (device + 1)] = tile[0:2, 384 : 384 + 4 * width]
        b.gate_bias[:, 2 * width * device : 2 * width * (device + 1)] = tile[2:3, 384 : 384 + 2 * width]
        few = HEADS * BUCKETS // count
        head, at = few * device // BUCKETS, few * device % BUCKETS
        b.table[head : head + 1, at : at + few] = tile[3:4, 384 : 384 + few]


def pack_small_grads(b, place):
    per = 2 * place.chips
    count = place.planes * per
    width = D // count
    few = HEADS * BUCKETS // count
    for device in range(count):
        tile = b.edges.at[device // per, (device % per) // 2, device % 2]
        for g in range(8):
            tile[0:6, 16 * g : 16 * g + width] = b.grads[6 * g : 6 * g + 6, width * device : width * device + width]
        for m in range(2):
            tile[6:7, 64 * m : 64 * m + 4 * width] = b.inner_grads[m : m + 1, 4 * width * device : 4 * width * (device + 1)]
        tile[7:8, 0 : 2 * width] = b.gate_grads[:, 2 * width * device : 2 * width * (device + 1)]
        head, at = few * device // BUCKETS, few * device % BUCKETS
        tile[7:8, 64 : 64 + few] = b.table_grad[head : head + 1, at : at + few]


INPUTS = (
    "inputs", "segments", "buckets", "cotangent", "ffn_norm", "ffn_in", "ffn_in_bias", "ffn_out", "ffn_out_bias", "attn_norm",
    "qkv_weight", "attn_out", "attn_out_bias", "rel_table", "conv_norm", "glu_weight", "glu_bias", "depth_kernel", "batch_norm",
    "conv_out", "conv_out_bias", "final_norm",
)
LOADED = ("inputs", "cotangent", "ffn_in", "ffn_out", "qkv_weight", "attn_out", "glu_weight", "conv_out")
OUTPUTS = ("output", "grad_x", "shard", "thin")
GATHERS = ((SMALL, 48, 32), (IN0 + 32, 32, 16), (OUT0, 64, 32), (QKV, 64, 32), (GLU, 48, 32), (IN1, 64, 32), (OUT1, 64, 32))
REDUCES = (
    (OUT1, OUT1, 64, 32), (IN1, IN1, 64, 32), (CONV, CONV, 16, 16), (GLU, GLU, 32, 16),
    (ATT, ATT, 16, 16), (QKV, QKV, 48, 32), (OUT1, OUT0, 32, 16),
    (OUT1 + 32, OUT0 + 32, 32, 16), (IN1, IN0, 32, 16), (IN1 + 32, IN0 + 32, 32, 16),
)


def scratch_of(planes, chips):
    wide, low, big = pltpu.VMEM((L, D), F32), pltpu.VMEM((L, D), BF16), pltpu.VMEM((L, FF), BF16)
    pads = pltpu.VMEM((4, L + 2 * PAD, 128), F32)
    stats = pltpu.VMEM((2, D), F32)
    return dict(
        weights=pltpu.VMEM((planes, chips, 2, ROWS, D), BF16),
        twin=pltpu.VMEM((planes, chips, GRADS, D), BF16),
        diagonal=pltpu.VMEM((chips, GRADS, D), BF16),
        from_x=pltpu.VMEM((chips, GRADS, D), BF16),
        from_y=pltpu.VMEM((chips, GRADS, D), BF16),
        from_z=pltpu.VMEM((chips - 1, GRADS, D), BF16),
        edges=pltpu.VMEM((planes, chips, 2, 8, 128), F32),
        edge_near=pltpu.VMEM((2 * planes, chips, 8, 128), F32),
        edge_part=pltpu.VMEM((chips, 8, 128), F32),
        edge_far=pltpu.VMEM((chips, 8, 128), F32),
        small=pltpu.VMEM((S_ROWS, D), F32),
        inner_bias=pltpu.VMEM((2, FF), F32),
        gate_bias=pltpu.VMEM((1, 2 * D), F32),
        table=pltpu.VMEM((HEADS, BUCKETS), F32),
        tile=pltpu.VMEM((16, D), F32),
        grads=pltpu.VMEM((S_ROWS, D), F32),
        inner_grads=pltpu.VMEM((2, FF), F32),
        gate_grads=pltpu.VMEM((1, 2 * D), F32),
        table_grad=pltpu.VMEM((HEADS, BUCKETS), F32),
        lines=pltpu.VMEM((HEADS, 2 * L), F32),
        choice=pltpu.VMEM((1, 2 * L), jnp.int32),
        bounds=pltpu.VMEM((L + 2 * PAD, 128), F32),
        marks=pltpu.VMEM((1, L), F32),
        front_own=stats, back_own=stats, front_sums=stats, back_sums=stats, front_part=stats, back_part=stats,
        front_near=pltpu.VMEM((2 * planes, 2, D), F32), back_near=pltpu.VMEM((2 * planes, 2, D), F32),
        front_far=pltpu.VMEM((chips, 2, D), F32), back_far=pltpu.VMEM((chips, 2, D), F32),
        x1=wide, x2=wide, x3=wide, x4=wide, normed_a=low, normed_c=low, normed1=low,
        active0=big, slope0=big, active1=big, slope1=big, mixed=pltpu.VMEM((L, 3 * D), BF16),
        probs=pltpu.VMEM((HEADS, L, L), BF16), joined=wide, recips=wide, diagonals=pltpu.VMEM((8, HEADS, 2 * L), F32), sigma=low, tilt=low, gated=pads, middle=wide, active_c=low, slope_c=low,
        padded=pads, low=low, hold=wide, total=wide, taps=pltpu.VMEM((TAPS, 8, D), F32),
        x0=low, given=low, result=low,
        load_sems=pltpu.SemaphoreType.DMA((17,)),
        edge_sems=pltpu.SemaphoreType.DMA((4,)),
        gather_sends=pltpu.SemaphoreType.DMA((len(GATHERS) * Gather.semaphores(chips),)),
        gather_receives=pltpu.SemaphoreType.DMA((len(GATHERS) * Gather.semaphores(chips),)),
        reduce_sends=pltpu.SemaphoreType.DMA((len(REDUCES) * (chips + 7),)),
        reduce_receives=pltpu.SemaphoreType.DMA((len(REDUCES) * (chips + 7),)),
        total_sends=pltpu.SemaphoreType.DMA((3 * (2 * planes + chips),)),
        total_receives=pltpu.SemaphoreType.DMA((3 * (2 * planes + chips),)),
    )


def whole_kernel(names, *refs):
    b = Bag()
    for name, ref in zip(names, refs):
        setattr(b, name, ref)
    place = Place()
    planes, chips = place.planes, place.chips
    frames = L * planes * chips * 2
    barrier = pltpu.get_barrier_semaphore()
    near = [device for device, rank in place.members] + [place.along[d] for d in range(1, chips)]
    for device in near:
        pl.semaphore_signal(barrier, inc=1, device_id=device, device_id_type=MESH)
    loads = load_weights(b, place)
    load_x = pltpu.make_async_copy(b.inputs.at[0], b.x0, b.edge_sems.at[0])
    load_cotangent = pltpu.make_async_copy(b.cotangent.at[0], b.given, b.edge_sems.at[1])
    load_x.start()
    load_cotangent.start()
    pack_small(b, b.tile)
    b.weights[place.plane, place.z, place.core, 0:16, :] = b.tile[...].astype(BF16)
    pl.semaphore_wait(barrier, len(near))

    gathers = Copies(b.gather_sends, b.gather_receives, place)
    rounds = [
        Gather(place, b.weights, gathers, i * Gather.semaphores(chips), begin, size, split)
        for i, (begin, size, split) in enumerate(GATHERS)
    ]
    r0, r1, r2, r3, r4, r5, r6 = rounds
    for r, (begin, size, _) in zip(rounds, GATHERS):
        for row, copy in loads.items():
            if begin <= row < begin + size:
                copy.wait()
        r.along_z()
        if r in rounds[:5]:
            r.own()
    b.marks[...] = b.segments[...].astype(F32)
    b.bounds[...] = jnp.full(b.bounds.shape, -1.0, F32)
    b.bounds[PAD : PAD + L, :] = jnp.broadcast_to(b.marks[...], (128, L)).T
    b.choice[...] = jnp.full(b.choice.shape, -1, jnp.int32)
    b.choice[:, 0 : 2 * L - 1] = b.buckets[...].reshape(1, 2 * L - 1)
    attention_mask(b.x4, b.bounds, b.marks)
    for step in (r0.forward, r1.forward, r0.turn, r1.turn, r2.forward, r0.across, r0.done):
        step()
    unpack_small(b, place)

    x0 = b.x0
    load_x.wait()
    raws = (b.hold, b.total)
    feed_inner(
        x0, b.normed_c, b.active0, b.slope0, raws, b.weights, b.small, b.inner_bias, 0,
        at_points({(2, 0): (r1.across, r1.done, r3.forward)}),
    )
    attention_squares(b.lines, b.twin, b.table, b.choice)
    for step in (r2.turn, r3.turn, r4.forward, r5.own, r2.across, r2.done):
        step()
    feed_outer(x0, b.active0, b.x1, b.hold, b.weights, b.small, 0)
    r3.across()
    r3.done()
    attention_mix(b.x1, b.normed_a, b.mixed, b.weights, b.small)
    for step in (r4.turn, r5.forward, r6.own, r6.forward):
        step()
    attention_forward(
        b.x1, b.mixed, b.probs, b.joined, b.recips, b.x2, b.twin, b.x4, b.hold, b.x3, b.weights, b.small, still
    )
    r4.across()
    r4.done()
    conv_front(
        b.x2, b.normed_c, b.sigma, b.tilt, b.gated, b.middle, b.front_own, b.hold, b.total, b.weights, b.small, b.gate_bias, b.bounds,
        at_points({(5, 0): (r5.turn,)}),
    )
    totals = Copies(b.total_sends, b.total_receives, place)
    front = Total(place, b.front_own, b.front_near, b.front_part, b.front_far, b.front_sums, totals, 0)
    front.start()
    r6.turn()
    front.turn()
    front.finish()
    conv_rest(b.x2, b.middle, b.front_sums, b.middle, b.active_c, b.slope_c, b.x3, b.hold, b.weights, b.small, frames)
    r5.across()
    r5.done()
    feed_inner(b.x3, b.normed1, b.active1, b.slope1, raws, b.weights, b.small, b.inner_bias, 1, still)
    r6.across()
    r6.done()
    feed_outer(b.x3, b.active1, b.x4, b.hold, b.weights, b.small, 1)
    norm_rows(b.x4, b.result, b.small, S_FINAL)
    save_output = pltpu.make_async_copy(b.result, b.output.at[0], b.edge_sems.at[2])
    save_output.start()
    load_cotangent.wait()
    flow = b.x4
    norm_back(b.x4, b.given, None, flow, b.small, S_FINAL, b.grads)
    gathers.sent()

    early = Copies(b.reduce_sends, b.reduce_receives, place)
    reduces = Copies(b.reduce_sends, b.reduce_receives, place)
    landings = (b.twin, b.diagonal, b.from_x, b.from_y, b.from_z)

    def finish(begin, size):
        def act(value):
            b.shard[begin - IN0 : begin - IN0 + size, :] = value

        return act

    backs = [
        reduce_steps(
            place, b.weights, *landings, early if i < 2 else reduces, i * (chips + 7), begin, size, split, owner - IN0,
            finish(owner, size),
        )
        for i, (begin, owner, size, split) in enumerate(REDUCES)
    ]
    out1, in1, tip, glu, att, mix, out0, out0_end, in0, in0_end = backs
    feed_back_start(flow, b.low, b.grads, 1)
    feed_back_inner(b.normed1, b.slope1, b.low, raws, b.weights, None, b.inner_grads, 1, still)
    feed_back_outer(b.active1, b.low, b.weights, OUT1, still)
    out1[0]()
    product_back(b.slope1, b.normed1, b.total, b.weights, IN1, 4, still)
    in1[0]()
    out1[1]()
    norm_back(b.x3, b.total, flow, flow, b.small, S_FFN + 2, b.grads)
    in1[1]()
    grad_normal = b.x3
    conv_back_rest(flow, b.middle, b.slope_c, grad_normal, b.low, b.hold, b.weights, b.grads, b.back_own)
    back = Total(place, b.back_own, b.back_near, b.back_part, b.back_far, b.back_sums, totals, 2 * planes + chips)
    back.start()
    put_columns(b.weights, CONV, 0, dot_tn(b.active_c[...], b.low[...]))
    tip[0]()
    back.turn()
    out1[2]()
    tip[1]()
    back.finish()
    conv_back_front(
        b.sigma, b.tilt, b.gated, b.middle, grad_normal, b.front_sums, b.back_sums, b.padded, b.active1, b.hold, b.taps, b.small,
        b.bounds, b.grads, b.gate_grads, frames, at_points({(4, 0): (in1[2],), (8, 0): (tip[2],), (14, 0): (out1[3],)}),
    )
    product_back(b.active1, b.normed_c, b.total, b.weights, GLU, 2, still)
    glu[0]()
    norm_back(b.x2, b.total, flow, flow, b.small, S_CONV, b.grads)
    attention_back_start(flow, b.joined, b.recips, b.low, b.normed1, b.hold, b.weights, b.grads)
    att[0]()
    glu[1]()
    attention_backward(
        b.mixed, b.probs, b.normed1, b.joined, b.active1, b.slope1, b.hold, b.x3, b.total, b.diagonals, b.lines, b.choice,
        b.table_grad, at_points({(0, 1): (in1[3], att[1]), (2, 0): (tip[3],), (2, 1): (glu[2],), (3, 0): (out1[4],), (3, 1): (att[2],)}),
    )
    product_back(b.active1, b.normed_a, b.total, b.weights, QKV, 3, still)
    mix[0]()
    norm_back(b.x1, b.total, flow, flow, b.small, S_ATTN, b.grads)
    in1[4]()
    tip[4]()
    early.sent()
    feed_back_start(flow, b.low, b.grads, 0)
    feed_back_outer(b.active0, b.low, b.weights, OUT1, still)
    out0[0]()
    out0_end[0]()
    mix[1]()
    norm_rows(x0, b.normed_c, b.small, S_FFN)
    glu[3]()
    feed_back_inner(
        b.normed_c, b.slope0, b.low, raws, b.weights, IN1, b.inner_grads, 0,
        at_points({(1, 0): (in0[0], out0[1]), (2, 0): (out0_end[1],)}),
    )
    in0_end[0]()
    in0[1]()
    att[3]()
    product_back(b.slope0, None, b.total, b.weights, IN0, 4, still)
    in0_end[1]()
    norm_back(x0, b.total, flow, b.x3, b.small, S_FFN, b.grads)
    save_grad_x = pltpu.make_async_copy(b.x3, b.grad_x.at[0], b.edge_sems.at[3])
    save_grad_x.start()
    pack_small_grads(b, place)
    thin = Thin(place, b.edges, b.edge_near, b.edge_part, b.edge_far, b.thin, totals, 2 * (2 * planes + chips))
    thin.start()
    for step in (
        mix[2], thin.turn, out0[2], out0_end[2], in0[2], in0_end[2], glu[4], att[4], thin.finish, mix[3], out0[3], out0_end[3],
        mix[4], in0[3], out0[4], in0_end[3], out0_end[4], in0[4], in0_end[4],
    ):
        step()
    early.sent()
    reduces.sent()
    totals.sent()
    save_output.wait()
    save_grad_x.wait()


def finish_kernel(*refs):
    (
        output_in, grad_x_in, shard, thin, output, grad_x, grad_ffn_norm, grad_ffn_in, grad_ffn_in_bias, grad_ffn_out,
        grad_ffn_out_bias, grad_attn_norm, grad_qkv, grad_attn_out, grad_attn_out_bias, grad_rel, grad_conv_norm, grad_glu,
        grad_glu_bias, grad_depth, grad_batch, grad_conv_out, grad_conv_out_bias, grad_final, taps, semaphores,
    ) = refs
    copies = [
        pltpu.make_async_copy(output_in, output, semaphores.at[0]), pltpu.make_async_copy(grad_x_in, grad_x, semaphores.at[1])
    ]
    for copy in copies:
        copy.start()
    cut = lambda begin, size: shard[begin - IN0 : begin - IN0 + size, :]
    width = grad_final.shape[-1]

    def thin_rows(begin, count):
        rows = []
        for p in range(begin, begin + count):
            rows.append(thin[p % 6 : p % 6 + 1, 16 * (p // 6) : 16 * (p // 6) + width])
        return rows

    for layer in range(2):
        for c in range(FF // D):
            grad_ffn_in[layer, :, D * c : D * c + D] = cut((IN0, IN1)[layer] + 16 * c, 16)
        grad_ffn_out[layer] = cut((OUT0, OUT1)[layer], 64)
        grad_ffn_in_bias[layer : layer + 1, :] = thin[6:7, 64 * layer : 64 * layer + 4 * width]
        for r, row in enumerate(thin_rows(S_FFN + 2 * layer, 2)):
            grad_ffn_norm[layer, r : r + 1, :] = row
    for c in range(3):
        grad_qkv[:, D * c : D * c + D] = cut(QKV + 16 * c, 16)
    grad_attn_out[...] = cut(ATT, 16)
    for c in range(2):
        grad_glu[:, D * c : D * c + D] = cut(GLU + 16 * c, 16)
    grad_conv_out[...] = cut(CONV, 16)
    for ref, begin in (
        (grad_ffn_out_bias, S_FOB), (grad_attn_norm, S_ATTN), (grad_conv_norm, S_CONV), (grad_batch, S_BATCH),
        (grad_final, S_FINAL),
    ):
        for r, row in enumerate(thin_rows(begin, ref.shape[0])):
            ref[r : r + 1, :] = row
    for r, row in enumerate(thin_rows(S_TAPS, TAPS)):
        taps[r : r + 1, 0:width] = row
    grad_depth[...] = taps[...].T[0:width, 0:TAPS]
    grad_attn_out_bias[...] = thin_rows(S_AOB, 1)[0][0]
    grad_conv_out_bias[...] = thin_rows(S_COB, 1)[0][0]
    grad_glu_bias[...] = thin[7:8, 0 : 2 * width][0]
    grad_rel[...] = thin[7:8, 64 : 64 + grad_rel.shape[0]][0]
    for copy in copies:
        copy.wait()


def shape(dims, kind=F32):
    return jax.ShapeDtypeStruct(dims, kind)


def local(*args):
    planes, chips = lax.axis_size("dp"), lax.axis_size("fsdp") // 2
    scratch = scratch_of(planes, chips)
    names = INPUTS + OUTPUTS + tuple(scratch)
    vmem, anywhere = pl.BlockSpec(memory_space=pltpu.VMEM), pl.BlockSpec(memory_space=pl.ANY)
    given = dict(zip(INPUTS, args))
    given["depth_kernel"] = given["depth_kernel"].T
    firsts = [shape((1, L, D), BF16), shape((1, L, D))]
    passed = pl.pallas_call(
        lambda *refs: whole_kernel(names, *refs),
        out_shape=firsts + [shape((GRADS, D)), shape((8, 128))],
        in_specs=[anywhere if name in LOADED else vmem for name in INPUTS],
        out_specs=[anywhere, anywhere, vmem, vmem],
        scratch_shapes=list(scratch.values()),
        compiler_params=pltpu.CompilerParams(collective_id=0, has_side_effects=True, vmem_limit_bytes=VMEM_BYTES),
        name="layer",
    )(*given.values())
    outs = [
        shape(given[name].shape)
        for name in (
            "ffn_norm", "ffn_in", "ffn_in_bias", "ffn_out", "ffn_out_bias", "attn_norm", "qkv_weight", "attn_out",
            "attn_out_bias", "rel_table", "conv_norm", "glu_weight", "glu_bias", "depth_kernel", "batch_norm", "conv_out",
            "conv_out_bias", "final_norm",
        )
    ]
    grads = pl.pallas_call(
        finish_kernel,
        out_shape=firsts + outs,
        in_specs=[anywhere, anywhere, vmem, vmem],
        out_specs=[vmem] * (2 + len(outs)),
        scratch_shapes=[pltpu.VMEM((128, 128), F32), pltpu.SemaphoreType.DMA((2,))],
        name="unpack",
    )(*passed)
    grads = list(grads)
    grads[15] = grads[15].T
    return tuple(grads)


VMEM_BYTES = 127 * 512 * 1024


highest = lax.Precision.HIGHEST


def layer_norm(values, params):
    center = values - jnp.mean(values, axis=-1, keepdims=True)
    spread = jnp.mean(center * center, axis=-1, keepdims=True)
    return center * lax.rsqrt(spread + epsilon) * (1.0 + params[0]) + params[1]


def silu_slope(values):
    sigma = jax.nn.sigmoid(values)
    return sigma * (1.0 + values * (1.0 - sigma))


def product(left, right):
    return jnp.dot(left, right, preferred_element_type=jnp.float32)


def product_left(left, right):
    return lax.dot_general(
        left, right, (((0,), (0,)), ((), ())), preferred_element_type=jnp.float32
    )


def product_right(left, right):
    return lax.dot_general(
        left, right, (((1,), (1,)), ((), ())), preferred_element_type=jnp.float32
    )


def plain_fetch_feed(norms, inner_weight, inner_bias, outer_weight, outer_bias, layer):
    return (
        lax.all_gather(norms[layer], ("dp", "fsdp"), axis=1, tiled=True),
        lax.all_gather(inner_weight[layer], ("dp", "fsdp"), axis=0, tiled=True),
        lax.all_gather(inner_bias[layer], ("dp", "fsdp"), axis=0, tiled=True),
        lax.all_gather(outer_weight[layer], ("dp", "fsdp"), axis=0, tiled=True),
        lax.all_gather(outer_bias[layer], ("dp", "fsdp"), axis=0, tiled=True),
    )


def plain_reduce_feed(grads):
    return (
        lax.psum_scatter(grads[0], ("dp", "fsdp"), scatter_dimension=1, tiled=True),
        lax.psum_scatter(grads[1], ("dp", "fsdp"), scatter_dimension=0, tiled=True),
        lax.psum_scatter(grads[2], ("dp", "fsdp"), scatter_dimension=0, tiled=True),
        lax.psum_scatter(grads[3], ("dp", "fsdp"), scatter_dimension=0, tiled=True),
        lax.psum_scatter(grads[4], ("dp", "fsdp"), scatter_dimension=0, tiled=True),
    )


def fetch_attention(attn_norm, qkv_weight, attn_out, attn_out_bias, rel_table):
    return (
        lax.all_gather(attn_norm, ("dp", "fsdp"), axis=1, tiled=True),
        lax.all_gather(qkv_weight, ("dp", "fsdp"), axis=0, tiled=True),
        lax.all_gather(attn_out, ("dp", "fsdp"), axis=0, tiled=True),
        lax.all_gather(attn_out_bias, ("dp", "fsdp"), axis=0, tiled=True),
        lax.all_gather(rel_table, ("dp", "fsdp"), axis=0, tiled=True),
    )


def fetch_conv(
    conv_norm, glu_weight, glu_bias, depth_kernel, batch_norm, conv_out, conv_out_bias, final_norm
):
    return (
        lax.all_gather(conv_norm, ("dp", "fsdp"), axis=1, tiled=True),
        lax.all_gather(glu_weight, ("dp", "fsdp"), axis=0, tiled=True),
        lax.all_gather(glu_bias, ("dp", "fsdp"), axis=0, tiled=True),
        lax.all_gather(depth_kernel, ("dp", "fsdp"), axis=1, tiled=True),
        lax.all_gather(batch_norm, ("dp", "fsdp"), axis=1, tiled=True),
        lax.all_gather(conv_out, ("dp", "fsdp"), axis=0, tiled=True),
        lax.all_gather(conv_out_bias, ("dp", "fsdp"), axis=0, tiled=True),
        lax.all_gather(final_norm, ("dp", "fsdp"), axis=1, tiled=True),
    )


def plain_feed_forward(values, weights):
    norm, weight_in, bias_in, weight_out, bias_out = weights
    normed, norm_back = jax.vjp(layer_norm, values, norm.astype(jnp.float32))
    normed_low = normed.astype(jnp.bfloat16)
    inner = product(normed_low, weight_in) + bias_in.astype(jnp.float32)
    active = jax.nn.silu(inner).astype(jnp.bfloat16)
    result = values + 0.5 * (product(active, weight_out) + bias_out.astype(jnp.float32))
    return (result, (normed_low, inner, active, norm_back))


def plain_feed_backward(upstream, weights, saved):
    norm, weight_in, bias_in, weight_out, bias_out = weights
    normed_low, inner, active, norm_back = saved
    branch = 0.5 * upstream
    branch_low = branch.astype(jnp.bfloat16)
    grad_weight_out = product_left(active, branch_low)
    grad_inner = product_right(branch_low, weight_out) * silu_slope(inner)
    inner_low = grad_inner.astype(jnp.bfloat16)
    grad_weight_in = product_left(normed_low, inner_low)
    grad_values, grad_norm = norm_back(product_right(inner_low, weight_in))
    return (
        upstream + grad_values,
        (
            grad_norm,
            grad_weight_in,
            jnp.sum(grad_inner, axis=0),
            grad_weight_out,
            jnp.sum(branch, axis=0),
        ),
    )


def relative_lines(table, buckets):
    choose = (buckets[None, :] == jnp.arange(BUCKETS, dtype=jnp.int32)[:, None]).astype(jnp.float32)
    lines = jnp.dot(table.astype(jnp.float32).reshape(HEADS, BUCKETS), choose, precision=highest)
    return (lines, choose)


def bias_square(line, length):
    tiled = jnp.broadcast_to(line, (length, 2 * length - 1)).reshape(-1)
    tiled = jnp.concatenate([tiled, jnp.zeros((length,), line.dtype)])
    return tiled.reshape(length, 2 * length)[:, :length][::-1]


def diagonal_sums(square):
    length = square.shape[0]
    padded = jnp.concatenate([square[::-1], jnp.zeros_like(square)], axis=1).reshape(-1)
    return jnp.sum(padded[: length * (2 * length - 1)].reshape(length, 2 * length - 1), axis=0)


def head_scores(query, keys_head, line, same):
    raw = product_right(query, keys_head)
    return jnp.where(same, raw * HEAD_DIM ** (-0.5) + bias_square(line, query.shape[0]), -1e30)


def plain_attention_forward(values, weights, marks, buckets):
    norm, mixer, weight_out, bias_out, table = weights
    length = values.shape[0]
    normed, norm_back = jax.vjp(layer_norm, values, norm.astype(jnp.float32))
    normed_low = normed.astype(jnp.bfloat16)
    mixed = (
        product(normed_low, mixer)
        .astype(jnp.bfloat16)
        .reshape(length, 3, HEADS, HEAD_DIM)
        .transpose(1, 2, 0, 3)
    )
    lines, choose = relative_lines(table, buckets)
    same = marks[:, None] == marks[None, :]

    def head_forward(items):
        query, keys_head, contents, line = items
        scores = head_scores(query, keys_head, line, same)
        peak = jnp.max(scores, axis=1, keepdims=True)
        raised = jnp.exp(scores - peak)
        total = jnp.sum(raised, axis=1, keepdims=True)
        probs = (raised / total).astype(jnp.bfloat16)
        return (product(probs, contents).astype(jnp.bfloat16), (peak + jnp.log(total))[:, 0])

    attended, logsum = lax.map(head_forward, (mixed[0], mixed[1], mixed[2], lines))
    joined = attended.transpose(1, 0, 2).reshape(length, D)
    result = values + product(joined, weight_out) + bias_out.astype(jnp.float32)
    return (result, (normed_low, mixed, lines, choose, same, joined, logsum, norm_back))


def plain_attention_backward(upstream, weights, saved):
    norm, mixer, weight_out, bias_out, table = weights
    normed_low, mixed, lines, choose, same, joined, logsum, norm_back = saved
    length = upstream.shape[0]
    upstream_low = upstream.astype(jnp.bfloat16)
    grad_weight_out = product_left(joined, upstream_low)
    grad_joined = (
        product_right(upstream_low, weight_out)
        .astype(jnp.bfloat16)
        .reshape(length, HEADS, HEAD_DIM)
        .transpose(1, 0, 2)
    )

    def head_backward(items):
        query, keys_head, contents, line, incoming, logs = items
        scores = head_scores(query, keys_head, line, same)
        probs = jnp.exp(scores - logs[:, None])
        grad_contents = product_left(probs.astype(jnp.bfloat16), incoming)
        grad_probs = product_right(incoming, contents)
        grad_scores = probs * (grad_probs - jnp.sum(grad_probs * probs, axis=1, keepdims=True))
        scaled = (grad_scores * HEAD_DIM ** (-0.5)).astype(jnp.bfloat16)
        grad_query = product(scaled, keys_head)
        grad_keys = product_left(scaled, query)
        return (
            jnp.stack([grad_query, grad_keys, grad_contents]).astype(jnp.bfloat16),
            diagonal_sums(grad_scores),
        )

    grad_mixed, grad_lines = lax.map(
        head_backward, (mixed[0], mixed[1], mixed[2], lines, grad_joined, logsum)
    )
    grad_flat = grad_mixed.transpose(2, 1, 0, 3).reshape(length, 3 * D)
    grad_mixer = product_left(normed_low, grad_flat)
    grad_values, grad_norm = norm_back(product_right(grad_flat, mixer))
    grad_table = jnp.dot(grad_lines, choose.T, precision=highest).reshape(-1)
    return (
        upstream + grad_values,
        (grad_norm, grad_mixer, grad_weight_out, jnp.sum(upstream, axis=0), grad_table),
    )


def gate_unit(joined):
    width = joined.shape[1] // 2
    return joined[:, :width] * jax.nn.sigmoid(joined[:, width:])


def plain_depthwise(gated, kernel, marks):
    length = gated.shape[0]
    half = kernel.shape[0] // 2
    padded = jnp.pad(gated, ((half, half), (0, 0)))
    bounds = jnp.pad(marks, (half, half), constant_values=-1)
    total = jnp.zeros(gated.shape, gated.dtype)
    for step in range(kernel.shape[0]):
        same = (bounds[step : step + length] == marks)[:, None]
        total = total + jnp.where(same, padded[step : step + length], 0.0) * kernel[step]
    return total


def plain_conv_forward(values, weights, marks, frames):
    norm, weight_glu, bias_glu, kernel, batch, weight_out, bias_out, final = weights
    normed, norm_back = jax.vjp(layer_norm, values, norm.astype(jnp.float32))
    normed_low = normed.astype(jnp.bfloat16)
    joined = product(normed_low, weight_glu) + bias_glu.astype(jnp.float32)
    gated, gate_back = jax.vjp(gate_unit, joined)
    middle, depth_back = jax.vjp(
        lambda inner, taps: plain_depthwise(inner, taps, marks), gated, kernel.astype(jnp.float32)
    )
    sums = lax.psum((jnp.sum(middle, axis=0), jnp.sum(middle * middle, axis=0)), ("dp", "fsdp"))
    center = sums[0] / frames
    inverse = lax.rsqrt(sums[1] / frames - center * center + epsilon)
    gain = 1.0 + batch[0].astype(jnp.float32)
    unit = (middle - center) * inverse
    normal = unit * gain + batch[1].astype(jnp.float32)
    active = jax.nn.silu(normal).astype(jnp.bfloat16)
    result = values + product(active, weight_out) + bias_out.astype(jnp.float32)
    return (
        result,
        (normed_low, gate_back, depth_back, inverse, gain, unit, normal, active, norm_back),
    )


def plain_conv_backward(upstream, weights, saved, frames):
    norm, weight_glu, bias_glu, kernel, batch, weight_out, bias_out, final = weights
    normed_low, gate_back, depth_back, inverse, gain, unit, normal, active, norm_back = saved
    upstream_low = upstream.astype(jnp.bfloat16)
    grad_weight_out = product_left(active, upstream_low)
    grad_normal = product_right(upstream_low, weight_out) * silu_slope(normal)
    sums = lax.psum(
        (jnp.sum(grad_normal, axis=0), jnp.sum(grad_normal * unit, axis=0)), ("dp", "fsdp")
    )
    grad_middle = inverse * (
        grad_normal * gain - gain * sums[0] / frames - unit * (gain * sums[1] / frames)
    )
    grad_gated, grad_kernel = depth_back(grad_middle)
    grad_joined = gate_back(grad_gated)[0]
    joined_low = grad_joined.astype(jnp.bfloat16)
    grad_weight_glu = product_left(normed_low, joined_low)
    grad_values, grad_norm = norm_back(product_right(joined_low, weight_glu))
    grad_batch = jnp.stack([sums[1], sums[0]])
    return (
        upstream + grad_values,
        (
            grad_norm,
            grad_weight_glu,
            jnp.sum(grad_joined, axis=0),
            grad_kernel,
            grad_weight_out,
            jnp.sum(upstream, axis=0),
        ),
        grad_batch,
    )


def plain(
    inputs,
    segments,
    buckets,
    cotangent,
    ffn_norm,
    ffn_in,
    ffn_in_bias,
    ffn_out,
    ffn_out_bias,
    attn_norm,
    qkv_weight,
    attn_out,
    attn_out_bias,
    rel_table,
    conv_norm,
    glu_weight,
    glu_bias,
    depth_kernel,
    batch_norm,
    conv_out,
    conv_out_bias,
    final_norm,
):
    values = inputs[0].astype(jnp.float32)
    marks = segments[0]
    devices = lax.axis_size(("dp", "fsdp"))
    frames = values.shape[0] * devices
    feed_first = plain_fetch_feed(ffn_norm, ffn_in, ffn_in_bias, ffn_out, ffn_out_bias, 0)
    first, first_saved = plain_feed_forward(values, feed_first)
    attn_weights = fetch_attention(attn_norm, qkv_weight, attn_out, attn_out_bias, rel_table)
    second, attn_saved = plain_attention_forward(first, attn_weights, marks, buckets)
    conv_weights = fetch_conv(
        conv_norm,
        glu_weight,
        glu_bias,
        depth_kernel,
        batch_norm,
        conv_out,
        conv_out_bias,
        final_norm,
    )
    third, conv_saved = plain_conv_forward(second, conv_weights, marks, frames)
    feed_second = plain_fetch_feed(ffn_norm, ffn_in, ffn_in_bias, ffn_out, ffn_out_bias, 1)
    fourth, second_saved = plain_feed_forward(third, feed_second)
    result, final_back = jax.vjp(layer_norm, fourth, conv_weights[7].astype(jnp.float32))
    grad_fourth, grad_final = final_back(cotangent[0].astype(jnp.float32))
    second_back = plain_fetch_feed(ffn_norm, ffn_in, ffn_in_bias, ffn_out, ffn_out_bias, 1)
    grad_third, second_grads = plain_feed_backward(grad_fourth, second_back, second_saved)
    conv_back = fetch_conv(
        conv_norm,
        glu_weight,
        glu_bias,
        depth_kernel,
        batch_norm,
        conv_out,
        conv_out_bias,
        final_norm,
    )
    grad_second, conv_grads, grad_batch = plain_conv_backward(grad_third, conv_back, conv_saved, frames)
    attn_back = fetch_attention(attn_norm, qkv_weight, attn_out, attn_out_bias, rel_table)
    grad_first, attn_grads = plain_attention_backward(grad_second, attn_back, attn_saved)
    first_back = plain_fetch_feed(ffn_norm, ffn_in, ffn_in_bias, ffn_out, ffn_out_bias, 0)
    grad_start, first_grads = plain_feed_backward(grad_first, first_back, first_saved)
    first_shards = plain_reduce_feed(first_grads)
    second_shards = plain_reduce_feed(second_grads)
    attn_shards = (
        lax.psum_scatter(attn_grads[0], ("dp", "fsdp"), scatter_dimension=1, tiled=True),
        lax.psum_scatter(attn_grads[1], ("dp", "fsdp"), scatter_dimension=0, tiled=True),
        lax.psum_scatter(attn_grads[2], ("dp", "fsdp"), scatter_dimension=0, tiled=True),
        lax.psum_scatter(attn_grads[3], ("dp", "fsdp"), scatter_dimension=0, tiled=True),
        lax.psum_scatter(attn_grads[4], ("dp", "fsdp"), scatter_dimension=0, tiled=True),
    )
    conv_shards = (
        lax.psum_scatter(conv_grads[0], ("dp", "fsdp"), scatter_dimension=1, tiled=True),
        lax.psum_scatter(conv_grads[1], ("dp", "fsdp"), scatter_dimension=0, tiled=True),
        lax.psum_scatter(conv_grads[2], ("dp", "fsdp"), scatter_dimension=0, tiled=True),
        lax.psum_scatter(conv_grads[3], ("dp", "fsdp"), scatter_dimension=1, tiled=True),
        lax.psum_scatter(conv_grads[4], ("dp", "fsdp"), scatter_dimension=0, tiled=True),
        lax.psum_scatter(conv_grads[5], ("dp", "fsdp"), scatter_dimension=0, tiled=True),
        lax.psum_scatter(grad_final, ("dp", "fsdp"), scatter_dimension=1, tiled=True),
    )
    width = D // devices
    batch_shard = lax.dynamic_slice_in_dim(
        grad_batch, lax.axis_index(("dp", "fsdp")) * width, width, 1
    )
    return (
        result[None].astype(jnp.bfloat16),
        grad_start[None],
        jnp.stack([first_shards[0], second_shards[0]]),
        jnp.stack([first_shards[1], second_shards[1]]),
        jnp.stack([first_shards[2], second_shards[2]]),
        jnp.stack([first_shards[3], second_shards[3]]),
        jnp.stack([first_shards[4], second_shards[4]]),
        attn_shards[0],
        attn_shards[1],
        attn_shards[2],
        attn_shards[3],
        attn_shards[4],
        conv_shards[0],
        conv_shards[1],
        conv_shards[2],
        conv_shards[3],
        batch_shard,
        conv_shards[4],
        conv_shards[5],
        conv_shards[6],
    )


def solution(mesh):
    in_specs = (
        P(("dp", "fsdp"), None, None),
        P(("dp", "fsdp"), None),
        P(),
        P(("dp", "fsdp"), None, None),
        P(None, None, ("dp", "fsdp")),
        P(None, ("dp", "fsdp"), None),
        P(None, ("dp", "fsdp")),
        P(None, ("dp", "fsdp"), None),
        P(None, ("dp", "fsdp")),
        P(None, ("dp", "fsdp")),
        P(("dp", "fsdp"), None),
        P(("dp", "fsdp"), None),
        P(("dp", "fsdp")),
        P(("dp", "fsdp")),
        P(None, ("dp", "fsdp")),
        P(("dp", "fsdp"), None),
        P(("dp", "fsdp")),
        P(None, ("dp", "fsdp")),
        P(None, ("dp", "fsdp")),
        P(("dp", "fsdp"), None),
        P(("dp", "fsdp")),
        P(None, ("dp", "fsdp")),
    )
    out_specs = (
        P(("dp", "fsdp"), None, None),
        P(("dp", "fsdp"), None, None),
        P(None, None, ("dp", "fsdp")),
        P(None, ("dp", "fsdp"), None),
        P(None, ("dp", "fsdp")),
        P(None, ("dp", "fsdp"), None),
        P(None, ("dp", "fsdp")),
        P(None, ("dp", "fsdp")),
        P(("dp", "fsdp"), None),
        P(("dp", "fsdp"), None),
        P(("dp", "fsdp")),
        P(("dp", "fsdp")),
        P(None, ("dp", "fsdp")),
        P(("dp", "fsdp"), None),
        P(("dp", "fsdp")),
        P(None, ("dp", "fsdp")),
        P(None, ("dp", "fsdp")),
        P(("dp", "fsdp"), None),
        P(("dp", "fsdp")),
        P(None, ("dp", "fsdp")),
    )
    fast = mesh.shape["dp"] == 4 and mesh.shape["fsdp"] == 8
    return jax.shard_map(local if fast else plain, mesh=mesh, in_specs=in_specs, out_specs=out_specs, check_vma=False)
```
